32 devices in a mesh: sector: 16 (over z, y, core), radial: 2 (over x).
Axes of the slice: x: 2, y: 2, z: 4, core: 2. Of those that a mesh axis runs over, the one named last changes fastest.
Arguments:
- fields: float32 [16, 2, 140, 1024], P('sector', 'radial'), may hold values from -6 to 6
- pattern: int32 [16, 2, 1024], P('sector', 'radial'), may hold values from 0 to 15
- tent_order: int32 [16, 2, 1024], P('sector', 'radial'), may hold values from 0 to 1023, each once within a row
- level_sizes: int32 [16, 2, 4], P('sector', 'radial'), may hold values from 1 to 384, 1024 in all within a row
- send_rows: int32 [16, 2, 4, 128], P('sector', 'radial'), may hold values from 0 to 1023
- neighbours: int32 [16, 2, 4, 1024], P('sector', 'radial'), may hold values from 0 to 1535, as said below
- operator: float32 [140, 140], replicated, may hold values from -2 to 2, as said below
- trace_map: float32 [60, 140], replicated, may hold values from -0.5 to 0.5
- lift_map: float32 [4, 140, 60], replicated, may hold values from -0.375 to 0.375
- tent_height: float32 [16], replicated, may hold values from 0.15 to 0.5
Outputs:
- advanced: float32 [16, 2, 140, 1024], P('sector', 'radial')
The draws below stay inside these ranges and needn't reach their ends.
Inputs may be any that keep to these rules, and one draw needn't show every extreme that they name: `tent_order`: each block's entries are a permutation of 0 to 1023. `level_sizes`: each block's 4 sizes sum to 1024, and some level of every block has exactly 384 tents. `neighbours`: an entry below 1024 names an element of the same block; an entry 1024 + d * 128 + j names the j-th received trace of group d of extended; each of these 512 slots is named by face 0 of exactly one element of the block. `operator`: a skew-symmetric matrix minus a diagonal of positive damping rates.
All inputs are finite; a program needn't handle non-finite values.
Results may differ from the reference program's by a relative error of at most 0.0003.
Values sent between devices are 32-bit elements; how exact they have to be, the bound alone decides.
No kernel may reach another device: no remote copies, remote signals or barrier semaphores. Data moves between devices by JAX's collectives and lax.ppermute only.
A program may use at most 64 MiB of HBM per device.

```python
import math
import jax
import jax.numpy as jnp
import numpy as np
from jax import lax

FACES = 4
PATTERNS = 16
LEVELS = 4
SUBSTEPS = 2
TERMS = 4
ELEMS = 1024
COMP = 140
TRACE = 60
BND = 128
BLOCK = 384
SECS = 16
RADS = 2


def draw_neighbours(key, part):

    def one_block(block_key):
        key_local, key_order = jax.random.split(block_key)
        local_faces = jax.random.randint(key_local, (FACES, ELEMS), 0, ELEMS, dtype=jnp.int32)
        shuffled = jax.random.permutation(key_order, ELEMS)
        slots = ELEMS + jnp.arange(4 * BND, dtype=jnp.int32)
        first_face = local_faces[0].at[shuffled[:4 * BND]].set(slots)
        return local_faces.at[0].set(first_face)
    block_keys = jax.random.split(jax.random.fold_in(key, 17), SECS * RADS)
    drawn = jax.vmap(one_block)(block_keys)
    return drawn.reshape(SECS, RADS, FACES, ELEMS).astype(jnp.int32)


def draw_operator(key, part):
    key_skew, key_damp = jax.random.split(jax.random.fold_in(key, 29))
    gaussian = jax.random.normal(key_skew, (COMP, COMP), jnp.float32) / jnp.sqrt(COMP * 1.0)
    rotation = (gaussian - gaussian.T) / jnp.sqrt(2.0)
    damping = jnp.exp(jax.random.uniform(key_damp, (COMP,), jnp.float32, jnp.log(0.1), jnp.log(0.5)))
    return (rotation - jnp.diag(damping)).astype(jnp.float32)


def place_ends(values, key, smallest, high):
    extent = values.shape
    index_at = [jax.random.randint(jax.random.fold_in(key, axis), (), 0, extent[axis]) for axis in range(len(extent))]
    values = values.at[tuple(index_at)].set(smallest)
    longest = extent.index(max(extent))
    index_at[longest] = (index_at[longest] + 1) % extent[longest]
    return values.at[tuple(index_at)].set(high)


def level_of(rng, shape, cuts, low, high):
    def one(position, shards_of):
        steps = jax.random.uniform(jax.random.fold_in(jax.random.fold_in(rng, 6), position), (shards_of,), jnp.float32, low / len(cuts), high / len(cuts))
        return jnp.repeat(jnp.exp(steps), shape[position] // shards_of).reshape((-1,) + (1,) * (len(shape) - position - 1))

    loudness = one(*cuts[0])
    for cut in cuts[1:]:
        loudness = loudness * one(*cut)
    return loudness


def split_up(number_of, total, bound, lean):
    weights = [(1 << 20) // math.isqrt(rank ** lean) + 1 for rank in range(2, number_of + 1)]
    surplus, counts = total - bound - (number_of - 1), [1] * (number_of - 1)
    while surplus > 0:
        movable = [i for i in range(number_of - 1) if counts[i] < bound]
        whole, left = sum([weights[i] for i in movable]), surplus
        for i in movable:
            extra = min(bound - counts[i], max(1, left * weights[i] // whole), surplus)
            counts[i] = counts[i] + extra
            surplus = surplus - extra
    return np.array([bound] + counts)


def uneven_parts(own_key, number_of, total, bound, lean):
    if number_of == 2:
        one = jax.random.randint(own_key, (), max(1, total - bound), min(bound, total - 1) + 1)
        return jnp.stack([one, total - one])
    sizes = jnp.asarray(split_up(number_of, total, bound, lean), jnp.int32)
    twos = (number_of - 1) // 2
    source_of, sink = sizes[1:1 + 2 * twos:2], sizes[2:2 + 2 * twos:2]
    slack = jnp.minimum(source_of - 1, bound - sink)
    shifted = jax.random.randint(jax.random.fold_in(own_key, 1), (twos,), 0, 1 << 20) % (slack + 1)
    sizes = sizes.at[1:1 + 2 * twos:2].set(source_of - shifted).at[2:2 + 2 * twos:2].set(sink + shifted)
    return sizes[jax.random.permutation(jax.random.fold_in(own_key, 2), number_of)]


def bell_draw(own_key, dims, deviation, reach, cuts=(), kind=jnp.bfloat16):
    array = deviation * jax.random.normal(own_key, dims, jnp.float32)
    if cuts:
        array = array * level_of(own_key, dims, cuts, -0.22, 0.18)
    return jnp.clip(array, -reach, reach).astype(kind)


def setup_inputs(seed: int = 0) -> dict:
    keys = jax.random.split(jax.random.key(seed), 11)
    fields = bell_draw(keys[0], (SECS, RADS, COMP, ELEMS), 1.0, 6.0, ((0, 16), (1, 2)), jnp.float32)
    pattern = place_ends(jax.random.randint(keys[1], (SECS, RADS, ELEMS), 0, PATTERNS), jax.random.fold_in(keys[1], 1), 0, PATTERNS - 1).astype(jnp.int32)
    tent_order = jax.vmap(lambda own: jax.random.permutation(own, ELEMS))(jax.random.split(keys[2], SECS * RADS)).reshape((SECS, RADS, ELEMS)).astype(jnp.int32)
    level_sizes = jax.vmap(lambda own: uneven_parts(own, LEVELS, ELEMS, BLOCK, 1))(jax.random.split(keys[3], SECS * RADS)).reshape((SECS, RADS, LEVELS)).astype(jnp.int32)
    send_rows = place_ends(jax.random.randint(keys[4], (SECS, RADS, 4, BND), 0, ELEMS), jax.random.fold_in(keys[4], 1), 0, ELEMS - 1).astype(jnp.int32)
    neighbours = draw_neighbours(jax.random.fold_in(keys[10], 71), 0)
    operator = draw_operator(jax.random.fold_in(keys[10], 71), 0)
    trace_map = bell_draw(keys[7], (TRACE, COMP), COMP ** -0.5, 0.5, (), jnp.float32)
    lift_map = bell_draw(keys[8], (FACES, COMP, TRACE), (FACES * TRACE) ** -0.5, 0.375, (), jnp.float32)
    tent_height = jnp.clip(jnp.exp(jax.random.uniform(keys[9], (PATTERNS,), jnp.float32, math.log(0.15), math.log(0.5))), 0.15, 0.5)
    return {"fields": fields, "pattern": pattern, "tent_order": tent_order, "level_sizes": level_sizes, "send_rows": send_rows, "neighbours": neighbours, "operator": operator, "trace_map": trace_map, "lift_map": lift_map, "tent_height": tent_height}


precise = lax.Precision.HIGHEST


def propagate(loaded, heights, operator):
    for substep in range(SUBSTEPS):
        term_now = loaded
        summed = loaded
        for degree in range(1, TERMS + 1):
            term_now = jnp.dot(operator, term_now, precision=precise) * (heights / degree)
            summed = summed + term_now
        loaded = summed
    return loaded


def face_columns(source, faces_of):
    gathered = jnp.take(source, faces_of.reshape(-1), axis=1, mode="clip")
    gathered = gathered.reshape(source.shape[0], faces_of.shape[0], faces_of.shape[1])
    return jnp.transpose(gathered, (1, 0, 2)).reshape(-1, faces_of.shape[1])


def pick_rows(source, rows):
    picked = jnp.take(source, rows.reshape(-1), axis=1)
    return picked.reshape(source.shape[0], rows.shape[0], rows.shape[1])


def reference(fields, pattern, tent_order, level_sizes, send_rows, neighbours, operator, trace_map, lift_map, tent_height):
    heights_all = tent_height[pattern]
    starts = (jnp.cumsum(level_sizes, axis=-1) - level_sizes).astype(jnp.int32)
    tent_rows = jnp.concatenate([tent_order, jnp.zeros((SECS, RADS, BLOCK), jnp.int32)], axis=-1)
    lift_matrix = jnp.transpose(lift_map, (1, 0, 2)).reshape(lift_map.shape[1], -1)
    slot_ids = jnp.arange(BLOCK, dtype=jnp.int32)
    current = fields
    for level_index in range(LEVELS):
        outflow = jnp.einsum("tc,srce->srte", trace_map, current, precision=precise)
        outgoing = jax.vmap(jax.vmap(pick_rows))(outflow, send_rows)
        from_below = jnp.roll(outgoing[:, :, :, 0], 1, axis=0)
        from_above = jnp.roll(outgoing[:, :, :, 1], -1, axis=0)
        empty_rim = jnp.zeros_like(outgoing[:, :1, :, 2])
        inner_rim = jnp.concatenate([empty_rim, outgoing[:, :-1, :, 2]], axis=1)
        outer_rim = jnp.concatenate([outgoing[:, 1:, :, 3], empty_rim], axis=1)
        extended = jnp.concatenate([outflow, from_below, from_above, inner_rim, outer_rim], axis=-1)

        def advance(block_now, block_ext, block_faces, block_heights, block_rows, block_starts, block_counts):
            members = lax.dynamic_slice_in_dim(block_rows, block_starts[level_index], BLOCK)
            filled = slot_ids < block_counts[level_index]
            columns = jnp.take(block_now, members, axis=1)
            faces_of = jnp.take(block_faces, members, axis=1)
            loaded = columns + jnp.dot(lift_matrix, face_columns(block_ext, faces_of), precision=precise)
            loaded = propagate(loaded, jnp.take(block_heights, members), operator)
            target = jnp.where(filled, members, block_now.shape[1])
            return block_now.at[:, target].set(loaded, mode="drop")

        current = jax.vmap(jax.vmap(advance))(current, extended, neighbours, heights_all, tent_rows, starts, level_sizes)
    return current
```

```python
import jax
import jax.numpy as jnp
from jax import lax
from jax.sharding import PartitionSpec as P

LEVELS = 4
SUBSTEPS = 2
TERMS = 4
BLOCK = 384


precise = lax.Precision.HIGHEST


def pair_swaps(axis, to_up, to_down, periodic):
    count = lax.axis_size(axis)
    index = lax.axis_index(axis)
    odd = (index % 2) == 1
    first = [(i, i ^ 1) for i in range(count)]
    got_first = lax.ppermute(jnp.where(odd, to_down, to_up), axis, first)
    if count == 2 and not periodic:
        got_second = jnp.zeros_like(got_first)
    else:
        second = [(i, (i + 1) % count if i % 2 else (i - 1) % count) for i in range(count)]
        got_second = lax.ppermute(jnp.where(odd, to_up, to_down), axis, second)
    from_below = jnp.where(odd, got_first, got_second)
    from_above = jnp.where(odd, got_second, got_first)
    if not periodic:
        from_below = jnp.where(index == 0, 0.0, from_below)
        from_above = jnp.where(index == count - 1, 0.0, from_above)
    return from_below, from_above


def propagate(loaded, heights, operator):
    for substep in range(SUBSTEPS):
        term_now = loaded
        summed = loaded
        for degree in range(1, TERMS + 1):
            term_now = jnp.dot(operator, term_now, precision=precise) * (heights / degree)
            summed = summed + term_now
        loaded = summed
    return loaded


def face_stack(source, faces_of):
    gathered = jnp.take(source, faces_of.reshape(-1), axis=1, mode="clip")
    gathered = gathered.reshape(source.shape[0], faces_of.shape[0], faces_of.shape[1])
    return jnp.transpose(gathered, (1, 0, 2))


def receive_rims(outgoing):
    below, above = pair_swaps("sector", outgoing[0], outgoing[1], True)
    inner, outer = pair_swaps("radial", outgoing[2], outgoing[3], False)
    return jnp.concatenate([below, above, inner, outer], axis=1)


def body(
    fields,
    pattern,
    tent_order,
    level_sizes,
    send_rows,
    neighbours,
    operator,
    trace_map,
    lift_map,
    tent_height,
):
    current = fields[0, 0]
    elements = current.shape[1]
    send_list = send_rows[0, 0]
    border = send_list.shape[1]
    faces_all = neighbours[0, 0]
    counts = level_sizes[0, 0]
    starts = jnp.cumsum(counts) - counts
    tent_rows = jnp.concatenate([tent_order[0, 0], jnp.zeros((BLOCK,), jnp.int32)])
    pattern_ids = jnp.arange(tent_height.shape[0], dtype=jnp.int32)
    heights_all = jnp.sum(
        jnp.where(pattern[0, 0][None, :] == pattern_ids[:, None], tent_height[:, None], 0.0), axis=0
    )
    lift_matrix = jnp.transpose(lift_map, (1, 0, 2)).reshape(lift_map.shape[1], -1)
    slot_ids = jnp.arange(BLOCK, dtype=jnp.int32)
    for level_index in range(LEVELS):
        outflow = jnp.dot(trace_map, current, precision=precise)
        outgoing = jnp.take(outflow, send_list.reshape(-1), axis=1).reshape(
            outflow.shape[0], 4, border
        )
        outgoing = jnp.transpose(outgoing, (1, 0, 2))
        members = lax.dynamic_slice_in_dim(tent_rows, starts[level_index], BLOCK)
        filled = slot_ids < counts[level_index]
        columns = jnp.take(current, members, axis=1)
        faces_of = jnp.take(faces_all, members, axis=1)
        heights = jnp.take(heights_all, members)
        received = receive_rims(outgoing)
        extended = jnp.concatenate([outflow, received], axis=1)
        inflow = jnp.dot(
            lift_matrix, face_stack(extended, faces_of).reshape(-1, BLOCK), precision=precise
        )
        loaded = propagate(columns + inflow, heights, operator)
        target = jnp.where(filled, members, elements)
        current = current.at[:, target].set(loaded, mode="drop")
    return current[None, None]


def solution(mesh):
    in_specs = (
        P("sector", "radial", None, None),
        P("sector", "radial", None),
        P("sector", "radial", None),
        P("sector", "radial", None),
        P("sector", "radial", None, None),
        P("sector", "radial", None, None),
        P(),
        P(),
        P(),
        P(),
    )
    out_specs = P("sector", "radial", None, None)
    return jax.shard_map(body, mesh=mesh, in_specs=in_specs, out_specs=out_specs, check_vma=False)
```

```python
import functools
import math

import jax
import jax.numpy as jnp
from jax import lax
from jax.experimental import pallas as pl
from jax.experimental.pallas import tpu as pltpu
from jax.sharding import PartitionSpec as P

LEVELS = 4
SUBSTEPS = 2
TERMS = 4
BLOCK = 384
LANES = 128
NO_GROUP = 1 << 20

f32, bf16, i32 = jnp.float32, jnp.bfloat16, jnp.int32
precise = lax.Precision.HIGHEST


def rounded_up(size, unit):
    return -(-size // unit) * unit


def taylor_weights():
    once = [1.0 / math.factorial(k) for k in range(TERMS + 1)]
    whole = [1.0]
    for _ in range(SUBSTEPS):
        longer = [0.0] * (len(whole) + TERMS)
        for i, a in enumerate(whole):
            for j, b in enumerate(once):
                longer[i + j] += a * b
        whole = longer
    return whole


WEIGHTS = taylor_weights()
POWERS = len(WEIGHTS) - 1


def split(values):
    high = values.astype(bf16)
    return high, (values - high.astype(f32)).astype(bf16)


def stacked_columns(values):
    high, low = split(values)
    return jnp.concatenate([high, low, high], axis=0)


def stacked_matrix(values):
    high = values.astype(bf16).astype(f32)
    low = values - high
    return jnp.concatenate([high, high, low], axis=1).astype(bf16)


def product(matrix, columns):
    return jnp.dot(matrix, columns, preferred_element_type=f32)


def pad_rows(values, rows):
    short = rows - values.shape[0]
    if short == 0:
        return values
    return jnp.concatenate([values, jnp.zeros((short,) + values.shape[1:], values.dtype)], axis=0)


def pick(blocks, index, which, start=None):
    result = start
    for number, read in blocks:
        table = read()
        lane = jnp.broadcast_to(index & (LANES - 1), table.shape)
        got = jnp.take_along_axis(table, lane, axis=1, mode="promise_in_bounds")
        if result is None:
            result = got
        else:
            result = jnp.where(jnp.broadcast_to(which, table.shape) == number, got, result)
    return result


def ref_blocks(ref, count, rows=None):
    def reader(b):
        def read():
            values = ref[:, b * LANES:(b + 1) * LANES]
            return values if rows is None else pad_rows(values, rows)
        return read
    return [(b, reader(b)) for b in range(count)]


def value_blocks(values):
    return [
        (b, functools.partial(lambda b: values[:, b * LANES:(b + 1) * LANES], b))
        for b in range(values.shape[1] // LANES)
    ]


def first_kernel(fields_ref, trace_ref, send_ref, out_ref, *sends):
    rows = out_ref.shape[0]
    trace = pad_rows(trace_ref[...], rows)
    trace_high, trace_low = split(trace)
    both = jnp.concatenate([trace_high, trace_low], axis=0)
    high, low = split(fields_ref[...])
    upper = product(both, high)
    out_ref[...] = upper[:rows] + upper[rows:] + product(trace_high, low)
    count = out_ref.shape[1] // LANES
    for group, send in enumerate(sends):
        index = send_ref[group:group + 1, :]
        send[...] = pick(ref_blocks(out_ref, count), index, index >> 7)


def level_starts(sizes_ref):
    starts = [jnp.int32(0)]
    for level in range(LEVELS - 1):
        starts.append(starts[-1] + sizes_ref[level])
    return starts


def local_part(level, members_ref, joined_ref, fields_ref, out_ref, heights_ref, own_ref, faces_ref, weights_ref):
    faces = faces_in(joined_ref)
    count = fields_ref.shape[1] // LANES
    rows, trace_rows = own_ref.shape[0], out_ref.shape[0]
    for block in range(BLOCK // LANES):
        here = slice(block * LANES, (block + 1) * LANES)
        there = slice(level * BLOCK + block * LANES, level * BLOCK + (block + 1) * LANES)
        index = members_ref[0:1, there]
        own_ref[:, here] = pick(ref_blocks(fields_ref, count, rows), index, index >> 7)
        for face in range(faces):
            index = joined_ref[face:face + 1, there]
            faces_ref[face * trace_rows:(face + 1) * trace_rows, here] = pick(
                ref_blocks(out_ref, count), index, index >> 7)
        pattern = jnp.broadcast_to(joined_ref[faces:faces + 1, there], (8, LANES))
        height = jnp.take_along_axis(
            jnp.broadcast_to(heights_ref[...], (8, LANES)), pattern, axis=1, mode="promise_in_bounds")
        weight = jnp.ones((8, LANES), f32)
        for power in range(1, POWERS + 1):
            weight = weight * height
            weights_ref[power - 1:power, here] = weight[0:1] * WEIGHTS[power]


def faces_in(joined_ref):
    return joined_ref.shape[0] // 2


def matrix_powers(operator_ref, trace_ref, lift_ref, grow_ref, trace_grow_ref, lift_out_ref, rows, trace_rows):
    comp = operator_ref.shape[0]
    operator = pad_rows(operator_ref[...], rows)
    operator = jnp.concatenate([operator, jnp.zeros((rows, rows - comp), f32)], axis=1)
    trace = pad_rows(trace_ref[...], trace_rows)
    trace = jnp.concatenate([trace, jnp.zeros((trace_rows, rows - comp), f32)], axis=1)
    powers = operator
    have = 1
    while have < POWERS:
        take = min(have, POWERS - have)
        more = jnp.dot(powers[:take * rows], powers[(have - 1) * rows:have * rows],
                       precision=precise, preferred_element_type=f32)
        powers = jnp.concatenate([powers, more], axis=0)
        have += take
    grow_ref[...] = stacked_matrix(powers)
    traces = [trace]
    for power in range(POWERS):
        traces.append(jnp.dot(trace, powers[power * rows:(power + 1) * rows],
                              precision=precise, preferred_element_type=f32))
    trace_grow_ref[...] = stacked_matrix(jnp.concatenate(traces, axis=0))
    faces, tall, wide = lift_ref.shape
    lift = jnp.concatenate([
        jnp.concatenate([pad_rows(lift_ref[face], rows), jnp.zeros((rows, trace_rows - wide), f32)], axis=1)
        for face in range(faces)
    ], axis=1)
    lift_out_ref[...] = stacked_matrix(lift)


def plan_kernel(sizes_ref, fields_ref, order_ref, pattern_ref, neighbours_ref, send_ref, heights_ref,
                operator_ref, trace_ref, lift_ref, out_ref,
                members_ref, joined_ref, places_ref, send_places_ref, own_ref, faces_ref, weights_ref,
                grow_ref, trace_grow_ref, lift_out_ref, columns_ref):
    elements = fields_ref.shape[1]
    count = elements // LANES
    faces = neighbours_ref.shape[0]
    starts = level_starts(sizes_ref)
    order = order_ref[...]
    wide_order = jnp.broadcast_to(order, (8, elements))
    table = jnp.concatenate(
        [neighbours_ref[...], pattern_ref[...], jnp.zeros((faces - 1, elements), i32)], axis=0)
    for level in range(LEVELS):
        shift = jnp.where(starts[level] == 0, 0, elements - starts[level])
        members_ref[:, level * BLOCK:(level + 1) * BLOCK] = pltpu.roll(wide_order, shift, 1)[:, :BLOCK]
    for block in range(LEVELS * BLOCK // LANES):
        here = slice(block * LANES, (block + 1) * LANES)
        index = members_ref[:, here]
        joined_ref[:, here] = pick(value_blocks(table), index, index >> 7)
    for block in range(count):
        here = slice(block * LANES, (block + 1) * LANES)
        columns_ref[here, :] = jnp.transpose(jnp.broadcast_to(order[:, here], (LANES, LANES)))
    rank = lax.broadcasted_iota(i32, (elements, LANES), 0).astype(f32)
    for block in range(count):
        here = slice(block * LANES, (block + 1) * LANES)
        number = lax.broadcasted_iota(i32, (elements, LANES), 1) + block * LANES
        found = jnp.where(columns_ref[...] == number, rank, 0.0)
        place = jnp.sum(found, axis=0, keepdims=True).astype(i32)
        at = place
        for level in range(1, LEVELS):
            at = jnp.where(place >= starts[level], place - starts[level] + level * BLOCK, at)
        places_ref[:, here] = jnp.broadcast_to(at, (8, LANES))
    index = pad_rows(send_ref[...], 8)
    send_places_ref[...] = pick(ref_blocks(places_ref, count), index, index >> 7)
    matrix_powers(operator_ref, trace_ref, lift_ref, grow_ref, trace_grow_ref, lift_out_ref,
                  own_ref.shape[0], out_ref.shape[0])
    local_part(0, members_ref, joined_ref, fields_ref, out_ref, heights_ref, own_ref, faces_ref, weights_ref)


def grown(loaded, matrix_ref, weights_ref, rows, first):
    stacked = product(matrix_ref[...], stacked_columns(loaded))
    total = first if first is not None else stacked[:rows]
    skip = 0 if first is not None else 1
    for power in range(1, POWERS + 1):
        part = stacked[(power - 1 + skip) * rows:(power + skip) * rows]
        total = total + part * weights_ref[power - 1:power, :]
    return total


def settle(level, new_ref, places_ref, before, rows, block):
    here = slice(block * LANES, (block + 1) * LANES)
    index = places_ref[0:1, here]
    which = (index >> 7) - level * (BLOCK // LANES)
    return pick(ref_blocks(new_ref, BLOCK // LANES), index, which, before)


def between_kernel(level, members_ref, joined_ref, places_ref, fields_ref, old_out_ref, new_trace_ref,
                   heights_ref, loaded_ref, old_weights_ref, grow_ref, *rest):
    if level > 1:
        advanced_ref, rest = rest[0], rest[1:]
    out_ref, own_ref, faces_ref, weights_ref, new_advanced_ref, new_ref = rest
    elements = fields_ref.shape[1]
    for block in range(elements // LANES):
        here = slice(block * LANES, (block + 1) * LANES)
        out_ref[:, here] = settle(level - 1, new_trace_ref, places_ref, old_out_ref[:, here], None, block)
    local_part(level, members_ref, joined_ref, fields_ref, out_ref, heights_ref, own_ref, faces_ref, weights_ref)
    loaded = loaded_ref[...]
    new_ref[...] = grown(loaded, grow_ref, old_weights_ref, loaded.shape[0], loaded)
    for block in range(elements // LANES):
        here = slice(block * LANES, (block + 1) * LANES)
        before = advanced_ref[:, here] if level > 1 else None
        new_advanced_ref[:, here] = settle(level - 1, new_ref, places_ref, before, None, block)


def load(level, groups_ref, received, joined_ref, own_ref, faces_ref, lift_ref):
    faces = faces_in(joined_ref)
    trace_rows = faces_ref.shape[0] // faces
    own_groups = groups_ref[len(received)]
    parts = []
    for face in range(faces):
        across = []
        for block in range(BLOCK // LANES):
            here = slice(block * LANES, (block + 1) * LANES)
            there = slice(level * BLOCK + block * LANES, level * BLOCK + (block + 1) * LANES)
            index = joined_ref[face:face + 1, there]
            group = (index >> 7) - own_groups
            inner = faces_ref[face * trace_rows:(face + 1) * trace_rows, here]
            start = jnp.where(jnp.broadcast_to(group, inner.shape) >= 0, 0.0, inner)
            blocks = [(groups_ref[i], functools.partial(lambda ref: ref[...], ref))
                      for i, ref in enumerate(received)]
            across.append(pick(blocks, index, group, start))
        parts.append(jnp.concatenate(across, axis=1))
    return own_ref[...] + product(lift_ref[...], stacked_columns(jnp.concatenate(parts, axis=0)))


def level_kernel(level, messages, groups_ref, joined_ref, own_ref, faces_ref, weights_ref, lift_ref, trace_grow_ref,
                 send_places_ref, *rest):
    received, rest = rest[:messages], rest[messages:]
    sent, rest = rest[:messages], rest[messages:]
    loaded_ref, new_trace_ref, sends = rest[0], rest[1], rest[2:]
    loaded = load(level, groups_ref, received, joined_ref, own_ref, faces_ref, lift_ref)
    new_trace_ref[...] = grown(loaded, trace_grow_ref, weights_ref, new_trace_ref.shape[0], None)
    for group, (before, send) in enumerate(zip(sent, sends)):
        index = send_places_ref[group:group + 1, :]
        which = (index >> 7) - level * (BLOCK // LANES)
        send[...] = pick(ref_blocks(new_trace_ref, BLOCK // LANES), index, which, before[...])
    loaded_ref[...] = loaded


def last_kernel(level, messages, groups_ref, joined_ref, own_ref, faces_ref, weights_ref, lift_ref, grow_ref,
                places_ref, advanced_ref, *rest):
    received, (final_ref, new_ref) = rest[:messages], rest[messages:]
    loaded = load(level, groups_ref, received, joined_ref, own_ref, faces_ref, lift_ref)
    new_ref[...] = grown(loaded, grow_ref, weights_ref, loaded.shape[0], loaded)
    for block in range(final_ref.shape[1] // LANES):
        here = slice(block * LANES, (block + 1) * LANES)
        done = settle(level, new_ref, places_ref, advanced_ref[:, here], None, block)
        final_ref[:, here] = done[:final_ref.shape[0]]


def call(kernel, name, flops, scalars, vectors, outs, scratch=()):
    vmem, smem = pl.BlockSpec(memory_space=pltpu.VMEM), pl.BlockSpec(memory_space=pltpu.SMEM)
    return pl.pallas_call(
        kernel,
        out_shape=tuple(jax.ShapeDtypeStruct(shape, dtype) for shape, dtype in outs),
        in_specs=[smem] * len(scalars) + [vmem] * len(vectors),
        out_specs=tuple([vmem] * len(outs)),
        scratch_shapes=[pltpu.VMEM(shape, dtype) for shape, dtype in scratch],
        compiler_params=pltpu.CompilerParams(vmem_limit_bytes=16 * 1024 * 1024),
        cost_estimate=pl.CostEstimate(flops=flops, bytes_accessed=1 << 20, transcendentals=0),
        name=name,
    )(*scalars, *vectors)


def swap_plan(axis, periodic, low_group, high_group):
    count = lax.axis_size(axis)
    index = lax.axis_index(axis)
    odd = (index % 2) == 1
    first = [(i, i ^ 1) for i in range(count)]
    plan = [(first, jnp.where(odd, high_group, low_group), jnp.where(odd, low_group, high_group))]
    if count > 2 or periodic:
        second = [(i, (i + 1) % count if i % 2 else (i - 1) % count) for i in range(count)]
        came = jnp.where(odd, high_group, low_group)
        if not periodic:
            came = jnp.where((index == 0) | (index == count - 1), NO_GROUP, came)
        plan.append((second, jnp.where(odd, low_group, high_group), came))
    return plan


def body(fields, pattern, tent_order, level_sizes, send_rows, neighbours, operator, trace_map, lift_map, tent_height):
    fields, order, sizes = fields[0, 0], tent_order[0], level_sizes[0, 0]
    faces_of = neighbours[0, 0]
    comp, elements = fields.shape
    faces, trace = lift_map.shape[0], trace_map.shape[0]
    rows, trace_rows = rounded_up(comp, 16), rounded_up(trace, 16)
    padded = LEVELS * BLOCK
    bnd = send_rows.shape[-1]

    swaps = [("sector",) + one for one in swap_plan("sector", True, 0, 1)]
    swaps += [("radial",) + one for one in swap_plan("radial", False, 2, 3)]
    messages = len(swaps)
    send_list = jnp.concatenate([
        lax.dynamic_slice_in_dim(send_rows[0, 0], group, 1, axis=0) for _, _, group, _ in swaps])
    groups = jnp.stack([came for _, _, _, came in swaps] + [jnp.int32(elements // LANES)]).astype(i32)
    heights = jnp.pad(tent_height, (0, LANES - tent_height.shape[0]))[None]

    def exchange(sent):
        return [lax.ppermute(one, axis, pairs) for one, (axis, pairs, _, _) in zip(sent, swaps)]

    message = ((trace_rows, bnd), f32)
    own, face_stack = ((rows, BLOCK), f32), ((faces * trace_rows, BLOCK), f32)
    weight, table = ((POWERS, BLOCK), f32), ((trace_rows, elements), f32)
    whole = ((rows, elements), f32)

    out, *sent = call(first_kernel, "first", 10 ** 8, [], [fields, trace_map, send_list], [table] + [message] * messages)
    received = exchange(sent)
    members, joined, places, send_places, mine, inner, weights, grow, trace_grow, lift = call(
        plan_kernel, "plan", 2 * 10 ** 9, [sizes],
        [fields, order, pattern[0], faces_of, send_list, heights, operator, trace_map, lift_map, out],
        [((8, padded), i32), ((2 * faces, padded), i32), ((8, elements), i32), ((8, bnd), i32), own, face_stack, weight,
         ((POWERS * rows, 3 * rows), bf16), (((POWERS + 1) * trace_rows, 3 * rows), bf16),
         ((rows, 3 * faces * trace_rows), bf16)],
        [((elements, LANES), i32)])
    advanced = []
    for level in range(LEVELS):
        if level == LEVELS - 1:
            final, = call(
                functools.partial(last_kernel, level, messages), "last", 10 ** 9, [groups],
                [joined, mine, inner, weights, lift, grow, places] + advanced + received,
                [((comp, elements), f32)], [own])
            return final[None, None]
        loaded, new_trace, *sent = call(
            functools.partial(level_kernel, level, messages), "level", 10 ** 8, [groups],
            [joined, mine, inner, weights, lift, trace_grow, send_places] + received + sent,
            [own, ((trace_rows, BLOCK), f32)] + [message] * messages)
        received = exchange(sent)
        out, mine, inner, weights, *advanced = call(
            functools.partial(between_kernel, level + 1), "between", 2 * 10 ** 9, [],
            [members, joined, places, fields, out, new_trace, heights, loaded, weights, grow] + advanced,
            [table, own, face_stack, weight, whole], [own])


def solution(mesh):
    in_specs = (
        P("sector", "radial", None, None),
        P("sector", "radial", None),
        P("sector", "radial", None),
        P("sector", "radial", None),
        P("sector", "radial", None, None),
        P("sector", "radial", None, None),
        P(),
        P(),
        P(),
        P(),
    )
    out_specs = P("sector", "radial", None, None)
    return jax.shard_map(body, mesh=mesh, in_specs=in_specs, out_specs=out_specs, check_vma=False)
```

```python
import functools
import math

import jax
import jax.numpy as jnp
from jax import lax
from jax.experimental import pallas as pl
from jax.experimental.pallas import tpu as pltpu
from jax.sharding import PartitionSpec as P

LEVELS = 4
SUBSTEPS = 2
TERMS = 4
BLOCK = 384
LANES = 128
NO_GROUP = 1 << 20

f32, bf16, i32 = jnp.float32, jnp.bfloat16, jnp.int32
precise = lax.Precision.HIGHEST


def rounded_up(size, unit):
    return -(-size // unit) * unit


def taylor_weights():
    once = [1.0 / math.factorial(k) for k in range(TERMS + 1)]
    whole = [1.0]
    for _ in range(SUBSTEPS):
        longer = [0.0] * (len(whole) + TERMS)
        for i, a in enumerate(whole):
            for j, b in enumerate(once):
                longer[i + j] += a * b
        whole = longer
    return whole


WEIGHTS = taylor_weights()
POWERS = len(WEIGHTS) - 1


def split(values):
    high = values.astype(bf16)
    return high, (values - high.astype(f32)).astype(bf16)


def stacked_columns(values):
    high, low = split(values)
    return jnp.concatenate([high, low, high], axis=0)


def stacked_matrix(values):
    high = values.astype(bf16).astype(f32)
    low = values - high
    return jnp.concatenate([high, high, low], axis=1).astype(bf16)


def product(matrix, columns):
    return jnp.dot(matrix, columns, preferred_element_type=f32)


def pad_rows(values, rows):
    short = rows - values.shape[0]
    if short == 0:
        return values
    return jnp.concatenate([values, jnp.zeros((short,) + values.shape[1:], values.dtype)], axis=0)


def exact_product(left, right):
    left_high, left_low = split(left)
    right_high, right_low = split(right)
    rows = left.shape[0]
    both = product(jnp.concatenate([left_high, left_low], axis=0), right_high)
    return both[:rows] + both[rows:] + product(left_high, right_low)


def pick(blocks, index, which, start=None):
    result = start
    for number, read in blocks:
        table = read()
        lane = jnp.broadcast_to(index & (LANES - 1), table.shape)
        got = jnp.take_along_axis(table, lane, axis=1, mode="promise_in_bounds")
        if result is None:
            result = got
        else:
            result = jnp.where(jnp.broadcast_to(which, table.shape) == number, got, result)
    return result


def block_at(block):
    return slice(block * LANES, (block + 1) * LANES)


def ref_blocks(ref, count):
    return [(b, functools.partial(lambda b: ref[:, block_at(b)], b)) for b in range(count)]


def value_blocks(values):
    return [(b, functools.partial(lambda b: values[:, block_at(b)], b)) for b in range(values.shape[1] // LANES)]


def row_blocks(table, rows):
    return [
        (b, functools.partial(lambda b: jnp.broadcast_to(table[b:b + 1, :], (rows, LANES)), b))
        for b in range(table.shape[0])
    ]


def summed_powers(stacked, weights_ref, rows, total):
    for power in range(1, POWERS + 1):
        total = total + stacked[(power - 1) * rows:power * rows] * weights_ref[power - 1:power, :]
    return total


def first_kernel(fields_ref, trace_ref, send_ref, columns_ref, out_ref, *sends):
    rows = out_ref.shape[0]
    elements = out_ref.shape[1]
    count = elements // LANES
    comp = fields_ref.shape[0] // count
    trace = pad_rows(trace_ref[...], rows)
    trace_high, trace_low = split(trace)
    both = jnp.concatenate([trace_high, trace_low], axis=0)
    fields = jnp.concatenate([fields_ref[pl.ds(b, comp, stride=count), :] for b in range(count)], axis=1)
    high, low = split(fields)
    upper = product(both, high)
    out_ref[...] = upper[:rows] + upper[rows:] + product(trace_high, low)
    for group, send in enumerate(sends):
        index = send_ref[group:group + 1, :]
        send[...] = pick(ref_blocks(out_ref, count), index, index >> 7)
    columns_ref[...] = pad_rows(fields, columns_ref.shape[0])


def faces_in(joined_ref):
    return joined_ref.shape[0] // 2


def local_part(level, members_ref, joined_ref, columns_ref, out_ref, heights_ref, trace_grow_ref,
               own_ref, faces_ref, weights_ref, base_ref):
    faces = faces_in(joined_ref)
    count = columns_ref.shape[1] // LANES
    trace_rows = out_ref.shape[0]
    for block in range(BLOCK // LANES):
        here = block_at(block)
        there = block_at(level * (BLOCK // LANES) + block)
        index = members_ref[0:1, there]
        own_ref[:, here] = pick(ref_blocks(columns_ref, count), index, index >> 7)
        pattern = jnp.broadcast_to(joined_ref[faces:faces + 1, there], (8, LANES))
        height = jnp.take_along_axis(
            jnp.broadcast_to(heights_ref[...], (8, LANES)), pattern, axis=1, mode="promise_in_bounds")
        weight = jnp.ones((8, LANES), f32)
        for power in range(1, POWERS + 1):
            weight = weight * height
            weights_ref[power - 1:power, here] = weight[0:1] * WEIGHTS[power]
    stacked = product(trace_grow_ref[...], stacked_columns(own_ref[...]))
    for block in range(BLOCK // LANES):
        here = block_at(block)
        there = block_at(level * (BLOCK // LANES) + block)
        for face in range(faces):
            index = joined_ref[face:face + 1, there]
            faces_ref[face * trace_rows:(face + 1) * trace_rows, here] = pick(
                ref_blocks(out_ref, count), index, index >> 7, jnp.zeros((trace_rows, LANES), f32))
    base_ref[...] = summed_powers(stacked[trace_rows:], weights_ref, trace_rows, stacked[:trace_rows])


def matrix_powers(operator_ref, trace_ref, lift_ref, grow_ref, trace_grow_ref, mix_ref, lift_out_ref):
    comp = operator_ref.shape[0]
    faces, _, trace_comp = lift_ref.shape
    rows = lift_out_ref.shape[0]
    trace_rows = trace_grow_ref.shape[0] // (POWERS + 1)
    operator = pad_rows(operator_ref[...], rows)
    operator = jnp.concatenate([operator, jnp.zeros((rows, rows - comp), f32)], axis=1)
    traces = pad_rows(trace_ref[...], trace_rows)
    traces = jnp.concatenate([traces, jnp.zeros((trace_rows, rows - comp), f32)], axis=1)
    lift = jnp.concatenate([
        jnp.concatenate([pad_rows(lift_ref[face], rows), jnp.zeros((rows, trace_rows - trace_comp), f32)], axis=1)
        for face in range(faces)
    ], axis=1)
    powers, have = operator, 1
    while have < POWERS:
        more = exact_product(jnp.concatenate([traces, powers], axis=0), powers[(have - 1) * rows:have * rows])
        traces = jnp.concatenate([traces, more[:have * trace_rows]], axis=0)
        powers = jnp.concatenate([powers, more[have * trace_rows:]], axis=0)
        have *= 2
    traces = jnp.concatenate([traces, exact_product(traces[:trace_rows], powers[-rows:])], axis=0)
    mix_ref[...] = stacked_matrix(exact_product(traces, lift))
    trace_grow_ref[...] = stacked_matrix(traces)
    lift_out_ref[...] = stacked_matrix(lift)
    grow_ref[...] = stacked_matrix(powers)


def plan_kernel(sizes_ref, columns_ref, order_ref, pattern_ref, neighbours_ref, send_ref, heights_ref,
                operator_ref, trace_ref, lift_ref, out_ref,
                members_ref, joined_ref, places_ref, send_places_ref, own_ref, faces_ref, weights_ref, base_ref,
                grow_ref, trace_grow_ref, mix_ref, lift_out_ref):
    elements = columns_ref.shape[1]
    count = elements // LANES
    faces = neighbours_ref.shape[0]
    starts = [jnp.int32(0)]
    for level in range(LEVELS - 1):
        starts.append(starts[-1] + sizes_ref[level])
    wide_order = jnp.broadcast_to(order_ref[...], (8, elements))
    table = jnp.concatenate(
        [neighbours_ref[...], pattern_ref[...], jnp.zeros((faces - 1, elements), i32)], axis=0)
    for level in range(LEVELS):
        shift = jnp.where(starts[level] == 0, 0, elements - starts[level])
        members_ref[:, level * BLOCK:(level + 1) * BLOCK] = pltpu.roll(wide_order, shift, 1)[:, :BLOCK]
    for block in range(LEVELS * BLOCK // LANES):
        index = members_ref[:, block_at(block)]
        joined_ref[:, block_at(block)] = pick(value_blocks(table), index, index >> 7)
    ranks = lax.broadcasted_iota(i32, (count, elements), 1)
    in_block = (wide_order[:count] >> 7) == lax.broadcasted_iota(i32, (count, elements), 0)
    left = jnp.concatenate([
        jnp.where(in_block, ranks >> 5, 0).astype(f32), jnp.where(in_block, ranks & 31, 0).astype(f32)], axis=0)
    at_lane = jnp.broadcast_to(order_ref[...] & (LANES - 1), (LANES, elements)) == lax.broadcasted_iota(
        i32, (LANES, elements), 0)
    rank = lax.dot_general(left.astype(bf16), jnp.where(at_lane, 1.0, 0.0).astype(bf16), (((1,), (1,)), ((), ())),
                           preferred_element_type=f32)
    place = rank[:count].astype(i32) * 32 + rank[count:].astype(i32)
    at = place
    for level in range(1, LEVELS):
        at = jnp.where(place >= starts[level], place - starts[level] + level * BLOCK, at)
    places_ref[...] = at
    index = pad_rows(send_ref[...], 8)
    send_places_ref[...] = pick(row_blocks(at, 8), index, index >> 7)
    matrix_powers(operator_ref, trace_ref, lift_ref, grow_ref, trace_grow_ref, mix_ref, lift_out_ref)
    local_part(0, members_ref, joined_ref, columns_ref, out_ref, heights_ref, trace_grow_ref,
               own_ref, faces_ref, weights_ref, base_ref)


def advanced_columns(own_ref, inflow_ref, lift_ref, grow_ref, weights_ref):
    loaded = own_ref[...] + product(lift_ref[...], stacked_columns(inflow_ref[...]))
    stacked = product(grow_ref[...], stacked_columns(loaded))
    return summed_powers(stacked, weights_ref, loaded.shape[0], loaded)


def settle(level, new_ref, places_ref, before, block):
    index = places_ref[block:block + 1, :]
    which = (index >> 7) - level * (BLOCK // LANES)
    return pick(ref_blocks(new_ref, BLOCK // LANES), index, which, before)


def between_kernel(level, members_ref, joined_ref, places_ref, columns_ref, old_out_ref, new_trace_ref, heights_ref,
                   old_own_ref, inflow_ref, old_weights_ref, lift_ref, grow_ref, trace_grow_ref, *rest):
    if level > 1:
        advanced_ref, rest = rest[0], rest[1:]
    out_ref, own_ref, faces_ref, weights_ref, base_ref, new_advanced_ref, new_ref = rest
    elements = columns_ref.shape[1]
    for block in range(elements // LANES):
        here = block_at(block)
        out_ref[:, here] = settle(level - 1, new_trace_ref, places_ref, old_out_ref[:, here], block)
    local_part(level, members_ref, joined_ref, columns_ref, out_ref, heights_ref, trace_grow_ref,
               own_ref, faces_ref, weights_ref, base_ref)
    new_ref[...] = advanced_columns(old_own_ref, inflow_ref, lift_ref, grow_ref, old_weights_ref)
    for block in range(elements // LANES):
        here = block_at(block)
        before = advanced_ref[:, here] if level > 1 else None
        new_advanced_ref[:, here] = settle(level - 1, new_ref, places_ref, before, block)


def gather_inflow(level, groups_ref, received, joined_ref, faces_ref, inflow_ref):
    faces = faces_in(joined_ref)
    trace_rows = faces_ref.shape[0] // faces
    own_groups = groups_ref[len(received)]
    blocks = [(groups_ref[i], functools.partial(lambda ref: ref[...], ref)) for i, ref in enumerate(received)]
    for block in range(BLOCK // LANES):
        here = block_at(block)
        there = block_at(level * (BLOCK // LANES) + block)
        for face in range(faces):
            part = slice(face * trace_rows, (face + 1) * trace_rows)
            index = joined_ref[face:face + 1, there]
            inflow_ref[part, here] = pick(blocks, index, (index >> 7) - own_groups, faces_ref[part, here])


def level_kernel(level, messages, groups_ref, joined_ref, faces_ref, weights_ref, base_ref, mix_ref, send_places_ref,
                 *rest):
    received, rest = rest[:messages], rest[messages:]
    sent, rest = rest[:messages], rest[messages:]
    inflow_ref, new_trace_ref, sends = rest[0], rest[1], rest[2:]
    trace_rows = new_trace_ref.shape[0]
    gather_inflow(level, groups_ref, received, joined_ref, faces_ref, inflow_ref)
    stacked = product(mix_ref[...], stacked_columns(inflow_ref[...]))
    new_trace_ref[...] = summed_powers(
        stacked[trace_rows:], weights_ref, trace_rows, base_ref[...] + stacked[:trace_rows])
    for group, (before, send) in enumerate(zip(sent, sends)):
        index = send_places_ref[group:group + 1, :]
        which = (index >> 7) - level * (BLOCK // LANES)
        send[...] = pick(ref_blocks(new_trace_ref, BLOCK // LANES), index, which, before[...])


def last_kernel(level, messages, groups_ref, joined_ref, own_ref, faces_ref, weights_ref, lift_ref, grow_ref,
                places_ref, advanced_ref, *rest):
    received, (final_ref, inflow_ref, new_ref) = rest[:messages], rest[messages:]
    gather_inflow(level, groups_ref, received, joined_ref, faces_ref, inflow_ref)
    new_ref[...] = advanced_columns(own_ref, inflow_ref, lift_ref, grow_ref, weights_ref)
    count = places_ref.shape[0]
    comp = final_ref.shape[0] // count
    for block in range(count):
        done = settle(level, new_ref, places_ref, advanced_ref[:, block_at(block)], block)
        final_ref[pl.ds(block, comp, stride=count), :] = done[:comp]


def call(kernel, name, flops, scalars, vectors, outs, scratch=()):
    vmem, smem = pl.BlockSpec(memory_space=pltpu.VMEM), pl.BlockSpec(memory_space=pltpu.SMEM)
    return pl.pallas_call(
        kernel,
        out_shape=tuple(jax.ShapeDtypeStruct(shape, dtype) for shape, dtype in outs),
        in_specs=[smem] * len(scalars) + [vmem] * len(vectors),
        out_specs=tuple([vmem] * len(outs)),
        scratch_shapes=[pltpu.VMEM(shape, dtype) for shape, dtype in scratch],
        compiler_params=pltpu.CompilerParams(vmem_limit_bytes=16 * 1024 * 1024),
        cost_estimate=pl.CostEstimate(flops=flops, bytes_accessed=1 << 20, transcendentals=0),
        name=name,
    )(*scalars, *vectors)


def swap_plan(axis, periodic, low_group, high_group):
    count = lax.axis_size(axis)
    index = lax.axis_index(axis)
    odd = (index % 2) == 1
    first = [(i, i ^ 1) for i in range(count)]
    plan = [(first, jnp.where(odd, high_group, low_group), jnp.where(odd, low_group, high_group))]
    if count > 2 or periodic:
        second = [(i, (i + 1) % count if i % 2 else (i - 1) % count) for i in range(count)]
        came = jnp.where(odd, high_group, low_group)
        if not periodic:
            came = jnp.where((index == 0) | (index == count - 1), NO_GROUP, came)
        plan.append((second, jnp.where(odd, low_group, high_group), came))
    return plan


def body(fields, pattern, tent_order, level_sizes, send_rows, neighbours, operator, trace_map, lift_map, tent_height):
    fields, order, sizes = fields[0, 0], tent_order[0], level_sizes[0, 0]
    faces_of = neighbours[0, 0]
    comp, elements = fields.shape
    faces, trace = lift_map.shape[0], trace_map.shape[0]
    rows, trace_rows = rounded_up(comp, 16), rounded_up(trace, 16)
    padded = LEVELS * BLOCK
    bnd = send_rows.shape[-1]

    swaps = [("sector",) + one for one in swap_plan("sector", True, 0, 1)]
    swaps += [("radial",) + one for one in swap_plan("radial", False, 2, 3)]
    messages = len(swaps)
    send_list = jnp.concatenate([
        lax.dynamic_slice_in_dim(send_rows[0, 0], group, 1, axis=0) for _, _, group, _ in swaps])
    groups = jnp.stack([came for _, _, _, came in swaps] + [jnp.int32(elements // LANES)]).astype(i32)
    heights = jnp.pad(tent_height, (0, LANES - tent_height.shape[0]))[None]

    def exchange(sent):
        return [lax.ppermute(one, axis, pairs) for one, (axis, pairs, _, _) in zip(sent, swaps)]

    message = ((trace_rows, bnd), f32)
    own, face_stack = ((rows, BLOCK), f32), ((faces * trace_rows, BLOCK), f32)
    weight, table, traced = ((POWERS, BLOCK), f32), ((trace_rows, elements), f32), ((trace_rows, BLOCK), f32)
    whole = ((rows, elements), f32)
    flat = (comp * elements // LANES, LANES)

    columns, out, *sent = call(
        first_kernel, "first", 10 ** 8, [], [fields.reshape(flat), trace_map, send_list],
        [whole, table] + [message] * messages)
    received = exchange(sent)
    members, joined, places, send_places, mine, inner, weights, base, grow, trace_grow, mix, lift = call(
        plan_kernel, "plan", 2 * 10 ** 9, [sizes],
        [columns, order, pattern[0], faces_of, send_list, heights, operator, trace_map, lift_map, out],
        [((8, padded), i32), ((2 * faces, padded), i32), ((elements // LANES, LANES), i32), ((8, bnd), i32),
         own, face_stack, weight, traced,
         ((POWERS * rows, 3 * rows), bf16), (((POWERS + 1) * trace_rows, 3 * rows), bf16),
         (((POWERS + 1) * trace_rows, 3 * faces * trace_rows), bf16), ((rows, 3 * faces * trace_rows), bf16)])
    advanced = []
    for level in range(LEVELS):
        if level == LEVELS - 1:
            final, = call(
                functools.partial(last_kernel, level, messages), "last", 10 ** 9, [groups],
                [joined, mine, inner, weights, lift, grow, places] + advanced + received,
                [(flat, f32)], [face_stack, own])
            return final.reshape(1, 1, comp, elements)
        inflow, new_trace, *sent = call(
            functools.partial(level_kernel, level, messages), "level", 10 ** 8, [groups],
            [joined, inner, weights, base, mix, send_places] + received + sent,
            [face_stack, traced] + [message] * messages)
        received = exchange(sent)
        out, mine, inner, weights, base, *advanced = call(
            functools.partial(between_kernel, level + 1), "between", 2 * 10 ** 9, [],
            [members, joined, places, columns, out, new_trace, heights, mine, inflow, weights, lift, grow, trace_grow]
            + advanced,
            [table, own, face_stack, weight, traced, whole], [own])


def solution(mesh):
    in_specs = (
        P("sector", "radial", None, None),
        P("sector", "radial", None),
        P("sector", "radial", None),
        P("sector", "radial", None),
        P("sector", "radial", None, None),
        P("sector", "radial", None, None),
        P(),
        P(),
        P(),
        P(),
    )
    out_specs = P("sector", "radial", None, None)
    return jax.shard_map(body, mesh=mesh, in_specs=in_specs, out_specs=out_specs, check_vma=False)
```

```python
import functools
import math

import jax
import jax.numpy as jnp
from jax import lax
from jax.experimental import pallas as pl
from jax.experimental.pallas import tpu as pltpu
from jax.sharding import PartitionSpec as P

LEVELS = 4
SUBSTEPS = 2
TERMS = 4
BLOCK = 384
LANES = 128
NO_GROUP = 1 << 20
ARGUMENTS = 10

f32, bf16, i32 = jnp.float32, jnp.bfloat16, jnp.int32
precise = lax.Precision.HIGHEST


def rounded_up(size, unit):
    return -(-size // unit) * unit


def taylor_weights():
    once = [1.0 / math.factorial(k) for k in range(TERMS + 1)]
    whole = [1.0]
    for _ in range(SUBSTEPS):
        longer = [0.0] * (len(whole) + TERMS)
        for i, a in enumerate(whole):
            for j, b in enumerate(once):
                longer[i + j] += a * b
        whole = longer
    return whole


WEIGHTS = taylor_weights()
POWERS = len(WEIGHTS) - 1


def split(values):
    high = values.astype(bf16)
    return high, (values - high.astype(f32)).astype(bf16)


def stacked_columns(values):
    high, low = split(values)
    return jnp.concatenate([high, low, high], axis=0)


def stacked_matrix(values):
    high = values.astype(bf16).astype(f32)
    low = values - high
    return jnp.concatenate([high, high, low], axis=1).astype(bf16)


def product(matrix, columns):
    return jnp.dot(matrix, columns, preferred_element_type=f32)


def pad_rows(values, rows):
    short = rows - values.shape[0]
    if short == 0:
        return values
    return jnp.concatenate([values, jnp.zeros((short,) + values.shape[1:], values.dtype)], axis=0)


def exact_product(left, right):
    left_high, left_low = split(left)
    right_high, right_low = split(right)
    rows = left.shape[0]
    both = product(jnp.concatenate([left_high, left_low], axis=0), right_high)
    return both[:rows] + both[rows:] + product(left_high, right_low)


def pick(blocks, index, which, start=None):
    result = start
    for number, read in blocks:
        table = read()
        lane = jnp.broadcast_to(index & (LANES - 1), table.shape)
        got = jnp.take_along_axis(table, lane, axis=1, mode="promise_in_bounds")
        if result is None:
            result = got
        else:
            result = jnp.where(jnp.broadcast_to(which, table.shape) == number, got, result)
    return result


def block_at(block):
    return slice(block * LANES, (block + 1) * LANES)


def ref_blocks(ref, count):
    return [(b, functools.partial(lambda b: ref[:, block_at(b)], b)) for b in range(count)]


def value_blocks(values):
    return [(b, functools.partial(lambda b: values[:, block_at(b)], b)) for b in range(values.shape[1] // LANES)]


def row_blocks(table, rows):
    return [
        (b, functools.partial(lambda b: jnp.broadcast_to(table[b:b + 1, :], (rows, LANES)), b))
        for b in range(table.shape[0])
    ]


def summed_powers(stacked, weights_ref, rows, total):
    for power in range(1, POWERS + 1):
        total = total + stacked[(power - 1) * rows:power * rows] * weights_ref[power - 1:power, :]
    return total


def sent_rows(send_ref, swaps):
    rows = []
    for axis, _, low, high, _ in swaps:
        odd, even = send_ref[high:high + 1, :], send_ref[low:low + 1, :]
        rows.append(jnp.where(is_odd(axis), odd, even))
    return rows


def first_kernel(swaps, *refs):
    (fields_hbm, *given), refs = refs[:ARGUMENTS], refs[ARGUMENTS:]
    (columns_ref, out_ref), refs = refs[:2], refs[2:]
    sends, refs = refs[:len(swaps)], refs[len(swaps):]
    *held, fields_ref, arrived = refs
    copies = [
        pltpu.make_async_copy(source, target, arrived.at[i])
        for i, (source, target) in enumerate(zip([fields_hbm] + given, [fields_ref] + held))
    ]
    for copy in copies:
        copy.start()
    for copy in copies[:3]:
        copy.wait()
    trace_ref, send_ref = held[:2]
    rows = out_ref.shape[0]
    elements = out_ref.shape[1]
    count = elements // LANES
    comp = fields_ref.shape[0] // count
    trace = pad_rows(trace_ref[...], rows)
    trace_high, trace_low = split(trace)
    both = jnp.concatenate([trace_high, trace_low], axis=0)
    fields = jnp.concatenate([fields_ref[pl.ds(b, comp, stride=count), :] for b in range(count)], axis=1)
    high, low = split(fields)
    upper = product(both, high)
    out_ref[...] = upper[:rows] + upper[rows:] + product(trace_high, low)
    for index, send in zip(sent_rows(send_ref, swaps), sends):
        send[...] = pick(ref_blocks(out_ref, count), index, index >> 7)
    columns_ref[...] = pad_rows(fields, columns_ref.shape[0])
    for copy in copies[3:]:
        copy.wait()


def faces_in(joined_ref):
    return joined_ref.shape[0] // 2


def local_part(level, members_ref, joined_ref, columns_ref, out_ref, heights_ref, trace_grow_ref,
               own_ref, faces_ref, weights_ref, base_ref=None):
    faces = faces_in(joined_ref)
    count = columns_ref.shape[1] // LANES
    trace_rows = out_ref.shape[0]
    for block in range(BLOCK // LANES):
        here = block_at(block)
        there = block_at(level * (BLOCK // LANES) + block)
        index = members_ref[0:1, there]
        own_ref[:, here] = pick(ref_blocks(columns_ref, count), index, index >> 7)
        pattern = jnp.broadcast_to(joined_ref[faces:faces + 1, there], (8, LANES))
        height = jnp.take_along_axis(
            jnp.broadcast_to(heights_ref[...], (8, LANES)), pattern, axis=1, mode="promise_in_bounds")
        weight = jnp.ones((8, LANES), f32)
        for power in range(1, POWERS + 1):
            weight = weight * height
            weights_ref[power - 1:power, here] = weight[0:1] * WEIGHTS[power]
    if base_ref is not None:
        stacked = product(trace_grow_ref[...], stacked_columns(own_ref[...]))
    for block in range(BLOCK // LANES):
        here = block_at(block)
        there = block_at(level * (BLOCK // LANES) + block)
        for face in range(faces):
            index = joined_ref[face:face + 1, there]
            faces_ref[face * trace_rows:(face + 1) * trace_rows, here] = pick(
                ref_blocks(out_ref, count), index, index >> 7, jnp.zeros((trace_rows, LANES), f32))
    if base_ref is not None:
        base_ref[...] = summed_powers(stacked[trace_rows:], weights_ref, trace_rows, stacked[:trace_rows])


def matrix_powers(operator_ref, trace_ref, lift_ref, grow_ref, trace_grow_ref, mix_ref, lift_out_ref):
    comp = operator_ref.shape[0]
    trace_comp, faces, _ = lift_ref.shape
    rows = lift_out_ref.shape[0]
    trace_rows = trace_grow_ref.shape[0] // (POWERS + 1)
    operator = pad_rows(operator_ref[...], rows)
    operator = jnp.concatenate([operator, jnp.zeros((rows, rows - comp), f32)], axis=1)
    traces = pad_rows(trace_ref[...], trace_rows)
    traces = jnp.concatenate([traces, jnp.zeros((trace_rows, rows - comp), f32)], axis=1)
    lift = jnp.concatenate([pad_rows(lift_ref[:, face, :], trace_rows) for face in range(faces)], axis=0)
    lift = pad_rows(jnp.transpose(lift), rows)
    powers, have = operator, 1
    while have < POWERS:
        more = exact_product(jnp.concatenate([traces, powers], axis=0), powers[(have - 1) * rows:have * rows])
        traces = jnp.concatenate([traces, more[:have * trace_rows]], axis=0)
        powers = jnp.concatenate([powers, more[have * trace_rows:]], axis=0)
        have *= 2
    traces = jnp.concatenate([traces, exact_product(traces[:trace_rows], powers[-rows:])], axis=0)
    mix_ref[...] = stacked_matrix(exact_product(traces, lift))
    trace_grow_ref[...] = stacked_matrix(traces)
    lift_out_ref[...] = stacked_matrix(lift)
    grow_ref[...] = stacked_matrix(powers)


def plan_kernel(swaps, trace_ref, send_ref, order_ref, pattern_ref, sizes_ref, neighbours_ref, operator_ref,
                lift_ref, heights_ref, columns_ref, out_ref,
                members_ref, joined_ref, places_ref, send_places_ref, own_ref, faces_ref, weights_ref, base_ref,
                grow_ref, trace_grow_ref, mix_ref, lift_out_ref, wide_heights_ref):
    elements = columns_ref.shape[1]
    count = elements // LANES
    faces = neighbours_ref.shape[0]
    sizes = sizes_ref[...].astype(f32)
    number = lax.broadcasted_iota(i32, sizes.shape, 1)
    starts = [jnp.sum(jnp.where(number < level, sizes, 0.0)).astype(i32) for level in range(LEVELS)]
    wide_order = jnp.broadcast_to(order_ref[...], (8, elements))
    neighbours = neighbours_ref[...]
    group = (neighbours >> 7) - count
    message = jnp.full(neighbours.shape, count + len(swaps), i32)
    for number, swap in enumerate(swaps):
        message = jnp.where(group == came_group(swap), count + number, message)
    neighbours = jnp.where(group >= 0, message * LANES + (neighbours & (LANES - 1)), neighbours)
    table = jnp.concatenate(
        [neighbours, pattern_ref[...], jnp.zeros((faces - 1, elements), i32)], axis=0)
    heights = heights_ref[...]
    wide_heights_ref[...] = jnp.concatenate(
        [heights, jnp.zeros((1, LANES - heights.shape[1]), f32)], axis=1)
    for level in range(LEVELS):
        shift = jnp.where(starts[level] == 0, 0, elements - starts[level])
        members_ref[:, level * BLOCK:(level + 1) * BLOCK] = pltpu.roll(wide_order, shift, 1)[:, :BLOCK]
    for block in range(LEVELS * BLOCK // LANES):
        index = members_ref[:, block_at(block)]
        joined_ref[:, block_at(block)] = pick(value_blocks(table), index, index >> 7)
    ranks = lax.broadcasted_iota(i32, (count, elements), 1)
    in_block = (wide_order[:count] >> 7) == lax.broadcasted_iota(i32, (count, elements), 0)
    left = jnp.concatenate([
        jnp.where(in_block, ranks >> 5, 0).astype(f32), jnp.where(in_block, ranks & 31, 0).astype(f32)], axis=0)
    at_lane = jnp.broadcast_to(order_ref[...] & (LANES - 1), (LANES, elements)) == lax.broadcasted_iota(
        i32, (LANES, elements), 0)
    rank = lax.dot_general(left.astype(bf16), jnp.where(at_lane, 1.0, 0.0).astype(bf16), (((1,), (1,)), ((), ())),
                           preferred_element_type=f32)
    place = rank[:count].astype(i32) * 32 + rank[count:].astype(i32)
    at = place
    for level in range(1, LEVELS):
        at = jnp.where(place >= starts[level], place - starts[level] + level * BLOCK, at)
    places_ref[...] = at
    index = pad_rows(jnp.concatenate(sent_rows(send_ref, swaps), axis=0), 8)
    send_places_ref[...] = pick(row_blocks(at, 8), index, index >> 7)
    matrix_powers(operator_ref, trace_ref, lift_ref, grow_ref, trace_grow_ref, mix_ref, lift_out_ref)
    local_part(0, members_ref, joined_ref, columns_ref, out_ref, wide_heights_ref, trace_grow_ref,
               own_ref, faces_ref, weights_ref, base_ref)


def advanced_columns(own_ref, inflow_ref, lift_ref, grow_ref, weights_ref):
    loaded = own_ref[...] + product(lift_ref[...], stacked_columns(inflow_ref[...]))
    stacked = product(grow_ref[...], stacked_columns(loaded))
    return summed_powers(stacked, weights_ref, loaded.shape[0], loaded)


def settle(level, new_ref, places_ref, before, block):
    index = places_ref[block:block + 1, :]
    which = (index >> 7) - level * (BLOCK // LANES)
    return pick(ref_blocks(new_ref, BLOCK // LANES), index, which, before)


def between_kernel(level, members_ref, joined_ref, places_ref, columns_ref, old_out_ref, new_trace_ref, heights_ref,
                   old_own_ref, inflow_ref, old_weights_ref, lift_ref, grow_ref, trace_grow_ref, *rest):
    if level > 1:
        advanced_ref, rest = rest[0], rest[1:]
    if level == LEVELS - 1:
        own_ref, faces_ref, weights_ref, new_advanced_ref, out_ref, new_ref = rest
        base_ref = None
    else:
        out_ref, own_ref, faces_ref, weights_ref, base_ref, new_advanced_ref, new_ref = rest
    elements = columns_ref.shape[1]
    for block in range(elements // LANES):
        here = block_at(block)
        out_ref[:, here] = settle(level - 1, new_trace_ref, places_ref, old_out_ref[:, here], block)
    local_part(level, members_ref, joined_ref, columns_ref, out_ref, heights_ref, trace_grow_ref,
               own_ref, faces_ref, weights_ref, base_ref)
    new_ref[...] = advanced_columns(old_own_ref, inflow_ref, lift_ref, grow_ref, old_weights_ref)
    for block in range(elements // LANES):
        here = block_at(block)
        before = advanced_ref[:, here] if level > 1 else None
        new_advanced_ref[:, here] = settle(level - 1, new_ref, places_ref, before, block)


def gather_inflow(level, received, joined_ref, faces_ref, inflow_ref, count):
    faces = faces_in(joined_ref)
    trace_rows = faces_ref.shape[0] // faces
    blocks = [(count + i, functools.partial(lambda ref: ref[...], ref)) for i, ref in enumerate(received)]
    for block in range(BLOCK // LANES):
        here = block_at(block)
        there = block_at(level * (BLOCK // LANES) + block)
        for face in range(faces):
            part = slice(face * trace_rows, (face + 1) * trace_rows)
            index = joined_ref[face:face + 1, there]
            inflow_ref[part, here] = pick(blocks, index, index >> 7, faces_ref[part, here])


def level_kernel(level, messages, count, joined_ref, faces_ref, weights_ref, base_ref, mix_ref, send_places_ref,
                 *rest):
    received, rest = rest[:messages], rest[messages:]
    sent, rest = rest[:messages], rest[messages:]
    inflow_ref, new_trace_ref, sends = rest[0], rest[1], rest[2:]
    trace_rows = new_trace_ref.shape[0]
    gather_inflow(level, received, joined_ref, faces_ref, inflow_ref, count)
    stacked = product(mix_ref[...], stacked_columns(inflow_ref[...]))
    new_trace_ref[...] = summed_powers(
        stacked[trace_rows:], weights_ref, trace_rows, base_ref[...] + stacked[:trace_rows])
    for group, (before, send) in enumerate(zip(sent, sends)):
        index = send_places_ref[group:group + 1, :]
        which = (index >> 7) - level * (BLOCK // LANES)
        send[...] = pick(ref_blocks(new_trace_ref, BLOCK // LANES), index, which, before[...])


def last_kernel(level, messages, joined_ref, own_ref, faces_ref, weights_ref, lift_ref, grow_ref,
                places_ref, advanced_ref, *rest):
    received, (final_ref, inflow_ref, new_ref) = rest[:messages], rest[messages:]
    count = places_ref.shape[0]
    gather_inflow(level, received, joined_ref, faces_ref, inflow_ref, count)
    new_ref[...] = advanced_columns(own_ref, inflow_ref, lift_ref, grow_ref, weights_ref)
    comp = final_ref.shape[0] // count
    for block in range(count):
        done = settle(level, new_ref, places_ref, advanced_ref[:, block_at(block)], block)
        final_ref[pl.ds(block, comp, stride=count), :] = done[:comp]


def call(kernel, name, flops, operands, outs, scratch=(), hbm=False):
    vmem = pl.BlockSpec(memory_space=pltpu.VMEM)
    given = pl.BlockSpec(memory_space=pltpu.HBM) if hbm else vmem
    if hbm:
        operands = [pltpu.with_memory_space_constraint(one, pltpu.HBM) for one in operands]
    return pl.pallas_call(
        kernel,
        out_shape=tuple(jax.ShapeDtypeStruct(shape, dtype) for shape, dtype in outs),
        in_specs=[given] * len(operands),
        out_specs=tuple([vmem] * len(outs)),
        scratch_shapes=[one if not isinstance(one, tuple) else pltpu.VMEM(*one) for one in scratch],
        compiler_params=pltpu.CompilerParams(vmem_limit_bytes=16 * 1024 * 1024),
        cost_estimate=pl.CostEstimate(flops=flops, bytes_accessed=1 << 20, transcendentals=0),
        name=name,
    )(*operands)


def is_odd(axis):
    return (lax.axis_index(axis) & 1) == 1


def swap_plan(axis, periodic, low, high):
    count = lax.axis_size(axis)
    plan = [(axis, [(i, i ^ 1) for i in range(count)], low, high, False)]
    if count > 2 or periodic:
        pairs = [(i, (i + 1) % count if i % 2 else (i - 1) % count) for i in range(count)]
        plan.append((axis, pairs, high, low, not periodic))
    return plan


def came_group(swap):
    axis, _, even, odd, is_open = swap
    came = jnp.where(is_odd(axis), even, odd)
    if is_open:
        index = lax.axis_index(axis)
        came = jnp.where((index == 0) | (index == lax.axis_size(axis) - 1), NO_GROUP, came)
    return came


def body(fields, pattern, tent_order, level_sizes, send_rows, neighbours, operator, trace_map, lift_map, tent_height):
    fields, order, sizes = fields[0, 0], tent_order[0], level_sizes[0]
    faces_of, send_list = neighbours[0, 0], send_rows[0, 0]
    comp, elements = fields.shape
    faces, trace = lift_map.shape[0], trace_map.shape[0]
    rows, trace_rows = rounded_up(comp, 16), rounded_up(trace, 16)
    padded, count = LEVELS * BLOCK, elements // LANES
    bnd = send_list.shape[-1]

    swaps = swap_plan("sector", True, 0, 1) + swap_plan("radial", False, 2, 3)
    messages = len(swaps)

    def exchange(sent):
        return [lax.ppermute(one, swap[0], swap[1]) for one, swap in zip(sent, swaps)]

    message = ((trace_rows, bnd), f32)
    own, face_stack = ((rows, BLOCK), f32), ((faces * trace_rows, BLOCK), f32)
    weight, table, traced = ((POWERS, BLOCK), f32), ((trace_rows, elements), f32), ((trace_rows, BLOCK), f32)
    whole = ((rows, elements), f32)
    flat = (comp * count, LANES)

    arguments = [trace_map, send_list, order, pattern[0], sizes, faces_of, operator,
                 jnp.transpose(lift_map, (2, 0, 1)), tent_height[None]]
    columns, out, *rest = call(
        functools.partial(first_kernel, swaps), "first", 10 ** 8, [fields.reshape(flat)] + arguments,
        [whole, table] + [message] * messages + [(one.shape, one.dtype) for one in arguments],
        [(flat, f32), pltpu.SemaphoreType.DMA((ARGUMENTS,))], hbm=True)
    sent, held = rest[:messages], rest[messages:]
    received = exchange(sent)
    members, joined, places, send_places, mine, inner, weights, base, grow, trace_grow, mix, lift, heights = call(
        functools.partial(plan_kernel, swaps), "plan", 2 * 10 ** 9, held + [columns, out],
        [((8, padded), i32), ((2 * faces, padded), i32), ((count, LANES), i32), ((8, bnd), i32),
         own, face_stack, weight, traced,
         ((POWERS * rows, 3 * rows), bf16), (((POWERS + 1) * trace_rows, 3 * rows), bf16),
         (((POWERS + 1) * trace_rows, 3 * faces * trace_rows), bf16), ((rows, 3 * faces * trace_rows), bf16),
         ((1, LANES), f32)])
    advanced = []
    for level in range(LEVELS - 1):
        inflow, new_trace, *sent = call(
            functools.partial(level_kernel, level, messages, count), "level", 10 ** 8,
            [joined, inner, weights, base, mix, send_places] + received + sent,
            [face_stack, traced] + [message] * messages)
        received = exchange(sent)
        beside = functools.partial(between_kernel, level + 1)
        operands = [members, joined, places, columns, out, new_trace, heights, mine, inflow, weights, lift, grow,
                    trace_grow] + advanced
        if level + 1 < LEVELS - 1:
            out, mine, inner, weights, base, *advanced = call(
                beside, "between", 2 * 10 ** 9, operands, [table, own, face_stack, weight, traced, whole], [own])
        else:
            mine, inner, weights, *advanced = call(
                beside, "between", 2 * 10 ** 9, operands, [own, face_stack, weight, whole], [table, own])
    final, = call(
        functools.partial(last_kernel, LEVELS - 1, messages), "last", 10 ** 9,
        [joined, mine, inner, weights, lift, grow, places] + advanced + received,
        [(flat, f32)], [face_stack, own])
    return final.reshape(1, 1, comp, elements)


def solution(mesh):
    in_specs = (
        P("sector", "radial", None, None),
        P("sector", "radial", None),
        P("sector", "radial", None),
        P("sector", "radial", None),
        P("sector", "radial", None, None),
        P("sector", "radial", None, None),
        P(),
        P(),
        P(),
        P(),
    )
    out_specs = P("sector", "radial", None, None)
    return jax.shard_map(body, mesh=mesh, in_specs=in_specs, out_specs=out_specs, check_vma=False)
```

```python
import functools
import math

import jax
import jax.numpy as jnp
from jax import lax
from jax.experimental import pallas as pl
from jax.experimental.pallas import tpu as pltpu
from jax.sharding import PartitionSpec as P

LEVELS = 4
SUBSTEPS = 2
TERMS = 4
BLOCK = 384
LANES = 128
NO_GROUP = 1 << 20
ARGUMENTS = 10
FIELD_COPIES = 4
ROW_CHUNK = 48

f32, bf16, i32 = jnp.float32, jnp.bfloat16, jnp.int32
precise = lax.Precision.HIGHEST


def rounded_up(size, unit):
    return -(-size // unit) * unit


def taylor_weights():
    once = [1.0 / math.factorial(k) for k in range(TERMS + 1)]
    whole = [1.0]
    for _ in range(SUBSTEPS):
        longer = [0.0] * (len(whole) + TERMS)
        for i, a in enumerate(whole):
            for j, b in enumerate(once):
                longer[i + j] += a * b
        whole = longer
    return whole


WEIGHTS = taylor_weights()
POWERS = len(WEIGHTS) - 1


def split(values):
    high = values.astype(bf16)
    return high, (values - high.astype(f32)).astype(bf16)


def stacked_columns(values):
    high, low = split(values)
    return jnp.concatenate([high, low, high], axis=0)


def stacked_matrix(values):
    high = values.astype(bf16).astype(f32)
    low = values - high
    return jnp.concatenate([high, high, low], axis=1).astype(bf16)


def product(matrix, columns):
    return jnp.dot(matrix, columns, preferred_element_type=f32)


def pad_rows(values, rows):
    short = rows - values.shape[0]
    if short == 0:
        return values
    return jnp.concatenate([values, jnp.zeros((short,) + values.shape[1:], values.dtype)], axis=0)


def exact_product(left, right):
    left_high, left_low = split(left)
    right_high, right_low = split(right)
    rows = left.shape[0]
    both = product(jnp.concatenate([left_high, left_low], axis=0), right_high)
    return both[:rows] + both[rows:] + product(left_high, right_low)


def pick(blocks, index, which, start=None):
    result = start
    for number, read in blocks:
        table = read()
        lane = jnp.broadcast_to(index & (LANES - 1), table.shape)
        got = jnp.take_along_axis(table, lane, axis=1, mode="promise_in_bounds")
        if result is None:
            result = got
        else:
            result = jnp.where(jnp.broadcast_to(which, table.shape) == number, got, result)
    return result


def block_at(block):
    return slice(block * LANES, (block + 1) * LANES)


def ref_blocks(ref, count):
    return [(b, functools.partial(lambda b: ref[:, block_at(b)], b)) for b in range(count)]


def value_blocks(values):
    return [(b, functools.partial(lambda b: values[:, block_at(b)], b)) for b in range(values.shape[1] // LANES)]


def row_blocks(table, rows):
    return [
        (b, functools.partial(lambda b: jnp.broadcast_to(table[b:b + 1, :], (rows, LANES)), b))
        for b in range(table.shape[0])
    ]


def summed_powers(stacked, weights_ref, rows, total):
    for power in range(1, POWERS + 1):
        total = total + stacked[(power - 1) * rows:power * rows] * weights_ref[power - 1:power, :]
    return total


def sent_rows(send_ref, swaps):
    rows = []
    for axis, _, low, high, _ in swaps:
        odd, even = send_ref[high:high + 1, :], send_ref[low:low + 1, :]
        rows.append(jnp.where(is_odd(axis), odd, even))
    return rows


def first_kernel(swaps, *refs):
    (fields_hbm, *given), refs = refs[:ARGUMENTS], refs[ARGUMENTS:]
    (columns_ref, out_ref), refs = refs[:2], refs[2:]
    sends, refs = refs[:len(swaps)], refs[len(swaps):]
    *held, fields_ref, arrived = refs
    share = fields_ref.shape[0] // FIELD_COPIES
    pairs = list(zip(given[:2], held[:2]))
    pairs += [(fields_hbm.at[pl.ds(i * share, share)], fields_ref.at[pl.ds(i * share, share)])
              for i in range(FIELD_COPIES)]
    needed = len(pairs)
    pairs += list(zip(given[2:], held[2:]))
    copies = [pltpu.make_async_copy(source, target, arrived.at[i]) for i, (source, target) in enumerate(pairs)]
    for copy in copies:
        copy.start()
    for copy in copies[:needed]:
        copy.wait()
    trace_ref, send_ref = held[:2]
    rows = out_ref.shape[0]
    elements = out_ref.shape[1]
    count = elements // LANES
    comp = fields_ref.shape[0] // count
    trace = pad_rows(trace_ref[...], rows)
    trace_high, trace_low = split(trace)
    both = jnp.concatenate([trace_high, trace_low], axis=0)
    fields = jnp.concatenate([fields_ref[pl.ds(b, comp, stride=count), :] for b in range(count)], axis=1)
    high, low = split(fields)
    upper = product(both, high)
    out_ref[...] = upper[:rows] + upper[rows:] + product(trace_high, low)
    for index, send in zip(sent_rows(send_ref, swaps), sends):
        send[...] = pick(ref_blocks(out_ref, count), index, index >> 7)
    columns_ref[...] = pad_rows(fields, columns_ref.shape[0])
    for copy in copies[needed:]:
        copy.wait()


def faces_in(joined_ref):
    return joined_ref.shape[0] // 2


def own_block(level, block, members_ref, joined_ref, columns_ref, heights_ref, own_ref, weights_ref):
    faces = faces_in(joined_ref)
    here, there = block_at(block), block_at(level * (BLOCK // LANES) + block)
    index = members_ref[0:1, there]
    own_ref[:, here] = pick(ref_blocks(columns_ref, columns_ref.shape[1] // LANES), index, index >> 7)
    pattern = jnp.broadcast_to(joined_ref[faces:faces + 1, there], (8, LANES))
    height = jnp.take_along_axis(
        jnp.broadcast_to(heights_ref[...], (8, LANES)), pattern, axis=1, mode="promise_in_bounds")
    weight = jnp.ones((8, LANES), f32)
    for power in range(1, POWERS + 1):
        weight = weight * height
        weights_ref[power - 1:power, here] = weight[0:1] * WEIGHTS[power]


def face_block(level, block, joined_ref, out_ref, faces_ref):
    trace_rows = out_ref.shape[0]
    here, there = block_at(block), block_at(level * (BLOCK // LANES) + block)
    for face in range(faces_in(joined_ref)):
        index = joined_ref[face:face + 1, there]
        faces_ref[face * trace_rows:(face + 1) * trace_rows, here] = pick(
            ref_blocks(out_ref, out_ref.shape[1] // LANES), index, index >> 7, jnp.zeros((trace_rows, LANES), f32))


def base_traces(own_ref, trace_grow_ref, weights_ref, rows):
    stacked = product(trace_grow_ref[...], stacked_columns(own_ref[...]))
    return summed_powers(stacked[rows:], weights_ref, rows, stacked[:rows])


def row_chunks(rows):
    return [slice(low, low + ROW_CHUNK) for low in range(0, rows, ROW_CHUNK)]


def grown_rows(chunk, stacked, loaded, grow_ref, weights_ref):
    rows = loaded.shape[0]
    matrix = jnp.concatenate(
        [grow_ref[power * rows + chunk.start:power * rows + chunk.stop, :] for power in range(POWERS)], axis=0)
    return summed_powers(product(matrix, stacked), weights_ref, ROW_CHUNK, loaded[chunk])


def matrix_powers(operator_ref, trace_ref, lift_ref, grow_ref, trace_grow_ref, mix_ref, lift_out_ref):
    comp = operator_ref.shape[0]
    trace_comp, faces, _ = lift_ref.shape
    rows = lift_out_ref.shape[0]
    trace_rows = trace_grow_ref.shape[0] // (POWERS + 1)
    operator = pad_rows(operator_ref[...], rows)
    operator = jnp.concatenate([operator, jnp.zeros((rows, rows - comp), f32)], axis=1)
    traces = pad_rows(trace_ref[...], trace_rows)
    traces = jnp.concatenate([traces, jnp.zeros((trace_rows, rows - comp), f32)], axis=1)
    lift = jnp.concatenate([pad_rows(lift_ref[:, face, :], trace_rows) for face in range(faces)], axis=0)
    lift = pad_rows(jnp.transpose(lift), rows)
    powers, have = operator, 1
    while have < POWERS:
        more = exact_product(jnp.concatenate([traces, powers], axis=0), powers[(have - 1) * rows:have * rows])
        traces = jnp.concatenate([traces, more[:have * trace_rows]], axis=0)
        powers = jnp.concatenate([powers, more[have * trace_rows:]], axis=0)
        have *= 2
    traces = jnp.concatenate([traces, exact_product(traces[:trace_rows], powers[-rows:])], axis=0)
    mix_ref[...] = stacked_matrix(exact_product(traces, lift))
    trace_grow_ref[...] = stacked_matrix(traces)
    lift_out_ref[...] = stacked_matrix(lift)
    grow_ref[...] = stacked_matrix(powers)


def plan_kernel(swaps, trace_ref, send_ref, order_ref, pattern_ref, sizes_ref, neighbours_ref, operator_ref,
                lift_ref, heights_ref, columns_ref, out_ref,
                members_ref, joined_ref, places_ref, send_places_ref, own_ref, faces_ref, weights_ref, base_ref,
                grow_ref, trace_grow_ref, mix_ref, lift_out_ref, wide_heights_ref):
    elements = columns_ref.shape[1]
    count = elements // LANES
    faces = neighbours_ref.shape[0]
    sizes = sizes_ref[...].astype(f32)
    number = lax.broadcasted_iota(i32, sizes.shape, 1)
    starts = [jnp.sum(jnp.where(number < level, sizes, 0.0)).astype(i32) for level in range(LEVELS)]
    wide_order = jnp.broadcast_to(order_ref[...], (8, elements))
    neighbours = neighbours_ref[...]
    group = (neighbours >> 7) - count
    message = jnp.full(neighbours.shape, count + len(swaps), i32)
    for number, swap in enumerate(swaps):
        message = jnp.where(group == came_group(swap), count + number, message)
    neighbours = jnp.where(group >= 0, message * LANES + (neighbours & (LANES - 1)), neighbours)
    table = jnp.concatenate(
        [neighbours, pattern_ref[...], jnp.zeros((faces - 1, elements), i32)], axis=0)
    heights = heights_ref[...]
    wide_heights_ref[...] = jnp.concatenate(
        [heights, jnp.zeros((1, LANES - heights.shape[1]), f32)], axis=1)
    for level in range(LEVELS):
        shift = jnp.where(starts[level] == 0, 0, elements - starts[level])
        members_ref[:, level * BLOCK:(level + 1) * BLOCK] = pltpu.roll(wide_order, shift, 1)[:, :BLOCK]
    for block in range(LEVELS * BLOCK // LANES):
        index = members_ref[:, block_at(block)]
        joined_ref[:, block_at(block)] = pick(value_blocks(table), index, index >> 7)
    ranks = lax.broadcasted_iota(i32, (count, elements), 1)
    in_block = (wide_order[:count] >> 7) == lax.broadcasted_iota(i32, (count, elements), 0)
    left = jnp.concatenate([
        jnp.where(in_block, ranks >> 5, 0).astype(f32), jnp.where(in_block, ranks & 31, 0).astype(f32)], axis=0)
    at_lane = jnp.broadcast_to(order_ref[...] & (LANES - 1), (LANES, elements)) == lax.broadcasted_iota(
        i32, (LANES, elements), 0)
    rank = lax.dot_general(left.astype(bf16), jnp.where(at_lane, 1.0, 0.0).astype(bf16), (((1,), (1,)), ((), ())),
                           preferred_element_type=f32)
    place = rank[:count].astype(i32) * 32 + rank[count:].astype(i32)
    at = place
    for level in range(1, LEVELS):
        at = jnp.where(place >= starts[level], place - starts[level] + level * BLOCK, at)
    places_ref[...] = at
    index = pad_rows(jnp.concatenate(sent_rows(send_ref, swaps), axis=0), 8)
    send_places_ref[...] = pick(row_blocks(at, 8), index, index >> 7)
    matrix_powers(operator_ref, trace_ref, lift_ref, grow_ref, trace_grow_ref, mix_ref, lift_out_ref)
    for block in range(BLOCK // LANES):
        own_block(0, block, members_ref, joined_ref, columns_ref, wide_heights_ref, own_ref, weights_ref)
    base_ref[...] = base_traces(own_ref, trace_grow_ref, weights_ref, out_ref.shape[0])
    for block in range(BLOCK // LANES):
        face_block(0, block, joined_ref, out_ref, faces_ref)


def settle(level, blocks, places_ref, before, block):
    index = places_ref[block:block + 1, :]
    which = (index >> 7) - level * (BLOCK // LANES)
    return pick(blocks, index, which, before)


def between_kernel(level, members_ref, joined_ref, places_ref, columns_ref, old_out_ref, new_trace_ref, heights_ref,
                   old_own_ref, inflow_ref, old_weights_ref, lift_ref, grow_ref, trace_grow_ref, *rest):
    if level > 1:
        advanced_ref, rest = rest[0], rest[1:]
    if level == LEVELS - 1:
        own_ref, faces_ref, weights_ref, new_advanced_ref, out_ref = rest
    else:
        out_ref, own_ref, faces_ref, weights_ref, base_ref, new_advanced_ref = rest
    count = places_ref.shape[0]
    done = level - 1
    loaded = old_own_ref[...] + product(lift_ref[...], stacked_columns(inflow_ref[...]))
    for block in range(count):
        here = block_at(block)
        out_ref[:, here] = settle(
            done, ref_blocks(new_trace_ref, BLOCK // LANES), places_ref, old_out_ref[:, here], block)
    stacked = stacked_columns(loaded)
    chunks = row_chunks(loaded.shape[0])
    pieces = BLOCK // LANES
    for number, chunk in enumerate(chunks):
        new = grown_rows(chunk, stacked, loaded, grow_ref, old_weights_ref)
        for block in range(number * pieces // len(chunks), (number + 1) * pieces // len(chunks)):
            own_block(level, block, members_ref, joined_ref, columns_ref, heights_ref, own_ref, weights_ref)
            face_block(level, block, joined_ref, out_ref, faces_ref)
        for block in range(count):
            here = block_at(block)
            before = advanced_ref[chunk, here] if level > 1 else None
            new_advanced_ref[chunk, here] = settle(done, value_blocks(new), places_ref, before, block)
    if level < LEVELS - 1:
        base_ref[...] = base_traces(own_ref, trace_grow_ref, weights_ref, out_ref.shape[0])


def inflow_block(level, block, received, joined_ref, faces_ref, count):
    faces = faces_in(joined_ref)
    trace_rows = faces_ref.shape[0] // faces
    blocks = [(count + i, functools.partial(lambda ref: ref[...], ref)) for i, ref in enumerate(received)]
    here, there = block_at(block), block_at(level * (BLOCK // LANES) + block)
    parts = []
    for face in range(faces):
        index = joined_ref[face:face + 1, there]
        parts.append(pick(blocks, index, index >> 7, faces_ref[face * trace_rows:(face + 1) * trace_rows, here]))
    return jnp.concatenate(parts, axis=0)


def level_kernel(level, messages, count, joined_ref, faces_ref, weights_ref, base_ref, mix_ref, send_places_ref,
                 *rest):
    received, rest = rest[:messages], rest[messages:]
    sent, rest = rest[:messages], rest[messages:]
    inflow_ref, new_trace_ref, sends = rest[0], rest[1], rest[2:]
    trace_rows = new_trace_ref.shape[0]
    blocks = range(BLOCK // LANES)
    for tile in (blocks[:2], blocks[2:]):
        across = slice(tile[0] * LANES, (tile[-1] + 1) * LANES)
        inflow = jnp.concatenate(
            [inflow_block(level, block, received, joined_ref, faces_ref, count) for block in tile], axis=1)
        inflow_ref[:, across] = inflow
        stacked = product(mix_ref[...], stacked_columns(inflow))
        total = base_ref[:, across] + stacked[:trace_rows]
        for power in range(1, POWERS + 1):
            total = total + stacked[power * trace_rows:(power + 1) * trace_rows] * weights_ref[power - 1:power, across]
        new_trace_ref[:, across] = total
    for group, (before, send) in enumerate(zip(sent, sends)):
        index = send_places_ref[group:group + 1, :]
        which = (index >> 7) - level * (BLOCK // LANES)
        send[...] = pick(ref_blocks(new_trace_ref, BLOCK // LANES), index, which, before[...])


def last_kernel(level, messages, joined_ref, own_ref, faces_ref, weights_ref, lift_ref, grow_ref,
                places_ref, advanced_ref, *rest):
    received, (final_hbm, final_ref, sent) = rest[:messages], rest[messages:]
    count = places_ref.shape[0]
    comp = final_ref.shape[0] // count
    inflow = jnp.concatenate(
        [inflow_block(level, block, received, joined_ref, faces_ref, count) for block in range(BLOCK // LANES)], axis=1)
    loaded = own_ref[...] + product(lift_ref[...], stacked_columns(inflow))
    stacked = stacked_columns(loaded)
    copies = []
    for number, chunk in enumerate(row_chunks(loaded.shape[0])):
        new = grown_rows(chunk, stacked, loaded, grow_ref, weights_ref)
        height = min(chunk.stop, comp) - chunk.start
        for block in range(count):
            done = settle(level, value_blocks(new), places_ref, advanced_ref[chunk, block_at(block)], block)
            final_ref[pl.ds(chunk.start * count + block, height, stride=count), :] = done[:height]
        part = pl.ds(chunk.start * count, height * count)
        copies.append(pltpu.make_async_copy(final_ref.at[part], final_hbm.at[part], sent.at[number]))
        copies[-1].start()
    for copy in copies:
        copy.wait()


def call(kernel, name, flops, operands, outs, scratch=(), hbm=False, out_hbm=False):
    vmem = pl.BlockSpec(memory_space=pltpu.VMEM)
    given = pl.BlockSpec(memory_space=pltpu.HBM) if hbm else vmem
    if hbm:
        operands = [pltpu.with_memory_space_constraint(one, pltpu.HBM) for one in operands]
    return pl.pallas_call(
        kernel,
        out_shape=tuple(jax.ShapeDtypeStruct(shape, dtype) for shape, dtype in outs),
        in_specs=[given] * len(operands),
        out_specs=tuple([pl.BlockSpec(memory_space=pltpu.HBM) if out_hbm else vmem] * len(outs)),
        scratch_shapes=[one if not isinstance(one, tuple) else pltpu.VMEM(*one) for one in scratch],
        compiler_params=pltpu.CompilerParams(vmem_limit_bytes=16 * 1024 * 1024),
        cost_estimate=pl.CostEstimate(flops=flops, bytes_accessed=1 << 20, transcendentals=0),
        name=name,
    )(*operands)


def is_odd(axis):
    return (lax.axis_index(axis) & 1) == 1


def swap_plan(axis, periodic, low, high):
    count = lax.axis_size(axis)
    plan = [(axis, [(i, i ^ 1) for i in range(count)], low, high, False)]
    if count > 2 or periodic:
        pairs = [(i, (i + 1) % count if i % 2 else (i - 1) % count) for i in range(count)]
        plan.append((axis, pairs, high, low, not periodic))
    return plan


def came_group(swap):
    axis, _, even, odd, is_open = swap
    came = jnp.where(is_odd(axis), even, odd)
    if is_open:
        index = lax.axis_index(axis)
        came = jnp.where((index == 0) | (index == lax.axis_size(axis) - 1), NO_GROUP, came)
    return came


def body(fields, pattern, tent_order, level_sizes, send_rows, neighbours, operator, trace_map, lift_map, tent_height):
    fields, order, sizes = fields[0, 0], tent_order[0], level_sizes[0]
    faces_of, send_list = neighbours[0, 0], send_rows[0, 0]
    comp, elements = fields.shape
    faces, trace = lift_map.shape[0], trace_map.shape[0]
    rows, trace_rows = rounded_up(comp, 16), rounded_up(trace, 16)
    padded, count = LEVELS * BLOCK, elements // LANES
    bnd = send_list.shape[-1]

    near, *far = swap_plan("sector", True, 0, 1)
    swaps = far + swap_plan("radial", False, 2, 3) + [near]
    messages = len(swaps)

    def exchange(sent):
        return [lax.ppermute(one, swap[0], swap[1]) for one, swap in zip(sent, swaps)]

    message = ((trace_rows, bnd), f32)
    own, face_stack = ((rows, BLOCK), f32), ((faces * trace_rows, BLOCK), f32)
    weight, table, traced = ((POWERS, BLOCK), f32), ((trace_rows, elements), f32), ((trace_rows, BLOCK), f32)
    whole = ((rows, elements), f32)
    flat = (comp * count, LANES)

    arguments = [trace_map, send_list, order, pattern[0], sizes, faces_of, operator,
                 jnp.transpose(lift_map, (2, 0, 1)), tent_height[None]]
    columns, out, *rest = call(
        functools.partial(first_kernel, swaps), "first", 10 ** 8, [fields.reshape(flat)] + arguments,
        [whole, table] + [message] * messages + [(one.shape, one.dtype) for one in arguments],
        [(flat, f32), pltpu.SemaphoreType.DMA((ARGUMENTS - 1 + FIELD_COPIES,))], hbm=True)
    sent, held = rest[:messages], rest[messages:]
    received = exchange(sent)
    members, joined, places, send_places, mine, inner, weights, base, grow, trace_grow, mix, lift, heights = call(
        functools.partial(plan_kernel, swaps), "plan", 2 * 10 ** 9, held + [columns, out],
        [((8, padded), i32), ((2 * faces, padded), i32), ((count, LANES), i32), ((8, bnd), i32),
         own, face_stack, weight, traced,
         ((POWERS * rows, 3 * rows), bf16), (((POWERS + 1) * trace_rows, 3 * rows), bf16),
         (((POWERS + 1) * trace_rows, 3 * faces * trace_rows), bf16), ((rows, 3 * faces * trace_rows), bf16),
         ((1, LANES), f32)])
    advanced = []
    for level in range(LEVELS - 1):
        inflow, new_trace, *sent = call(
            functools.partial(level_kernel, level, messages, count), "level", 10 ** 8,
            [joined, inner, weights, base, mix, send_places] + received + sent,
            [face_stack, traced] + [message] * messages)
        received = exchange(sent)
        beside = functools.partial(between_kernel, level + 1)
        operands = [members, joined, places, columns, out, new_trace, heights, mine, inflow, weights, lift, grow,
                    trace_grow] + advanced
        if level + 1 < LEVELS - 1:
            out, mine, inner, weights, base, *advanced = call(
                beside, "between", 2 * 10 ** 9, operands, [table, own, face_stack, weight, traced, whole])
        else:
            mine, inner, weights, *advanced = call(
                beside, "between", 2 * 10 ** 9, operands, [own, face_stack, weight, whole], [table])
    final, = call(
        functools.partial(last_kernel, LEVELS - 1, messages), "last", 10 ** 9,
        [joined, mine, inner, weights, lift, grow, places] + advanced + received,
        [(flat, f32)], [(flat, f32), pltpu.SemaphoreType.DMA((-(-rows // ROW_CHUNK),))], out_hbm=True)
    return final.reshape(1, 1, comp, elements)


def solution(mesh):
    in_specs = (
        P("sector", "radial", None, None),
        P("sector", "radial", None),
        P("sector", "radial", None),
        P("sector", "radial", None),
        P("sector", "radial", None, None),
        P("sector", "radial", None, None),
        P(),
        P(),
        P(),
        P(),
    )
    out_specs = P("sector", "radial", None, None)
    return jax.shard_map(body, mesh=mesh, in_specs=in_specs, out_specs=out_specs, check_vma=False)
```

```python
import functools
import math

import jax
import jax.numpy as jnp
from jax import lax
from jax.experimental import pallas as pl
from jax.experimental.pallas import tpu as pltpu
from jax.sharding import PartitionSpec as P

LEVELS = 4
SUBSTEPS = 2
TERMS = 4
BLOCK = 384
LANES = 128
NO_GROUP = 1 << 20
ARGUMENTS = 10
FIELD_COPIES = 4
ROW_CHUNK = 48

f32, bf16, i32 = jnp.float32, jnp.bfloat16, jnp.int32
precise = lax.Precision.HIGHEST


def rounded_up(size, unit):
    return -(-size // unit) * unit


def taylor_weights():
    once = [1.0 / math.factorial(k) for k in range(TERMS + 1)]
    whole = [1.0]
    for _ in range(SUBSTEPS):
        longer = [0.0] * (len(whole) + TERMS)
        for i, a in enumerate(whole):
            for j, b in enumerate(once):
                longer[i + j] += a * b
        whole = longer
    return whole


WEIGHTS = taylor_weights()
POWERS = len(WEIGHTS) - 1


def split(values):
    high = values.astype(bf16)
    return high, (values - high.astype(f32)).astype(bf16)


def stacked_columns(values):
    high, low = split(values)
    return jnp.concatenate([high, low, high], axis=0)


def stacked_matrix(values):
    high = values.astype(bf16).astype(f32)
    low = values - high
    return jnp.concatenate([high, high, low], axis=1).astype(bf16)


def product(matrix, columns):
    return jnp.dot(matrix, columns, preferred_element_type=f32)


def pad_rows(values, rows):
    short = rows - values.shape[0]
    if short == 0:
        return values
    return jnp.concatenate([values, jnp.zeros((short,) + values.shape[1:], values.dtype)], axis=0)


def exact_product(left, right):
    left_high, left_low = split(left)
    right_high, right_low = split(right)
    rows = left.shape[0]
    both = product(jnp.concatenate([left_high, left_low], axis=0), right_high)
    return both[:rows] + both[rows:] + product(left_high, right_low)


def pick(blocks, index, which, start=None):
    result = start
    for number, read in blocks:
        table = read()
        lane = jnp.broadcast_to(index & (LANES - 1), table.shape)
        got = jnp.take_along_axis(table, lane, axis=1, mode="promise_in_bounds")
        if result is None:
            result = got
        else:
            result = jnp.where(jnp.broadcast_to(which, table.shape) == number, got, result)
    return result


def block_at(block):
    return slice(block * LANES, (block + 1) * LANES)


def ref_blocks(ref, count):
    return [(b, functools.partial(lambda b: ref[:, block_at(b)], b)) for b in range(count)]


def value_blocks(values):
    return [(b, functools.partial(lambda b: values[:, block_at(b)], b)) for b in range(values.shape[1] // LANES)]


def row_blocks(table, rows):
    return [
        (b, functools.partial(lambda b: jnp.broadcast_to(table[b:b + 1, :], (rows, LANES)), b))
        for b in range(table.shape[0])
    ]


def summed_powers(stacked, weights_ref, rows, total):
    for power in range(1, POWERS + 1):
        total = total + stacked[(power - 1) * rows:power * rows] * weights_ref[power - 1:power, :]
    return total


def sent_rows(send_ref, swaps):
    rows = []
    for axis, _, low, high, _ in swaps:
        odd, even = send_ref[high:high + 1, :], send_ref[low:low + 1, :]
        rows.append(jnp.where(is_odd(axis), odd, even))
    return rows


def first_kernel(swaps, *refs):
    (fields_hbm, *given), refs = refs[:ARGUMENTS], refs[ARGUMENTS:]
    (columns_ref, out_ref), refs = refs[:2], refs[2:]
    sends, refs = refs[:len(swaps)], refs[len(swaps):]
    *held, fields_ref, arrived = refs
    share = fields_ref.shape[0] // FIELD_COPIES
    pairs = list(zip(given[:2], held[:2]))
    pairs += [(fields_hbm.at[pl.ds(i * share, share)], fields_ref.at[pl.ds(i * share, share)])
              for i in range(FIELD_COPIES)]
    needed = len(pairs)
    pairs += list(zip(given[2:], held[2:]))
    copies = [pltpu.make_async_copy(source, target, arrived.at[i]) for i, (source, target) in enumerate(pairs)]
    for copy in copies:
        copy.start()
    for copy in copies[:needed]:
        copy.wait()
    trace_ref, send_ref = held[:2]
    rows = out_ref.shape[0]
    elements = out_ref.shape[1]
    count = elements // LANES
    comp = fields_ref.shape[0] // count
    trace = pad_rows(trace_ref[...], rows)
    trace_high, trace_low = split(trace)
    both = jnp.concatenate([trace_high, trace_low], axis=0)
    fields = jnp.concatenate([fields_ref[pl.ds(b, comp, stride=count), :] for b in range(count)], axis=1)
    high, low = split(fields)
    upper = product(both, high)
    out_ref[...] = upper[:rows] + upper[rows:] + product(trace_high, low)
    for index, send in zip(sent_rows(send_ref, swaps), sends):
        send[...] = pick(ref_blocks(out_ref, count), index, index >> 7)
    columns_ref[...] = pad_rows(fields, columns_ref.shape[0])
    for copy in copies[needed:]:
        copy.wait()


def faces_in(joined_ref):
    return joined_ref.shape[0] // 2


def own_block(level, block, members_ref, joined_ref, columns_ref, heights_ref, own_ref, weights_ref):
    faces = faces_in(joined_ref)
    here, there = block_at(block), block_at(level * (BLOCK // LANES) + block)
    index = members_ref[0:1, there]
    own_ref[:, here] = pick(ref_blocks(columns_ref, columns_ref.shape[1] // LANES), index, index >> 7)
    pattern = jnp.broadcast_to(joined_ref[faces:faces + 1, there], (8, LANES))
    height = jnp.take_along_axis(
        jnp.broadcast_to(heights_ref[...], (8, LANES)), pattern, axis=1, mode="promise_in_bounds")
    weight = jnp.ones((8, LANES), f32)
    for power in range(1, POWERS + 1):
        weight = weight * height
        weights_ref[power - 1:power, here] = weight[0:1] * WEIGHTS[power]


def face_block(level, block, joined_ref, out_ref, faces_ref):
    trace_rows = out_ref.shape[0]
    here, there = block_at(block), block_at(level * (BLOCK // LANES) + block)
    for face in range(faces_in(joined_ref)):
        index = joined_ref[face:face + 1, there]
        faces_ref[face * trace_rows:(face + 1) * trace_rows, here] = pick(
            ref_blocks(out_ref, out_ref.shape[1] // LANES), index, index >> 7, jnp.zeros((trace_rows, LANES), f32))


def base_traces(own_ref, trace_grow_ref, weights_ref, rows):
    stacked = product(trace_grow_ref[...], stacked_columns(own_ref[...]))
    return summed_powers(stacked[rows:], weights_ref, rows, stacked[:rows])


def row_chunks(rows):
    return [slice(low, low + ROW_CHUNK) for low in range(0, rows, ROW_CHUNK)]


def grown_rows(chunk, stacked, loaded, grow_ref, weights_ref):
    rows = loaded.shape[0]
    matrix = jnp.concatenate(
        [grow_ref[power * rows + chunk.start:power * rows + chunk.stop, :] for power in range(POWERS)], axis=0)
    return summed_powers(product(matrix, stacked), weights_ref, ROW_CHUNK, loaded[chunk])


def matrix_powers(operator_ref, trace_ref, lift_ref, grow_ref, trace_grow_ref, mix_ref, lift_out_ref):
    comp = operator_ref.shape[0]
    trace_comp, faces, _ = lift_ref.shape
    rows = lift_out_ref.shape[0]
    trace_rows = trace_grow_ref.shape[0] // (POWERS + 1)
    operator = pad_rows(operator_ref[...], rows)
    operator = jnp.concatenate([operator, jnp.zeros((rows, rows - comp), f32)], axis=1)
    traces = pad_rows(trace_ref[...], trace_rows)
    traces = jnp.concatenate([traces, jnp.zeros((trace_rows, rows - comp), f32)], axis=1)
    lift = jnp.concatenate([pad_rows(lift_ref[:, face, :], trace_rows) for face in range(faces)], axis=0)
    lift = pad_rows(jnp.transpose(lift), rows)
    powers, have = operator, 1
    while have < POWERS:
        more = exact_product(jnp.concatenate([traces, powers], axis=0), powers[(have - 1) * rows:have * rows])
        traces = jnp.concatenate([traces, more[:have * trace_rows]], axis=0)
        powers = jnp.concatenate([powers, more[have * trace_rows:]], axis=0)
        have *= 2
    traces = jnp.concatenate([traces, exact_product(traces[:trace_rows], powers[-rows:])], axis=0)
    mix_ref[...] = stacked_matrix(exact_product(traces, lift))
    trace_grow_ref[...] = stacked_matrix(traces)
    lift_out_ref[...] = stacked_matrix(lift)
    grow_ref[...] = stacked_matrix(powers)


def plan_kernel(swaps, trace_ref, send_ref, order_ref, pattern_ref, sizes_ref, neighbours_ref, operator_ref,
                lift_ref, heights_ref, columns_ref, out_ref,
                members_ref, joined_ref, places_ref, send_places_ref, own_ref, faces_ref, weights_ref, base_ref,
                grow_ref, trace_grow_ref, mix_ref, lift_out_ref, wide_heights_ref):
    elements = columns_ref.shape[1]
    count = elements // LANES
    faces = neighbours_ref.shape[0]
    sizes = sizes_ref[...].astype(f32)
    number = lax.broadcasted_iota(i32, sizes.shape, 1)
    starts = [jnp.sum(jnp.where(number < level, sizes, 0.0)).astype(i32) for level in range(LEVELS)]
    wide_order = jnp.broadcast_to(order_ref[...], (8, elements))
    neighbours = neighbours_ref[...]
    group = (neighbours >> 7) - count
    message = jnp.full(neighbours.shape, count + len(swaps), i32)
    for number, swap in enumerate(swaps):
        message = jnp.where(group == came_group(swap), count + number, message)
    neighbours = jnp.where(group >= 0, message * LANES + (neighbours & (LANES - 1)), neighbours)
    table = jnp.concatenate(
        [neighbours, pattern_ref[...], jnp.zeros((faces - 1, elements), i32)], axis=0)
    heights = heights_ref[...]
    wide_heights_ref[...] = jnp.concatenate(
        [heights, jnp.zeros((1, LANES - heights.shape[1]), f32)], axis=1)
    for level in range(LEVELS):
        shift = jnp.where(starts[level] == 0, 0, elements - starts[level])
        members_ref[:, level * BLOCK:(level + 1) * BLOCK] = pltpu.roll(wide_order, shift, 1)[:, :BLOCK]
    for block in range(LEVELS * BLOCK // LANES):
        index = members_ref[:, block_at(block)]
        joined_ref[:, block_at(block)] = pick(value_blocks(table), index, index >> 7)
    ranks = lax.broadcasted_iota(i32, (count, elements), 1)
    in_block = (wide_order[:count] >> 7) == lax.broadcasted_iota(i32, (count, elements), 0)
    left = jnp.concatenate([
        jnp.where(in_block, ranks >> 5, 0).astype(f32), jnp.where(in_block, ranks & 31, 0).astype(f32)], axis=0)
    at_lane = jnp.broadcast_to(order_ref[...] & (LANES - 1), (LANES, elements)) == lax.broadcasted_iota(
        i32, (LANES, elements), 0)
    rank = lax.dot_general(left.astype(bf16), jnp.where(at_lane, 1.0, 0.0).astype(bf16), (((1,), (1,)), ((), ())),
                           preferred_element_type=f32)
    place = rank[:count].astype(i32) * 32 + rank[count:].astype(i32)
    at = place
    for level in range(1, LEVELS):
        at = jnp.where(place >= starts[level], place - starts[level] + level * BLOCK, at)
    places_ref[...] = at
    index = pad_rows(jnp.concatenate(sent_rows(send_ref, swaps), axis=0), 8)
    send_places_ref[...] = pick(row_blocks(at, 8), index, index >> 7)
    matrix_powers(operator_ref, trace_ref, lift_ref, grow_ref, trace_grow_ref, mix_ref, lift_out_ref)
    for block in range(BLOCK // LANES):
        own_block(0, block, members_ref, joined_ref, columns_ref, wide_heights_ref, own_ref, weights_ref)
    base_ref[...] = base_traces(own_ref, trace_grow_ref, weights_ref, out_ref.shape[0])
    for block in range(BLOCK // LANES):
        face_block(0, block, joined_ref, out_ref, faces_ref)


def settle(level, blocks, places_ref, before, block):
    index = places_ref[block:block + 1, :]
    which = (index >> 7) - level * (BLOCK // LANES)
    return pick(blocks, index, which, before)


def between_kernel(level, members_ref, joined_ref, places_ref, columns_ref, old_out_ref, new_trace_ref, heights_ref,
                   old_own_ref, inflow_ref, old_weights_ref, lift_ref, grow_ref, trace_grow_ref, *rest):
    if level > 1:
        advanced_ref, rest = rest[0], rest[1:]
    if level == LEVELS - 1:
        own_ref, faces_ref, weights_ref, new_advanced_ref, out_ref = rest
    else:
        out_ref, own_ref, faces_ref, weights_ref, base_ref, new_advanced_ref = rest
    count = places_ref.shape[0]
    done = level - 1
    loaded = old_own_ref[...] + product(lift_ref[...], stacked_columns(inflow_ref[...]))
    for block in range(count):
        here = block_at(block)
        out_ref[:, here] = settle(
            done, ref_blocks(new_trace_ref, BLOCK // LANES), places_ref, old_out_ref[:, here], block)
    stacked = stacked_columns(loaded)
    chunks = row_chunks(loaded.shape[0])
    pieces = BLOCK // LANES
    for number, chunk in enumerate(chunks):
        new = grown_rows(chunk, stacked, loaded, grow_ref, old_weights_ref)
        for block in range(number * pieces // len(chunks), (number + 1) * pieces // len(chunks)):
            own_block(level, block, members_ref, joined_ref, columns_ref, heights_ref, own_ref, weights_ref)
            face_block(level, block, joined_ref, out_ref, faces_ref)
        for block in range(count):
            here = block_at(block)
            before = advanced_ref[chunk, here] if level > 1 else None
            new_advanced_ref[chunk, here] = settle(done, value_blocks(new), places_ref, before, block)
    if level < LEVELS - 1:
        base_ref[...] = base_traces(own_ref, trace_grow_ref, weights_ref, out_ref.shape[0])


def inflow_block(level, block, received, joined_ref, faces_ref, count):
    faces = faces_in(joined_ref)
    trace_rows = faces_ref.shape[0] // faces
    blocks = [(count + i, functools.partial(lambda ref: ref[...], ref)) for i, ref in enumerate(received)]
    here, there = block_at(block), block_at(level * (BLOCK // LANES) + block)
    parts = []
    for face in range(faces):
        index = joined_ref[face:face + 1, there]
        parts.append(pick(blocks, index, index >> 7, faces_ref[face * trace_rows:(face + 1) * trace_rows, here]))
    return jnp.concatenate(parts, axis=0)


def level_kernel(level, messages, count, joined_ref, faces_ref, weights_ref, base_ref, mix_ref, send_places_ref,
                 *rest):
    received, rest = rest[:messages], rest[messages:]
    sent, rest = rest[:messages], rest[messages:]
    inflow_ref, new_trace_ref, sends = rest[0], rest[1], rest[2:]
    trace_rows = new_trace_ref.shape[0]
    blocks = range(BLOCK // LANES)
    for tile in (blocks[:2], blocks[2:]):
        across = slice(tile[0] * LANES, (tile[-1] + 1) * LANES)
        inflow = jnp.concatenate(
            [inflow_block(level, block, received, joined_ref, faces_ref, count) for block in tile], axis=1)
        inflow_ref[:, across] = inflow
        stacked = product(mix_ref[...], stacked_columns(inflow))
        total = base_ref[:, across] + stacked[:trace_rows]
        for power in range(1, POWERS + 1):
            total = total + stacked[power * trace_rows:(power + 1) * trace_rows] * weights_ref[power - 1:power, across]
        new_trace_ref[:, across] = total
    for group, (before, send) in enumerate(zip(sent, sends)):
        index = send_places_ref[group:group + 1, :]
        which = (index >> 7) - level * (BLOCK // LANES)
        send[...] = pick(ref_blocks(new_trace_ref, BLOCK // LANES), index, which, before[...])


def last_kernel(level, messages, joined_ref, own_ref, faces_ref, weights_ref, lift_ref, grow_ref,
                places_ref, advanced_ref, *rest):
    received, (final_hbm, final_ref, sent) = rest[:messages], rest[messages:]
    count = places_ref.shape[0]
    comp = final_ref.shape[0] // count
    inflow = jnp.concatenate(
        [inflow_block(level, block, received, joined_ref, faces_ref, count) for block in range(BLOCK // LANES)], axis=1)
    loaded = own_ref[...] + product(lift_ref[...], stacked_columns(inflow))
    stacked = stacked_columns(loaded)
    copies = []
    for number, chunk in enumerate(row_chunks(loaded.shape[0])):
        new = grown_rows(chunk, stacked, loaded, grow_ref, weights_ref)
        height = min(chunk.stop, comp) - chunk.start
        for block in range(count):
            done = settle(level, value_blocks(new), places_ref, advanced_ref[chunk, block_at(block)], block)
            final_ref[pl.ds(chunk.start * count + block, height, stride=count), :] = done[:height]
        part = pl.ds(chunk.start * count, height * count)
        copies.append(pltpu.make_async_copy(final_ref.at[part], final_hbm.at[part], sent.at[number]))
        copies[-1].start()
    for copy in copies:
        copy.wait()


def call(kernel, name, flops, operands, outs, scratch=(), hbm=False, out_hbm=False):
    vmem = pl.BlockSpec(memory_space=pltpu.VMEM)
    given = pl.BlockSpec(memory_space=pltpu.HBM) if hbm else vmem
    if hbm:
        operands = [pltpu.with_memory_space_constraint(one, pltpu.HBM) for one in operands]
    return pl.pallas_call(
        kernel,
        out_shape=tuple(jax.ShapeDtypeStruct(shape, dtype) for shape, dtype in outs),
        in_specs=[given] * len(operands),
        out_specs=tuple([pl.BlockSpec(memory_space=pltpu.HBM) if out_hbm else vmem] * len(outs)),
        scratch_shapes=[one if not isinstance(one, tuple) else pltpu.VMEM(*one) for one in scratch],
        compiler_params=pltpu.CompilerParams(vmem_limit_bytes=16 * 1024 * 1024),
        cost_estimate=pl.CostEstimate(flops=flops, bytes_accessed=1 << 20, transcendentals=0),
        name=name,
    )(*operands)


def is_odd(axis):
    return (lax.axis_index(axis) & 1) == 1


def swap_plan(axis, periodic, low, high):
    count = lax.axis_size(axis)
    plan = [(axis, [(i, i ^ 1) for i in range(count)], low, high, False)]
    if count > 2 or periodic:
        pairs = [(i, (i + 1) % count if i % 2 else (i - 1) % count) for i in range(count)]
        plan.append((axis, pairs, high, low, not periodic))
    return plan


def came_group(swap):
    axis, _, even, odd, is_open = swap
    came = jnp.where(is_odd(axis), even, odd)
    if is_open:
        index = lax.axis_index(axis)
        came = jnp.where((index == 0) | (index == lax.axis_size(axis) - 1), NO_GROUP, came)
    return came


def body(fields, pattern, tent_order, level_sizes, send_rows, neighbours, operator, trace_map, lift_map, tent_height):
    fields, order, sizes = fields[0, 0], tent_order[0], level_sizes[0]
    faces_of, send_list = neighbours[0, 0], send_rows[0, 0]
    comp, elements = fields.shape
    faces, trace = lift_map.shape[0], trace_map.shape[0]
    rows, trace_rows = rounded_up(comp, 16), rounded_up(trace, 16)
    padded, count = LEVELS * BLOCK, elements // LANES
    bnd = send_list.shape[-1]

    near, *far = swap_plan("sector", True, 0, 1)
    swaps = far + swap_plan("radial", False, 2, 3) + [near]
    messages = len(swaps)

    def exchange(sent):
        got = []
        for one, (axis, pairs, *_) in zip(sent, swaps):
            if one is sent[0]:
                groups = [pair for pair in pairs if pair[0] < pair[1]]
                both = lax.all_gather(one, axis, axis_index_groups=groups)
                index = lax.axis_index(axis)
                partner_first = (index & 1) == 0
                partner_first = partner_first & (index > 0) | (index == lax.axis_size(axis) - 1)
                got.append(jnp.where(partner_first, both[0], both[1]))
            else:
                got.append(lax.ppermute(one, axis, pairs))
        return got

    message = ((trace_rows, bnd), f32)
    own, face_stack = ((rows, BLOCK), f32), ((faces * trace_rows, BLOCK), f32)
    weight, table, traced = ((POWERS, BLOCK), f32), ((trace_rows, elements), f32), ((trace_rows, BLOCK), f32)
    whole = ((rows, elements), f32)
    flat = (comp * count, LANES)

    arguments = [trace_map, send_list, order, pattern[0], sizes, faces_of, operator,
                 jnp.transpose(lift_map, (2, 0, 1)), tent_height[None]]
    columns, out, *rest = call(
        functools.partial(first_kernel, swaps), "first", 10 ** 8, [fields.reshape(flat)] + arguments,
        [whole, table] + [message] * messages + [(one.shape, one.dtype) for one in arguments],
        [(flat, f32), pltpu.SemaphoreType.DMA((ARGUMENTS - 1 + FIELD_COPIES,))], hbm=True)
    sent, held = rest[:messages], rest[messages:]
    received = exchange(sent)
    members, joined, places, send_places, mine, inner, weights, base, grow, trace_grow, mix, lift, heights = call(
        functools.partial(plan_kernel, swaps), "plan", 2 * 10 ** 9, held + [columns, out],
        [((8, padded), i32), ((2 * faces, padded), i32), ((count, LANES), i32), ((8, bnd), i32),
         own, face_stack, weight, traced,
         ((POWERS * rows, 3 * rows), bf16), (((POWERS + 1) * trace_rows, 3 * rows), bf16),
         (((POWERS + 1) * trace_rows, 3 * faces * trace_rows), bf16), ((rows, 3 * faces * trace_rows), bf16),
         ((1, LANES), f32)])
    advanced = []
    for level in range(LEVELS - 1):
        inflow, new_trace, *sent = call(
            functools.partial(level_kernel, level, messages, count), "level", 10 ** 8,
            [joined, inner, weights, base, mix, send_places] + received + sent,
            [face_stack, traced] + [message] * messages)
        received = exchange(sent)
        beside = functools.partial(between_kernel, level + 1)
        operands = [members, joined, places, columns, out, new_trace, heights, mine, inflow, weights, lift, grow,
                    trace_grow] + advanced
        if level + 1 < LEVELS - 1:
            out, mine, inner, weights, base, *advanced = call(
                beside, "between", 2 * 10 ** 9, operands, [table, own, face_stack, weight, traced, whole])
        else:
            mine, inner, weights, *advanced = call(
                beside, "between", 2 * 10 ** 9, operands, [own, face_stack, weight, whole], [table])
    final, = call(
        functools.partial(last_kernel, LEVELS - 1, messages), "last", 10 ** 9,
        [joined, mine, inner, weights, lift, grow, places] + advanced + received,
        [(flat, f32)], [(flat, f32), pltpu.SemaphoreType.DMA((-(-rows // ROW_CHUNK),))], out_hbm=True)
    return final.reshape(1, 1, comp, elements)


def solution(mesh):
    in_specs = (
        P("sector", "radial", None, None),
        P("sector", "radial", None),
        P("sector", "radial", None),
        P("sector", "radial", None),
        P("sector", "radial", None, None),
        P("sector", "radial", None, None),
        P(),
        P(),
        P(),
        P(),
    )
    out_specs = P("sector", "radial", None, None)
    return jax.shard_map(body, mesh=mesh, in_specs=in_specs, out_specs=out_specs, check_vma=False)
```

```python
import functools
import math

import jax
import jax.numpy as jnp
from jax import lax
from jax.experimental import pallas as pl
from jax.experimental.pallas import tpu as pltpu
from jax.sharding import PartitionSpec as P

LEVELS = 4
SUBSTEPS = 2
TERMS = 4
BLOCK = 384
LANES = 128
NO_GROUP = 1 << 20
ARGUMENTS = 10
ROW_CHUNK = 48

f32, bf16, i32 = jnp.float32, jnp.bfloat16, jnp.int32
precise = lax.Precision.HIGHEST


def rounded_up(size, unit):
    return -(-size // unit) * unit


def taylor_weights():
    once = [1.0 / math.factorial(k) for k in range(TERMS + 1)]
    whole = [1.0]
    for _ in range(SUBSTEPS):
        longer = [0.0] * (len(whole) + TERMS)
        for i, a in enumerate(whole):
            for j, b in enumerate(once):
                longer[i + j] += a * b
        whole = longer
    return whole


WEIGHTS = taylor_weights()
POWERS = len(WEIGHTS) - 1


def split(values):
    high = values.astype(bf16)
    return high, (values - high.astype(f32)).astype(bf16)


def stacked_columns(values):
    high, low = split(values)
    return jnp.concatenate([high, low, high], axis=0)


def stacked_matrix(values):
    high = values.astype(bf16).astype(f32)
    low = values - high
    return jnp.concatenate([high, high, low], axis=1).astype(bf16)


def product(matrix, columns):
    return jnp.dot(matrix, columns, preferred_element_type=f32)


def pad_rows(values, rows):
    short = rows - values.shape[0]
    if short == 0:
        return values
    return jnp.concatenate([values, jnp.zeros((short,) + values.shape[1:], values.dtype)], axis=0)


def exact_product(left, right):
    left_high, left_low = split(left)
    right_high, right_low = split(right)
    rows = left.shape[0]
    both = product(jnp.concatenate([left_high, left_low], axis=0), right_high)
    return both[:rows] + both[rows:] + product(left_high, right_low)


def pick(blocks, index, which, start=None):
    result = start
    for number, read in blocks:
        table = read()
        lane = jnp.broadcast_to(index & (LANES - 1), table.shape)
        got = jnp.take_along_axis(table, lane, axis=1, mode="promise_in_bounds")
        if result is None:
            result = got
        else:
            result = jnp.where(jnp.broadcast_to(which, table.shape) == number, got, result)
    return result


def block_at(block):
    return slice(block * LANES, (block + 1) * LANES)


def ref_blocks(ref, count):
    return [(b, functools.partial(lambda b: ref[:, block_at(b)], b)) for b in range(count)]


def value_blocks(values):
    return [(b, functools.partial(lambda b: values[:, block_at(b)], b)) for b in range(values.shape[1] // LANES)]


def row_blocks(table, rows):
    return [
        (b, functools.partial(lambda b: jnp.broadcast_to(table[b:b + 1, :], (rows, LANES)), b))
        for b in range(table.shape[0])
    ]


def row_blocks_of(row, rows):
    return [
        (b, functools.partial(lambda b: jnp.broadcast_to(row[:, block_at(b)], (rows, LANES)), b))
        for b in range(row.shape[1] // LANES)
    ]


def summed_powers(stacked, weights_ref, rows, total):
    for power in range(1, POWERS + 1):
        total = total + stacked[(power - 1) * rows:power * rows] * weights_ref[power - 1:power, :]
    return total


def sent_rows(send_ref, swaps):
    rows = []
    for axis, _, low, high, _ in swaps:
        odd, even = send_ref[high:high + 1, :], send_ref[low:low + 1, :]
        rows.append(jnp.where(is_odd(axis), odd, even))
    return rows


def first_kernel(swaps, *refs):
    (fields_hbm, *given), refs = refs[:ARGUMENTS], refs[ARGUMENTS:]
    (columns_ref, out_ref), refs = refs[:2], refs[2:]
    sends, refs = refs[:len(swaps)], refs[len(swaps):]
    *held, fields_ref, arrived = refs
    copies = [
        pltpu.make_async_copy(source, target, arrived.at[i])
        for i, (source, target) in enumerate(zip([fields_hbm] + given, [fields_ref] + held))
    ]
    for copy in copies:
        copy.start()
    needed = 3
    for copy in copies[:needed]:
        copy.wait()
    trace_ref, send_ref = held[:2]
    rows = out_ref.shape[0]
    elements = out_ref.shape[1]
    count = elements // LANES
    comp = fields_ref.shape[0] // count
    trace = pad_rows(trace_ref[...], rows)
    trace_high, trace_low = split(trace)
    both = jnp.concatenate([trace_high, trace_low], axis=0)
    fields = jnp.concatenate([fields_ref[pl.ds(b, comp, stride=count), :] for b in range(count)], axis=1)
    high, low = split(fields)
    upper = product(both, high)
    out_ref[...] = upper[:rows] + upper[rows:] + product(trace_high, low)
    for index, send in zip(sent_rows(send_ref, swaps), sends):
        send[...] = pick(ref_blocks(out_ref, count), index, index >> 7)
    columns_ref[...] = pad_rows(fields, columns_ref.shape[0])
    for copy in copies[needed:]:
        copy.wait()


def faces_in(joined_ref):
    return joined_ref.shape[0] // 2


def own_block(level, block, members_ref, joined_ref, columns_ref, heights_ref, own_ref, weights_ref):
    faces = faces_in(joined_ref)
    here, there = block_at(block), block_at(level * (BLOCK // LANES) + block)
    index = members_ref[0:1, there]
    own_ref[:, here] = pick(ref_blocks(columns_ref, columns_ref.shape[1] // LANES), index, index >> 7)
    pattern = jnp.broadcast_to(joined_ref[faces:faces + 1, there], (8, LANES))
    height = jnp.take_along_axis(
        jnp.broadcast_to(heights_ref[...], (8, LANES)), pattern, axis=1, mode="promise_in_bounds")
    weight = jnp.ones((8, LANES), f32)
    for power in range(1, POWERS + 1):
        weight = weight * height
        weights_ref[power - 1:power, here] = weight[0:1] * WEIGHTS[power]


def face_block(level, block, joined_ref, out_ref, faces_ref):
    trace_rows = out_ref.shape[0]
    here, there = block_at(block), block_at(level * (BLOCK // LANES) + block)
    for face in range(faces_in(joined_ref)):
        index = joined_ref[face:face + 1, there]
        faces_ref[face * trace_rows:(face + 1) * trace_rows, here] = pick(
            ref_blocks(out_ref, out_ref.shape[1] // LANES), index, index >> 7, jnp.zeros((trace_rows, LANES), f32))


def local_part(level, members_ref, joined_ref, columns_ref, out_ref, heights_ref, lift_ref,
               loaded_ref, weights_ref, faces_ref):
    for block in range(BLOCK // LANES):
        own_block(level, block, members_ref, joined_ref, columns_ref, heights_ref, loaded_ref, weights_ref)
        face_block(level, block, joined_ref, out_ref, faces_ref)
    loaded_ref[...] = loaded_ref[...] + product(lift_ref[...], stacked_columns(faces_ref[...]))


def advanced_traces(loaded, matrix_ref, weights_ref, rows):
    stacked = product(matrix_ref[...], stacked_columns(loaded))
    return summed_powers(stacked[rows:], weights_ref, rows, stacked[:rows])


def local_messages(level, trace_ref, send_places_ref, sent, messages):
    for group, (before, message) in enumerate(zip(sent, messages)):
        index = send_places_ref[group:group + 1, :]
        which = (index >> 7) - level * (BLOCK // LANES)
        message[...] = pick(ref_blocks(trace_ref, BLOCK // LANES), index, which, before[...])


def row_chunks(rows):
    return [slice(low, low + ROW_CHUNK) for low in range(0, rows, ROW_CHUNK)]


def grown_rows(chunk, stacked, loaded, grow_ref, weights_ref):
    rows = loaded.shape[0]
    matrix = jnp.concatenate(
        [grow_ref[power * rows + chunk.start:power * rows + chunk.stop, :] for power in range(POWERS)], axis=0)
    return summed_powers(product(matrix, stacked), weights_ref, ROW_CHUNK, loaded[chunk])


def matrix_powers(operator_ref, trace_ref, lift_ref, grow_ref, trace_grow_ref, mix_ref, mix_first_ref,
                  lift_out_ref, lift_first_ref):
    comp = operator_ref.shape[0]
    trace_comp, faces, _ = lift_ref.shape
    rows = lift_out_ref.shape[0]
    trace_rows = trace_grow_ref.shape[0] // (POWERS + 1)
    operator = pad_rows(operator_ref[...], rows)
    operator = jnp.concatenate([operator, jnp.zeros((rows, rows - comp), f32)], axis=1)
    traces = pad_rows(trace_ref[...], trace_rows)
    traces = jnp.concatenate([traces, jnp.zeros((trace_rows, rows - comp), f32)], axis=1)
    lift = jnp.concatenate([pad_rows(lift_ref[:, face, :], trace_rows) for face in range(faces)], axis=0)
    lift = pad_rows(jnp.transpose(lift), rows)
    powers, have = operator, 1
    while have < POWERS:
        more = exact_product(jnp.concatenate([traces, powers], axis=0), powers[(have - 1) * rows:have * rows])
        traces = jnp.concatenate([traces, more[:have * trace_rows]], axis=0)
        powers = jnp.concatenate([powers, more[have * trace_rows:]], axis=0)
        have *= 2
    traces = jnp.concatenate([traces, exact_product(traces[:trace_rows], powers[-rows:])], axis=0)
    mix = exact_product(traces, lift)
    mix_ref[...] = stacked_matrix(mix)
    mix_first_ref[...] = stacked_matrix(mix[:, :trace_rows])
    lift_first_ref[...] = stacked_matrix(lift[:, :trace_rows])
    trace_grow_ref[...] = stacked_matrix(traces)
    lift_out_ref[...] = stacked_matrix(lift)
    grow_ref[...] = stacked_matrix(powers)


def plan_kernel(swaps, *refs):
    (trace_ref, send_ref, order_ref, pattern_ref, sizes_ref, neighbours_ref, operator_ref, lift_ref, heights_ref,
     columns_ref, out_ref), refs = refs[:11], refs[11:]
    messages = len(swaps)
    sent, refs = refs[:messages], refs[messages:]
    (members_ref, joined_ref, places_ref, send_places_ref, send_codes_ref, slot_weights_ref, flags_ref, loaded_ref,
     weights_ref, new_trace_ref, grow_ref, trace_grow_ref, mix_ref, mix_first_ref, lift_out_ref, lift_first_ref,
     wide_heights_ref), refs = refs[:17], refs[17:]
    prepared, (faces_ref,) = refs[:messages], refs[messages:]
    elements = columns_ref.shape[1]
    count = elements // LANES
    faces = neighbours_ref.shape[0]
    sizes = sizes_ref[...].astype(f32)
    number = lax.broadcasted_iota(i32, sizes.shape, 1)
    starts = [jnp.sum(jnp.where(number < level, sizes, 0.0)).astype(i32) for level in range(LEVELS)]
    wide_order = jnp.broadcast_to(order_ref[...], (8, elements))
    neighbours = neighbours_ref[...]
    group = (neighbours >> 7) - count
    message = jnp.full(neighbours.shape, count + len(swaps), i32)
    for number, swap in enumerate(swaps):
        message = jnp.where(group == came_group(swap), count + number, message)
    neighbours = jnp.where(group >= 0, message * LANES + (neighbours & (LANES - 1)), neighbours)
    table = jnp.concatenate(
        [neighbours, pattern_ref[...], jnp.zeros((faces - 1, elements), i32)], axis=0)
    heights = heights_ref[...]
    wide_heights_ref[...] = jnp.concatenate(
        [heights, jnp.zeros((1, LANES - heights.shape[1]), f32)], axis=1)
    for level in range(LEVELS):
        shift = jnp.where(starts[level] == 0, 0, elements - starts[level])
        members_ref[:, level * BLOCK:(level + 1) * BLOCK] = pltpu.roll(wide_order, shift, 1)[:, :BLOCK]
    for block in range(LEVELS * BLOCK // LANES):
        index = members_ref[:, block_at(block)]
        joined_ref[:, block_at(block)] = pick(value_blocks(table), index, index >> 7)
    ranks = lax.broadcasted_iota(i32, (count, elements), 1)
    in_block = (wide_order[:count] >> 7) == lax.broadcasted_iota(i32, (count, elements), 0)
    left = jnp.concatenate([
        jnp.where(in_block, ranks >> 5, 0).astype(f32), jnp.where(in_block, ranks & 31, 0).astype(f32)], axis=0)
    at_lane = jnp.broadcast_to(order_ref[...] & (LANES - 1), (LANES, elements)) == lax.broadcasted_iota(
        i32, (LANES, elements), 0)
    rank = lax.dot_general(left.astype(bf16), jnp.where(at_lane, 1.0, 0.0).astype(bf16), (((1,), (1,)), ((), ())),
                           preferred_element_type=f32)
    place = rank[:count].astype(i32) * 32 + rank[count:].astype(i32)
    at = place
    for level in range(1, LEVELS):
        at = jnp.where(place >= starts[level], place - starts[level] + level * BLOCK, at)
    places_ref[...] = at
    index = pad_rows(jnp.concatenate(sent_rows(send_ref, swaps), axis=0), 8)
    send_places_ref[...] = pick(row_blocks(at, 8), index, index >> 7)
    send_codes_ref[...] = pick(row_blocks_of(neighbours[:1], 8), index, index >> 7)
    block = jnp.broadcast_to(neighbours[:1] >> 7, (8, elements)) - count
    named = jnp.where(block == lax.broadcasted_iota(i32, (8, elements), 0),
                      jnp.broadcast_to(pattern_ref[...], (8, elements)), 0).astype(f32).astype(bf16)
    slot_lane = jnp.broadcast_to(neighbours[:1] & (LANES - 1), (LANES, elements)) == lax.broadcasted_iota(
        i32, (LANES, elements), 0)
    slot_pattern = lax.dot_general(named, jnp.where(slot_lane, 1.0, 0.0).astype(bf16), (((1,), (1,)), ((), ())),
                                   preferred_element_type=f32).astype(i32)
    height = jnp.take_along_axis(jnp.broadcast_to(wide_heights_ref[...], (8, LANES)), slot_pattern & (LANES - 1),
                                 axis=1, mode="promise_in_bounds")
    weight = jnp.ones((8, LANES), f32)
    for power in range(1, POWERS + 1):
        weight = weight * height
        for number in range(messages):
            slot_weights_ref[power - 1:power, block_at(number)] = weight[number:number + 1] * WEIGHTS[power]
    for level in range(LEVELS):
        code = joined_ref[1:faces, level * BLOCK:(level + 1) * BLOCK]
        code = jnp.max(jnp.where(code >= elements, 1.0, 0.0), axis=0, keepdims=True)
        row = code[:, block_at(0)]
        for number in range(1, BLOCK // LANES):
            row = jnp.maximum(row, code[:, block_at(number)])
        flags_ref[level:level + 1, :] = row
    matrix_powers(operator_ref, trace_ref, lift_ref, grow_ref, trace_grow_ref, mix_ref, mix_first_ref,
                  lift_out_ref, lift_first_ref)
    local_part(0, members_ref, joined_ref, columns_ref, out_ref, wide_heights_ref, lift_out_ref,
               loaded_ref, weights_ref, faces_ref)
    new_trace_ref[...] = advanced_traces(loaded_ref[...], trace_grow_ref, weights_ref, out_ref.shape[0])
    local_messages(0, new_trace_ref, send_places_ref, sent, prepared)


def settle(level, blocks, places_ref, before, block):
    index = places_ref[block:block + 1, :]
    which = (index >> 7) - level * (BLOCK // LANES)
    return pick(blocks, index, which, before)


def received_blocks(received, count):
    return [(count + i, functools.partial(lambda ref: ref[...], ref)) for i, ref in enumerate(received)]


def received_traces(level, face, received, joined_ref, count):
    parts = []
    for block in range(BLOCK // LANES):
        index = joined_ref[face:face + 1, block_at(level * (BLOCK // LANES) + block)]
        zeros = jnp.zeros(received[0].shape, f32)
        parts.append(pick(received_blocks(received, count), index, index >> 7, zeros))
    return jnp.concatenate(parts, axis=1)


def other_traces(level, received, joined_ref, count):
    parts = [received_traces(level, face, received, joined_ref, count) for face in range(1, faces_in(joined_ref))]
    return jnp.concatenate([jnp.zeros_like(parts[0])] + parts, axis=0)


def any_other(level, flags_ref):
    return jnp.max(flags_ref[level:level + 1, :]) > 0.0


def add_received(level, received, joined_ref, count, flags_ref, local_ref, lift_ref, lift_first_ref, loaded_ref):
    first = received_traces(level, 0, received, joined_ref, count)
    loaded_ref[...] = local_ref[...] + product(lift_first_ref[...], stacked_columns(first))

    @pl.when(any_other(level, flags_ref))
    def _():
        others = other_traces(level, received, joined_ref, count)
        loaded_ref[...] = loaded_ref[...] + product(lift_ref[...], stacked_columns(others))


def between_kernel(level, messages, members_ref, joined_ref, places_ref, columns_ref, old_out_ref, old_trace_ref,
                   moved_ref, extra_ref, heights_ref, local_ref, old_weights_ref, lift_ref, lift_first_ref, grow_ref,
                   trace_grow_ref, flags_ref, send_places_ref, *rest):
    received, rest = rest[:messages], rest[messages:]
    final = level == LEVELS - 1
    if not final:
        sent, rest = rest[:messages], rest[messages:]
    if level > 1:
        advanced_ref, rest = rest[0], rest[1:]
    if final:
        loaded_ref, weights_ref, new_advanced_ref, out_ref, faces_ref, trace_ref, whole_ref = rest
    else:
        out_ref, loaded_ref, weights_ref, new_trace_ref, new_advanced_ref = rest[:5]
        prepared, (faces_ref, trace_ref, whole_ref) = rest[5:5 + messages], rest[5 + messages:]
    count = places_ref.shape[0]
    done = level - 1
    add_received(done, received, joined_ref, count, flags_ref, local_ref, lift_ref, lift_first_ref, whole_ref)
    for block in range(BLOCK // LANES):
        here = block_at(block)
        index = joined_ref[0:1, block_at(done * (BLOCK // LANES) + block)]
        moved = [(count + i, read) for i, read in ref_blocks(moved_ref, messages)]
        trace_ref[:, here] = old_trace_ref[:, here] + extra_ref[:, here] + pick(
            moved, index, index >> 7, jnp.zeros((old_trace_ref.shape[0], LANES), f32))
    for block in range(count):
        here = block_at(block)
        out_ref[:, here] = settle(
            done, ref_blocks(trace_ref, BLOCK // LANES), places_ref, old_out_ref[:, here], block)
    whole = whole_ref[...]
    stacked = stacked_columns(whole)
    chunks = row_chunks(whole.shape[0])
    pieces = BLOCK // LANES
    for number, chunk in enumerate(chunks):
        new = grown_rows(chunk, stacked, whole, grow_ref, old_weights_ref)
        for block in range(number * pieces // len(chunks), (number + 1) * pieces // len(chunks)):
            own_block(level, block, members_ref, joined_ref, columns_ref, heights_ref, loaded_ref, weights_ref)
            face_block(level, block, joined_ref, out_ref, faces_ref)
        for block in range(count):
            here = block_at(block)
            before = advanced_ref[chunk, here] if level > 1 else None
            new_advanced_ref[chunk, here] = settle(done, value_blocks(new), places_ref, before, block)
    loaded = loaded_ref[...] + product(lift_ref[...], stacked_columns(faces_ref[...]))
    loaded_ref[...] = loaded
    if not final:
        new_trace_ref[...] = advanced_traces(loaded, trace_grow_ref, weights_ref, out_ref.shape[0])
        local_messages(level, new_trace_ref, send_places_ref, sent, prepared)


def level_kernel(level, messages, count, flags_ref, joined_ref, weights_ref, slot_weights_ref, mix_ref, mix_first_ref,
                 send_places_ref, send_codes_ref, *rest):
    received, rest = rest[:messages], rest[messages:]
    prepared, rest = rest[:messages], rest[messages:]
    moved_ref, extra_ref, sends = rest[0], rest[1], rest[2:]
    rows = moved_ref.shape[0]
    pieces = BLOCK // LANES
    arrived = jnp.concatenate([ref[...] for ref in received], axis=1)
    stacked = product(mix_first_ref[...], stacked_columns(arrived))
    moved_ref[...] = summed_powers(stacked[rows:], slot_weights_ref, rows, stacked[:rows])
    extra_ref[...] = jnp.zeros(extra_ref.shape, f32)
    moved = [(count + i, read) for i, read in ref_blocks(moved_ref, messages)]
    for group, (before, send) in enumerate(zip(prepared, sends)):
        place, code = send_places_ref[group:group + 1, :], send_codes_ref[group:group + 1, :]
        here = ((place >> 7) >= level * pieces) & ((place >> 7) < (level + 1) * pieces)
        send[...] = before[...] + pick(
            moved, code, jnp.where(here, code >> 7, 0), jnp.zeros(before.shape, f32))

    @pl.when(any_other(level, flags_ref))
    def _():
        others = other_traces(level, received, joined_ref, count)
        stacked = product(mix_ref[...], stacked_columns(others))
        extra_ref[...] = summed_powers(stacked[rows:], weights_ref, rows, stacked[:rows])
        for group, send in enumerate(sends):
            place = send_places_ref[group:group + 1, :]
            send[...] = send[...] + pick(
                ref_blocks(extra_ref, pieces), place, (place >> 7) - level * pieces, jnp.zeros(send.shape, f32))


def last_kernel(level, messages, flags_ref, joined_ref, local_ref, weights_ref, lift_ref, lift_first_ref, grow_ref,
                places_ref, advanced_ref, *rest):
    received, (final_hbm, final_ref, whole_ref, sent) = rest[:messages], rest[messages:]
    count = places_ref.shape[0]
    comp = final_ref.shape[0] // count
    add_received(level, received, joined_ref, count, flags_ref, local_ref, lift_ref, lift_first_ref, whole_ref)
    whole = whole_ref[...]
    stacked = stacked_columns(whole)
    copies = []
    for number, chunk in enumerate(row_chunks(whole.shape[0])):
        new = grown_rows(chunk, stacked, whole, grow_ref, weights_ref)
        height = min(chunk.stop, comp) - chunk.start
        for block in range(count):
            done = settle(level, value_blocks(new), places_ref, advanced_ref[chunk, block_at(block)], block)
            final_ref[pl.ds(chunk.start * count + block, height, stride=count), :] = done[:height]
        part = pl.ds(chunk.start * count, height * count)
        copies.append(pltpu.make_async_copy(final_ref.at[part], final_hbm.at[part], sent.at[number]))
        copies[-1].start()
    for copy in copies:
        copy.wait()


def call(kernel, name, flops, operands, outs, scratch=(), hbm=False, out_hbm=False):
    vmem = pl.BlockSpec(memory_space=pltpu.VMEM)
    given = pl.BlockSpec(memory_space=pltpu.HBM) if hbm else vmem
    if hbm:
        operands = [pltpu.with_memory_space_constraint(one, pltpu.HBM) for one in operands]
    return pl.pallas_call(
        kernel,
        out_shape=tuple(jax.ShapeDtypeStruct(shape, dtype) for shape, dtype in outs),
        in_specs=[given] * len(operands),
        out_specs=tuple([pl.BlockSpec(memory_space=pltpu.HBM) if out_hbm else vmem] * len(outs)),
        scratch_shapes=[one if not isinstance(one, tuple) else pltpu.VMEM(*one) for one in scratch],
        compiler_params=pltpu.CompilerParams(vmem_limit_bytes=16 * 1024 * 1024),
        cost_estimate=pl.CostEstimate(flops=flops, bytes_accessed=1 << 20, transcendentals=0),
        name=name,
    )(*operands)


def is_odd(axis):
    return (lax.axis_index(axis) & 1) == 1


def swap_plan(axis, periodic, low, high):
    count = lax.axis_size(axis)
    plan = [(axis, [(i, i ^ 1) for i in range(count)], low, high, False)]
    if count > 2 or periodic:
        pairs = [(i, (i + 1) % count if i % 2 else (i - 1) % count) for i in range(count)]
        plan.append((axis, pairs, high, low, not periodic))
    return plan


def came_group(swap):
    axis, _, even, odd, is_open = swap
    came = jnp.where(is_odd(axis), even, odd)
    if is_open:
        index = lax.axis_index(axis)
        came = jnp.where((index == 0) | (index == lax.axis_size(axis) - 1), NO_GROUP, came)
    return came


def body(fields, pattern, tent_order, level_sizes, send_rows, neighbours, operator, trace_map, lift_map, tent_height):
    fields, order, sizes = fields[0, 0], tent_order[0], level_sizes[0]
    faces_of, send_list = neighbours[0, 0], send_rows[0, 0]
    comp, elements = fields.shape
    faces, trace = lift_map.shape[0], trace_map.shape[0]
    rows, trace_rows = rounded_up(comp, 16), rounded_up(trace, 16)
    padded, count = LEVELS * BLOCK, elements // LANES
    bnd = send_list.shape[-1]

    near, *far = swap_plan("sector", True, 0, 1)
    swaps = far + swap_plan("radial", False, 2, 3) + [near]
    messages = len(swaps)

    def exchange(sent):
        return [lax.ppermute(one, swap[0], swap[1]) for one, swap in zip(sent, swaps)]

    message = ((trace_rows, bnd), f32)
    own, face_stack = ((rows, BLOCK), f32), ((faces * trace_rows, BLOCK), f32)
    weight, table, traced = ((POWERS, BLOCK), f32), ((trace_rows, elements), f32), ((trace_rows, BLOCK), f32)
    whole = ((rows, elements), f32)
    flat = (comp * count, LANES)

    arguments = [trace_map, send_list, order, pattern[0], sizes, faces_of, operator,
                 jnp.transpose(lift_map, (2, 0, 1)), tent_height[None]]
    columns, out, *rest = call(
        functools.partial(first_kernel, swaps), "first", 10 ** 8, [fields.reshape(flat)] + arguments,
        [whole, table] + [message] * messages + [(one.shape, one.dtype) for one in arguments],
        [(flat, f32), pltpu.SemaphoreType.DMA((ARGUMENTS,))], hbm=True)
    sent, held = rest[:messages], rest[messages:]
    received = exchange(sent)
    slots = ((trace_rows, messages * LANES), f32)
    (members, joined, places, send_places, send_codes, slot_weights, flags, loaded, weights, new_trace, grow,
     trace_grow, mix, mix_first, lift, lift_first, heights, *prepared) = call(
        functools.partial(plan_kernel, swaps), "plan", 2 * 10 ** 9, held + [columns, out] + sent,
        [((8, padded), i32), ((2 * faces, padded), i32), ((count, LANES), i32), ((8, bnd), i32), ((8, bnd), i32),
         ((POWERS, messages * LANES), f32), ((LEVELS, LANES), f32), own, weight, traced,
         ((POWERS * rows, 3 * rows), bf16), (((POWERS + 1) * trace_rows, 3 * rows), bf16),
         (((POWERS + 1) * trace_rows, 3 * faces * trace_rows), bf16), (((POWERS + 1) * trace_rows, 3 * trace_rows), bf16),
         ((rows, 3 * faces * trace_rows), bf16), ((rows, 3 * trace_rows), bf16), ((1, LANES), f32)]
        + [message] * messages, [face_stack])
    advanced = []
    for level in range(LEVELS - 1):
        moved, extra, *sent = call(
            functools.partial(level_kernel, level, messages, count), "level", 10 ** 8,
            [flags, joined, weights, slot_weights, mix, mix_first, send_places, send_codes] + received + prepared,
            [slots, traced] + [message] * messages)
        arrived, received = received, exchange(sent)
        beside = functools.partial(between_kernel, level + 1, messages)
        operands = [members, joined, places, columns, out, new_trace, moved, extra, heights, loaded, weights, lift,
                    lift_first, grow, trace_grow, flags, send_places] + arrived
        scratch = [face_stack, traced, own]
        if level + 1 < LEVELS - 1:
            out, loaded, weights, new_trace, *rest = call(
                beside, "between", 2 * 10 ** 9, operands + sent + advanced,
                [table, own, weight, traced, whole] + [message] * messages, scratch)
            advanced, prepared = rest[:1], rest[1:]
        else:
            loaded, weights, *advanced = call(
                beside, "between", 2 * 10 ** 9, operands + advanced, [own, weight, whole], [table] + scratch)
    final, = call(
        functools.partial(last_kernel, LEVELS - 1, messages), "last", 10 ** 9,
        [flags, joined, loaded, weights, lift, lift_first, grow, places] + advanced + received,
        [(flat, f32)], [(flat, f32), own, pltpu.SemaphoreType.DMA((-(-rows // ROW_CHUNK),))], out_hbm=True)
    return final.reshape(1, 1, comp, elements)


def solution(mesh):
    in_specs = (
        P("sector", "radial", None, None),
        P("sector", "radial", None),
        P("sector", "radial", None),
        P("sector", "radial", None),
        P("sector", "radial", None, None),
        P("sector", "radial", None, None),
        P(),
        P(),
        P(),
        P(),
    )
    out_specs = P("sector", "radial", None, None)
    return jax.shard_map(body, mesh=mesh, in_specs=in_specs, out_specs=out_specs, check_vma=False)
```

```python
import functools
import math

import jax
import jax.numpy as jnp
from jax import lax
from jax.experimental import pallas as pl
from jax.experimental.pallas import tpu as pltpu
from jax.sharding import PartitionSpec as P

LEVELS = 4
SUBSTEPS = 2
TERMS = 4
BLOCK = 384
LANES = 128
NO_GROUP = 1 << 20
ARGUMENTS = 10
ROW_CHUNK = 48

f32, bf16, i32 = jnp.float32, jnp.bfloat16, jnp.int32
precise = lax.Precision.HIGHEST


def rounded_up(size, unit):
    return -(-size // unit) * unit


def taylor_weights():
    once = [1.0 / math.factorial(k) for k in range(TERMS + 1)]
    whole = [1.0]
    for _ in range(SUBSTEPS):
        longer = [0.0] * (len(whole) + TERMS)
        for i, a in enumerate(whole):
            for j, b in enumerate(once):
                longer[i + j] += a * b
        whole = longer
    return whole


WEIGHTS = taylor_weights()
POWERS = len(WEIGHTS) - 1


def split(values):
    high = values.astype(bf16)
    return high, (values - high.astype(f32)).astype(bf16)


def whole_lanes(size):
    return size // LANES * LANES


def stacked_columns(values):
    high, low = split(values)
    main = whole_lanes(values.shape[0])
    parts = [high[:main], low[:main], high[:main], high[main:], low[main:], high[main:]]
    return jnp.concatenate([part for part in parts if part.shape[0]], axis=0)


def stacked_matrix(values):
    high = values.astype(bf16).astype(f32)
    low = values - high
    main = whole_lanes(values.shape[1])
    parts = [high[:, :main], high[:, :main], low[:, :main], high[:, main:], high[:, main:], low[:, main:]]
    return jnp.concatenate([part for part in parts if part.shape[1]], axis=1).astype(bf16)


def product(matrix, columns):
    return jnp.dot(matrix, columns, preferred_element_type=f32)


def pad_rows(values, rows):
    short = rows - values.shape[0]
    if short == 0:
        return values
    return jnp.concatenate([values, jnp.zeros((short,) + values.shape[1:], values.dtype)], axis=0)


def exact_product(left, right):
    left_high, left_low = split(left)
    right_high, right_low = split(right)
    rows = left.shape[0]
    both = product(jnp.concatenate([left_high, left_low], axis=0), right_high)
    return both[:rows] + both[rows:] + product(left_high, right_low)


def pick(blocks, index, which, start=None):
    result = start
    for number, read in blocks:
        table = read()
        lane = jnp.broadcast_to(index & (LANES - 1), table.shape)
        got = jnp.take_along_axis(table, lane, axis=1, mode="promise_in_bounds")
        if result is None:
            result = got
        else:
            result = jnp.where(jnp.broadcast_to(which, table.shape) == number, got, result)
    return result


def block_at(block):
    return slice(block * LANES, (block + 1) * LANES)


def ref_blocks(ref, count):
    return [(b, functools.partial(lambda b: ref[:, block_at(b)], b)) for b in range(count)]


def value_blocks(values):
    return [(b, functools.partial(lambda b: values[:, block_at(b)], b)) for b in range(values.shape[1] // LANES)]


def row_blocks(table, rows):
    return [
        (b, functools.partial(lambda b: jnp.broadcast_to(table[b:b + 1, :], (rows, LANES)), b))
        for b in range(table.shape[0])
    ]


def row_blocks_of(row, rows):
    return [
        (b, functools.partial(lambda b: jnp.broadcast_to(row[:, block_at(b)], (rows, LANES)), b))
        for b in range(row.shape[1] // LANES)
    ]


def summed_powers(stacked, weights_ref, rows, total):
    for power in range(1, POWERS + 1):
        total = total + stacked[(power - 1) * rows:power * rows] * weights_ref[power - 1:power, :]
    return total


def sent_rows(send_ref, swaps):
    rows = []
    for axis, _, low, high, _ in swaps:
        odd, even = send_ref[high:high + 1, :], send_ref[low:low + 1, :]
        rows.append(jnp.where(is_odd(axis), odd, even))
    return rows


def first_kernel(swaps, *refs):
    (fields_hbm, *given), refs = refs[:ARGUMENTS], refs[ARGUMENTS:]
    (columns_ref, out_ref), refs = refs[:2], refs[2:]
    sends, refs = refs[:len(swaps)], refs[len(swaps):]
    *held, fields_ref, arrived = refs
    copies = [
        pltpu.make_async_copy(source, target, arrived.at[i])
        for i, (source, target) in enumerate(zip([fields_hbm] + given, [fields_ref] + held))
    ]
    for copy in copies:
        copy.start()
    needed = 3
    for copy in copies[:needed]:
        copy.wait()
    trace_ref, send_ref = held[:2]
    rows = out_ref.shape[0]
    elements = out_ref.shape[1]
    count = elements // LANES
    comp = fields_ref.shape[0] // count
    trace = pad_rows(trace_ref[...], rows)
    trace_high, trace_low = split(trace)
    both = jnp.concatenate([trace_high, trace_low], axis=0)
    fields = jnp.concatenate([fields_ref[pl.ds(b, comp, stride=count), :] for b in range(count)], axis=1)
    high, low = split(fields)
    upper = product(both, high)
    out_ref[...] = upper[:rows] + upper[rows:] + product(trace_high, low)
    for index, send in zip(sent_rows(send_ref, swaps), sends):
        send[...] = pick(ref_blocks(out_ref, count), index, index >> 7)
    columns_ref[...] = pad_rows(fields, columns_ref.shape[0])
    for copy in copies[needed:]:
        copy.wait()


def faces_in(joined_ref):
    return joined_ref.shape[0] // 2


def own_block(level, block, members_ref, joined_ref, columns_ref, heights_ref, own_ref, weights_ref):
    faces = faces_in(joined_ref)
    here, there = block_at(block), block_at(level * (BLOCK // LANES) + block)
    index = members_ref[0:1, there]
    own_ref[:, here] = pick(ref_blocks(columns_ref, columns_ref.shape[1] // LANES), index, index >> 7)
    pattern = jnp.broadcast_to(joined_ref[faces:faces + 1, there], (8, LANES))
    height = jnp.take_along_axis(
        jnp.broadcast_to(heights_ref[...], (8, LANES)), pattern, axis=1, mode="promise_in_bounds")
    weight = jnp.ones((8, LANES), f32)
    for power in range(1, POWERS + 1):
        weight = weight * height
        weights_ref[power - 1:power, here] = weight[0:1] * WEIGHTS[power]


def face_block(level, block, joined_ref, out_ref, faces_ref):
    trace_rows = out_ref.shape[0]
    here, there = block_at(block), block_at(level * (BLOCK // LANES) + block)
    for face in range(faces_in(joined_ref)):
        index = joined_ref[face:face + 1, there]
        faces_ref[face * trace_rows:(face + 1) * trace_rows, here] = pick(
            ref_blocks(out_ref, out_ref.shape[1] // LANES), index, index >> 7, jnp.zeros((trace_rows, LANES), f32))


def advanced_traces(loaded, matrix_ref, weights_ref, rows):
    stacked = product(matrix_ref[...], stacked_columns(loaded))
    return summed_powers(stacked[rows:], weights_ref, rows, stacked[:rows])


def local_messages(level, trace_ref, send_places_ref, sent, messages):
    for group, (before, message) in enumerate(zip(sent, messages)):
        index = send_places_ref[group:group + 1, :]
        which = (index >> 7) - level * (BLOCK // LANES)
        message[...] = pick(ref_blocks(trace_ref, BLOCK // LANES), index, which, before[...])


def row_chunks(rows):
    return [slice(low, low + ROW_CHUNK) for low in range(0, rows, ROW_CHUNK)]


def grown_rows(chunk, stacked, loaded, grow_ref, weights_ref):
    rows = loaded.shape[0]
    matrix = jnp.concatenate(
        [grow_ref[power * rows + chunk.start:power * rows + chunk.stop, :] for power in range(POWERS)], axis=0)
    return summed_powers(product(matrix, stacked), weights_ref, ROW_CHUNK, loaded[chunk])


def matrix_powers(operator_ref, trace_ref, lift_ref, grow_ref, trace_grow_ref, mix_ref, lift_out_ref,
                  lift_first_ref):
    comp = operator_ref.shape[0]
    trace_comp, faces, _ = lift_ref.shape
    rows = lift_out_ref.shape[0]
    trace_rows = trace_grow_ref.shape[0] // (POWERS + 1)
    operator = pad_rows(operator_ref[...], rows)
    operator = jnp.concatenate([operator, jnp.zeros((rows, rows - comp), f32)], axis=1)
    traces = pad_rows(trace_ref[...], trace_rows)
    traces = jnp.concatenate([traces, jnp.zeros((trace_rows, rows - comp), f32)], axis=1)
    lift = jnp.concatenate([pad_rows(lift_ref[:, face, :], trace_rows) for face in range(faces)], axis=0)
    lift = pad_rows(jnp.transpose(lift), rows)
    lift_out_ref[...] = stacked_matrix(lift)
    lift_first_ref[...] = stacked_matrix(lift[:, :trace_rows])
    powers, have = operator, 1
    while have < POWERS:
        more = exact_product(jnp.concatenate([traces, powers], axis=0), powers[(have - 1) * rows:have * rows])
        traces = jnp.concatenate([traces, more[:have * trace_rows]], axis=0)
        powers = jnp.concatenate([powers, more[have * trace_rows:]], axis=0)
        have *= 2
        yield
    traces = jnp.concatenate([traces, exact_product(traces[:trace_rows], powers[-rows:])], axis=0)
    trace_grow_ref[...] = stacked_matrix(traces)
    yield
    mix_ref[...] = stacked_matrix(exact_product(traces, lift[:, :trace_rows]))
    grow_ref[...] = stacked_matrix(powers)
    yield


def plan_kernel(swaps, *refs):
    (trace_ref, send_ref, order_ref, pattern_ref, sizes_ref, neighbours_ref, operator_ref, lift_ref, heights_ref,
     columns_ref, out_ref), refs = refs[:11], refs[11:]
    messages = len(swaps)
    sent, refs = refs[:messages], refs[messages:]
    (members_ref, joined_ref, places_ref, send_places_ref, send_codes_ref, slot_weights_ref, flags_ref, loaded_ref,
     weights_ref, new_trace_ref, grow_ref, trace_grow_ref, mix_ref, lift_out_ref, lift_first_ref,
     wide_heights_ref), refs = refs[:16], refs[16:]
    prepared, (faces_ref,) = refs[:messages], refs[messages:]
    elements = columns_ref.shape[1]
    count = elements // LANES
    faces = neighbours_ref.shape[0]
    steps = matrix_powers(operator_ref, trace_ref, lift_ref, grow_ref, trace_grow_ref, mix_ref, lift_out_ref,
                          lift_first_ref)
    next(steps)
    sizes = sizes_ref[...].astype(f32)
    number = lax.broadcasted_iota(i32, sizes.shape, 1)
    starts = [jnp.sum(jnp.where(number < level, sizes, 0.0)).astype(i32) for level in range(LEVELS)]
    wide_order = jnp.broadcast_to(order_ref[...], (8, elements))
    neighbours = neighbours_ref[...]
    group = (neighbours >> 7) - count
    message = jnp.full(neighbours.shape, count + len(swaps), i32)
    for number, swap in enumerate(swaps):
        message = jnp.where(group == came_group(swap), count + number, message)
    neighbours = jnp.where(group >= 0, message * LANES + (neighbours & (LANES - 1)), neighbours)
    table = jnp.concatenate(
        [neighbours, pattern_ref[...], jnp.zeros((faces - 1, elements), i32)], axis=0)
    heights = heights_ref[...]
    wide_heights_ref[...] = jnp.concatenate(
        [heights, jnp.zeros((1, LANES - heights.shape[1]), f32)], axis=1)
    for level in range(LEVELS):
        shift = jnp.where(starts[level] == 0, 0, elements - starts[level])
        members_ref[:, level * BLOCK:(level + 1) * BLOCK] = pltpu.roll(wide_order, shift, 1)[:, :BLOCK]
    for block in range(LEVELS * BLOCK // LANES):
        index = members_ref[:, block_at(block)]
        joined_ref[:, block_at(block)] = pick(value_blocks(table), index, index >> 7)
    ranks = lax.broadcasted_iota(i32, (count, elements), 1)
    in_block = (wide_order[:count] >> 7) == lax.broadcasted_iota(i32, (count, elements), 0)
    left = jnp.concatenate([
        jnp.where(in_block, ranks >> 5, 0).astype(f32), jnp.where(in_block, ranks & 31, 0).astype(f32)], axis=0)
    at_lane = jnp.broadcast_to(order_ref[...] & (LANES - 1), (LANES, elements)) == lax.broadcasted_iota(
        i32, (LANES, elements), 0)
    rank = lax.dot_general(left.astype(bf16), jnp.where(at_lane, 1.0, 0.0).astype(bf16), (((1,), (1,)), ((), ())),
                           preferred_element_type=f32)
    place = rank[:count].astype(i32) * 32 + rank[count:].astype(i32)
    at = place
    for level in range(1, LEVELS):
        at = jnp.where(place >= starts[level], place - starts[level] + level * BLOCK, at)
    places_ref[...] = at
    index = pad_rows(jnp.concatenate(sent_rows(send_ref, swaps), axis=0), 8)
    send_places_ref[...] = pick(row_blocks(at, 8), index, index >> 7)
    send_codes_ref[...] = pick(row_blocks_of(neighbours[:1], 8), index, index >> 7)
    block = jnp.broadcast_to(neighbours[:1] >> 7, (8, elements)) - count
    named = jnp.where(block == lax.broadcasted_iota(i32, (8, elements), 0),
                      jnp.broadcast_to(pattern_ref[...], (8, elements)), 0).astype(f32).astype(bf16)
    slot_lane = jnp.broadcast_to(neighbours[:1] & (LANES - 1), (LANES, elements)) == lax.broadcasted_iota(
        i32, (LANES, elements), 0)
    slot_pattern = lax.dot_general(named, jnp.where(slot_lane, 1.0, 0.0).astype(bf16), (((1,), (1,)), ((), ())),
                                   preferred_element_type=f32).astype(i32)
    height = jnp.take_along_axis(jnp.broadcast_to(wide_heights_ref[...], (8, LANES)), slot_pattern & (LANES - 1),
                                 axis=1, mode="promise_in_bounds")
    weight = jnp.ones((8, LANES), f32)
    for power in range(1, POWERS + 1):
        weight = weight * height
        for number in range(messages):
            slot_weights_ref[power - 1:power, block_at(number)] = weight[number:number + 1] * WEIGHTS[power]
    for level in range(LEVELS):
        code = joined_ref[1:faces, level * BLOCK:(level + 1) * BLOCK]
        code = jnp.max(jnp.where(code >= elements, 1.0, 0.0), axis=0, keepdims=True)
        row = code[:, block_at(0)]
        for number in range(1, BLOCK // LANES):
            row = jnp.maximum(row, code[:, block_at(number)])
        flags_ref[level:level + 1, :] = row
    next(steps)
    for block in range(BLOCK // LANES):
        own_block(0, block, members_ref, joined_ref, columns_ref, wide_heights_ref, loaded_ref, weights_ref)
        face_block(0, block, joined_ref, out_ref, faces_ref)
        next(steps)
    loaded = loaded_ref[...] + product(lift_out_ref[...], stacked_columns(faces_ref[...]))
    loaded_ref[...] = loaded
    new_trace_ref[...] = advanced_traces(loaded, trace_grow_ref, weights_ref, out_ref.shape[0])
    local_messages(0, new_trace_ref, send_places_ref, sent, prepared)


def settle(level, blocks, places_ref, before, block):
    index = places_ref[block:block + 1, :]
    which = (index >> 7) - level * (BLOCK // LANES)
    return pick(blocks, index, which, before)


def received_blocks(received, count):
    return [(count + i, functools.partial(lambda ref: ref[...], ref)) for i, ref in enumerate(received)]


def received_traces(level, face, received, joined_ref, count):
    parts = []
    for block in range(BLOCK // LANES):
        index = joined_ref[face:face + 1, block_at(level * (BLOCK // LANES) + block)]
        zeros = jnp.zeros(received[0].shape, f32)
        parts.append(pick(received_blocks(received, count), index, index >> 7, zeros))
    return jnp.concatenate(parts, axis=1)


def other_traces(level, received, joined_ref, count):
    parts = [received_traces(level, face, received, joined_ref, count) for face in range(1, faces_in(joined_ref))]
    return jnp.concatenate([jnp.zeros_like(parts[0])] + parts, axis=0)


def any_other(level, flags_ref):
    return jnp.max(flags_ref[level:level + 1, :]) > 0.0


def add_received(level, received, joined_ref, count, flags_ref, local_ref, lift_ref, lift_first_ref, loaded_ref):
    first = received_traces(level, 0, received, joined_ref, count)
    loaded_ref[...] = local_ref[...] + product(lift_first_ref[...], stacked_columns(first))

    @pl.when(any_other(level, flags_ref))
    def _():
        others = other_traces(level, received, joined_ref, count)
        loaded_ref[...] = loaded_ref[...] + product(lift_ref[...], stacked_columns(others))


def between_kernel(level, messages, members_ref, joined_ref, places_ref, columns_ref, old_out_ref, old_trace_ref,
                   moved_ref, extra_ref, extra_trace_ref, heights_ref, local_ref, old_weights_ref, lift_ref,
                   lift_first_ref, grow_ref, trace_grow_ref, send_places_ref, *rest):
    received, rest = rest[:messages], rest[messages:]
    final = level == LEVELS - 1
    if not final:
        sent, rest = rest[:messages], rest[messages:]
    if level > 1:
        advanced_ref, rest = rest[0], rest[1:]
    if final:
        loaded_ref, weights_ref, new_advanced_ref, out_ref, faces_ref, trace_ref, whole_ref = rest
    else:
        out_ref, loaded_ref, weights_ref, new_trace_ref, new_advanced_ref = rest[:5]
        prepared, (faces_ref, trace_ref, whole_ref) = rest[5:5 + messages], rest[5 + messages:]
    count = places_ref.shape[0]
    done = level - 1
    first = received_traces(done, 0, received, joined_ref, count)
    inflow = product(lift_first_ref[...], stacked_columns(first))
    for block in range(BLOCK // LANES):
        here = block_at(block)
        index = joined_ref[0:1, block_at(done * (BLOCK // LANES) + block)]
        moved = [(count + i, read) for i, read in ref_blocks(moved_ref, messages)]
        trace_ref[:, here] = old_trace_ref[:, here] + extra_trace_ref[:, here] + pick(
            moved, index, index >> 7, jnp.zeros((old_trace_ref.shape[0], LANES), f32))
    whole = local_ref[...] + inflow + extra_ref[...]
    stacked = stacked_columns(whole)
    chunks = row_chunks(whole.shape[0])
    pieces = BLOCK // LANES

    def gather_own(part):
        for block in range(part * pieces // len(chunks), (part + 1) * pieces // len(chunks)):
            own_block(level, block, members_ref, joined_ref, columns_ref, heights_ref, loaded_ref, weights_ref)

    def gather_faces(part):
        for block in range(part * pieces // len(chunks), (part + 1) * pieces // len(chunks)):
            face_block(level, block, joined_ref, out_ref, faces_ref)

    def put_out(part):
        for block in range(part * count // len(chunks), (part + 1) * count // len(chunks)):
            here = block_at(block)
            out_ref[:, here] = settle(
                done, ref_blocks(trace_ref, pieces), places_ref, old_out_ref[:, here], block)

    def put_columns(chunk):
        for block in range(count):
            here = block_at(block)
            before = advanced_ref[chunk, here] if level > 1 else None
            new_advanced_ref[chunk, here] = settle(
                done, [(b, functools.partial(lambda b: whole_ref[chunk, block_at(b)], b)) for b in range(pieces)],
                places_ref, before, block)

    for part in range(len(chunks)):
        put_out(part)
    for part, chunk in enumerate(chunks):
        whole_ref[chunk, :] = grown_rows(chunk, stacked, whole, grow_ref, old_weights_ref)
        gather_own(part)
        gather_faces(part)
    loaded = loaded_ref[...] + product(lift_ref[...], stacked_columns(faces_ref[...]))
    put_columns(chunks[0])
    loaded_ref[...] = loaded
    if not final:
        traces = advanced_traces(loaded, trace_grow_ref, weights_ref, out_ref.shape[0])
    for chunk in chunks[1:]:
        put_columns(chunk)
    if not final:
        new_trace_ref[...] = traces
        local_messages(level, new_trace_ref, send_places_ref, sent, prepared)


def level_kernel(level, messages, count, flags_ref, joined_ref, weights_ref, slot_weights_ref, mix_ref, lift_ref,
                 trace_grow_ref, send_places_ref, send_codes_ref, *rest):
    received, rest = rest[:messages], rest[messages:]
    prepared, rest = rest[:messages], rest[messages:]
    moved_ref, extra_ref, extra_trace_ref, sends = rest[0], rest[1], rest[2], rest[3:]
    rows = moved_ref.shape[0]
    pieces = BLOCK // LANES
    arrived = jnp.concatenate([ref[...] for ref in received], axis=1)
    stacked = product(mix_ref[...], stacked_columns(arrived))
    moved_ref[...] = summed_powers(stacked[rows:], slot_weights_ref, rows, stacked[:rows])
    extra_ref[...] = jnp.zeros(extra_ref.shape, f32)
    extra_trace_ref[...] = jnp.zeros(extra_trace_ref.shape, f32)
    moved = [(count + i, read) for i, read in ref_blocks(moved_ref, messages)]
    for group, (before, send) in enumerate(zip(prepared, sends)):
        place, code = send_places_ref[group:group + 1, :], send_codes_ref[group:group + 1, :]
        here = ((place >> 7) >= level * pieces) & ((place >> 7) < (level + 1) * pieces)
        send[...] = before[...] + pick(
            moved, code, jnp.where(here, code >> 7, 0), jnp.zeros(before.shape, f32))

    @pl.when(any_other(level, flags_ref))
    def _():
        others = other_traces(level, received, joined_ref, count)
        extra = product(lift_ref[...], stacked_columns(others))
        extra_ref[...] = extra
        extra_trace_ref[...] = advanced_traces(extra, trace_grow_ref, weights_ref, rows)
        for group, send in enumerate(sends):
            place = send_places_ref[group:group + 1, :]
            send[...] = send[...] + pick(
                ref_blocks(extra_trace_ref, pieces), place, (place >> 7) - level * pieces, jnp.zeros(send.shape, f32))


def last_kernel(level, messages, flags_ref, joined_ref, local_ref, weights_ref, lift_ref, lift_first_ref, grow_ref,
                places_ref, advanced_ref, *rest):
    received, (final_hbm, final_ref, whole_ref, sent) = rest[:messages], rest[messages:]
    count = places_ref.shape[0]
    comp = final_ref.shape[0] // count
    add_received(level, received, joined_ref, count, flags_ref, local_ref, lift_ref, lift_first_ref, whole_ref)
    whole = whole_ref[...]
    stacked = stacked_columns(whole)
    copies = []
    for number, chunk in enumerate(row_chunks(whole.shape[0])):
        new = grown_rows(chunk, stacked, whole, grow_ref, weights_ref)
        height = min(chunk.stop, comp) - chunk.start
        for block in range(count):
            done = settle(level, value_blocks(new), places_ref, advanced_ref[chunk, block_at(block)], block)
            final_ref[pl.ds(chunk.start * count + block, height, stride=count), :] = done[:height]
        part = pl.ds(chunk.start * count, height * count)
        copies.append(pltpu.make_async_copy(final_ref.at[part], final_hbm.at[part], sent.at[number]))
        copies[-1].start()
    for copy in copies:
        copy.wait()


def call(kernel, name, flops, operands, outs, scratch=(), hbm=False, out_hbm=False):
    vmem = pl.BlockSpec(memory_space=pltpu.VMEM)
    given = pl.BlockSpec(memory_space=pltpu.HBM) if hbm else vmem
    if hbm:
        operands = [pltpu.with_memory_space_constraint(one, pltpu.HBM) for one in operands]
    return pl.pallas_call(
        kernel,
        out_shape=tuple(jax.ShapeDtypeStruct(shape, dtype) for shape, dtype in outs),
        in_specs=[given] * len(operands),
        out_specs=tuple([pl.BlockSpec(memory_space=pltpu.HBM) if out_hbm else vmem] * len(outs)),
        scratch_shapes=[one if not isinstance(one, tuple) else pltpu.VMEM(*one) for one in scratch],
        compiler_params=pltpu.CompilerParams(vmem_limit_bytes=16 * 1024 * 1024),
        cost_estimate=pl.CostEstimate(flops=flops, bytes_accessed=1 << 20, transcendentals=0),
        name=name,
    )(*operands)


def is_odd(axis):
    return (lax.axis_index(axis) & 1) == 1


def swap_plan(axis, periodic, low, high):
    count = lax.axis_size(axis)
    plan = [(axis, [(i, i ^ 1) for i in range(count)], low, high, False)]
    if count > 2 or periodic:
        pairs = [(i, (i + 1) % count if i % 2 else (i - 1) % count) for i in range(count)]
        plan.append((axis, pairs, high, low, not periodic))
    return plan


def came_group(swap):
    axis, _, even, odd, is_open = swap
    came = jnp.where(is_odd(axis), even, odd)
    if is_open:
        index = lax.axis_index(axis)
        came = jnp.where((index == 0) | (index == lax.axis_size(axis) - 1), NO_GROUP, came)
    return came


def body(fields, pattern, tent_order, level_sizes, send_rows, neighbours, operator, trace_map, lift_map, tent_height):
    fields, order, sizes = fields[0, 0], tent_order[0], level_sizes[0]
    faces_of, send_list = neighbours[0, 0], send_rows[0, 0]
    comp, elements = fields.shape
    faces, trace = lift_map.shape[0], trace_map.shape[0]
    rows, trace_rows = rounded_up(comp, 16), rounded_up(trace, 16)
    padded, count = LEVELS * BLOCK, elements // LANES
    bnd = send_list.shape[-1]

    near, *far = swap_plan("sector", True, 0, 1)
    swaps = far + swap_plan("radial", False, 2, 3) + [near]
    messages = len(swaps)

    def exchange(sent):
        return [lax.ppermute(one, swap[0], swap[1]) for one, swap in zip(sent, swaps)]

    message = ((trace_rows, bnd), f32)
    own, face_stack = ((rows, BLOCK), f32), ((faces * trace_rows, BLOCK), f32)
    weight, table, traced = ((POWERS, BLOCK), f32), ((trace_rows, elements), f32), ((trace_rows, BLOCK), f32)
    whole = ((rows, elements), f32)
    flat = (comp * count, LANES)

    arguments = [trace_map, send_list, order, pattern[0], sizes, faces_of, operator,
                 jnp.transpose(lift_map, (2, 0, 1)), tent_height[None]]
    columns, out, *rest = call(
        functools.partial(first_kernel, swaps), "first", 10 ** 8, [fields.reshape(flat)] + arguments,
        [whole, table] + [message] * messages + [(one.shape, one.dtype) for one in arguments],
        [(flat, f32), pltpu.SemaphoreType.DMA((ARGUMENTS,))], hbm=True)
    sent, held = rest[:messages], rest[messages:]
    received = exchange(sent)
    slots = ((trace_rows, messages * LANES), f32)
    (members, joined, places, send_places, send_codes, slot_weights, flags, loaded, weights, new_trace, grow,
     trace_grow, mix, lift, lift_first, heights, *prepared) = call(
        functools.partial(plan_kernel, swaps), "plan", 2 * 10 ** 9, held + [columns, out] + sent,
        [((8, padded), i32), ((2 * faces, padded), i32), ((count, LANES), i32), ((8, bnd), i32), ((8, bnd), i32),
         ((POWERS, messages * LANES), f32), ((LEVELS, LANES), f32), own, weight, traced,
         ((POWERS * rows, 3 * rows), bf16), (((POWERS + 1) * trace_rows, 3 * rows), bf16),
         (((POWERS + 1) * trace_rows, 3 * trace_rows), bf16), ((rows, 3 * faces * trace_rows), bf16), ((rows, 3 * trace_rows), bf16), ((1, LANES), f32)]
        + [message] * messages, [face_stack])
    advanced = []
    for level in range(LEVELS - 1):
        moved, extra, extra_trace, *sent = call(
            functools.partial(level_kernel, level, messages, count), "level", 10 ** 8,
            [flags, joined, weights, slot_weights, mix, lift, trace_grow, send_places, send_codes] + received + prepared,
            [slots, own, traced] + [message] * messages)
        arrived, received = received, exchange(sent)
        beside = functools.partial(between_kernel, level + 1, messages)
        operands = [members, joined, places, columns, out, new_trace, moved, extra, extra_trace, heights, loaded,
                    weights, lift, lift_first, grow, trace_grow, send_places] + arrived
        scratch = [face_stack, traced, own]
        if level + 1 < LEVELS - 1:
            out, loaded, weights, new_trace, *rest = call(
                beside, "between", 2 * 10 ** 9, operands + sent + advanced,
                [table, own, weight, traced, whole] + [message] * messages, scratch)
            advanced, prepared = rest[:1], rest[1:]
        else:
            loaded, weights, *advanced = call(
                beside, "between", 2 * 10 ** 9, operands + advanced, [own, weight, whole], [table] + scratch)
    final, = call(
        functools.partial(last_kernel, LEVELS - 1, messages), "last", 10 ** 9,
        [flags, joined, loaded, weights, lift, lift_first, grow, places] + advanced + received,
        [(flat, f32)], [(flat, f32), own, pltpu.SemaphoreType.DMA((-(-rows // ROW_CHUNK),))], out_hbm=True)
    return final.reshape(1, 1, comp, elements)


def solution(mesh):
    in_specs = (
        P("sector", "radial", None, None),
        P("sector", "radial", None),
        P("sector", "radial", None),
        P("sector", "radial", None),
        P("sector", "radial", None, None),
        P("sector", "radial", None, None),
        P(),
        P(),
        P(),
        P(),
    )
    out_specs = P("sector", "radial", None, None)
    return jax.shard_map(body, mesh=mesh, in_specs=in_specs, out_specs=out_specs, check_vma=False)
```

```python
import functools
import math

import jax
import jax.numpy as jnp
from jax import lax
from jax.experimental import pallas as pl
from jax.experimental.pallas import tpu as pltpu
from jax.sharding import PartitionSpec as P

LEVELS = 4
SUBSTEPS = 2
TERMS = 4
BLOCK = 384
LANES = 128
NO_GROUP = 1 << 20
ARGUMENTS = 10
ROW_CHUNK = 48

f32, bf16, i32 = jnp.float32, jnp.bfloat16, jnp.int32
precise = lax.Precision.HIGHEST


def rounded_up(size, unit):
    return -(-size // unit) * unit


def taylor_weights():
    once = [1.0 / math.factorial(k) for k in range(TERMS + 1)]
    whole = [1.0]
    for _ in range(SUBSTEPS):
        longer = [0.0] * (len(whole) + TERMS)
        for i, a in enumerate(whole):
            for j, b in enumerate(once):
                longer[i + j] += a * b
        whole = longer
    return whole


WEIGHTS = taylor_weights()
POWERS = len(WEIGHTS) - 1


def split(values):
    high = values.astype(bf16)
    return high, (values - high.astype(f32)).astype(bf16)


def whole_lanes(size):
    return size // LANES * LANES


def stacked_columns(values):
    high, low = split(values)
    main = whole_lanes(values.shape[0])
    parts = [high[:main], low[:main], high[:main], high[main:], low[main:], high[main:]]
    return jnp.concatenate([part for part in parts if part.shape[0]], axis=0)


def stacked_matrix(values):
    high = values.astype(bf16).astype(f32)
    low = values - high
    main = whole_lanes(values.shape[1])
    parts = [high[:, :main], high[:, :main], low[:, :main], high[:, main:], high[:, main:], low[:, main:]]
    return jnp.concatenate([part for part in parts if part.shape[1]], axis=1).astype(bf16)


def product(matrix, columns):
    return jnp.dot(matrix, columns, preferred_element_type=f32)


def pad_rows(values, rows):
    short = rows - values.shape[0]
    if short == 0:
        return values
    return jnp.concatenate([values, jnp.zeros((short,) + values.shape[1:], values.dtype)], axis=0)


def exact_product(left, right):
    left_high, left_low = split(left)
    right_high, right_low = split(right)
    rows = left.shape[0]
    both = product(jnp.concatenate([left_high, left_low], axis=0), right_high)
    return both[:rows] + both[rows:] + product(left_high, right_low)


def pick(blocks, index, which, start=None):
    result = start
    for number, read in blocks:
        table = read()
        lane = jnp.broadcast_to(index & (LANES - 1), table.shape)
        got = jnp.take_along_axis(table, lane, axis=1, mode="promise_in_bounds")
        if result is None:
            result = got
        else:
            result = jnp.where(jnp.broadcast_to(which, table.shape) == number, got, result)
    return result


def block_at(block):
    return slice(block * LANES, (block + 1) * LANES)


def ref_blocks(ref, count):
    return [(b, functools.partial(lambda b: ref[:, block_at(b)], b)) for b in range(count)]


def value_blocks(values):
    return [(b, functools.partial(lambda b: values[:, block_at(b)], b)) for b in range(values.shape[1] // LANES)]


def row_blocks(table, rows):
    return [
        (b, functools.partial(lambda b: jnp.broadcast_to(table[b:b + 1, :], (rows, LANES)), b))
        for b in range(table.shape[0])
    ]


def row_blocks_of(row, rows):
    return [
        (b, functools.partial(lambda b: jnp.broadcast_to(row[:, block_at(b)], (rows, LANES)), b))
        for b in range(row.shape[1] // LANES)
    ]


def summed_powers(stacked, weights_ref, rows, total):
    for power in range(1, POWERS + 1):
        total = total + stacked[(power - 1) * rows:power * rows] * weights_ref[power - 1:power, :]
    return total


def sent_rows(send_ref, swaps):
    rows = []
    for axis, _, low, high, _ in swaps:
        odd, even = send_ref[high:high + 1, :], send_ref[low:low + 1, :]
        rows.append(jnp.where(is_odd(axis), odd, even))
    return rows


def first_kernel(swaps, *refs):
    (fields_hbm, *given), refs = refs[:ARGUMENTS], refs[ARGUMENTS:]
    (columns_ref, out_ref), refs = refs[:2], refs[2:]
    sends, refs = refs[:len(swaps)], refs[len(swaps):]
    *held, fields_ref, arrived = refs
    copies = [
        pltpu.make_async_copy(source, target, arrived.at[i])
        for i, (source, target) in enumerate(zip([fields_hbm] + given, [fields_ref] + held))
    ]
    needed = 3
    for copy in copies[:needed]:
        copy.start()
    for copy in copies[:needed]:
        copy.wait()
    for copy in copies[needed:]:
        copy.start()
    trace_ref, send_ref = held[:2]
    rows = out_ref.shape[0]
    elements = out_ref.shape[1]
    count = elements // LANES
    comp = fields_ref.shape[0] // count
    trace = pad_rows(trace_ref[...], rows)
    trace_high, trace_low = split(trace)
    both = jnp.concatenate([trace_high, trace_low], axis=0)
    fields = jnp.concatenate([fields_ref[pl.ds(b, comp, stride=count), :] for b in range(count)], axis=1)
    high, low = split(fields)
    upper = product(both, high)
    out_ref[...] = upper[:rows] + upper[rows:] + product(trace_high, low)
    for index, send in zip(sent_rows(send_ref, swaps), sends):
        send[...] = pick(ref_blocks(out_ref, count), index, index >> 7)
    columns_ref[...] = pad_rows(fields, columns_ref.shape[0])
    for copy in copies[needed:]:
        copy.wait()


def faces_in(joined_ref):
    return joined_ref.shape[0] // 2


def own_block(level, block, members_ref, joined_ref, columns_ref, heights_ref, own_ref, weights_ref):
    faces = faces_in(joined_ref)
    here, there = block_at(block), block_at(level * (BLOCK // LANES) + block)
    index = members_ref[0:1, there]
    own_ref[:, here] = pick(ref_blocks(columns_ref, columns_ref.shape[1] // LANES), index, index >> 7)
    pattern = jnp.broadcast_to(joined_ref[faces:faces + 1, there], (8, LANES))
    height = jnp.take_along_axis(
        jnp.broadcast_to(heights_ref[...], (8, LANES)), pattern, axis=1, mode="promise_in_bounds")
    weight = jnp.ones((8, LANES), f32)
    for power in range(1, POWERS + 1):
        weight = weight * height
        weights_ref[power - 1:power, here] = weight[0:1] * WEIGHTS[power]


def face_block(level, block, joined_ref, out_ref, faces_ref):
    trace_rows = out_ref.shape[0]
    here, there = block_at(block), block_at(level * (BLOCK // LANES) + block)
    for face in range(faces_in(joined_ref)):
        index = joined_ref[face:face + 1, there]
        faces_ref[face * trace_rows:(face + 1) * trace_rows, here] = pick(
            ref_blocks(out_ref, out_ref.shape[1] // LANES), index, index >> 7, jnp.zeros((trace_rows, LANES), f32))


def advanced_traces(loaded, matrix_ref, weights_ref, rows):
    stacked = product(matrix_ref[...], stacked_columns(loaded))
    return summed_powers(stacked[rows:], weights_ref, rows, stacked[:rows])


def local_messages(level, trace_ref, send_places_ref, sent, messages):
    for group, (before, message) in enumerate(zip(sent, messages)):
        index = send_places_ref[group:group + 1, :]
        which = (index >> 7) - level * (BLOCK // LANES)
        message[...] = pick(ref_blocks(trace_ref, BLOCK // LANES), index, which, before[...])


def row_chunks(rows):
    return [slice(low, low + ROW_CHUNK) for low in range(0, rows, ROW_CHUNK)]


def grown_rows(chunk, stacked, loaded, grow_ref, weights_ref):
    rows = loaded.shape[0]
    matrix = jnp.concatenate(
        [grow_ref[power * rows + chunk.start:power * rows + chunk.stop, :] for power in range(POWERS)], axis=0)
    return summed_powers(product(matrix, stacked), weights_ref, chunk.stop - chunk.start, loaded[chunk])


def matrix_powers(operator_ref, trace_ref, lift_ref, grow_ref, trace_grow_ref, mix_ref, lift_out_ref,
                  lift_first_ref):
    comp = operator_ref.shape[0]
    trace_comp, faces, _ = lift_ref.shape
    rows = lift_out_ref.shape[0]
    trace_rows = trace_grow_ref.shape[0] // (POWERS + 1)
    operator = pad_rows(operator_ref[...], rows)
    operator = jnp.concatenate([operator, jnp.zeros((rows, rows - comp), f32)], axis=1)
    traces = pad_rows(trace_ref[...], trace_rows)
    traces = jnp.concatenate([traces, jnp.zeros((trace_rows, rows - comp), f32)], axis=1)
    lift = jnp.concatenate([pad_rows(lift_ref[:, face, :], trace_rows) for face in range(faces)], axis=0)
    lift = pad_rows(jnp.transpose(lift), rows)
    lift_out_ref[...] = stacked_matrix(lift)
    lift_first_ref[...] = stacked_matrix(lift[:, :trace_rows])
    powers, have = operator, 1
    while have < POWERS:
        more = exact_product(jnp.concatenate([traces, powers], axis=0), powers[(have - 1) * rows:have * rows])
        traces = jnp.concatenate([traces, more[:have * trace_rows]], axis=0)
        powers = jnp.concatenate([powers, more[have * trace_rows:]], axis=0)
        have *= 2
        yield
    traces = jnp.concatenate([traces, exact_product(traces[:trace_rows], powers[-rows:])], axis=0)
    trace_grow_ref[...] = stacked_matrix(traces)
    yield
    mix_ref[...] = stacked_matrix(exact_product(traces, lift[:, :trace_rows]))
    grow_ref[...] = stacked_matrix(powers)
    yield


def plan_kernel(swaps, *refs):
    (trace_ref, send_ref, order_ref, pattern_ref, sizes_ref, neighbours_ref, operator_ref, lift_ref, heights_ref,
     columns_ref, out_ref), refs = refs[:11], refs[11:]
    messages = len(swaps)
    sent, refs = refs[:messages], refs[messages:]
    (members_ref, joined_ref, places_ref, send_places_ref, send_codes_ref, slot_weights_ref, flags_ref, loaded_ref,
     weights_ref, new_trace_ref, grow_ref, trace_grow_ref, mix_ref, lift_out_ref, lift_first_ref,
     wide_heights_ref), refs = refs[:16], refs[16:]
    prepared, (faces_ref,) = refs[:messages], refs[messages:]
    elements = columns_ref.shape[1]
    count = elements // LANES
    faces = neighbours_ref.shape[0]
    steps = matrix_powers(operator_ref, trace_ref, lift_ref, grow_ref, trace_grow_ref, mix_ref, lift_out_ref,
                          lift_first_ref)
    next(steps)
    sizes = sizes_ref[...].astype(f32)
    number = lax.broadcasted_iota(i32, sizes.shape, 1)
    starts = [jnp.sum(jnp.where(number < level, sizes, 0.0)).astype(i32) for level in range(LEVELS)]
    wide_order = jnp.broadcast_to(order_ref[...], (8, elements))
    neighbours = neighbours_ref[...]
    group = (neighbours >> 7) - count
    message = jnp.full(neighbours.shape, count + len(swaps), i32)
    for number, swap in enumerate(swaps):
        message = jnp.where(group == came_group(swap), count + number, message)
    neighbours = jnp.where(group >= 0, message * LANES + (neighbours & (LANES - 1)), neighbours)
    table = jnp.concatenate(
        [neighbours, pattern_ref[...], jnp.zeros((faces - 1, elements), i32)], axis=0)
    heights = heights_ref[...]
    wide_heights_ref[...] = jnp.concatenate(
        [heights, jnp.zeros((1, LANES - heights.shape[1]), f32)], axis=1)
    for level in range(LEVELS):
        shift = jnp.where(starts[level] == 0, 0, elements - starts[level])
        members_ref[:, level * BLOCK:(level + 1) * BLOCK] = pltpu.roll(wide_order, shift, 1)[:, :BLOCK]
    for block in range(LEVELS * BLOCK // LANES):
        index = members_ref[:, block_at(block)]
        joined_ref[:, block_at(block)] = pick(value_blocks(table), index, index >> 7)
    ranks = lax.broadcasted_iota(i32, (count, elements), 1)
    in_block = (wide_order[:count] >> 7) == lax.broadcasted_iota(i32, (count, elements), 0)
    left = jnp.concatenate([
        jnp.where(in_block, ranks >> 5, 0).astype(f32), jnp.where(in_block, ranks & 31, 0).astype(f32)], axis=0)
    at_lane = jnp.broadcast_to(order_ref[...] & (LANES - 1), (LANES, elements)) == lax.broadcasted_iota(
        i32, (LANES, elements), 0)
    rank = lax.dot_general(left.astype(bf16), jnp.where(at_lane, 1.0, 0.0).astype(bf16), (((1,), (1,)), ((), ())),
                           preferred_element_type=f32)
    place = rank[:count].astype(i32) * 32 + rank[count:].astype(i32)
    at = place
    for level in range(1, LEVELS):
        at = jnp.where(place >= starts[level], place - starts[level] + level * BLOCK, at)
    places_ref[...] = at
    index = pad_rows(jnp.concatenate(sent_rows(send_ref, swaps), axis=0), 8)
    send_places_ref[...] = pick(row_blocks(at, 8), index, index >> 7)
    send_codes_ref[...] = pick(row_blocks_of(neighbours[:1], 8), index, index >> 7)
    block = jnp.broadcast_to(neighbours[:1] >> 7, (8, elements)) - count
    named = jnp.where(block == lax.broadcasted_iota(i32, (8, elements), 0),
                      jnp.broadcast_to(pattern_ref[...], (8, elements)), 0).astype(f32).astype(bf16)
    slot_lane = jnp.broadcast_to(neighbours[:1] & (LANES - 1), (LANES, elements)) == lax.broadcasted_iota(
        i32, (LANES, elements), 0)
    slot_pattern = lax.dot_general(named, jnp.where(slot_lane, 1.0, 0.0).astype(bf16), (((1,), (1,)), ((), ())),
                                   preferred_element_type=f32).astype(i32)
    height = jnp.take_along_axis(jnp.broadcast_to(wide_heights_ref[...], (8, LANES)), slot_pattern & (LANES - 1),
                                 axis=1, mode="promise_in_bounds")
    weight = jnp.ones((8, LANES), f32)
    for power in range(1, POWERS + 1):
        weight = weight * height
        for number in range(messages):
            slot_weights_ref[power - 1:power, block_at(number)] = weight[number:number + 1] * WEIGHTS[power]
    for level in range(LEVELS):
        code = joined_ref[1:faces, level * BLOCK:(level + 1) * BLOCK]
        code = jnp.max(jnp.where(code >= elements, 1.0, 0.0), axis=0, keepdims=True)
        row = code[:, block_at(0)]
        for number in range(1, BLOCK // LANES):
            row = jnp.maximum(row, code[:, block_at(number)])
        flags_ref[level:level + 1, :] = row
    next(steps)
    for block in range(BLOCK // LANES):
        own_block(0, block, members_ref, joined_ref, columns_ref, wide_heights_ref, loaded_ref, weights_ref)
        face_block(0, block, joined_ref, out_ref, faces_ref)
        next(steps)
    loaded = loaded_ref[...] + product(lift_out_ref[...], stacked_columns(faces_ref[...]))
    loaded_ref[...] = loaded
    new_trace_ref[...] = advanced_traces(loaded, trace_grow_ref, weights_ref, out_ref.shape[0])
    local_messages(0, new_trace_ref, send_places_ref, sent, prepared)


def settle(level, blocks, places_ref, before, block):
    index = places_ref[block:block + 1, :]
    which = (index >> 7) - level * (BLOCK // LANES)
    return pick(blocks, index, which, before)


def received_blocks(received, count):
    return [(count + i, functools.partial(lambda ref: ref[...], ref)) for i, ref in enumerate(received)]


def received_traces(level, face, received, joined_ref, count):
    parts = []
    for block in range(BLOCK // LANES):
        index = joined_ref[face:face + 1, block_at(level * (BLOCK // LANES) + block)]
        zeros = jnp.zeros(received[0].shape, f32)
        parts.append(pick(received_blocks(received, count), index, index >> 7, zeros))
    return jnp.concatenate(parts, axis=1)


def other_traces(level, received, joined_ref, count):
    parts = [received_traces(level, face, received, joined_ref, count) for face in range(1, faces_in(joined_ref))]
    return jnp.concatenate([jnp.zeros_like(parts[0])] + parts, axis=0)


def any_other(level, flags_ref):
    return jnp.max(flags_ref[level:level + 1, :]) > 0.0


def between_kernel(level, messages, members_ref, joined_ref, places_ref, columns_ref, old_out_ref, old_trace_ref,
                   moved_ref, extra_ref, extra_trace_ref, heights_ref, local_ref, old_weights_ref, lift_ref,
                   lift_first_ref, grow_ref, trace_grow_ref, send_places_ref, *rest):
    received, rest = rest[:messages], rest[messages:]
    final = level == LEVELS - 1
    if not final:
        sent, rest = rest[:messages], rest[messages:]
    if level > 1:
        advanced_ref, rest = rest[0], rest[1:]
    if final:
        loaded_ref, weights_ref, new_advanced_ref, out_ref, faces_ref, trace_ref, whole_ref = rest
    else:
        out_ref, loaded_ref, weights_ref, new_trace_ref, new_advanced_ref = rest[:5]
        prepared, (faces_ref, trace_ref, whole_ref) = rest[5:5 + messages], rest[5 + messages:]
    count = places_ref.shape[0]
    done = level - 1
    first = received_traces(done, 0, received, joined_ref, count)
    inflow = product(lift_first_ref[...], stacked_columns(first))
    for block in range(BLOCK // LANES):
        here = block_at(block)
        index = joined_ref[0:1, block_at(done * (BLOCK // LANES) + block)]
        moved = [(count + i, read) for i, read in ref_blocks(moved_ref, messages)]
        trace_ref[:, here] = old_trace_ref[:, here] + extra_trace_ref[:, here] + pick(
            moved, index, index >> 7, jnp.zeros((old_trace_ref.shape[0], LANES), f32))
    whole = local_ref[...] + inflow + extra_ref[...]
    stacked = stacked_columns(whole)
    chunks = row_chunks(whole.shape[0])
    pieces = BLOCK // LANES

    def gather_own(part):
        for block in range(part * pieces // len(chunks), (part + 1) * pieces // len(chunks)):
            own_block(level, block, members_ref, joined_ref, columns_ref, heights_ref, loaded_ref, weights_ref)

    def gather_faces(part):
        for block in range(part * pieces // len(chunks), (part + 1) * pieces // len(chunks)):
            face_block(level, block, joined_ref, out_ref, faces_ref)

    def put_out(part):
        for block in range(part * count // len(chunks), (part + 1) * count // len(chunks)):
            here = block_at(block)
            out_ref[:, here] = settle(
                done, ref_blocks(trace_ref, pieces), places_ref, old_out_ref[:, here], block)

    def put_columns(chunk):
        for block in range(count):
            here = block_at(block)
            before = advanced_ref[chunk, here] if level > 1 else None
            new_advanced_ref[chunk, here] = settle(
                done, [(b, functools.partial(lambda b: whole_ref[chunk, block_at(b)], b)) for b in range(pieces)],
                places_ref, before, block)

    for part in range(len(chunks)):
        put_out(part)
    for part, chunk in enumerate(chunks):
        whole_ref[chunk, :] = grown_rows(chunk, stacked, whole, grow_ref, old_weights_ref)
        gather_own(part)
        gather_faces(part)
    loaded = loaded_ref[...] + product(lift_ref[...], stacked_columns(faces_ref[...]))
    put_columns(chunks[0])
    loaded_ref[...] = loaded
    if not final:
        traces = advanced_traces(loaded, trace_grow_ref, weights_ref, out_ref.shape[0])
    for chunk in chunks[1:]:
        put_columns(chunk)
    if not final:
        new_trace_ref[...] = traces
        local_messages(level, new_trace_ref, send_places_ref, sent, prepared)


def level_kernel(level, messages, count, flags_ref, joined_ref, weights_ref, slot_weights_ref, mix_ref, lift_ref,
                 trace_grow_ref, send_places_ref, send_codes_ref, *rest):
    received, rest = rest[:messages], rest[messages:]
    prepared, rest = rest[:messages], rest[messages:]
    moved_ref, extra_ref, extra_trace_ref, sends = rest[0], rest[1], rest[2], rest[3:]
    rows = moved_ref.shape[0]
    pieces = BLOCK // LANES
    arrived = jnp.concatenate([ref[...] for ref in received], axis=1)
    stacked = product(mix_ref[...], stacked_columns(arrived))
    moved_ref[...] = summed_powers(stacked[rows:], slot_weights_ref, rows, stacked[:rows])
    extra_ref[...] = jnp.zeros(extra_ref.shape, f32)
    extra_trace_ref[...] = jnp.zeros(extra_trace_ref.shape, f32)
    moved = [(count + i, read) for i, read in ref_blocks(moved_ref, messages)]
    for group, (before, send) in enumerate(zip(prepared, sends)):
        place, code = send_places_ref[group:group + 1, :], send_codes_ref[group:group + 1, :]
        here = ((place >> 7) >= level * pieces) & ((place >> 7) < (level + 1) * pieces)
        send[...] = before[...] + pick(
            moved, code, jnp.where(here, code >> 7, 0), jnp.zeros(before.shape, f32))

    @pl.when(any_other(level, flags_ref))
    def _():
        others = other_traces(level, received, joined_ref, count)
        extra = product(lift_ref[...], stacked_columns(others))
        extra_ref[...] = extra
        extra_trace_ref[...] = advanced_traces(extra, trace_grow_ref, weights_ref, rows)
        for group, send in enumerate(sends):
            place = send_places_ref[group:group + 1, :]
            send[...] = send[...] + pick(
                ref_blocks(extra_trace_ref, pieces), place, (place >> 7) - level * pieces, jnp.zeros(send.shape, f32))


def last_chunks(rows):
    units = rows // 16
    first = -(-units * 4 // 9)
    second = -(-(units - first) * 3 // 5)
    bounds = [0, first * 16, (first + second) * 16, rows]
    return [slice(low, high) for low, high in zip(bounds, bounds[1:]) if high > low]


def last_kernel(level, messages, flags_ref, joined_ref, local_ref, weights_ref, lift_ref, lift_first_ref, grow_ref,
                places_ref, advanced_ref, *rest):
    received, (final_hbm, final_ref, sent) = rest[:messages], rest[messages:]
    count = places_ref.shape[0]
    comp = final_ref.shape[0] // count

    def finish(whole):
        stacked = stacked_columns(whole)
        copies = []
        for number, chunk in enumerate(last_chunks(whole.shape[0])):
            new = grown_rows(chunk, stacked, whole, grow_ref, weights_ref)
            height = min(chunk.stop, comp) - chunk.start
            for block in range(count):
                done = settle(level, value_blocks(new), places_ref, advanced_ref[chunk, block_at(block)], block)
                final_ref[pl.ds(chunk.start * count + block, height, stride=count), :] = done[:height]
            part = pl.ds(chunk.start * count, height * count)
            copies.append(pltpu.make_async_copy(final_ref.at[part], final_hbm.at[part], sent.at[number]))
            copies[-1].start()
        for copy in copies:
            copy.wait()

    def whole_of(others):
        first = received_traces(level, 0, received, joined_ref, count)
        whole = local_ref[...] + product(lift_first_ref[...], stacked_columns(first))
        return whole if others is None else whole + product(lift_ref[...], stacked_columns(others))

    other = any_other(level, flags_ref)
    finish(whole_of(None))

    @pl.when(other)
    def _():
        finish(whole_of(other_traces(level, received, joined_ref, count)))


def call(kernel, name, flops, operands, outs, scratch=(), hbm=False, out_hbm=False):
    vmem = pl.BlockSpec(memory_space=pltpu.VMEM)
    given = pl.BlockSpec(memory_space=pltpu.HBM) if hbm else vmem
    if hbm:
        operands = [pltpu.with_memory_space_constraint(one, pltpu.HBM) for one in operands]
    return pl.pallas_call(
        kernel,
        out_shape=tuple(jax.ShapeDtypeStruct(shape, dtype) for shape, dtype in outs),
        in_specs=[given] * len(operands),
        out_specs=tuple([pl.BlockSpec(memory_space=pltpu.HBM) if out_hbm else vmem] * len(outs)),
        scratch_shapes=[one if not isinstance(one, tuple) else pltpu.VMEM(*one) for one in scratch],
        compiler_params=pltpu.CompilerParams(vmem_limit_bytes=16 * 1024 * 1024),
        cost_estimate=pl.CostEstimate(flops=flops, bytes_accessed=1 << 20, transcendentals=0),
        name=name,
    )(*operands)


def is_odd(axis):
    return (lax.axis_index(axis) & 1) == 1


def swap_plan(axis, periodic, low, high):
    count = lax.axis_size(axis)
    plan = [(axis, [(i, i ^ 1) for i in range(count)], low, high, False)]
    if count > 2 or periodic:
        pairs = [(i, (i + 1) % count if i % 2 else (i - 1) % count) for i in range(count)]
        plan.append((axis, pairs, high, low, not periodic))
    return plan


def came_group(swap):
    axis, _, even, odd, is_open = swap
    came = jnp.where(is_odd(axis), even, odd)
    if is_open:
        index = lax.axis_index(axis)
        came = jnp.where((index == 0) | (index == lax.axis_size(axis) - 1), NO_GROUP, came)
    return came


def body(fields, pattern, tent_order, level_sizes, send_rows, neighbours, operator, trace_map, lift_map, tent_height):
    fields, order, sizes = fields[0, 0], tent_order[0], level_sizes[0]
    faces_of, send_list = neighbours[0, 0], send_rows[0, 0]
    comp, elements = fields.shape
    faces, trace = lift_map.shape[0], trace_map.shape[0]
    rows, trace_rows = rounded_up(comp, 16), rounded_up(trace, 16)
    padded, count = LEVELS * BLOCK, elements // LANES
    bnd = send_list.shape[-1]

    near, *far = swap_plan("sector", True, 0, 1)
    swaps = far + swap_plan("radial", False, 2, 3) + [near]
    messages = len(swaps)

    def exchange(sent):
        return [lax.ppermute(one, swap[0], swap[1]) for one, swap in zip(sent, swaps)]

    message = ((trace_rows, bnd), f32)
    own, face_stack = ((rows, BLOCK), f32), ((faces * trace_rows, BLOCK), f32)
    weight, table, traced = ((POWERS, BLOCK), f32), ((trace_rows, elements), f32), ((trace_rows, BLOCK), f32)
    whole = ((rows, elements), f32)
    flat = (comp * count, LANES)

    arguments = [trace_map, send_list, order, pattern[0], sizes, faces_of, operator,
                 jnp.transpose(lift_map, (2, 0, 1)), tent_height[None]]
    columns, out, *rest = call(
        functools.partial(first_kernel, swaps), "first", 10 ** 8, [fields.reshape(flat)] + arguments,
        [whole, table] + [message] * messages + [(one.shape, one.dtype) for one in arguments],
        [(flat, f32), pltpu.SemaphoreType.DMA((ARGUMENTS,))], hbm=True)
    sent, held = rest[:messages], rest[messages:]
    received = exchange(sent)
    slots = ((trace_rows, messages * LANES), f32)
    (members, joined, places, send_places, send_codes, slot_weights, flags, loaded, weights, new_trace, grow,
     trace_grow, mix, lift, lift_first, heights, *prepared) = call(
        functools.partial(plan_kernel, swaps), "plan", 2 * 10 ** 9, held + [columns, out] + sent,
        [((8, padded), i32), ((2 * faces, padded), i32), ((count, LANES), i32), ((8, bnd), i32), ((8, bnd), i32),
         ((POWERS, messages * LANES), f32), ((LEVELS, LANES), f32), own, weight, traced,
         ((POWERS * rows, 3 * rows), bf16), (((POWERS + 1) * trace_rows, 3 * rows), bf16),
         (((POWERS + 1) * trace_rows, 3 * trace_rows), bf16), ((rows, 3 * faces * trace_rows), bf16), ((rows, 3 * trace_rows), bf16), ((1, LANES), f32)]
        + [message] * messages, [face_stack])
    advanced = []
    for level in range(LEVELS - 1):
        moved, extra, extra_trace, *sent = call(
            functools.partial(level_kernel, level, messages, count), "level", 10 ** 8,
            [flags, joined, weights, slot_weights, mix, lift, trace_grow, send_places, send_codes] + received + prepared,
            [slots, own, traced] + [message] * messages)
        arrived, received = received, exchange(sent)
        beside = functools.partial(between_kernel, level + 1, messages)
        operands = [members, joined, places, columns, out, new_trace, moved, extra, extra_trace, heights, loaded,
                    weights, lift, lift_first, grow, trace_grow, send_places] + arrived
        scratch = [face_stack, traced, own]
        if level + 1 < LEVELS - 1:
            out, loaded, weights, new_trace, *rest = call(
                beside, "between", 2 * 10 ** 9, operands + sent + advanced,
                [table, own, weight, traced, whole] + [message] * messages, scratch)
            advanced, prepared = rest[:1], rest[1:]
        else:
            loaded, weights, *advanced = call(
                beside, "between", 2 * 10 ** 9, operands + advanced, [own, weight, whole], [table] + scratch)
    final, = call(
        functools.partial(last_kernel, LEVELS - 1, messages), "last", 10 ** 9,
        [flags, joined, loaded, weights, lift, lift_first, grow, places] + advanced + received,
        [(flat, f32)], [(flat, f32), pltpu.SemaphoreType.DMA((len(last_chunks(rows)),))], out_hbm=True)
    return final.reshape(1, 1, comp, elements)


def solution(mesh):
    in_specs = (
        P("sector", "radial", None, None),
        P("sector", "radial", None),
        P("sector", "radial", None),
        P("sector", "radial", None),
        P("sector", "radial", None, None),
        P("sector", "radial", None, None),
        P(),
        P(),
        P(),
        P(),
    )
    out_specs = P("sector", "radial", None, None)
    return jax.shard_map(body, mesh=mesh, in_specs=in_specs, out_specs=out_specs, check_vma=False)
```

```python
import functools
import math

import jax
import jax.numpy as jnp
from jax import lax
from jax.experimental import pallas as pl
from jax.experimental.pallas import tpu as pltpu
from jax.sharding import PartitionSpec as P

LEVELS = 4
SUBSTEPS = 2
TERMS = 4
BLOCK = 384
LANES = 128
NO_GROUP = 1 << 20
ARGUMENTS = 10
ROW_CHUNK = 48

f32, bf16, i32 = jnp.float32, jnp.bfloat16, jnp.int32
precise = lax.Precision.HIGHEST


def rounded_up(size, unit):
    return -(-size // unit) * unit


def taylor_weights():
    once = [1.0 / math.factorial(k) for k in range(TERMS + 1)]
    whole = [1.0]
    for _ in range(SUBSTEPS):
        longer = [0.0] * (len(whole) + TERMS)
        for i, a in enumerate(whole):
            for j, b in enumerate(once):
                longer[i + j] += a * b
        whole = longer
    return whole


WEIGHTS = taylor_weights()
POWERS = len(WEIGHTS) - 1


def split(values):
    high = values.astype(bf16)
    return high, (values - high.astype(f32)).astype(bf16)


def whole_lanes(size):
    return size // LANES * LANES


def stacked_columns(values):
    high, low = split(values)
    main = whole_lanes(values.shape[0])
    parts = [high[:main], low[:main], high[:main], high[main:], low[main:], high[main:]]
    return jnp.concatenate([part for part in parts if part.shape[0]], axis=0)


def stacked_matrix(values):
    high = values.astype(bf16).astype(f32)
    low = values - high
    main = whole_lanes(values.shape[1])
    parts = [high[:, :main], high[:, :main], low[:, :main], high[:, main:], high[:, main:], low[:, main:]]
    return jnp.concatenate([part for part in parts if part.shape[1]], axis=1).astype(bf16)


def product(matrix, columns):
    return jnp.dot(matrix, columns, preferred_element_type=f32)


def pad_rows(values, rows):
    short = rows - values.shape[0]
    if short == 0:
        return values
    return jnp.concatenate([values, jnp.zeros((short,) + values.shape[1:], values.dtype)], axis=0)


def exact_product(left, right):
    left_high, left_low = split(left)
    right_high, right_low = split(right)
    rows = left.shape[0]
    both = product(jnp.concatenate([left_high, left_low], axis=0), right_high)
    return both[:rows] + both[rows:] + product(left_high, right_low)


def pick(blocks, index, which, start=None):
    result = start
    for number, read in blocks:
        table = read()
        lane = jnp.broadcast_to(index & (LANES - 1), table.shape)
        got = jnp.take_along_axis(table, lane, axis=1, mode="promise_in_bounds")
        if result is None:
            result = got
        else:
            result = jnp.where(jnp.broadcast_to(which, table.shape) == number, got, result)
    return result


def block_at(block):
    return slice(block * LANES, (block + 1) * LANES)


def ref_blocks(ref, count):
    return [(b, functools.partial(lambda b: ref[:, block_at(b)], b)) for b in range(count)]


def value_blocks(values):
    return [(b, functools.partial(lambda b: values[:, block_at(b)], b)) for b in range(values.shape[1] // LANES)]


def row_blocks(table, rows):
    return [
        (b, functools.partial(lambda b: jnp.broadcast_to(table[b:b + 1, :], (rows, LANES)), b))
        for b in range(table.shape[0])
    ]


def row_blocks_of(row, rows):
    return [
        (b, functools.partial(lambda b: jnp.broadcast_to(row[:, block_at(b)], (rows, LANES)), b))
        for b in range(row.shape[1] // LANES)
    ]


def summed_powers(stacked, weights_ref, rows, total):
    for power in range(1, POWERS + 1):
        total = total + stacked[(power - 1) * rows:power * rows] * weights_ref[power - 1:power, :]
    return total


def sent_rows(send_ref, swaps):
    rows = []
    for axis, _, low, high, _ in swaps:
        odd, even = send_ref[high:high + 1, :], send_ref[low:low + 1, :]
        rows.append(jnp.where(is_odd(axis), odd, even))
    return rows


def first_kernel(swaps, *refs):
    (fields_hbm, *given), refs = refs[:ARGUMENTS], refs[ARGUMENTS:]
    (columns_ref, out_ref), refs = refs[:2], refs[2:]
    sends, refs = refs[:len(swaps)], refs[len(swaps):]
    *held, fields_ref, arrived = refs
    rows = out_ref.shape[0]
    elements = out_ref.shape[1]
    count = elements // LANES
    comp = fields_ref.shape[0] // count
    cuts = [slice(0, rounded_up(comp // 2, 16)), slice(rounded_up(comp // 2, 16), comp)]
    parts = [pl.ds(cut.start * count, (cut.stop - cut.start) * count) for cut in cuts]
    trace_hbm, send_hbm, *others = given
    trace_ref, send_ref, *others_held = held
    pairs = [(fields_hbm.at[parts[0]], fields_ref.at[parts[0]]), (trace_hbm, trace_ref),
             (fields_hbm.at[parts[1]], fields_ref.at[parts[1]]), (send_hbm, send_ref)]
    pairs += list(zip(others, others_held))
    copies = [pltpu.make_async_copy(source, target, arrived.at[i]) for i, (source, target) in enumerate(pairs)]
    for copy in copies:
        copy.start()
    total = None
    for number, cut in enumerate(cuts):
        if number == 0:
            copies[0].wait()
            copies[1].wait()
            trace = pad_rows(trace_ref[...], rows)
        else:
            copies[2].wait()
        height = cut.stop - cut.start
        fields = jnp.concatenate(
            [fields_ref[pl.ds(cut.start * count + b, height, stride=count), :] for b in range(count)], axis=1)
        trace_high, trace_low = split(trace[:, cut])
        high, low = split(fields)
        upper = product(jnp.concatenate([trace_high, trace_low], axis=0), high)
        part = upper[:rows] + upper[rows:] + product(trace_high, low)
        total = part if total is None else total + part
        columns_ref[cut, :] = fields
    out_ref[...] = total
    copies[3].wait()
    for index, send in zip(sent_rows(send_ref, swaps), sends):
        send[...] = pick(ref_blocks(out_ref, count), index, index >> 7)
    columns_ref[comp:, :] = jnp.zeros((columns_ref.shape[0] - comp, elements), f32)
    for copy in copies[4:]:
        copy.wait()


def faces_in(joined_ref):
    return joined_ref.shape[0] // 2


def own_block(level, block, members_ref, joined_ref, columns_ref, heights_ref, own_ref, weights_ref):
    faces = faces_in(joined_ref)
    here, there = block_at(block), block_at(level * (BLOCK // LANES) + block)
    index = members_ref[0:1, there]
    own_ref[:, here] = pick(ref_blocks(columns_ref, columns_ref.shape[1] // LANES), index, index >> 7)
    pattern = jnp.broadcast_to(joined_ref[faces:faces + 1, there], (8, LANES))
    height = jnp.take_along_axis(
        jnp.broadcast_to(heights_ref[...], (8, LANES)), pattern, axis=1, mode="promise_in_bounds")
    weight = jnp.ones((8, LANES), f32)
    for power in range(1, POWERS + 1):
        weight = weight * height
        weights_ref[power - 1:power, here] = weight[0:1] * WEIGHTS[power]


def face_block(level, block, joined_ref, out_ref, faces_ref):
    trace_rows = out_ref.shape[0]
    here, there = block_at(block), block_at(level * (BLOCK // LANES) + block)
    for face in range(faces_in(joined_ref)):
        index = joined_ref[face:face + 1, there]
        faces_ref[face * trace_rows:(face + 1) * trace_rows, here] = pick(
            ref_blocks(out_ref, out_ref.shape[1] // LANES), index, index >> 7, jnp.zeros((trace_rows, LANES), f32))


def advanced_traces(loaded, matrix_ref, weights_ref, rows):
    stacked = product(matrix_ref[...], stacked_columns(loaded))
    return summed_powers(stacked[rows:], weights_ref, rows, stacked[:rows])


def local_messages(level, trace_ref, send_places_ref, sent, messages):
    for group, (before, message) in enumerate(zip(sent, messages)):
        index = send_places_ref[group:group + 1, :]
        which = (index >> 7) - level * (BLOCK // LANES)
        message[...] = pick(ref_blocks(trace_ref, BLOCK // LANES), index, which, before[...])


def row_chunks(rows):
    return [slice(low, low + ROW_CHUNK) for low in range(0, rows, ROW_CHUNK)]


def grown_rows(chunk, stacked, loaded, grow_ref, weights_ref):
    rows = loaded.shape[0]
    matrix = jnp.concatenate(
        [grow_ref[power * rows + chunk.start:power * rows + chunk.stop, :] for power in range(POWERS)], axis=0)
    return summed_powers(product(matrix, stacked), weights_ref, chunk.stop - chunk.start, loaded[chunk])


def matrix_powers(operator_ref, trace_ref, lift_ref, grow_ref, trace_grow_ref, mix_ref, lift_out_ref,
                  lift_first_ref):
    comp = operator_ref.shape[0]
    trace_comp, faces, _ = lift_ref.shape
    rows = lift_out_ref.shape[0]
    trace_rows = trace_grow_ref.shape[0] // (POWERS + 1)
    operator = pad_rows(operator_ref[...], rows)
    operator = jnp.concatenate([operator, jnp.zeros((rows, rows - comp), f32)], axis=1)
    traces = pad_rows(trace_ref[...], trace_rows)
    traces = jnp.concatenate([traces, jnp.zeros((trace_rows, rows - comp), f32)], axis=1)
    lift = jnp.concatenate([pad_rows(lift_ref[:, face, :], trace_rows) for face in range(faces)], axis=0)
    lift = pad_rows(jnp.transpose(lift), rows)
    lift_out_ref[...] = stacked_matrix(lift)
    lift_first_ref[...] = stacked_matrix(lift[:, :trace_rows])
    powers, have = operator, 1
    while have < POWERS:
        more = exact_product(jnp.concatenate([traces, powers], axis=0), powers[(have - 1) * rows:have * rows])
        traces = jnp.concatenate([traces, more[:have * trace_rows]], axis=0)
        powers = jnp.concatenate([powers, more[have * trace_rows:]], axis=0)
        have *= 2
        yield
    traces = jnp.concatenate([traces, exact_product(traces[:trace_rows], powers[-rows:])], axis=0)
    trace_grow_ref[...] = stacked_matrix(traces)
    yield
    mix_ref[...] = stacked_matrix(exact_product(traces, lift[:, :trace_rows]))
    grow_ref[...] = stacked_matrix(powers)
    yield


def plan_kernel(swaps, *refs):
    (trace_ref, send_ref, order_ref, pattern_ref, sizes_ref, neighbours_ref, operator_ref, lift_ref, heights_ref,
     columns_ref, out_ref), refs = refs[:11], refs[11:]
    messages = len(swaps)
    sent, refs = refs[:messages], refs[messages:]
    (members_ref, joined_ref, places_ref, send_places_ref, send_codes_ref, slot_weights_ref, flags_ref, loaded_ref,
     weights_ref, new_trace_ref, grow_ref, trace_grow_ref, mix_ref, lift_out_ref, lift_first_ref,
     wide_heights_ref), refs = refs[:16], refs[16:]
    prepared, (faces_ref,) = refs[:messages], refs[messages:]
    elements = columns_ref.shape[1]
    count = elements // LANES
    faces = neighbours_ref.shape[0]
    steps = matrix_powers(operator_ref, trace_ref, lift_ref, grow_ref, trace_grow_ref, mix_ref, lift_out_ref,
                          lift_first_ref)
    next(steps)
    sizes = sizes_ref[...].astype(f32)
    number = lax.broadcasted_iota(i32, sizes.shape, 1)
    starts = [jnp.sum(jnp.where(number < level, sizes, 0.0)).astype(i32) for level in range(LEVELS)]
    wide_order = jnp.broadcast_to(order_ref[...], (8, elements))
    neighbours = neighbours_ref[...]
    group = (neighbours >> 7) - count
    message = jnp.full(neighbours.shape, count + len(swaps), i32)
    for number, swap in enumerate(swaps):
        message = jnp.where(group == came_group(swap), count + number, message)
    neighbours = jnp.where(group >= 0, message * LANES + (neighbours & (LANES - 1)), neighbours)
    table = jnp.concatenate(
        [neighbours, pattern_ref[...], jnp.zeros((faces - 1, elements), i32)], axis=0)
    heights = heights_ref[...]
    wide_heights_ref[...] = jnp.concatenate(
        [heights, jnp.zeros((1, LANES - heights.shape[1]), f32)], axis=1)
    for level in range(LEVELS):
        shift = jnp.where(starts[level] == 0, 0, elements - starts[level])
        members_ref[:, level * BLOCK:(level + 1) * BLOCK] = pltpu.roll(wide_order, shift, 1)[:, :BLOCK]
    for block in range(LEVELS * BLOCK // LANES):
        index = members_ref[:, block_at(block)]
        joined_ref[:, block_at(block)] = pick(value_blocks(table), index, index >> 7)
    ranks = lax.broadcasted_iota(i32, (count, elements), 1)
    in_block = (wide_order[:count] >> 7) == lax.broadcasted_iota(i32, (count, elements), 0)
    left = jnp.concatenate([
        jnp.where(in_block, ranks >> 5, 0).astype(f32), jnp.where(in_block, ranks & 31, 0).astype(f32)], axis=0)
    at_lane = jnp.broadcast_to(order_ref[...] & (LANES - 1), (LANES, elements)) == lax.broadcasted_iota(
        i32, (LANES, elements), 0)
    rank = lax.dot_general(left.astype(bf16), jnp.where(at_lane, 1.0, 0.0).astype(bf16), (((1,), (1,)), ((), ())),
                           preferred_element_type=f32)
    place = rank[:count].astype(i32) * 32 + rank[count:].astype(i32)
    at = place
    for level in range(1, LEVELS):
        at = jnp.where(place >= starts[level], place - starts[level] + level * BLOCK, at)
    places_ref[...] = at
    index = pad_rows(jnp.concatenate(sent_rows(send_ref, swaps), axis=0), 8)
    send_places_ref[...] = pick(row_blocks(at, 8), index, index >> 7)
    send_codes_ref[...] = pick(row_blocks_of(neighbours[:1], 8), index, index >> 7)
    block = jnp.broadcast_to(neighbours[:1] >> 7, (8, elements)) - count
    named = jnp.where(block == lax.broadcasted_iota(i32, (8, elements), 0),
                      jnp.broadcast_to(pattern_ref[...], (8, elements)), 0).astype(f32).astype(bf16)
    slot_lane = jnp.broadcast_to(neighbours[:1] & (LANES - 1), (LANES, elements)) == lax.broadcasted_iota(
        i32, (LANES, elements), 0)
    slot_pattern = lax.dot_general(named, jnp.where(slot_lane, 1.0, 0.0).astype(bf16), (((1,), (1,)), ((), ())),
                                   preferred_element_type=f32).astype(i32)
    height = jnp.take_along_axis(jnp.broadcast_to(wide_heights_ref[...], (8, LANES)), slot_pattern & (LANES - 1),
                                 axis=1, mode="promise_in_bounds")
    weight = jnp.ones((8, LANES), f32)
    for power in range(1, POWERS + 1):
        weight = weight * height
        for number in range(messages):
            slot_weights_ref[power - 1:power, block_at(number)] = weight[number:number + 1] * WEIGHTS[power]
    for level in range(LEVELS):
        code = joined_ref[1:faces, level * BLOCK:(level + 1) * BLOCK]
        code = jnp.max(jnp.where(code >= elements, 1.0, 0.0), axis=0, keepdims=True)
        row = code[:, block_at(0)]
        for number in range(1, BLOCK // LANES):
            row = jnp.maximum(row, code[:, block_at(number)])
        flags_ref[level:level + 1, :] = row
    next(steps)
    for block in range(BLOCK // LANES):
        own_block(0, block, members_ref, joined_ref, columns_ref, wide_heights_ref, loaded_ref, weights_ref)
        face_block(0, block, joined_ref, out_ref, faces_ref)
        next(steps)
    loaded = loaded_ref[...] + product(lift_out_ref[...], stacked_columns(faces_ref[...]))
    loaded_ref[...] = loaded
    new_trace_ref[...] = advanced_traces(loaded, trace_grow_ref, weights_ref, out_ref.shape[0])
    local_messages(0, new_trace_ref, send_places_ref, sent, prepared)


def settle(level, blocks, places_ref, before, block):
    index = places_ref[block:block + 1, :]
    which = (index >> 7) - level * (BLOCK // LANES)
    return pick(blocks, index, which, before)


def received_blocks(received, count):
    return [(count + i, functools.partial(lambda ref: ref[...], ref)) for i, ref in enumerate(received)]


def received_traces(level, face, received, joined_ref, count):
    parts = []
    for block in range(BLOCK // LANES):
        index = joined_ref[face:face + 1, block_at(level * (BLOCK // LANES) + block)]
        zeros = jnp.zeros(received[0].shape, f32)
        parts.append(pick(received_blocks(received, count), index, index >> 7, zeros))
    return jnp.concatenate(parts, axis=1)


def other_traces(level, received, joined_ref, count):
    parts = [received_traces(level, face, received, joined_ref, count) for face in range(1, faces_in(joined_ref))]
    return jnp.concatenate([jnp.zeros_like(parts[0])] + parts, axis=0)


def any_other(level, flags_ref):
    return jnp.max(flags_ref[level:level + 1, :]) > 0.0


def between_kernel(level, messages, members_ref, joined_ref, places_ref, columns_ref, old_out_ref, old_trace_ref,
                   moved_ref, extra_ref, extra_trace_ref, heights_ref, local_ref, old_weights_ref, lift_ref,
                   lift_first_ref, grow_ref, trace_grow_ref, send_places_ref, *rest):
    received, rest = rest[:messages], rest[messages:]
    final = level == LEVELS - 1
    if not final:
        sent, rest = rest[:messages], rest[messages:]
    if level > 1:
        advanced_ref, rest = rest[0], rest[1:]
    if final:
        loaded_ref, weights_ref, new_advanced_ref, out_ref, faces_ref, trace_ref, whole_ref = rest
    else:
        out_ref, loaded_ref, weights_ref, new_trace_ref, new_advanced_ref = rest[:5]
        prepared, (faces_ref, trace_ref, whole_ref) = rest[5:5 + messages], rest[5 + messages:]
    count = places_ref.shape[0]
    done = level - 1
    first = received_traces(done, 0, received, joined_ref, count)
    inflow = product(lift_first_ref[...], stacked_columns(first))
    for block in range(BLOCK // LANES):
        here = block_at(block)
        index = joined_ref[0:1, block_at(done * (BLOCK // LANES) + block)]
        moved = [(count + i, read) for i, read in ref_blocks(moved_ref, messages)]
        trace_ref[:, here] = old_trace_ref[:, here] + extra_trace_ref[:, here] + pick(
            moved, index, index >> 7, jnp.zeros((old_trace_ref.shape[0], LANES), f32))
    whole = local_ref[...] + inflow + extra_ref[...]
    stacked = stacked_columns(whole)
    chunks = row_chunks(whole.shape[0])
    pieces = BLOCK // LANES

    def gather_own(part):
        for block in range(part * pieces // len(chunks), (part + 1) * pieces // len(chunks)):
            own_block(level, block, members_ref, joined_ref, columns_ref, heights_ref, loaded_ref, weights_ref)

    def gather_faces(part):
        for block in range(part * pieces // len(chunks), (part + 1) * pieces // len(chunks)):
            face_block(level, block, joined_ref, out_ref, faces_ref)

    def put_out(part):
        for block in range(part * count // len(chunks), (part + 1) * count // len(chunks)):
            here = block_at(block)
            out_ref[:, here] = settle(
                done, ref_blocks(trace_ref, pieces), places_ref, old_out_ref[:, here], block)

    def put_columns(chunk):
        for block in range(count):
            here = block_at(block)
            before = advanced_ref[chunk, here] if level > 1 else None
            new_advanced_ref[chunk, here] = settle(
                done, [(b, functools.partial(lambda b: whole_ref[chunk, block_at(b)], b)) for b in range(pieces)],
                places_ref, before, block)

    for part in range(len(chunks)):
        put_out(part)
    for part, chunk in enumerate(chunks):
        whole_ref[chunk, :] = grown_rows(chunk, stacked, whole, grow_ref, old_weights_ref)
        gather_own(part)
        gather_faces(part)
    loaded = loaded_ref[...] + product(lift_ref[...], stacked_columns(faces_ref[...]))
    put_columns(chunks[0])
    loaded_ref[...] = loaded
    if not final:
        traces = advanced_traces(loaded, trace_grow_ref, weights_ref, out_ref.shape[0])
    for chunk in chunks[1:]:
        put_columns(chunk)
    if not final:
        new_trace_ref[...] = traces
        local_messages(level, new_trace_ref, send_places_ref, sent, prepared)


def level_kernel(level, messages, count, flags_ref, joined_ref, weights_ref, slot_weights_ref, mix_ref, lift_ref,
                 trace_grow_ref, send_places_ref, send_codes_ref, *rest):
    received, rest = rest[:messages], rest[messages:]
    prepared, rest = rest[:messages], rest[messages:]
    moved_ref, extra_ref, extra_trace_ref, sends = rest[0], rest[1], rest[2], rest[3:]
    rows = moved_ref.shape[0]
    pieces = BLOCK // LANES
    other = any_other(level, flags_ref)
    arrived = jnp.concatenate([ref[...] for ref in received], axis=1)
    stacked = product(mix_ref[...], stacked_columns(arrived))
    moved_ref[...] = summed_powers(stacked[rows:], slot_weights_ref, rows, stacked[:rows])
    extra_ref[...] = jnp.zeros(extra_ref.shape, f32)
    extra_trace_ref[...] = jnp.zeros(extra_trace_ref.shape, f32)
    moved = [(count + i, read) for i, read in ref_blocks(moved_ref, messages)]
    for group, (before, send) in enumerate(zip(prepared, sends)):
        place, code = send_places_ref[group:group + 1, :], send_codes_ref[group:group + 1, :]
        here = ((place >> 7) >= level * pieces) & ((place >> 7) < (level + 1) * pieces)
        send[...] = before[...] + pick(
            moved, code, jnp.where(here, code >> 7, 0), jnp.zeros(before.shape, f32))

    @pl.when(other)
    def _():
        others = other_traces(level, received, joined_ref, count)
        extra = product(lift_ref[...], stacked_columns(others))
        extra_ref[...] = extra
        extra_trace_ref[...] = advanced_traces(extra, trace_grow_ref, weights_ref, rows)
        for group, send in enumerate(sends):
            place = send_places_ref[group:group + 1, :]
            send[...] = send[...] + pick(
                ref_blocks(extra_trace_ref, pieces), place, (place >> 7) - level * pieces, jnp.zeros(send.shape, f32))


def last_chunks(rows):
    units = rows // 16
    first = -(-units * 4 // 9)
    second = -(-(units - first) * 3 // 5)
    bounds = [0, first * 16, (first + second) * 16, rows]
    return [slice(low, high) for low, high in zip(bounds, bounds[1:]) if high > low]


def last_kernel(level, messages, flags_ref, joined_ref, local_ref, weights_ref, lift_ref, lift_first_ref, grow_ref,
                places_ref, advanced_ref, *rest):
    received, (final_hbm, final_ref, sent) = rest[:messages], rest[messages:]
    count = places_ref.shape[0]
    comp = final_ref.shape[0] // count

    def finish(whole):
        stacked = stacked_columns(whole)
        copies = []

        def put(number, chunk, new):
            height = min(chunk.stop, comp) - chunk.start
            for block in range(count):
                done = settle(level, value_blocks(new), places_ref, advanced_ref[chunk, block_at(block)], block)
                final_ref[pl.ds(chunk.start * count + block, height, stride=count), :] = done[:height]
            part = pl.ds(chunk.start * count, height * count)
            copies.append(pltpu.make_async_copy(final_ref.at[part], final_hbm.at[part], sent.at[number]))
            copies[-1].start()

        ahead = None
        for number, chunk in enumerate(last_chunks(whole.shape[0])):
            new = grown_rows(chunk, stacked, whole, grow_ref, weights_ref)
            if ahead is not None:
                put(*ahead)
            ahead = (number, chunk, new)
        put(*ahead)
        for copy in copies:
            copy.wait()

    def whole_of(others):
        first = received_traces(level, 0, received, joined_ref, count)
        whole = local_ref[...] + product(lift_first_ref[...], stacked_columns(first))
        return whole if others is None else whole + product(lift_ref[...], stacked_columns(others))

    other = any_other(level, flags_ref)
    finish(whole_of(None))

    @pl.when(other)
    def _():
        finish(whole_of(other_traces(level, received, joined_ref, count)))


def call(kernel, name, flops, operands, outs, scratch=(), hbm=False, out_hbm=False):
    vmem = pl.BlockSpec(memory_space=pltpu.VMEM)
    given = pl.BlockSpec(memory_space=pltpu.HBM) if hbm else vmem
    if hbm:
        operands = [pltpu.with_memory_space_constraint(one, pltpu.HBM) for one in operands]
    return pl.pallas_call(
        kernel,
        out_shape=tuple(jax.ShapeDtypeStruct(shape, dtype) for shape, dtype in outs),
        in_specs=[given] * len(operands),
        out_specs=tuple([pl.BlockSpec(memory_space=pltpu.HBM) if out_hbm else vmem] * len(outs)),
        scratch_shapes=[one if not isinstance(one, tuple) else pltpu.VMEM(*one) for one in scratch],
        compiler_params=pltpu.CompilerParams(vmem_limit_bytes=16 * 1024 * 1024),
        cost_estimate=pl.CostEstimate(flops=flops, bytes_accessed=1 << 20, transcendentals=0),
        name=name,
    )(*operands)


def is_odd(axis):
    return (lax.axis_index(axis) & 1) == 1


def swap_plan(axis, periodic, low, high):
    count = lax.axis_size(axis)
    plan = [(axis, [(i, i ^ 1) for i in range(count)], low, high, False)]
    if count > 2 or periodic:
        pairs = [(i, (i + 1) % count if i % 2 else (i - 1) % count) for i in range(count)]
        plan.append((axis, pairs, high, low, not periodic))
    return plan


def came_group(swap):
    axis, _, even, odd, is_open = swap
    came = jnp.where(is_odd(axis), even, odd)
    if is_open:
        index = lax.axis_index(axis)
        came = jnp.where((index == 0) | (index == lax.axis_size(axis) - 1), NO_GROUP, came)
    return came


def body(fields, pattern, tent_order, level_sizes, send_rows, neighbours, operator, trace_map, lift_map, tent_height):
    fields, order, sizes = fields[0, 0], tent_order[0], level_sizes[0]
    faces_of, send_list = neighbours[0, 0], send_rows[0, 0]
    comp, elements = fields.shape
    faces, trace = lift_map.shape[0], trace_map.shape[0]
    rows, trace_rows = rounded_up(comp, 16), rounded_up(trace, 16)
    padded, count = LEVELS * BLOCK, elements // LANES
    bnd = send_list.shape[-1]

    near, *far = swap_plan("sector", True, 0, 1)
    swaps = far + swap_plan("radial", False, 2, 3) + [near]
    messages = len(swaps)

    def exchange(sent):
        return [lax.ppermute(one, swap[0], swap[1]) for one, swap in zip(sent, swaps)]

    message = ((trace_rows, bnd), f32)
    own, face_stack = ((rows, BLOCK), f32), ((faces * trace_rows, BLOCK), f32)
    weight, table, traced = ((POWERS, BLOCK), f32), ((trace_rows, elements), f32), ((trace_rows, BLOCK), f32)
    whole = ((rows, elements), f32)
    flat = (comp * count, LANES)

    arguments = [trace_map, send_list, order, pattern[0], sizes, faces_of, operator,
                 jnp.transpose(lift_map, (2, 0, 1)), tent_height[None]]
    columns, out, *rest = call(
        functools.partial(first_kernel, swaps), "first", 10 ** 8, [fields.reshape(flat)] + arguments,
        [whole, table] + [message] * messages + [(one.shape, one.dtype) for one in arguments],
        [(flat, f32), pltpu.SemaphoreType.DMA((ARGUMENTS + 1,))], hbm=True)
    sent, held = rest[:messages], rest[messages:]
    received = exchange(sent)
    slots = ((trace_rows, messages * LANES), f32)
    (members, joined, places, send_places, send_codes, slot_weights, flags, loaded, weights, new_trace, grow,
     trace_grow, mix, lift, lift_first, heights, *prepared) = call(
        functools.partial(plan_kernel, swaps), "plan", 2 * 10 ** 9, held + [columns, out] + sent,
        [((8, padded), i32), ((2 * faces, padded), i32), ((count, LANES), i32), ((8, bnd), i32), ((8, bnd), i32),
         ((POWERS, messages * LANES), f32), ((LEVELS, LANES), f32), own, weight, traced,
         ((POWERS * rows, 3 * rows), bf16), (((POWERS + 1) * trace_rows, 3 * rows), bf16),
         (((POWERS + 1) * trace_rows, 3 * trace_rows), bf16), ((rows, 3 * faces * trace_rows), bf16), ((rows, 3 * trace_rows), bf16), ((1, LANES), f32)]
        + [message] * messages, [face_stack])
    advanced = []
    for level in range(LEVELS - 1):
        moved, extra, extra_trace, *sent = call(
            functools.partial(level_kernel, level, messages, count), "level", 10 ** 8,
            [flags, joined, weights, slot_weights, mix, lift, trace_grow, send_places, send_codes] + received + prepared,
            [slots, own, traced] + [message] * messages)
        arrived, received = received, exchange(sent)
        beside = functools.partial(between_kernel, level + 1, messages)
        operands = [members, joined, places, columns, out, new_trace, moved, extra, extra_trace, heights, loaded,
                    weights, lift, lift_first, grow, trace_grow, send_places] + arrived
        scratch = [face_stack, traced, own]
        if level + 1 < LEVELS - 1:
            out, loaded, weights, new_trace, *rest = call(
                beside, "between", 2 * 10 ** 9, operands + sent + advanced,
                [table, own, weight, traced, whole] + [message] * messages, scratch)
            advanced, prepared = rest[:1], rest[1:]
        else:
            loaded, weights, *advanced = call(
                beside, "between", 2 * 10 ** 9, operands + advanced, [own, weight, whole], [table] + scratch)
    final, = call(
        functools.partial(last_kernel, LEVELS - 1, messages), "last", 10 ** 9,
        [flags, joined, loaded, weights, lift, lift_first, grow, places] + advanced + received,
        [(flat, f32)], [(flat, f32), pltpu.SemaphoreType.DMA((len(last_chunks(rows)),))], out_hbm=True)
    return final.reshape(1, 1, comp, elements)


def solution(mesh):
    in_specs = (
        P("sector", "radial", None, None),
        P("sector", "radial", None),
        P("sector", "radial", None),
        P("sector", "radial", None),
        P("sector", "radial", None, None),
        P("sector", "radial", None, None),
        P(),
        P(),
        P(),
        P(),
    )
    out_specs = P("sector", "radial", None, None)
    return jax.shard_map(body, mesh=mesh, in_specs=in_specs, out_specs=out_specs, check_vma=False)
```

```python
import functools
import math

import jax
import jax.numpy as jnp
from jax import lax
from jax.experimental import pallas as pl
from jax.experimental.pallas import tpu as pltpu
from jax.sharding import PartitionSpec as P

LEVELS = 4
SUBSTEPS = 2
TERMS = 4
BLOCK = 384
LANES = 128
NO_GROUP = 1 << 20
ARGUMENTS = 10
ROW_CHUNK = 48

f32, bf16, i32 = jnp.float32, jnp.bfloat16, jnp.int32
precise = lax.Precision.HIGHEST


def rounded_up(size, unit):
    return -(-size // unit) * unit


def taylor_weights():
    once = [1.0 / math.factorial(k) for k in range(TERMS + 1)]
    whole = [1.0]
    for _ in range(SUBSTEPS):
        longer = [0.0] * (len(whole) + TERMS)
        for i, a in enumerate(whole):
            for j, b in enumerate(once):
                longer[i + j] += a * b
        whole = longer
    return whole


WEIGHTS = taylor_weights()
POWERS = len(WEIGHTS) - 1


def split(values):
    high = values.astype(bf16)
    return high, (values - high.astype(f32)).astype(bf16)


def whole_lanes(size):
    return size // LANES * LANES


def stacked_columns(values):
    high, low = split(values)
    main = whole_lanes(values.shape[0])
    parts = [high[:main], low[:main], high[:main], high[main:], low[main:], high[main:]]
    return jnp.concatenate([part for part in parts if part.shape[0]], axis=0)


def stacked_matrix(values):
    high = values.astype(bf16).astype(f32)
    low = values - high
    main = whole_lanes(values.shape[1])
    parts = [high[:, :main], high[:, :main], low[:, :main], high[:, main:], high[:, main:], low[:, main:]]
    return jnp.concatenate([part for part in parts if part.shape[1]], axis=1).astype(bf16)


def product(matrix, columns):
    return jnp.dot(matrix, columns, preferred_element_type=f32)


def pad_rows(values, rows):
    short = rows - values.shape[0]
    if short == 0:
        return values
    return jnp.concatenate([values, jnp.zeros((short,) + values.shape[1:], values.dtype)], axis=0)


def exact_product(left, right):
    left_high, left_low = split(left)
    right_high, right_low = split(right)
    rows = left.shape[0]
    both = product(jnp.concatenate([left_high, left_low], axis=0), right_high)
    return both[:rows] + both[rows:] + product(left_high, right_low)


def pick(blocks, index, which, start=None):
    result = start
    for number, read in blocks:
        table = read()
        lane = jnp.broadcast_to(index & (LANES - 1), table.shape)
        got = jnp.take_along_axis(table, lane, axis=1, mode="promise_in_bounds")
        if result is None:
            result = got
        else:
            result = jnp.where(jnp.broadcast_to(which, table.shape) == number, got, result)
    return result


def block_at(block):
    return slice(block * LANES, (block + 1) * LANES)


def ref_blocks(ref, count):
    return [(b, functools.partial(lambda b: ref[:, block_at(b)], b)) for b in range(count)]


def value_blocks(values):
    return [(b, functools.partial(lambda b: values[:, block_at(b)], b)) for b in range(values.shape[1] // LANES)]


def row_blocks(table, rows):
    return [
        (b, functools.partial(lambda b: jnp.broadcast_to(table[b:b + 1, :], (rows, LANES)), b))
        for b in range(table.shape[0])
    ]


def row_blocks_of(row, rows):
    return [
        (b, functools.partial(lambda b: jnp.broadcast_to(row[:, block_at(b)], (rows, LANES)), b))
        for b in range(row.shape[1] // LANES)
    ]


def summed_powers(stacked, weights_ref, rows, total):
    for power in range(1, POWERS + 1):
        total = total + stacked[(power - 1) * rows:power * rows] * weights_ref[power - 1:power, :]
    return total


def sent_rows(send_ref, swaps):
    rows = []
    for axis, _, low, high, _ in swaps:
        odd, even = send_ref[high:high + 1, :], send_ref[low:low + 1, :]
        rows.append(jnp.where(is_odd(axis), odd, even))
    return rows


def first_kernel(swaps, *refs):
    (fields_hbm, *given), refs = refs[:ARGUMENTS], refs[ARGUMENTS:]
    (columns_ref, out_ref), refs = refs[:2], refs[2:]
    sends, refs = refs[:len(swaps)], refs[len(swaps):]
    *held, fields_ref, arrived = refs
    rows = out_ref.shape[0]
    elements = out_ref.shape[1]
    count = elements // LANES
    comp = fields_ref.shape[0] // count
    cuts = [slice(0, rounded_up(comp // 2, 16)), slice(rounded_up(comp // 2, 16), comp)]
    parts = [pl.ds(cut.start * count, (cut.stop - cut.start) * count) for cut in cuts]
    trace_hbm, send_hbm, *others = given
    trace_ref, send_ref, *others_held = held
    pairs = [(fields_hbm.at[parts[0]], fields_ref.at[parts[0]]), (trace_hbm, trace_ref),
             (fields_hbm.at[parts[1]], fields_ref.at[parts[1]]), (send_hbm, send_ref)]
    pairs += list(zip(others, others_held))
    copies = [pltpu.make_async_copy(source, target, arrived.at[i]) for i, (source, target) in enumerate(pairs)]
    for copy in copies:
        copy.start()
    total = None
    for number, cut in enumerate(cuts):
        if number == 0:
            copies[0].wait()
            copies[1].wait()
            trace = pad_rows(trace_ref[...], rows)
        else:
            copies[2].wait()
        height = cut.stop - cut.start
        fields = jnp.concatenate(
            [fields_ref[pl.ds(cut.start * count + b, height, stride=count), :] for b in range(count)], axis=1)
        trace_high, trace_low = split(trace[:, cut])
        high, low = split(fields)
        upper = product(jnp.concatenate([trace_high, trace_low], axis=0), high)
        part = upper[:rows] + upper[rows:] + product(trace_high, low)
        total = part if total is None else total + part
        columns_ref[cut, :] = fields
    out_ref[...] = total
    copies[3].wait()
    for index, send in zip(sent_rows(send_ref, swaps), sends):
        send[...] = pick(ref_blocks(out_ref, count), index, index >> 7)[:send.shape[0]]
    columns_ref[comp:, :] = jnp.zeros((columns_ref.shape[0] - comp, elements), f32)
    for copy in copies[4:]:
        copy.wait()


def faces_in(joined_ref):
    return joined_ref.shape[0] // 2


def own_block(level, block, members_ref, joined_ref, columns_ref, heights_ref, own_ref, weights_ref):
    faces = faces_in(joined_ref)
    here, there = block_at(block), block_at(level * (BLOCK // LANES) + block)
    index = members_ref[0:1, there]
    own_ref[:, here] = pick(ref_blocks(columns_ref, columns_ref.shape[1] // LANES), index, index >> 7)
    pattern = jnp.broadcast_to(joined_ref[faces:faces + 1, there], (8, LANES))
    height = jnp.take_along_axis(
        jnp.broadcast_to(heights_ref[...], (8, LANES)), pattern, axis=1, mode="promise_in_bounds")
    weight = jnp.ones((8, LANES), f32)
    for power in range(1, POWERS + 1):
        weight = weight * height
        weights_ref[power - 1:power, here] = weight[0:1] * WEIGHTS[power]


def face_block(level, block, joined_ref, out_ref, faces_ref):
    trace_rows = out_ref.shape[0]
    here, there = block_at(block), block_at(level * (BLOCK // LANES) + block)
    for face in range(faces_in(joined_ref)):
        index = joined_ref[face:face + 1, there]
        faces_ref[face * trace_rows:(face + 1) * trace_rows, here] = pick(
            ref_blocks(out_ref, out_ref.shape[1] // LANES), index, index >> 7, jnp.zeros((trace_rows, LANES), f32))


def advanced_traces(loaded, matrix_ref, weights_ref, rows):
    stacked = product(matrix_ref[...], stacked_columns(loaded))
    return summed_powers(stacked[rows:], weights_ref, rows, stacked[:rows])


def local_messages(level, trace_ref, send_places_ref, sent, messages):
    for group, (before, message) in enumerate(zip(sent, messages)):
        index = send_places_ref[group:group + 1, :]
        which = (index >> 7) - level * (BLOCK // LANES)
        message[...] = pick(
            ref_blocks(trace_ref, BLOCK // LANES), index, which, pad_rows(before[...], message.shape[0]))


def row_chunks(rows):
    return [slice(low, low + ROW_CHUNK) for low in range(0, rows, ROW_CHUNK)]


def grown_rows(chunk, stacked, loaded, grow_ref, weights_ref):
    rows = loaded.shape[0]
    matrix = jnp.concatenate(
        [grow_ref[power * rows + chunk.start:power * rows + chunk.stop, :] for power in range(POWERS)], axis=0)
    return summed_powers(product(matrix, stacked), weights_ref, chunk.stop - chunk.start, loaded[chunk])


def matrix_powers(operator_ref, trace_ref, lift_ref, grow_ref, trace_grow_ref, mix_ref, lift_out_ref,
                  lift_first_ref):
    comp = operator_ref.shape[0]
    trace_comp, faces, _ = lift_ref.shape
    rows = lift_out_ref.shape[0]
    trace_rows = trace_grow_ref.shape[0] // (POWERS + 1)
    operator = pad_rows(operator_ref[...], rows)
    operator = jnp.concatenate([operator, jnp.zeros((rows, rows - comp), f32)], axis=1)
    traces = pad_rows(trace_ref[...], trace_rows)
    traces = jnp.concatenate([traces, jnp.zeros((trace_rows, rows - comp), f32)], axis=1)
    lift = jnp.concatenate([pad_rows(lift_ref[:, face, :], trace_rows) for face in range(faces)], axis=0)
    lift = pad_rows(jnp.transpose(lift), rows)
    lift_out_ref[...] = stacked_matrix(lift)
    lift_first_ref[...] = stacked_matrix(lift[:, :trace_rows])
    powers, have = operator, 1
    while have < POWERS:
        more = exact_product(jnp.concatenate([traces, powers], axis=0), powers[(have - 1) * rows:have * rows])
        traces = jnp.concatenate([traces, more[:have * trace_rows]], axis=0)
        powers = jnp.concatenate([powers, more[have * trace_rows:]], axis=0)
        have *= 2
        yield
    traces = jnp.concatenate([traces, exact_product(traces[:trace_rows], powers[-rows:])], axis=0)
    trace_grow_ref[...] = stacked_matrix(traces)
    yield
    mix_ref[...] = stacked_matrix(exact_product(traces, lift[:, :trace_rows]))
    grow_ref[...] = stacked_matrix(powers)
    yield


def plan_kernel(swaps, *refs):
    (trace_ref, send_ref, order_ref, pattern_ref, sizes_ref, neighbours_ref, operator_ref, lift_ref, heights_ref,
     columns_ref, out_ref), refs = refs[:11], refs[11:]
    messages = len(swaps)
    sent, refs = refs[:messages], refs[messages:]
    (members_ref, joined_ref, places_ref, send_places_ref, send_codes_ref, slot_weights_ref, flags_ref, loaded_ref,
     weights_ref, new_trace_ref, grow_ref, trace_grow_ref, mix_ref, lift_out_ref, lift_first_ref,
     wide_heights_ref), refs = refs[:16], refs[16:]
    prepared, (faces_ref,) = refs[:messages], refs[messages:]
    elements = columns_ref.shape[1]
    count = elements // LANES
    faces = neighbours_ref.shape[0]
    steps = matrix_powers(operator_ref, trace_ref, lift_ref, grow_ref, trace_grow_ref, mix_ref, lift_out_ref,
                          lift_first_ref)
    next(steps)
    sizes = sizes_ref[...].astype(f32)
    number = lax.broadcasted_iota(i32, sizes.shape, 1)
    starts = [jnp.sum(jnp.where(number < level, sizes, 0.0)).astype(i32) for level in range(LEVELS)]
    wide_order = jnp.broadcast_to(order_ref[...], (8, elements))
    neighbours = neighbours_ref[...]
    group = (neighbours >> 7) - count
    message = jnp.full(neighbours.shape, count + len(swaps), i32)
    for number, swap in enumerate(swaps):
        message = jnp.where(group == came_group(swap), count + number, message)
    neighbours = jnp.where(group >= 0, message * LANES + (neighbours & (LANES - 1)), neighbours)
    table = jnp.concatenate(
        [neighbours, pattern_ref[...], jnp.zeros((faces - 1, elements), i32)], axis=0)
    heights = heights_ref[...]
    wide_heights_ref[...] = jnp.concatenate(
        [heights, jnp.zeros((1, LANES - heights.shape[1]), f32)], axis=1)
    for level in range(LEVELS):
        shift = jnp.where(starts[level] == 0, 0, elements - starts[level])
        members_ref[:, level * BLOCK:(level + 1) * BLOCK] = pltpu.roll(wide_order, shift, 1)[:, :BLOCK]
    for block in range(LEVELS * BLOCK // LANES):
        index = members_ref[:, block_at(block)]
        joined_ref[:, block_at(block)] = pick(value_blocks(table), index, index >> 7)
    ranks = lax.broadcasted_iota(i32, (count, elements), 1)
    in_block = (wide_order[:count] >> 7) == lax.broadcasted_iota(i32, (count, elements), 0)
    left = jnp.concatenate([
        jnp.where(in_block, ranks >> 5, 0).astype(f32), jnp.where(in_block, ranks & 31, 0).astype(f32)], axis=0)
    at_lane = jnp.broadcast_to(order_ref[...] & (LANES - 1), (LANES, elements)) == lax.broadcasted_iota(
        i32, (LANES, elements), 0)
    rank = lax.dot_general(left.astype(bf16), jnp.where(at_lane, 1.0, 0.0).astype(bf16), (((1,), (1,)), ((), ())),
                           preferred_element_type=f32)
    place = rank[:count].astype(i32) * 32 + rank[count:].astype(i32)
    at = place
    for level in range(1, LEVELS):
        at = jnp.where(place >= starts[level], place - starts[level] + level * BLOCK, at)
    places_ref[...] = at
    index = pad_rows(jnp.concatenate(sent_rows(send_ref, swaps), axis=0), 8)
    send_places_ref[...] = pick(row_blocks(at, 8), index, index >> 7)
    send_codes_ref[...] = pick(row_blocks_of(neighbours[:1], 8), index, index >> 7)
    block = jnp.broadcast_to(neighbours[:1] >> 7, (8, elements)) - count
    named = jnp.where(block == lax.broadcasted_iota(i32, (8, elements), 0),
                      jnp.broadcast_to(pattern_ref[...], (8, elements)), 0).astype(f32).astype(bf16)
    slot_lane = jnp.broadcast_to(neighbours[:1] & (LANES - 1), (LANES, elements)) == lax.broadcasted_iota(
        i32, (LANES, elements), 0)
    slot_pattern = lax.dot_general(named, jnp.where(slot_lane, 1.0, 0.0).astype(bf16), (((1,), (1,)), ((), ())),
                                   preferred_element_type=f32).astype(i32)
    height = jnp.take_along_axis(jnp.broadcast_to(wide_heights_ref[...], (8, LANES)), slot_pattern & (LANES - 1),
                                 axis=1, mode="promise_in_bounds")
    weight = jnp.ones((8, LANES), f32)
    for power in range(1, POWERS + 1):
        weight = weight * height
        for number in range(messages):
            slot_weights_ref[power - 1:power, block_at(number)] = weight[number:number + 1] * WEIGHTS[power]
    for level in range(LEVELS):
        code = joined_ref[1:faces, level * BLOCK:(level + 1) * BLOCK]
        code = jnp.max(jnp.where(code >= elements, 1.0, 0.0), axis=0, keepdims=True)
        row = code[:, block_at(0)]
        for number in range(1, BLOCK // LANES):
            row = jnp.maximum(row, code[:, block_at(number)])
        flags_ref[level:level + 1, :] = row
    next(steps)
    for block in range(BLOCK // LANES):
        own_block(0, block, members_ref, joined_ref, columns_ref, wide_heights_ref, loaded_ref, weights_ref)
        face_block(0, block, joined_ref, out_ref, faces_ref)
        next(steps)
    loaded = loaded_ref[...] + product(lift_out_ref[...], stacked_columns(faces_ref[...]))
    loaded_ref[...] = loaded
    new_trace_ref[...] = advanced_traces(loaded, trace_grow_ref, weights_ref, out_ref.shape[0])
    local_messages(0, new_trace_ref, send_places_ref, sent, prepared)


def settle(level, blocks, places_ref, before, block):
    index = places_ref[block:block + 1, :]
    which = (index >> 7) - level * (BLOCK // LANES)
    return pick(blocks, index, which, before)


def received_blocks(received, count, rows):
    return [(count + i, functools.partial(lambda ref: pad_rows(ref[...], rows), ref)) for i, ref in enumerate(received)]


def received_traces(level, face, received, joined_ref, count):
    parts = []
    for block in range(BLOCK // LANES):
        index = joined_ref[face:face + 1, block_at(level * (BLOCK // LANES) + block)]
        rows = rounded_up(received[0].shape[0], 16)
        zeros = jnp.zeros((rows, LANES), f32)
        parts.append(pick(received_blocks(received, count, rows), index, index >> 7, zeros))
    return jnp.concatenate(parts, axis=1)


def other_traces(level, received, joined_ref, count):
    parts = [received_traces(level, face, received, joined_ref, count) for face in range(1, faces_in(joined_ref))]
    return jnp.concatenate([jnp.zeros_like(parts[0])] + parts, axis=0)


def any_other(level, flags_ref):
    return jnp.max(flags_ref[level:level + 1, :]) > 0.0


def between_kernel(level, messages, members_ref, joined_ref, places_ref, columns_ref, old_out_ref, old_trace_ref,
                   moved_ref, extra_ref, extra_trace_ref, heights_ref, local_ref, old_weights_ref, lift_ref,
                   lift_first_ref, grow_ref, trace_grow_ref, send_places_ref, *rest):
    received, rest = rest[:messages], rest[messages:]
    final = level == LEVELS - 1
    if not final:
        sent, rest = rest[:messages], rest[messages:]
    if level > 1:
        advanced_ref, rest = rest[0], rest[1:]
    if final:
        loaded_ref, weights_ref, new_advanced_ref, out_ref, faces_ref, trace_ref, whole_ref = rest
    else:
        out_ref, loaded_ref, weights_ref, new_trace_ref, new_advanced_ref = rest[:5]
        prepared, (faces_ref, trace_ref, whole_ref) = rest[5:5 + messages], rest[5 + messages:]
    count = places_ref.shape[0]
    done = level - 1
    first = received_traces(done, 0, received, joined_ref, count)
    inflow = product(lift_first_ref[...], stacked_columns(first))
    for block in range(BLOCK // LANES):
        here = block_at(block)
        index = joined_ref[0:1, block_at(done * (BLOCK // LANES) + block)]
        moved = [(count + i, read) for i, read in ref_blocks(moved_ref, messages)]
        trace_ref[:, here] = old_trace_ref[:, here] + extra_trace_ref[:, here] + pick(
            moved, index, index >> 7, jnp.zeros((old_trace_ref.shape[0], LANES), f32))
    whole = local_ref[...] + inflow + extra_ref[...]
    stacked = stacked_columns(whole)
    chunks = row_chunks(whole.shape[0])
    pieces = BLOCK // LANES

    def gather_own(part):
        for block in range(part * pieces // len(chunks), (part + 1) * pieces // len(chunks)):
            own_block(level, block, members_ref, joined_ref, columns_ref, heights_ref, loaded_ref, weights_ref)

    def gather_faces(part):
        for block in range(part * pieces // len(chunks), (part + 1) * pieces // len(chunks)):
            face_block(level, block, joined_ref, out_ref, faces_ref)

    def put_out(part):
        for block in range(part * count // len(chunks), (part + 1) * count // len(chunks)):
            here = block_at(block)
            out_ref[:, here] = settle(
                done, ref_blocks(trace_ref, pieces), places_ref, old_out_ref[:, here], block)

    def put_columns(chunk):
        for block in range(count):
            here = block_at(block)
            before = advanced_ref[chunk, here] if level > 1 else None
            new_advanced_ref[chunk, here] = settle(
                done, [(b, functools.partial(lambda b: whole_ref[chunk, block_at(b)], b)) for b in range(pieces)],
                places_ref, before, block)

    for part in range(len(chunks)):
        put_out(part)
    for part, chunk in enumerate(chunks):
        whole_ref[chunk, :] = grown_rows(chunk, stacked, whole, grow_ref, old_weights_ref)
        gather_own(part)
        gather_faces(part)
    loaded = loaded_ref[...] + product(lift_ref[...], stacked_columns(faces_ref[...]))
    put_columns(chunks[0])
    loaded_ref[...] = loaded
    if not final:
        traces = advanced_traces(loaded, trace_grow_ref, weights_ref, out_ref.shape[0])
    for chunk in chunks[1:]:
        put_columns(chunk)
    if not final:
        new_trace_ref[...] = traces
        local_messages(level, new_trace_ref, send_places_ref, sent, prepared)


def level_kernel(level, messages, count, flags_ref, joined_ref, weights_ref, slot_weights_ref, mix_ref, lift_ref,
                 trace_grow_ref, send_places_ref, send_codes_ref, *rest):
    received, rest = rest[:messages], rest[messages:]
    prepared, rest = rest[:messages], rest[messages:]
    moved_ref, extra_ref, extra_trace_ref, sends = rest[0], rest[1], rest[2], rest[3:]
    rows = moved_ref.shape[0]
    pieces = BLOCK // LANES
    other = any_other(level, flags_ref)
    arrived = jnp.concatenate([pad_rows(ref[...], rows) for ref in received], axis=1)
    stacked = product(mix_ref[...], stacked_columns(arrived))
    moved_ref[...] = summed_powers(stacked[rows:], slot_weights_ref, rows, stacked[:rows])
    extra_ref[...] = jnp.zeros(extra_ref.shape, f32)
    extra_trace_ref[...] = jnp.zeros(extra_trace_ref.shape, f32)
    moved = [(count + i, read) for i, read in ref_blocks(moved_ref, messages)]
    for group, (before, send) in enumerate(zip(prepared, sends)):
        place, code = send_places_ref[group:group + 1, :], send_codes_ref[group:group + 1, :]
        here = ((place >> 7) >= level * pieces) & ((place >> 7) < (level + 1) * pieces)
        total = before[...] + pick(moved, code, jnp.where(here, code >> 7, 0), jnp.zeros(before.shape, f32))
        send[...] = total[:send.shape[0]]

    @pl.when(other)
    def _():
        others = other_traces(level, received, joined_ref, count)
        extra = product(lift_ref[...], stacked_columns(others))
        extra_ref[...] = extra
        extra_trace_ref[...] = advanced_traces(extra, trace_grow_ref, weights_ref, rows)
        for group, send in enumerate(sends):
            place = send_places_ref[group:group + 1, :]
            more = pick(
                ref_blocks(extra_trace_ref, pieces), place, (place >> 7) - level * pieces, jnp.zeros((rows, LANES), f32))
            send[...] = send[...] + more[:send.shape[0]]


def last_chunks(rows):
    units = rows // 16
    first = -(-units * 4 // 9)
    second = -(-(units - first) * 3 // 5)
    bounds = [0, first * 16, (first + second) * 16, rows]
    return [slice(low, high) for low, high in zip(bounds, bounds[1:]) if high > low]


def last_kernel(level, messages, flags_ref, joined_ref, local_ref, weights_ref, lift_ref, lift_first_ref, grow_ref,
                places_ref, advanced_ref, *rest):
    received, (final_hbm, final_ref, sent) = rest[:messages], rest[messages:]
    count = places_ref.shape[0]
    comp = final_ref.shape[0] // count

    def finish(whole):
        stacked = stacked_columns(whole)
        copies = []

        def put(number, chunk, new):
            height = min(chunk.stop, comp) - chunk.start
            for block in range(count):
                done = settle(level, value_blocks(new), places_ref, advanced_ref[chunk, block_at(block)], block)
                final_ref[pl.ds(chunk.start * count + block, height, stride=count), :] = done[:height]
            part = pl.ds(chunk.start * count, height * count)
            copies.append(pltpu.make_async_copy(final_ref.at[part], final_hbm.at[part], sent.at[number]))
            copies[-1].start()

        ahead = None
        for number, chunk in enumerate(last_chunks(whole.shape[0])):
            new = grown_rows(chunk, stacked, whole, grow_ref, weights_ref)
            if ahead is not None:
                put(*ahead)
            ahead = (number, chunk, new)
        put(*ahead)
        for copy in copies:
            copy.wait()

    def whole_of(others):
        first = received_traces(level, 0, received, joined_ref, count)
        whole = local_ref[...] + product(lift_first_ref[...], stacked_columns(first))
        return whole if others is None else whole + product(lift_ref[...], stacked_columns(others))

    other = any_other(level, flags_ref)
    finish(whole_of(None))

    @pl.when(other)
    def _():
        finish(whole_of(other_traces(level, received, joined_ref, count)))


def call(kernel, name, flops, operands, outs, scratch=(), hbm=False, out_hbm=False):
    vmem = pl.BlockSpec(memory_space=pltpu.VMEM)
    given = pl.BlockSpec(memory_space=pltpu.HBM) if hbm else vmem
    if hbm:
        operands = [pltpu.with_memory_space_constraint(one, pltpu.HBM) for one in operands]
    return pl.pallas_call(
        kernel,
        out_shape=tuple(jax.ShapeDtypeStruct(shape, dtype) for shape, dtype in outs),
        in_specs=[given] * len(operands),
        out_specs=tuple([pl.BlockSpec(memory_space=pltpu.HBM) if out_hbm else vmem] * len(outs)),
        scratch_shapes=[one if not isinstance(one, tuple) else pltpu.VMEM(*one) for one in scratch],
        compiler_params=pltpu.CompilerParams(vmem_limit_bytes=16 * 1024 * 1024),
        cost_estimate=pl.CostEstimate(flops=flops, bytes_accessed=1 << 20, transcendentals=0),
        name=name,
    )(*operands)


def is_odd(axis):
    return (lax.axis_index(axis) & 1) == 1


def swap_plan(axis, periodic, low, high):
    count = lax.axis_size(axis)
    plan = [(axis, [(i, i ^ 1) for i in range(count)], low, high, False)]
    if count > 2 or periodic:
        pairs = [(i, (i + 1) % count if i % 2 else (i - 1) % count) for i in range(count)]
        plan.append((axis, pairs, high, low, not periodic))
    return plan


def came_group(swap):
    axis, _, even, odd, is_open = swap
    came = jnp.where(is_odd(axis), even, odd)
    if is_open:
        index = lax.axis_index(axis)
        came = jnp.where((index == 0) | (index == lax.axis_size(axis) - 1), NO_GROUP, came)
    return came


def body(fields, pattern, tent_order, level_sizes, send_rows, neighbours, operator, trace_map, lift_map, tent_height):
    fields, order, sizes = fields[0, 0], tent_order[0], level_sizes[0]
    faces_of, send_list = neighbours[0, 0], send_rows[0, 0]
    comp, elements = fields.shape
    faces, trace = lift_map.shape[0], trace_map.shape[0]
    rows, trace_rows = rounded_up(comp, 16), rounded_up(trace, 16)
    padded, count = LEVELS * BLOCK, elements // LANES
    bnd = send_list.shape[-1]

    near, *far = swap_plan("sector", True, 0, 1)
    swaps = far + [near] + swap_plan("radial", False, 2, 3)
    messages = len(swaps)

    def exchange(sent):
        return [lax.ppermute(one, swap[0], swap[1]) for one, swap in zip(sent, swaps)]

    message, prepared_message = ((trace, bnd), f32), ((trace_rows, bnd), f32)
    own, face_stack = ((rows, BLOCK), f32), ((faces * trace_rows, BLOCK), f32)
    weight, table, traced = ((POWERS, BLOCK), f32), ((trace_rows, elements), f32), ((trace_rows, BLOCK), f32)
    whole = ((rows, elements), f32)
    flat = (comp * count, LANES)

    arguments = [trace_map, send_list, order, pattern[0], sizes, faces_of, operator,
                 jnp.transpose(lift_map, (2, 0, 1)), tent_height[None]]
    columns, out, *rest = call(
        functools.partial(first_kernel, swaps), "first", 10 ** 8, [fields.reshape(flat)] + arguments,
        [whole, table] + [message] * messages + [(one.shape, one.dtype) for one in arguments],
        [(flat, f32), pltpu.SemaphoreType.DMA((ARGUMENTS + 1,))], hbm=True)
    sent, held = rest[:messages], rest[messages:]
    received = exchange(sent)
    slots = ((trace_rows, messages * LANES), f32)
    (members, joined, places, send_places, send_codes, slot_weights, flags, loaded, weights, new_trace, grow,
     trace_grow, mix, lift, lift_first, heights, *prepared) = call(
        functools.partial(plan_kernel, swaps), "plan", 2 * 10 ** 9, held + [columns, out] + sent,
        [((8, padded), i32), ((2 * faces, padded), i32), ((count, LANES), i32), ((8, bnd), i32), ((8, bnd), i32),
         ((POWERS, messages * LANES), f32), ((LEVELS, LANES), f32), own, weight, traced,
         ((POWERS * rows, 3 * rows), bf16), (((POWERS + 1) * trace_rows, 3 * rows), bf16),
         (((POWERS + 1) * trace_rows, 3 * trace_rows), bf16), ((rows, 3 * faces * trace_rows), bf16), ((rows, 3 * trace_rows), bf16), ((1, LANES), f32)]
        + [prepared_message] * messages, [face_stack])
    advanced = []
    for level in range(LEVELS - 1):
        moved, extra, extra_trace, *sent = call(
            functools.partial(level_kernel, level, messages, count), "level", 10 ** 8,
            [flags, joined, weights, slot_weights, mix, lift, trace_grow, send_places, send_codes] + received + prepared,
            [slots, own, traced] + [message] * messages)
        arrived, received = received, exchange(sent)
        beside = functools.partial(between_kernel, level + 1, messages)
        operands = [members, joined, places, columns, out, new_trace, moved, extra, extra_trace, heights, loaded,
                    weights, lift, lift_first, grow, trace_grow, send_places] + arrived
        scratch = [face_stack, traced, own]
        if level + 1 < LEVELS - 1:
            out, loaded, weights, new_trace, *rest = call(
                beside, "between", 2 * 10 ** 9, operands + sent + advanced,
                [table, own, weight, traced, whole] + [prepared_message] * messages, scratch)
            advanced, prepared = rest[:1], rest[1:]
        else:
            loaded, weights, *advanced = call(
                beside, "between", 2 * 10 ** 9, operands + advanced, [own, weight, whole], [table] + scratch)
    final, = call(
        functools.partial(last_kernel, LEVELS - 1, messages), "last", 10 ** 9,
        [flags, joined, loaded, weights, lift, lift_first, grow, places] + advanced + received,
        [(flat, f32)], [(flat, f32), pltpu.SemaphoreType.DMA((len(last_chunks(rows)),))], out_hbm=True)
    return final.reshape(1, 1, comp, elements)


def solution(mesh):
    in_specs = (
        P("sector", "radial", None, None),
        P("sector", "radial", None),
        P("sector", "radial", None),
        P("sector", "radial", None),
        P("sector", "radial", None, None),
        P("sector", "radial", None, None),
        P(),
        P(),
        P(),
        P(),
    )
    out_specs = P("sector", "radial", None, None)
    return jax.shard_map(body, mesh=mesh, in_specs=in_specs, out_specs=out_specs, check_vma=False)
```

```python
import functools
import math

import jax
import jax.numpy as jnp
from jax import lax
from jax.experimental import pallas as pl
from jax.experimental.pallas import tpu as pltpu
from jax.sharding import PartitionSpec as P

LEVELS = 4
SUBSTEPS = 2
TERMS = 4
BLOCK = 384
LANES = 128
NO_GROUP = 1 << 20
ARGUMENTS = 10
ROW_CHUNK = 48

f32, bf16, i32 = jnp.float32, jnp.bfloat16, jnp.int32
precise = lax.Precision.HIGHEST


def rounded_up(size, unit):
    return -(-size // unit) * unit


def taylor_weights():
    once = [1.0 / math.factorial(k) for k in range(TERMS + 1)]
    whole = [1.0]
    for _ in range(SUBSTEPS):
        longer = [0.0] * (len(whole) + TERMS)
        for i, a in enumerate(whole):
            for j, b in enumerate(once):
                longer[i + j] += a * b
        whole = longer
    return whole


WEIGHTS = taylor_weights()
POWERS = len(WEIGHTS) - 1


def split(values):
    high = values.astype(bf16)
    return high, (values - high.astype(f32)).astype(bf16)


def whole_lanes(size):
    return size // LANES * LANES


def stacked_columns(values):
    high, low = split(values)
    main = whole_lanes(values.shape[0])
    parts = [high[:main], low[:main], high[:main], high[main:], low[main:], high[main:]]
    return jnp.concatenate([part for part in parts if part.shape[0]], axis=0)


def stacked_matrix(values):
    high = values.astype(bf16).astype(f32)
    low = values - high
    main = whole_lanes(values.shape[1])
    parts = [high[:, :main], high[:, :main], low[:, :main], high[:, main:], high[:, main:], low[:, main:]]
    return jnp.concatenate([part for part in parts if part.shape[1]], axis=1).astype(bf16)


def product(matrix, columns):
    return jnp.dot(matrix, columns, preferred_element_type=f32)


def pad_rows(values, rows):
    short = rows - values.shape[0]
    if short == 0:
        return values
    return jnp.concatenate([values, jnp.zeros((short,) + values.shape[1:], values.dtype)], axis=0)


def exact_product(left, right):
    left_high, left_low = split(left)
    right_high, right_low = split(right)
    rows = left.shape[0]
    both = product(jnp.concatenate([left_high, left_low], axis=0), right_high)
    return both[:rows] + both[rows:] + product(left_high, right_low)


def pick(blocks, index, which, start=None):
    result = start
    for number, read in blocks:
        table = read()
        lane = jnp.broadcast_to(index & (LANES - 1), table.shape)
        got = jnp.take_along_axis(table, lane, axis=1, mode="promise_in_bounds")
        if result is None:
            result = got
        else:
            result = jnp.where(jnp.broadcast_to(which, table.shape) == number, got, result)
    return result


def block_at(block):
    return slice(block * LANES, (block + 1) * LANES)


def ref_blocks(ref, count):
    return [(b, functools.partial(lambda b: ref[:, block_at(b)], b)) for b in range(count)]


def value_blocks(values):
    return [(b, functools.partial(lambda b: values[:, block_at(b)], b)) for b in range(values.shape[1] // LANES)]


def row_blocks(table, rows):
    return [
        (b, functools.partial(lambda b: jnp.broadcast_to(table[b:b + 1, :], (rows, LANES)), b))
        for b in range(table.shape[0])
    ]


def row_blocks_of(row, rows):
    return [
        (b, functools.partial(lambda b: jnp.broadcast_to(row[:, block_at(b)], (rows, LANES)), b))
        for b in range(row.shape[1] // LANES)
    ]


def summed_powers(stacked, weights_ref, rows, total):
    for power in range(1, POWERS + 1):
        total = total + stacked[(power - 1) * rows:power * rows] * weights_ref[power - 1:power, :]
    return total


def sent_rows(send_ref, swaps):
    rows = []
    for axis, _, low, high, _ in swaps:
        odd, even = send_ref[high:high + 1, :], send_ref[low:low + 1, :]
        rows.append(jnp.where(is_odd(axis), odd, even))
    return rows


def first_kernel(swaps, *refs):
    (fields_hbm, *given), refs = refs[:ARGUMENTS], refs[ARGUMENTS:]
    (columns_ref, out_ref), refs = refs[:2], refs[2:]
    sends, refs = refs[:len(swaps)], refs[len(swaps):]
    *held, fields_ref, arrived = refs
    rows = out_ref.shape[0]
    elements = out_ref.shape[1]
    count = elements // LANES
    comp = fields_ref.shape[0] // count
    cuts = [slice(0, rounded_up(comp // 2, 16)), slice(rounded_up(comp // 2, 16), comp)]
    parts = [pl.ds(cut.start * count, (cut.stop - cut.start) * count) for cut in cuts]
    trace_hbm, send_hbm, *others = given
    trace_ref, send_ref, *others_held = held
    pairs = [(fields_hbm.at[parts[0]], fields_ref.at[parts[0]]), (trace_hbm, trace_ref),
             (fields_hbm.at[parts[1]], fields_ref.at[parts[1]]), (send_hbm, send_ref)]
    pairs += list(zip(others, others_held))
    copies = [pltpu.make_async_copy(source, target, arrived.at[i]) for i, (source, target) in enumerate(pairs)]
    for copy in copies:
        copy.start()
    total = None
    for number, cut in enumerate(cuts):
        if number == 0:
            copies[0].wait()
            copies[1].wait()
            trace = pad_rows(trace_ref[...], rows)
        else:
            copies[2].wait()
        height = cut.stop - cut.start
        fields = jnp.concatenate(
            [fields_ref[pl.ds(cut.start * count + b, height, stride=count), :] for b in range(count)], axis=1)
        trace_high, trace_low = split(trace[:, cut])
        high, low = split(fields)
        upper = product(jnp.concatenate([trace_high, trace_low], axis=0), high)
        part = upper[:rows] + upper[rows:] + product(trace_high, low)
        total = part if total is None else total + part
        columns_ref[cut, :] = fields
    out_ref[...] = total
    copies[3].wait()
    for index, send in zip(sent_rows(send_ref, swaps), sends):
        send[...] = pick(ref_blocks(out_ref, count), index, index >> 7)[:send.shape[0]]
    columns_ref[comp:, :] = jnp.zeros((columns_ref.shape[0] - comp, elements), f32)
    for copy in copies[4:]:
        copy.wait()


def faces_in(joined_ref):
    return joined_ref.shape[0] // 2


def own_block(level, block, members_ref, joined_ref, columns_ref, heights_ref, own_ref, weights_ref):
    faces = faces_in(joined_ref)
    here, there = block_at(block), block_at(level * (BLOCK // LANES) + block)
    index = members_ref[0:1, there]
    own_ref[:, here] = pick(ref_blocks(columns_ref, columns_ref.shape[1] // LANES), index, index >> 7)
    pattern = jnp.broadcast_to(joined_ref[faces:faces + 1, there], (8, LANES))
    height = jnp.take_along_axis(
        jnp.broadcast_to(heights_ref[...], (8, LANES)), pattern, axis=1, mode="promise_in_bounds")
    weight = jnp.ones((8, LANES), f32)
    for power in range(1, POWERS + 1):
        weight = weight * height
        weights_ref[power - 1:power, here] = weight[0:1] * WEIGHTS[power]


def face_block(level, block, joined_ref, out_ref, faces_ref):
    trace_rows = out_ref.shape[0]
    here, there = block_at(block), block_at(level * (BLOCK // LANES) + block)
    for face in range(faces_in(joined_ref)):
        index = joined_ref[face:face + 1, there]
        faces_ref[face * trace_rows:(face + 1) * trace_rows, here] = pick(
            ref_blocks(out_ref, out_ref.shape[1] // LANES), index, index >> 7, jnp.zeros((trace_rows, LANES), f32))


def advanced_traces(loaded, matrix_ref, weights_ref, rows):
    stacked = product(matrix_ref[...], stacked_columns(loaded))
    return summed_powers(stacked[rows:], weights_ref, rows, stacked[:rows])


def local_messages(level, trace_ref, send_places_ref, sent, messages):
    for group, (before, message) in enumerate(zip(sent, messages)):
        index = send_places_ref[group:group + 1, :]
        which = (index >> 7) - level * (BLOCK // LANES)
        message[...] = pick(
            ref_blocks(trace_ref, BLOCK // LANES), index, which, pad_rows(before[...], message.shape[0]))


def row_chunks(rows):
    return [slice(low, low + ROW_CHUNK) for low in range(0, rows, ROW_CHUNK)]


def grown_rows(chunk, stacked, loaded, grow_ref, weights_ref):
    rows = loaded.shape[0]
    matrix = jnp.concatenate(
        [grow_ref[power * rows + chunk.start:power * rows + chunk.stop, :] for power in range(POWERS)], axis=0)
    return summed_powers(product(matrix, stacked), weights_ref, chunk.stop - chunk.start, loaded[chunk])


def matrix_powers(operator_ref, trace_ref, lift_ref, grow_ref, trace_grow_ref, mix_ref, lift_out_ref,
                  lift_first_ref):
    comp = operator_ref.shape[0]
    trace_comp, faces, _ = lift_ref.shape
    rows = lift_out_ref.shape[0]
    trace_rows = trace_grow_ref.shape[0] // (POWERS + 1)
    operator = pad_rows(operator_ref[...], rows)
    operator = jnp.concatenate([operator, jnp.zeros((rows, rows - comp), f32)], axis=1)
    traces = pad_rows(trace_ref[...], trace_rows)
    traces = jnp.concatenate([traces, jnp.zeros((trace_rows, rows - comp), f32)], axis=1)
    lift = jnp.concatenate([pad_rows(lift_ref[:, face, :], trace_rows) for face in range(faces)], axis=0)
    lift = pad_rows(jnp.transpose(lift), rows)
    lift_out_ref[...] = stacked_matrix(lift)
    lift_first_ref[...] = stacked_matrix(lift[:, :trace_rows])
    powers, have = operator, 1
    while have < POWERS:
        more = exact_product(jnp.concatenate([traces, powers], axis=0), powers[(have - 1) * rows:have * rows])
        traces = jnp.concatenate([traces, more[:have * trace_rows]], axis=0)
        powers = jnp.concatenate([powers, more[have * trace_rows:]], axis=0)
        have *= 2
        yield
    traces = jnp.concatenate([traces, exact_product(traces[:trace_rows], powers[-rows:])], axis=0)
    trace_grow_ref[...] = stacked_matrix(traces)
    yield
    mix_ref[...] = stacked_matrix(exact_product(traces, lift[:, :trace_rows]))
    grow_ref[...] = stacked_matrix(powers)
    yield


def plan_kernel(swaps, *refs):
    (trace_ref, send_ref, order_ref, pattern_ref, sizes_ref, neighbours_ref, operator_ref, lift_ref, heights_ref,
     columns_ref, out_ref), refs = refs[:11], refs[11:]
    messages = len(swaps)
    sent, refs = refs[:messages], refs[messages:]
    (members_ref, joined_ref, places_ref, send_places_ref, send_codes_ref, slot_weights_ref, flags_ref, loaded_ref,
     weights_ref, new_trace_ref, grow_ref, trace_grow_ref, mix_ref, lift_out_ref, lift_first_ref,
     wide_heights_ref), refs = refs[:16], refs[16:]
    prepared, (faces_ref,) = refs[:messages], refs[messages:]
    elements = columns_ref.shape[1]
    count = elements // LANES
    faces = neighbours_ref.shape[0]
    steps = matrix_powers(operator_ref, trace_ref, lift_ref, grow_ref, trace_grow_ref, mix_ref, lift_out_ref,
                          lift_first_ref)
    next(steps)
    sizes = sizes_ref[...].astype(f32)
    number = lax.broadcasted_iota(i32, sizes.shape, 1)
    starts = [jnp.sum(jnp.where(number < level, sizes, 0.0)).astype(i32) for level in range(LEVELS)]
    wide_order = jnp.broadcast_to(order_ref[...], (8, elements))
    neighbours = neighbours_ref[...]
    group = (neighbours >> 7) - count
    message = jnp.full(neighbours.shape, count + len(swaps), i32)
    for number, swap in enumerate(swaps):
        message = jnp.where(group == came_group(swap), count + number, message)
    neighbours = jnp.where(group >= 0, message * LANES + (neighbours & (LANES - 1)), neighbours)
    table = jnp.concatenate(
        [neighbours, pattern_ref[...], jnp.zeros((faces - 1, elements), i32)], axis=0)
    heights = heights_ref[...]
    wide_heights_ref[...] = jnp.concatenate(
        [heights, jnp.zeros((1, LANES - heights.shape[1]), f32)], axis=1)
    for level in range(LEVELS):
        shift = jnp.where(starts[level] == 0, 0, elements - starts[level])
        members_ref[:, level * BLOCK:(level + 1) * BLOCK] = pltpu.roll(wide_order, shift, 1)[:, :BLOCK]
    for block in range(LEVELS * BLOCK // LANES):
        index = members_ref[:, block_at(block)]
        joined_ref[:, block_at(block)] = pick(value_blocks(table), index, index >> 7)
    ranks = lax.broadcasted_iota(i32, (count, elements), 1)
    in_block = (wide_order[:count] >> 7) == lax.broadcasted_iota(i32, (count, elements), 0)
    left = jnp.concatenate([
        jnp.where(in_block, ranks >> 5, 0).astype(f32), jnp.where(in_block, ranks & 31, 0).astype(f32)], axis=0)
    at_lane = jnp.broadcast_to(order_ref[...] & (LANES - 1), (LANES, elements)) == lax.broadcasted_iota(
        i32, (LANES, elements), 0)
    rank = lax.dot_general(left.astype(bf16), jnp.where(at_lane, 1.0, 0.0).astype(bf16), (((1,), (1,)), ((), ())),
                           preferred_element_type=f32)
    place = rank[:count].astype(i32) * 32 + rank[count:].astype(i32)
    at = place
    for level in range(1, LEVELS):
        at = jnp.where(place >= starts[level], place - starts[level] + level * BLOCK, at)
    places_ref[...] = at
    index = pad_rows(jnp.concatenate(sent_rows(send_ref, swaps), axis=0), 8)
    send_places_ref[...] = pick(row_blocks(at, 8), index, index >> 7)
    send_codes_ref[...] = pick(row_blocks_of(neighbours[:1], 8), index, index >> 7)
    block = jnp.broadcast_to(neighbours[:1] >> 7, (8, elements)) - count
    named = jnp.where(block == lax.broadcasted_iota(i32, (8, elements), 0),
                      jnp.broadcast_to(pattern_ref[...], (8, elements)), 0).astype(f32).astype(bf16)
    slot_lane = jnp.broadcast_to(neighbours[:1] & (LANES - 1), (LANES, elements)) == lax.broadcasted_iota(
        i32, (LANES, elements), 0)
    slot_pattern = lax.dot_general(named, jnp.where(slot_lane, 1.0, 0.0).astype(bf16), (((1,), (1,)), ((), ())),
                                   preferred_element_type=f32).astype(i32)
    height = jnp.take_along_axis(jnp.broadcast_to(wide_heights_ref[...], (8, LANES)), slot_pattern & (LANES - 1),
                                 axis=1, mode="promise_in_bounds")
    weight = jnp.ones((8, LANES), f32)
    for power in range(1, POWERS + 1):
        weight = weight * height
        for number in range(messages):
            slot_weights_ref[power - 1:power, block_at(number)] = weight[number:number + 1] * WEIGHTS[power]
    for level in range(LEVELS):
        code = joined_ref[1:faces, level * BLOCK:(level + 1) * BLOCK]
        code = jnp.max(jnp.where(code >= elements, 1.0, 0.0), axis=0, keepdims=True)
        row = code[:, block_at(0)]
        for number in range(1, BLOCK // LANES):
            row = jnp.maximum(row, code[:, block_at(number)])
        flags_ref[level:level + 1, :] = row
    next(steps)
    for block in range(BLOCK // LANES):
        own_block(0, block, members_ref, joined_ref, columns_ref, wide_heights_ref, loaded_ref, weights_ref)
        face_block(0, block, joined_ref, out_ref, faces_ref)
        next(steps)
    loaded = loaded_ref[...] + product(lift_out_ref[...], stacked_columns(faces_ref[...]))
    loaded_ref[...] = loaded
    new_trace_ref[...] = advanced_traces(loaded, trace_grow_ref, weights_ref, out_ref.shape[0])
    local_messages(0, new_trace_ref, send_places_ref, sent, prepared)


def settle(level, blocks, places_ref, before, block):
    index = places_ref[block:block + 1, :]
    which = (index >> 7) - level * (BLOCK // LANES)
    return pick(blocks, index, which, before)


def received_blocks(received, count, rows):
    return [(count + i, functools.partial(lambda ref: pad_rows(ref[...], rows), ref)) for i, ref in enumerate(received)]


def received_traces(level, face, received, joined_ref, count):
    parts = []
    for block in range(BLOCK // LANES):
        index = joined_ref[face:face + 1, block_at(level * (BLOCK // LANES) + block)]
        rows = rounded_up(received[0].shape[0], 16)
        zeros = jnp.zeros((rows, LANES), f32)
        parts.append(pick(received_blocks(received, count, rows), index, index >> 7, zeros))
    return jnp.concatenate(parts, axis=1)


def gather_received(level, low, received, joined_ref, count, traces_ref):
    faces = faces_in(joined_ref)
    rows = traces_ref.shape[0] // faces
    if low:
        traces_ref[:low * rows, :] = jnp.zeros((low * rows, traces_ref.shape[1]), f32)

    def step(face, carry):
        for block in range(BLOCK // LANES):
            there = block_at(level * (BLOCK // LANES) + block)
            index = joined_ref[low:low + 1, there]
            for other in range(low + 1, faces):
                index = jnp.where(face == other, joined_ref[other:other + 1, there], index)
            traces_ref[pl.ds(pl.multiple_of(face * rows, rows), rows), block_at(block)] = pick(
                received_blocks(received, count, rows), index, index >> 7, jnp.zeros((rows, LANES), f32))
        return carry

    lax.fori_loop(low, faces, step, 0)


def for_blocks(body):
    def step(block, carry):
        body(pl.ds(pl.multiple_of(block * LANES, LANES), LANES))
        return carry

    lax.fori_loop(0, BLOCK // LANES, step, 0)


def any_other(level, flags_ref):
    return jnp.max(flags_ref[level:level + 1, :]) > 0.0


def between_kernel(level, messages, members_ref, joined_ref, places_ref, columns_ref, old_out_ref, old_trace_ref,
                   moved_ref, extra_ref, extra_trace_ref, heights_ref, local_ref, old_weights_ref, lift_ref,
                   lift_first_ref, grow_ref, trace_grow_ref, send_places_ref, *rest):
    received, rest = rest[:messages], rest[messages:]
    final = level == LEVELS - 1
    if not final:
        sent, rest = rest[:messages], rest[messages:]
    if level > 1:
        advanced_ref, rest = rest[0], rest[1:]
    if final:
        loaded_ref, weights_ref, new_advanced_ref, out_ref, faces_ref, trace_ref, whole_ref = rest
    else:
        out_ref, loaded_ref, weights_ref, new_trace_ref, new_advanced_ref = rest[:5]
        prepared, (faces_ref, trace_ref, whole_ref) = rest[5:5 + messages], rest[5 + messages:]
    count = places_ref.shape[0]
    done = level - 1
    first = received_traces(done, 0, received, joined_ref, count)
    inflow = product(lift_first_ref[...], stacked_columns(first))
    for block in range(BLOCK // LANES):
        here = block_at(block)
        index = joined_ref[0:1, block_at(done * (BLOCK // LANES) + block)]
        moved = [(count + i, read) for i, read in ref_blocks(moved_ref, messages)]
        trace_ref[:, here] = old_trace_ref[:, here] + extra_trace_ref[:, here] + pick(
            moved, index, index >> 7, jnp.zeros((old_trace_ref.shape[0], LANES), f32))
    whole = local_ref[...] + inflow + extra_ref[...]
    stacked = stacked_columns(whole)
    chunks = row_chunks(whole.shape[0])
    pieces = BLOCK // LANES

    def gather_own(part):
        for block in range(part * pieces // len(chunks), (part + 1) * pieces // len(chunks)):
            own_block(level, block, members_ref, joined_ref, columns_ref, heights_ref, loaded_ref, weights_ref)

    def gather_faces(part):
        for block in range(part * pieces // len(chunks), (part + 1) * pieces // len(chunks)):
            face_block(level, block, joined_ref, out_ref, faces_ref)

    def put_out(part):
        for block in range(part * count // len(chunks), (part + 1) * count // len(chunks)):
            here = block_at(block)
            out_ref[:, here] = settle(
                done, ref_blocks(trace_ref, pieces), places_ref, old_out_ref[:, here], block)

    def put_columns(chunk):
        for block in range(count):
            here = block_at(block)
            before = advanced_ref[chunk, here] if level > 1 else None
            new_advanced_ref[chunk, here] = settle(
                done, [(b, functools.partial(lambda b: whole_ref[chunk, block_at(b)], b)) for b in range(pieces)],
                places_ref, before, block)

    for part in range(len(chunks)):
        put_out(part)
    for part, chunk in enumerate(chunks):
        whole_ref[chunk, :] = grown_rows(chunk, stacked, whole, grow_ref, old_weights_ref)
        gather_own(part)
        gather_faces(part)
    loaded = loaded_ref[...] + product(lift_ref[...], stacked_columns(faces_ref[...]))
    put_columns(chunks[0])
    loaded_ref[...] = loaded
    if not final:
        traces = advanced_traces(loaded, trace_grow_ref, weights_ref, out_ref.shape[0])
    for chunk in chunks[1:]:
        put_columns(chunk)
    if not final:
        new_trace_ref[...] = traces
        local_messages(level, new_trace_ref, send_places_ref, sent, prepared)


def level_kernel(level, messages, count, flags_ref, joined_ref, weights_ref, slot_weights_ref, mix_ref, lift_ref,
                 trace_grow_ref, send_places_ref, send_codes_ref, *rest):
    received, rest = rest[:messages], rest[messages:]
    prepared, rest = rest[:messages], rest[messages:]
    moved_ref, extra_ref, extra_trace_ref, sends = rest[0], rest[1], rest[2], rest[3:3 + messages]
    traces_ref, = rest[3 + messages:]
    rows = moved_ref.shape[0]
    pieces = BLOCK // LANES
    other = any_other(level, flags_ref)
    arrived = jnp.concatenate([pad_rows(ref[...], rows) for ref in received], axis=1)
    stacked = product(mix_ref[...], stacked_columns(arrived))
    moved_ref[...] = summed_powers(stacked[rows:], slot_weights_ref, rows, stacked[:rows])
    extra_ref[...] = jnp.zeros(extra_ref.shape, f32)
    extra_trace_ref[...] = jnp.zeros(extra_trace_ref.shape, f32)
    moved = [(count + i, read) for i, read in ref_blocks(moved_ref, messages)]
    for group, (before, send) in enumerate(zip(prepared, sends)):
        place, code = send_places_ref[group:group + 1, :], send_codes_ref[group:group + 1, :]
        here = ((place >> 7) >= level * pieces) & ((place >> 7) < (level + 1) * pieces)
        total = before[...] + pick(moved, code, jnp.where(here, code >> 7, 0), jnp.zeros(before.shape, f32))
        send[...] = total[:send.shape[0]]

    @pl.when(other)
    def _():
        gather_received(level, 1, received, joined_ref, count, traces_ref)

        def add_block(here):
            extra = product(lift_ref[...], stacked_columns(traces_ref[:, here]))
            extra_ref[:, here] = extra
            extra_trace_ref[:, here] = advanced_traces(extra, trace_grow_ref, weights_ref[:, here], rows)

        for_blocks(add_block)
        for group, send in enumerate(sends):
            place = send_places_ref[group:group + 1, :]
            more = pick(
                ref_blocks(extra_trace_ref, pieces), place, (place >> 7) - level * pieces, jnp.zeros((rows, LANES), f32))
            send[...] = send[...] + more[:send.shape[0]]


def last_chunks(rows):
    units = rows // 16
    first = -(-units * 4 // 9)
    second = -(-(units - first) * 3 // 5)
    bounds = [0, first * 16, (first + second) * 16, rows]
    return [slice(low, high) for low, high in zip(bounds, bounds[1:]) if high > low]


def last_kernel(level, messages, flags_ref, joined_ref, local_ref, weights_ref, lift_ref, lift_first_ref, grow_ref,
                places_ref, advanced_ref, *rest):
    received, (final_hbm, final_ref, traces_ref, whole_ref, sent) = rest[:messages], rest[messages:]
    count = places_ref.shape[0]
    comp = final_hbm.shape[0] // count

    def finish(whole):
        stacked = stacked_columns(whole)
        copies = []

        def put(number, chunk, new):
            height = min(chunk.stop, comp) - chunk.start
            for block in range(count):
                done = settle(level, value_blocks(new), places_ref, advanced_ref[chunk, block_at(block)], block)
                final_ref[pl.ds(chunk.start * count + block, height, stride=count), :] = done[:height]
            part = pl.ds(chunk.start * count, height * count)
            copies.append(pltpu.make_async_copy(final_ref.at[part], final_hbm.at[part], sent.at[number]))
            copies[-1].start()

        ahead = None
        for number, chunk in enumerate(last_chunks(whole.shape[0])):
            new = grown_rows(chunk, stacked, whole, grow_ref, weights_ref)
            if ahead is not None:
                put(*ahead)
            ahead = (number, chunk, new)
        put(*ahead)
        for copy in copies:
            copy.wait()

    other = any_other(level, flags_ref)
    first = received_traces(level, 0, received, joined_ref, count)
    finish(local_ref[...] + product(lift_first_ref[...], stacked_columns(first)))

    @pl.when(other)
    def _():
        gather_received(level, 0, received, joined_ref, count, traces_ref)

        def load_block(here):
            whole_ref[:, here] = local_ref[:, here] + product(lift_ref[...], stacked_columns(traces_ref[:, here]))

        for_blocks(load_block)
        rows, height = whole_ref.shape[0], 16

        def step(number, carry):
            start = pl.multiple_of(number * height, height)
            matrix = jnp.concatenate(
                [grow_ref[pl.ds(power * rows + start, height), :] for power in range(POWERS)], axis=0)
            new = summed_powers(product(matrix, stacked_columns(whole_ref[...])), weights_ref, height,
                                whole_ref[pl.ds(start, height), :])
            for block in range(count):
                before = advanced_ref[pl.ds(start, height), block_at(block)]
                done = settle(level, value_blocks(new), places_ref, before, block)
                final_ref[pl.ds(start * count + block, height, stride=count), :] = done
            return carry

        lax.fori_loop(0, rows // height, step, 0)
        copy = pltpu.make_async_copy(final_ref.at[pl.ds(0, comp * count)], final_hbm, sent.at[0])
        copy.start()
        copy.wait()


def call(kernel, name, flops, operands, outs, scratch=(), hbm=False, out_hbm=False):
    vmem = pl.BlockSpec(memory_space=pltpu.VMEM)
    given = pl.BlockSpec(memory_space=pltpu.HBM) if hbm else vmem
    if hbm:
        operands = [pltpu.with_memory_space_constraint(one, pltpu.HBM) for one in operands]
    return pl.pallas_call(
        kernel,
        out_shape=tuple(jax.ShapeDtypeStruct(shape, dtype) for shape, dtype in outs),
        in_specs=[given] * len(operands),
        out_specs=tuple([pl.BlockSpec(memory_space=pltpu.HBM) if out_hbm else vmem] * len(outs)),
        scratch_shapes=[one if not isinstance(one, tuple) else pltpu.VMEM(*one) for one in scratch],
        compiler_params=pltpu.CompilerParams(vmem_limit_bytes=16 * 1024 * 1024),
        cost_estimate=pl.CostEstimate(flops=flops, bytes_accessed=1 << 20, transcendentals=0),
        name=name,
    )(*operands)


def is_odd(axis):
    return (lax.axis_index(axis) & 1) == 1


def swap_plan(axis, periodic, low, high):
    count = lax.axis_size(axis)
    plan = [(axis, [(i, i ^ 1) for i in range(count)], low, high, False)]
    if count > 2 or periodic:
        pairs = [(i, (i + 1) % count if i % 2 else (i - 1) % count) for i in range(count)]
        plan.append((axis, pairs, high, low, not periodic))
    return plan


def came_group(swap):
    axis, _, even, odd, is_open = swap
    came = jnp.where(is_odd(axis), even, odd)
    if is_open:
        index = lax.axis_index(axis)
        came = jnp.where((index == 0) | (index == lax.axis_size(axis) - 1), NO_GROUP, came)
    return came


def body(fields, pattern, tent_order, level_sizes, send_rows, neighbours, operator, trace_map, lift_map, tent_height):
    fields, order, sizes = fields[0, 0], tent_order[0], level_sizes[0]
    faces_of, send_list = neighbours[0, 0], send_rows[0, 0]
    comp, elements = fields.shape
    faces, trace = lift_map.shape[0], trace_map.shape[0]
    rows, trace_rows = rounded_up(comp, 16), rounded_up(trace, 16)
    padded, count = LEVELS * BLOCK, elements // LANES
    bnd = send_list.shape[-1]

    near, *far = swap_plan("sector", True, 0, 1)
    swaps = far + [near] + swap_plan("radial", False, 2, 3)
    messages = len(swaps)

    def exchange(sent):
        return [lax.ppermute(one, swap[0], swap[1]) for one, swap in zip(sent, swaps)]

    message, prepared_message = ((trace, bnd), f32), ((trace_rows, bnd), f32)
    own, face_stack = ((rows, BLOCK), f32), ((faces * trace_rows, BLOCK), f32)
    weight, table, traced = ((POWERS, BLOCK), f32), ((trace_rows, elements), f32), ((trace_rows, BLOCK), f32)
    whole = ((rows, elements), f32)
    flat = (comp * count, LANES)

    arguments = [trace_map, send_list, order, pattern[0], sizes, faces_of, operator,
                 jnp.transpose(lift_map, (2, 0, 1)), tent_height[None]]
    columns, out, *rest = call(
        functools.partial(first_kernel, swaps), "first", 10 ** 8, [fields.reshape(flat)] + arguments,
        [whole, table] + [message] * messages + [(one.shape, one.dtype) for one in arguments],
        [(flat, f32), pltpu.SemaphoreType.DMA((ARGUMENTS + 1,))], hbm=True)
    sent, held = rest[:messages], rest[messages:]
    received = exchange(sent)
    slots = ((trace_rows, messages * LANES), f32)
    (members, joined, places, send_places, send_codes, slot_weights, flags, loaded, weights, new_trace, grow,
     trace_grow, mix, lift, lift_first, heights, *prepared) = call(
        functools.partial(plan_kernel, swaps), "plan", 2 * 10 ** 9, held + [columns, out] + sent,
        [((8, padded), i32), ((2 * faces, padded), i32), ((count, LANES), i32), ((8, bnd), i32), ((8, bnd), i32),
         ((POWERS, messages * LANES), f32), ((LEVELS, LANES), f32), own, weight, traced,
         ((POWERS * rows, 3 * rows), bf16), (((POWERS + 1) * trace_rows, 3 * rows), bf16),
         (((POWERS + 1) * trace_rows, 3 * trace_rows), bf16), ((rows, 3 * faces * trace_rows), bf16), ((rows, 3 * trace_rows), bf16), ((1, LANES), f32)]
        + [prepared_message] * messages, [face_stack])
    advanced = []
    for level in range(LEVELS - 1):
        moved, extra, extra_trace, *sent = call(
            functools.partial(level_kernel, level, messages, count), "level", 10 ** 8,
            [flags, joined, weights, slot_weights, mix, lift, trace_grow, send_places, send_codes] + received + prepared,
            [slots, own, traced] + [message] * messages, [face_stack])
        arrived, received = received, exchange(sent)
        beside = functools.partial(between_kernel, level + 1, messages)
        operands = [members, joined, places, columns, out, new_trace, moved, extra, extra_trace, heights, loaded,
                    weights, lift, lift_first, grow, trace_grow, send_places] + arrived
        scratch = [face_stack, traced, own]
        if level + 1 < LEVELS - 1:
            out, loaded, weights, new_trace, *rest = call(
                beside, "between", 2 * 10 ** 9, operands + sent + advanced,
                [table, own, weight, traced, whole] + [prepared_message] * messages, scratch)
            advanced, prepared = rest[:1], rest[1:]
        else:
            loaded, weights, *advanced = call(
                beside, "between", 2 * 10 ** 9, operands + advanced, [own, weight, whole], [table] + scratch)
    final, = call(
        functools.partial(last_kernel, LEVELS - 1, messages), "last", 10 ** 9,
        [flags, joined, loaded, weights, lift, lift_first, grow, places] + advanced + received,
        [(flat, f32)],
        [((rows * count, LANES), f32), face_stack, own, pltpu.SemaphoreType.DMA((len(last_chunks(rows)),))], out_hbm=True)
    return final.reshape(1, 1, comp, elements)


def solution(mesh):
    in_specs = (
        P("sector", "radial", None, None),
        P("sector", "radial", None),
        P("sector", "radial", None),
        P("sector", "radial", None),
        P("sector", "radial", None, None),
        P("sector", "radial", None, None),
        P(),
        P(),
        P(),
        P(),
    )
    out_specs = P("sector", "radial", None, None)
    return jax.shard_map(body, mesh=mesh, in_specs=in_specs, out_specs=out_specs, check_vma=False)
```

```python
import functools
import math

import jax
import jax.numpy as jnp
from jax import lax
from jax.experimental import pallas as pl
from jax.experimental.pallas import tpu as pltpu
from jax.sharding import PartitionSpec as P

LEVELS = 4
SUBSTEPS = 2
TERMS = 4
BLOCK = 384
LANES = 128
NO_GROUP = 1 << 20
ARGUMENTS = 10
ROW_CHUNK = 48

f32, bf16, i32 = jnp.float32, jnp.bfloat16, jnp.int32
precise = lax.Precision.HIGHEST


def rounded_up(size, unit):
    return -(-size // unit) * unit


def taylor_weights():
    once = [1.0 / math.factorial(k) for k in range(TERMS + 1)]
    whole = [1.0]
    for _ in range(SUBSTEPS):
        longer = [0.0] * (len(whole) + TERMS)
        for i, a in enumerate(whole):
            for j, b in enumerate(once):
                longer[i + j] += a * b
        whole = longer
    return whole


WEIGHTS = taylor_weights()
POWERS = len(WEIGHTS) - 1


def split(values):
    high = values.astype(bf16)
    return high, (values - high.astype(f32)).astype(bf16)


def whole_lanes(size):
    return size // LANES * LANES


def stacked_columns(values):
    high, low = split(values)
    main = whole_lanes(values.shape[0])
    parts = [high[:main], low[:main], high[:main], high[main:], low[main:], high[main:]]
    return jnp.concatenate([part for part in parts if part.shape[0]], axis=0)


def stacked_matrix(values):
    high = values.astype(bf16).astype(f32)
    low = values - high
    main = whole_lanes(values.shape[1])
    parts = [high[:, :main], high[:, :main], low[:, :main], high[:, main:], high[:, main:], low[:, main:]]
    return jnp.concatenate([part for part in parts if part.shape[1]], axis=1).astype(bf16)


def product(matrix, columns):
    return jnp.dot(matrix, columns, preferred_element_type=f32)


def pad_rows(values, rows):
    short = rows - values.shape[0]
    if short == 0:
        return values
    return jnp.concatenate([values, jnp.zeros((short,) + values.shape[1:], values.dtype)], axis=0)


def exact_product(left, right):
    left_high, left_low = split(left)
    right_high, right_low = split(right)
    rows = left.shape[0]
    both = product(jnp.concatenate([left_high, left_low], axis=0), right_high)
    return both[:rows] + both[rows:] + product(left_high, right_low)


def pick(blocks, index, which, start=None):
    result = start
    for number, read in blocks:
        table = read()
        lane = jnp.broadcast_to(index & (LANES - 1), table.shape)
        got = jnp.take_along_axis(table, lane, axis=1, mode="promise_in_bounds")
        if result is None:
            result = got
        else:
            result = jnp.where(jnp.broadcast_to(which, table.shape) == number, got, result)
    return result


def block_at(block):
    return slice(block * LANES, (block + 1) * LANES)


def ref_blocks(ref, count):
    return [(b, functools.partial(lambda b: ref[:, block_at(b)], b)) for b in range(count)]


def value_blocks(values):
    return [(b, functools.partial(lambda b: values[:, block_at(b)], b)) for b in range(values.shape[1] // LANES)]


def row_blocks(table, rows):
    return [
        (b, functools.partial(lambda b: jnp.broadcast_to(table[b:b + 1, :], (rows, LANES)), b))
        for b in range(table.shape[0])
    ]


def row_blocks_of(row, rows):
    return [
        (b, functools.partial(lambda b: jnp.broadcast_to(row[:, block_at(b)], (rows, LANES)), b))
        for b in range(row.shape[1] // LANES)
    ]


def summed_powers(stacked, weights_ref, rows, total):
    for power in range(1, POWERS + 1):
        total = total + stacked[(power - 1) * rows:power * rows] * weights_ref[power - 1:power, :]
    return total


def sent_rows(send_ref, swaps):
    rows = []
    for axis, _, low, high, _ in swaps:
        odd, even = send_ref[high:high + 1, :], send_ref[low:low + 1, :]
        rows.append(jnp.where(is_odd(axis), odd, even))
    return rows


def first_kernel(swaps, *refs):
    (fields_hbm, *given), refs = refs[:ARGUMENTS], refs[ARGUMENTS:]
    (columns_ref, out_ref), refs = refs[:2], refs[2:]
    sends, refs = refs[:len(swaps)], refs[len(swaps):]
    *held, fields_ref, arrived = refs
    rows = out_ref.shape[0]
    elements = out_ref.shape[1]
    count = elements // LANES
    comp = fields_hbm.shape[0] // count
    cuts = [slice(0, rounded_up(comp // 2, 16)), slice(rounded_up(comp // 2, 16), comp)]
    parts = [pl.ds(cut.start * count, (cut.stop - cut.start) * count) for cut in cuts]
    trace_hbm, send_hbm, *others = given
    trace_ref, send_ref, *others_held = held
    pairs = [(fields_hbm.at[parts[0]], fields_ref.at[parts[0]]), (trace_hbm, trace_ref),
             (fields_hbm.at[parts[1]], fields_ref.at[parts[1]]), (send_hbm, send_ref)]
    pairs += [(source, target if source.shape == target.shape else target.at[pl.ds(0, source.shape[0])])
              for source, target in zip(others, others_held)]
    copies = [pltpu.make_async_copy(source, target, arrived.at[i]) for i, (source, target) in enumerate(pairs)]
    for copy in copies:
        copy.start()
    total = None
    for number, cut in enumerate(cuts):
        if number == 0:
            copies[0].wait()
            copies[1].wait()
            trace = pad_rows(trace_ref[...], rows)
        else:
            copies[2].wait()
        height = cut.stop - cut.start
        fields = jnp.concatenate(
            [fields_ref[pl.ds(cut.start * count + b, height, stride=count), :] for b in range(count)], axis=1)
        trace_high, trace_low = split(trace[:, cut])
        high, low = split(fields)
        upper = product(jnp.concatenate([trace_high, trace_low], axis=0), high)
        part = upper[:rows] + upper[rows:] + product(trace_high, low)
        total = part if total is None else total + part
        columns_ref[cut, :] = fields
    out_ref[...] = total
    copies[3].wait()
    for index, send in zip(sent_rows(send_ref, swaps), sends):
        send[...] = pick(ref_blocks(out_ref, count), index, index >> 7)[:send.shape[0]]
    columns_ref[comp:, :] = jnp.zeros((columns_ref.shape[0] - comp, elements), f32)
    for copy in copies[4:]:
        copy.wait()


def faces_in(joined_ref):
    return joined_ref.shape[0] // 2


def own_block(level, block, members_ref, joined_ref, columns_ref, heights_ref, own_ref, weights_ref):
    faces = faces_in(joined_ref)
    here, there = block_at(block), block_at(level * (BLOCK // LANES) + block)
    index = members_ref[0:1, there]
    own_ref[:, here] = pick(ref_blocks(columns_ref, columns_ref.shape[1] // LANES), index, index >> 7)
    pattern = jnp.broadcast_to(joined_ref[faces:faces + 1, there], (8, LANES))
    height = jnp.take_along_axis(
        jnp.broadcast_to(heights_ref[...], (8, LANES)), pattern, axis=1, mode="promise_in_bounds")
    weight = jnp.ones((8, LANES), f32)
    for power in range(1, POWERS + 1):
        weight = weight * height
        weights_ref[power - 1:power, here] = weight[0:1] * WEIGHTS[power]


def face_block(level, block, joined_ref, out_ref, faces_ref):
    trace_rows = out_ref.shape[0]
    here, there = block_at(block), block_at(level * (BLOCK // LANES) + block)
    for face in range(faces_in(joined_ref)):
        index = joined_ref[face:face + 1, there]
        faces_ref[face * trace_rows:(face + 1) * trace_rows, here] = pick(
            ref_blocks(out_ref, out_ref.shape[1] // LANES), index, index >> 7, jnp.zeros((trace_rows, LANES), f32))


def advanced_traces(loaded, matrix_ref, weights_ref, rows):
    stacked = product(matrix_ref[...], stacked_columns(loaded))
    return summed_powers(stacked[rows:], weights_ref, rows, stacked[:rows])


def local_messages(level, trace_ref, send_places_ref, sent, messages):
    for group, (before, message) in enumerate(zip(sent, messages)):
        index = send_places_ref[group:group + 1, :]
        which = (index >> 7) - level * (BLOCK // LANES)
        message[...] = pick(
            ref_blocks(trace_ref, BLOCK // LANES), index, which, pad_rows(before[...], message.shape[0]))


def row_chunks(rows):
    return [slice(low, low + ROW_CHUNK) for low in range(0, rows, ROW_CHUNK)]


def grown_rows(chunk, stacked, loaded, grow_ref, weights_ref):
    rows = loaded.shape[0]
    matrix = jnp.concatenate(
        [grow_ref[power * rows + chunk.start:power * rows + chunk.stop, :] for power in range(POWERS)], axis=0)
    return summed_powers(product(matrix, stacked), weights_ref, chunk.stop - chunk.start, loaded[chunk])


def matrix_powers(operator_ref, trace_ref, lift_ref, grow_ref, trace_grow_ref, mix_ref, lift_out_ref,
                  lift_first_ref):
    comp = operator_ref.shape[0]
    faces = lift_ref.shape[1]
    trace_comp = trace_ref.shape[0]
    rows = lift_out_ref.shape[0]
    trace_rows = trace_grow_ref.shape[0] // (POWERS + 1)
    operator = pad_rows(operator_ref[...], rows)
    operator = jnp.concatenate([operator, jnp.zeros((rows, rows - comp), f32)], axis=1)
    traces = pad_rows(trace_ref[...], trace_rows)
    traces = jnp.concatenate([traces, jnp.zeros((trace_rows, rows - comp), f32)], axis=1)
    filled = lax.broadcasted_iota(i32, (trace_rows, comp), 0) < trace_comp
    lift = jnp.concatenate([jnp.where(filled, lift_ref[:, face, :], 0.0) for face in range(faces)], axis=0)
    lift = pad_rows(jnp.transpose(lift), rows)
    lift_out_ref[...] = stacked_matrix(lift)
    lift_first_ref[...] = stacked_matrix(lift[:, :trace_rows])
    powers, have = operator, 1
    while have < POWERS:
        more = exact_product(jnp.concatenate([traces, powers], axis=0), powers[(have - 1) * rows:have * rows])
        traces = jnp.concatenate([traces, more[:have * trace_rows]], axis=0)
        powers = jnp.concatenate([powers, more[have * trace_rows:]], axis=0)
        have *= 2
        yield
    traces = jnp.concatenate([traces, exact_product(traces[:trace_rows], powers[-rows:])], axis=0)
    trace_grow_ref[...] = stacked_matrix(traces)
    yield
    mix_ref[...] = stacked_matrix(exact_product(traces, lift[:, :trace_rows]))
    grow_ref[...] = stacked_matrix(powers)
    yield


def plan_kernel(swaps, *refs):
    (trace_ref, send_ref, order_ref, pattern_ref, sizes_ref, neighbours_ref, operator_ref, lift_ref, heights_ref,
     columns_ref, out_ref), refs = refs[:11], refs[11:]
    messages = len(swaps)
    sent, refs = refs[:messages], refs[messages:]
    (members_ref, joined_ref, places_ref, send_places_ref, send_codes_ref, slot_weights_ref, flags_ref, loaded_ref,
     weights_ref, new_trace_ref, grow_ref, trace_grow_ref, mix_ref, lift_out_ref, lift_first_ref,
     wide_heights_ref), refs = refs[:16], refs[16:]
    prepared, (faces_ref,) = refs[:messages], refs[messages:]
    elements = columns_ref.shape[1]
    count = elements // LANES
    faces = neighbours_ref.shape[0]
    steps = matrix_powers(operator_ref, trace_ref, lift_ref, grow_ref, trace_grow_ref, mix_ref, lift_out_ref,
                          lift_first_ref)
    next(steps)
    sizes = sizes_ref[...].astype(f32)
    number = lax.broadcasted_iota(i32, sizes.shape, 1)
    starts = [jnp.sum(jnp.where(number < level, sizes, 0.0)).astype(i32) for level in range(LEVELS)]
    wide_order = jnp.broadcast_to(order_ref[...], (8, elements))
    neighbours = neighbours_ref[...]
    group = (neighbours >> 7) - count
    message = jnp.full(neighbours.shape, count + len(swaps), i32)
    for number, swap in enumerate(swaps):
        message = jnp.where(group == came_group(swap), count + number, message)
    neighbours = jnp.where(group >= 0, message * LANES + (neighbours & (LANES - 1)), neighbours)
    table = jnp.concatenate(
        [neighbours, pattern_ref[...], jnp.zeros((faces - 1, elements), i32)], axis=0)
    heights = heights_ref[...]
    wide_heights_ref[...] = jnp.concatenate(
        [heights, jnp.zeros((1, LANES - heights.shape[1]), f32)], axis=1)
    for level in range(LEVELS):
        shift = jnp.where(starts[level] == 0, 0, elements - starts[level])
        members_ref[:, level * BLOCK:(level + 1) * BLOCK] = pltpu.roll(wide_order, shift, 1)[:, :BLOCK]
    for block in range(LEVELS * BLOCK // LANES):
        index = members_ref[:, block_at(block)]
        joined_ref[:, block_at(block)] = pick(value_blocks(table), index, index >> 7)
    ranks = lax.broadcasted_iota(i32, (count, elements), 1)
    in_block = (wide_order[:count] >> 7) == lax.broadcasted_iota(i32, (count, elements), 0)
    left = jnp.concatenate([
        jnp.where(in_block, ranks >> 5, 0).astype(f32), jnp.where(in_block, ranks & 31, 0).astype(f32)], axis=0)
    at_lane = jnp.broadcast_to(order_ref[...] & (LANES - 1), (LANES, elements)) == lax.broadcasted_iota(
        i32, (LANES, elements), 0)
    rank = lax.dot_general(left.astype(bf16), jnp.where(at_lane, 1.0, 0.0).astype(bf16), (((1,), (1,)), ((), ())),
                           preferred_element_type=f32)
    place = rank[:count].astype(i32) * 32 + rank[count:].astype(i32)
    at = place
    for level in range(1, LEVELS):
        at = jnp.where(place >= starts[level], place - starts[level] + level * BLOCK, at)
    places_ref[...] = at
    index = pad_rows(jnp.concatenate(sent_rows(send_ref, swaps), axis=0), 8)
    send_places_ref[...] = pick(row_blocks(at, 8), index, index >> 7)
    send_codes_ref[...] = pick(row_blocks_of(neighbours[:1], 8), index, index >> 7)
    block = jnp.broadcast_to(neighbours[:1] >> 7, (8, elements)) - count
    named = jnp.where(block == lax.broadcasted_iota(i32, (8, elements), 0),
                      jnp.broadcast_to(pattern_ref[...], (8, elements)), 0).astype(f32).astype(bf16)
    slot_lane = jnp.broadcast_to(neighbours[:1] & (LANES - 1), (LANES, elements)) == lax.broadcasted_iota(
        i32, (LANES, elements), 0)
    slot_pattern = lax.dot_general(named, jnp.where(slot_lane, 1.0, 0.0).astype(bf16), (((1,), (1,)), ((), ())),
                                   preferred_element_type=f32).astype(i32)
    height = jnp.take_along_axis(jnp.broadcast_to(wide_heights_ref[...], (8, LANES)), slot_pattern & (LANES - 1),
                                 axis=1, mode="promise_in_bounds")
    weight = jnp.ones((8, LANES), f32)
    for power in range(1, POWERS + 1):
        weight = weight * height
        for number in range(messages):
            slot_weights_ref[power - 1:power, block_at(number)] = weight[number:number + 1] * WEIGHTS[power]
    for level in range(LEVELS):
        code = joined_ref[1:faces, level * BLOCK:(level + 1) * BLOCK]
        code = jnp.max(jnp.where(code >= elements, 1.0, 0.0), axis=0, keepdims=True)
        row = code[:, block_at(0)]
        for number in range(1, BLOCK // LANES):
            row = jnp.maximum(row, code[:, block_at(number)])
        flags_ref[level:level + 1, :] = row
    next(steps)
    for block in range(BLOCK // LANES):
        own_block(0, block, members_ref, joined_ref, columns_ref, wide_heights_ref, loaded_ref, weights_ref)
        face_block(0, block, joined_ref, out_ref, faces_ref)
        next(steps)
    loaded = loaded_ref[...] + product(lift_out_ref[...], stacked_columns(faces_ref[...]))
    loaded_ref[...] = loaded
    new_trace_ref[...] = advanced_traces(loaded, trace_grow_ref, weights_ref, out_ref.shape[0])
    local_messages(0, new_trace_ref, send_places_ref, sent, prepared)


def settle(level, blocks, places_ref, before, block):
    index = places_ref[block:block + 1, :]
    which = (index >> 7) - level * (BLOCK // LANES)
    return pick(blocks, index, which, before)


def received_blocks(received, count, rows):
    return [(count + i, functools.partial(lambda ref: pad_rows(ref[...], rows), ref)) for i, ref in enumerate(received)]


def received_traces(level, face, received, joined_ref, count):
    parts = []
    for block in range(BLOCK // LANES):
        index = joined_ref[face:face + 1, block_at(level * (BLOCK // LANES) + block)]
        rows = rounded_up(received[0].shape[0], 16)
        zeros = jnp.zeros((rows, LANES), f32)
        parts.append(pick(received_blocks(received, count, rows), index, index >> 7, zeros))
    return jnp.concatenate(parts, axis=1)


def gather_received(level, low, received, joined_ref, count, traces_ref):
    faces = faces_in(joined_ref)
    rows = traces_ref.shape[0] // faces
    if low:
        traces_ref[:low * rows, :] = jnp.zeros((low * rows, traces_ref.shape[1]), f32)

    def step(face, carry):
        for block in range(BLOCK // LANES):
            there = block_at(level * (BLOCK // LANES) + block)
            index = joined_ref[low:low + 1, there]
            for other in range(low + 1, faces):
                index = jnp.where(face == other, joined_ref[other:other + 1, there], index)
            traces_ref[pl.ds(pl.multiple_of(face * rows, rows), rows), block_at(block)] = pick(
                received_blocks(received, count, rows), index, index >> 7, jnp.zeros((rows, LANES), f32))
        return carry

    lax.fori_loop(low, faces, step, 0)


def for_blocks(body):
    def step(block, carry):
        body(pl.ds(pl.multiple_of(block * LANES, LANES), LANES))
        return carry

    lax.fori_loop(0, BLOCK // LANES, step, 0)


def any_other(level, flags_ref):
    return jnp.max(flags_ref[level:level + 1, :]) > 0.0


def between_kernel(level, messages, members_ref, joined_ref, places_ref, columns_ref, old_out_ref, old_trace_ref,
                   moved_ref, extra_ref, extra_trace_ref, heights_ref, local_ref, old_weights_ref, lift_ref,
                   lift_first_ref, grow_ref, trace_grow_ref, send_places_ref, *rest):
    received, rest = rest[:messages], rest[messages:]
    final = level == LEVELS - 1
    if not final:
        sent, rest = rest[:messages], rest[messages:]
    if level > 1:
        advanced_ref, rest = rest[0], rest[1:]
    if final:
        loaded_ref, weights_ref, new_advanced_ref, out_ref, faces_ref, trace_ref, whole_ref = rest
    else:
        out_ref, loaded_ref, weights_ref, new_trace_ref, new_advanced_ref = rest[:5]
        prepared, (faces_ref, trace_ref, whole_ref) = rest[5:5 + messages], rest[5 + messages:]
    count = places_ref.shape[0]
    done = level - 1
    first = received_traces(done, 0, received, joined_ref, count)
    inflow = product(lift_first_ref[...], stacked_columns(first))
    for block in range(BLOCK // LANES):
        here = block_at(block)
        index = joined_ref[0:1, block_at(done * (BLOCK // LANES) + block)]
        moved = [(count + i, read) for i, read in ref_blocks(moved_ref, messages)]
        trace_ref[:, here] = old_trace_ref[:, here] + extra_trace_ref[:, here] + pick(
            moved, index, index >> 7, jnp.zeros((old_trace_ref.shape[0], LANES), f32))
    whole = local_ref[...] + inflow + extra_ref[...]
    stacked = stacked_columns(whole)
    chunks = row_chunks(whole.shape[0])
    pieces = BLOCK // LANES

    def gather_own(part):
        for block in range(part * pieces // len(chunks), (part + 1) * pieces // len(chunks)):
            own_block(level, block, members_ref, joined_ref, columns_ref, heights_ref, loaded_ref, weights_ref)

    def gather_faces(part):
        for block in range(part * pieces // len(chunks), (part + 1) * pieces // len(chunks)):
            face_block(level, block, joined_ref, out_ref, faces_ref)

    def put_out(part):
        for block in range(part * count // len(chunks), (part + 1) * count // len(chunks)):
            here = block_at(block)
            out_ref[:, here] = settle(
                done, ref_blocks(trace_ref, pieces), places_ref, old_out_ref[:, here], block)

    def put_columns(chunk):
        for block in range(count):
            here = block_at(block)
            before = advanced_ref[chunk, here] if level > 1 else None
            new_advanced_ref[chunk, here] = settle(
                done, [(b, functools.partial(lambda b: whole_ref[chunk, block_at(b)], b)) for b in range(pieces)],
                places_ref, before, block)

    for part in range(len(chunks)):
        put_out(part)
    for part, chunk in enumerate(chunks):
        whole_ref[chunk, :] = grown_rows(chunk, stacked, whole, grow_ref, old_weights_ref)
        gather_own(part)
        gather_faces(part)
    loaded = loaded_ref[...] + product(lift_ref[...], stacked_columns(faces_ref[...]))
    put_columns(chunks[0])
    loaded_ref[...] = loaded
    if not final:
        traces = advanced_traces(loaded, trace_grow_ref, weights_ref, out_ref.shape[0])
    for chunk in chunks[1:]:
        put_columns(chunk)
    if not final:
        new_trace_ref[...] = traces
        local_messages(level, new_trace_ref, send_places_ref, sent, prepared)


def level_kernel(level, messages, count, flags_ref, joined_ref, weights_ref, slot_weights_ref, mix_ref, lift_ref,
                 trace_grow_ref, send_places_ref, send_codes_ref, *rest):
    received, rest = rest[:messages], rest[messages:]
    prepared, rest = rest[:messages], rest[messages:]
    moved_ref, extra_ref, extra_trace_ref, sends = rest[0], rest[1], rest[2], rest[3:3 + messages]
    traces_ref, = rest[3 + messages:]
    rows = moved_ref.shape[0]
    pieces = BLOCK // LANES
    other = any_other(level, flags_ref)
    arrived = jnp.concatenate([pad_rows(ref[...], rows) for ref in received], axis=1)
    stacked = product(mix_ref[...], stacked_columns(arrived))
    moved_ref[...] = summed_powers(stacked[rows:], slot_weights_ref, rows, stacked[:rows])
    extra_ref[...] = jnp.zeros(extra_ref.shape, f32)
    extra_trace_ref[...] = jnp.zeros(extra_trace_ref.shape, f32)
    moved = [(count + i, read) for i, read in ref_blocks(moved_ref, messages)]
    for group, (before, send) in enumerate(zip(prepared, sends)):
        place, code = send_places_ref[group:group + 1, :], send_codes_ref[group:group + 1, :]
        here = ((place >> 7) >= level * pieces) & ((place >> 7) < (level + 1) * pieces)
        total = before[...] + pick(moved, code, jnp.where(here, code >> 7, 0), jnp.zeros(before.shape, f32))
        send[...] = total[:send.shape[0]]

    @pl.when(other)
    def _():
        gather_received(level, 1, received, joined_ref, count, traces_ref)

        def add_block(here):
            extra = product(lift_ref[...], stacked_columns(traces_ref[:, here]))
            extra_ref[:, here] = extra
            extra_trace_ref[:, here] = advanced_traces(extra, trace_grow_ref, weights_ref[:, here], rows)

        for_blocks(add_block)
        for group, send in enumerate(sends):
            place = send_places_ref[group:group + 1, :]
            more = pick(
                ref_blocks(extra_trace_ref, pieces), place, (place >> 7) - level * pieces, jnp.zeros((rows, LANES), f32))
            send[...] = send[...] + more[:send.shape[0]]


def last_chunks(rows):
    units = rows // 16
    first = -(-units * 4 // 9)
    second = -(-(units - first) * 3 // 5)
    bounds = [0, first * 16, (first + second) * 16, rows]
    return [slice(low, high) for low, high in zip(bounds, bounds[1:]) if high > low]


def last_kernel(level, messages, flags_ref, joined_ref, local_ref, weights_ref, lift_ref, lift_first_ref, grow_ref,
                places_ref, advanced_ref, *rest):
    received, (final_hbm, final_ref, traces_ref, whole_ref, sent) = rest[:messages], rest[messages:]
    count = places_ref.shape[0]
    comp = final_hbm.shape[0] // count

    def finish(whole):
        stacked = stacked_columns(whole)
        copies = []

        def put(number, chunk, new):
            height = min(chunk.stop, comp) - chunk.start
            for block in range(count):
                done = settle(level, value_blocks(new), places_ref, advanced_ref[chunk, block_at(block)], block)
                final_ref[pl.ds(chunk.start * count + block, height, stride=count), :] = done[:height]
            part = pl.ds(chunk.start * count, height * count)
            copies.append(pltpu.make_async_copy(final_ref.at[part], final_hbm.at[part], sent.at[number]))
            copies[-1].start()

        ahead = None
        for number, chunk in enumerate(last_chunks(whole.shape[0])):
            new = grown_rows(chunk, stacked, whole, grow_ref, weights_ref)
            if ahead is not None:
                put(*ahead)
            ahead = (number, chunk, new)
        put(*ahead)
        for copy in copies:
            copy.wait()

    other = any_other(level, flags_ref)
    first = received_traces(level, 0, received, joined_ref, count)
    finish(local_ref[...] + product(lift_first_ref[...], stacked_columns(first)))

    @pl.when(other)
    def _():
        gather_received(level, 0, received, joined_ref, count, traces_ref)

        def load_block(here):
            whole_ref[:, here] = local_ref[:, here] + product(lift_ref[...], stacked_columns(traces_ref[:, here]))

        for_blocks(load_block)
        rows, height = whole_ref.shape[0], 16

        def step(number, carry):
            start = pl.multiple_of(number * height, height)
            matrix = jnp.concatenate(
                [grow_ref[pl.ds(power * rows + start, height), :] for power in range(POWERS)], axis=0)
            new = summed_powers(product(matrix, stacked_columns(whole_ref[...])), weights_ref, height,
                                whole_ref[pl.ds(start, height), :])
            for block in range(count):
                before = advanced_ref[pl.ds(start, height), block_at(block)]
                done = settle(level, value_blocks(new), places_ref, before, block)
                final_ref[pl.ds(start * count + block, height, stride=count), :] = done
            return carry

        lax.fori_loop(0, rows // height, step, 0)
        copy = pltpu.make_async_copy(final_ref.at[pl.ds(0, comp * count)], final_hbm, sent.at[0])
        copy.start()
        copy.wait()


def call(kernel, name, flops, operands, outs, scratch=(), hbm=False, out_hbm=False):
    vmem = pl.BlockSpec(memory_space=pltpu.VMEM)
    given = pl.BlockSpec(memory_space=pltpu.HBM) if hbm else vmem
    if hbm:
        operands = [pltpu.with_memory_space_constraint(one, pltpu.HBM) for one in operands]
    return pl.pallas_call(
        kernel,
        out_shape=tuple(jax.ShapeDtypeStruct(shape, dtype) for shape, dtype in outs),
        in_specs=[given] * len(operands),
        out_specs=tuple([pl.BlockSpec(memory_space=pltpu.HBM) if out_hbm else vmem] * len(outs)),
        scratch_shapes=[one if not isinstance(one, tuple) else pltpu.VMEM(*one) for one in scratch],
        compiler_params=pltpu.CompilerParams(vmem_limit_bytes=16 * 1024 * 1024),
        cost_estimate=pl.CostEstimate(flops=flops, bytes_accessed=1 << 20, transcendentals=0),
        name=name,
    )(*operands)


def is_odd(axis):
    return (lax.axis_index(axis) & 1) == 1


def swap_plan(axis, periodic, low, high):
    count = lax.axis_size(axis)
    plan = [(axis, [(i, i ^ 1) for i in range(count)], low, high, False)]
    if count > 2 or periodic:
        pairs = [(i, (i + 1) % count if i % 2 else (i - 1) % count) for i in range(count)]
        plan.append((axis, pairs, high, low, not periodic))
    return plan


def came_group(swap):
    axis, _, even, odd, is_open = swap
    came = jnp.where(is_odd(axis), even, odd)
    if is_open:
        index = lax.axis_index(axis)
        came = jnp.where((index == 0) | (index == lax.axis_size(axis) - 1), NO_GROUP, came)
    return came


def body(fields, pattern, tent_order, level_sizes, send_rows, neighbours, operator, trace_map, lift_map, tent_height):
    fields, order, sizes = fields[0, 0], tent_order[0], level_sizes[0]
    faces_of, send_list = neighbours[0, 0], send_rows[0, 0]
    comp, elements = fields.shape
    faces, trace = lift_map.shape[0], trace_map.shape[0]
    rows, trace_rows = rounded_up(comp, 16), rounded_up(trace, 16)
    padded, count = LEVELS * BLOCK, elements // LANES
    bnd = send_list.shape[-1]

    near, *far = swap_plan("sector", True, 0, 1)
    swaps = far + [near] + swap_plan("radial", False, 2, 3)
    messages = len(swaps)

    def exchange(sent):
        return [lax.ppermute(one, swap[0], swap[1]) for one, swap in zip(sent, swaps)]

    message = ((trace_rows, bnd), f32)
    own, face_stack = ((rows, BLOCK), f32), ((faces * trace_rows, BLOCK), f32)
    weight, table, traced = ((POWERS, BLOCK), f32), ((trace_rows, elements), f32), ((trace_rows, BLOCK), f32)
    whole = ((rows, elements), f32)
    flat = (comp * count, LANES)

    arguments = [trace_map, send_list, order, pattern[0], sizes, faces_of, operator,
                 jnp.transpose(lift_map, (2, 0, 1)), tent_height[None]]
    columns, out, *rest = call(
        functools.partial(first_kernel, swaps), "first", 10 ** 8, [fields.reshape(flat)] + arguments,
        [whole, table] + [message] * messages
        + [((trace_rows,) + one.shape[1:] if one.ndim == 3 else one.shape, one.dtype) for one in arguments],
        [((rows * count, LANES), f32), pltpu.SemaphoreType.DMA((ARGUMENTS + 1,))], hbm=True)
    sent, held = rest[:messages], rest[messages:]
    received = exchange(sent)
    slots = ((trace_rows, messages * LANES), f32)
    (members, joined, places, send_places, send_codes, slot_weights, flags, loaded, weights, new_trace, grow,
     trace_grow, mix, lift, lift_first, heights, *prepared) = call(
        functools.partial(plan_kernel, swaps), "plan", 2 * 10 ** 9, held + [columns, out] + sent,
        [((8, padded), i32), ((2 * faces, padded), i32), ((count, LANES), i32), ((8, bnd), i32), ((8, bnd), i32),
         ((POWERS, messages * LANES), f32), ((LEVELS, LANES), f32), own, weight, traced,
         ((POWERS * rows, 3 * rows), bf16), (((POWERS + 1) * trace_rows, 3 * rows), bf16),
         (((POWERS + 1) * trace_rows, 3 * trace_rows), bf16), ((rows, 3 * faces * trace_rows), bf16), ((rows, 3 * trace_rows), bf16), ((1, LANES), f32)]
        + [message] * messages, [face_stack])
    advanced = []
    for level in range(LEVELS - 1):
        moved, extra, extra_trace, *sent = call(
            functools.partial(level_kernel, level, messages, count), "level", 10 ** 8,
            [flags, joined, weights, slot_weights, mix, lift, trace_grow, send_places, send_codes] + received + prepared,
            [slots, own, traced] + [message] * messages, [face_stack])
        arrived, received = received, exchange(sent)
        beside = functools.partial(between_kernel, level + 1, messages)
        operands = [members, joined, places, columns, out, new_trace, moved, extra, extra_trace, heights, loaded,
                    weights, lift, lift_first, grow, trace_grow, send_places] + arrived
        scratch = [face_stack, traced, own]
        if level + 1 < LEVELS - 1:
            out, loaded, weights, new_trace, *rest = call(
                beside, "between", 2 * 10 ** 9, operands + sent + advanced,
                [table, own, weight, traced, whole] + [message] * messages, scratch)
            advanced, prepared = rest[:1], rest[1:]
        else:
            loaded, weights, *advanced = call(
                beside, "between", 2 * 10 ** 9, operands + advanced, [own, weight, whole], [table] + scratch)
    final, = call(
        functools.partial(last_kernel, LEVELS - 1, messages), "last", 10 ** 9,
        [flags, joined, loaded, weights, lift, lift_first, grow, places] + advanced + received,
        [(flat, f32)],
        [((rows * count, LANES), f32), face_stack, own, pltpu.SemaphoreType.DMA((len(last_chunks(rows)),))], out_hbm=True)
    return final.reshape(1, 1, comp, elements)


def solution(mesh):
    in_specs = (
        P("sector", "radial", None, None),
        P("sector", "radial", None),
        P("sector", "radial", None),
        P("sector", "radial", None),
        P("sector", "radial", None, None),
        P("sector", "radial", None, None),
        P(),
        P(),
        P(),
        P(),
    )
    out_specs = P("sector", "radial", None, None)
    return jax.shard_map(body, mesh=mesh, in_specs=in_specs, out_specs=out_specs, check_vma=False)
```

```python
import functools
import math

import jax
import jax.numpy as jnp
from jax import lax
from jax.experimental import pallas as pl
from jax.experimental.pallas import tpu as pltpu
from jax.sharding import PartitionSpec as P

LEVELS = 4
SUBSTEPS = 2
TERMS = 4
BLOCK = 384
LANES = 128
NO_GROUP = 1 << 20
ARGUMENTS = 10
ROW_CHUNK = 48

f32, bf16, i32 = jnp.float32, jnp.bfloat16, jnp.int32
precise = lax.Precision.HIGHEST


def rounded_up(size, unit):
    return -(-size // unit) * unit


def taylor_weights():
    once = [1.0 / math.factorial(k) for k in range(TERMS + 1)]
    whole = [1.0]
    for _ in range(SUBSTEPS):
        longer = [0.0] * (len(whole) + TERMS)
        for i, a in enumerate(whole):
            for j, b in enumerate(once):
                longer[i + j] += a * b
        whole = longer
    return whole


WEIGHTS = taylor_weights()
POWERS = len(WEIGHTS) - 1


def split(values):
    high = values.astype(bf16)
    return high, (values - high.astype(f32)).astype(bf16)


def whole_lanes(size):
    return size // LANES * LANES


def stacked_columns(values):
    high, low = split(values)
    main = whole_lanes(values.shape[0])
    parts = [high[:main], low[:main], high[:main], high[main:], low[main:], high[main:]]
    return jnp.concatenate([part for part in parts if part.shape[0]], axis=0)


def stacked_matrix(values):
    high = values.astype(bf16).astype(f32)
    low = values - high
    main = whole_lanes(values.shape[1])
    parts = [high[:, :main], high[:, :main], low[:, :main], high[:, main:], high[:, main:], low[:, main:]]
    return jnp.concatenate([part for part in parts if part.shape[1]], axis=1).astype(bf16)


def product(matrix, columns):
    return jnp.dot(matrix, columns, preferred_element_type=f32)


def pad_rows(values, rows):
    short = rows - values.shape[0]
    if short == 0:
        return values
    return jnp.concatenate([values, jnp.zeros((short,) + values.shape[1:], values.dtype)], axis=0)


def exact_product(left, right):
    left_high, left_low = split(left)
    right_high, right_low = split(right)
    rows = left.shape[0]
    both = product(jnp.concatenate([left_high, left_low], axis=0), right_high)
    return both[:rows] + both[rows:] + product(left_high, right_low)


def pick(blocks, index, which, start=None):
    result = start
    for number, read in blocks:
        table = read()
        lane = jnp.broadcast_to(index & (LANES - 1), table.shape)
        got = jnp.take_along_axis(table, lane, axis=1, mode="promise_in_bounds")
        if result is None:
            result = got
        else:
            result = jnp.where(jnp.broadcast_to(which, table.shape) == number, got, result)
    return result


def block_at(block):
    return slice(block * LANES, (block + 1) * LANES)


def ref_blocks(ref, count):
    return [(b, functools.partial(lambda b: ref[:, block_at(b)], b)) for b in range(count)]


def value_blocks(values):
    return [(b, functools.partial(lambda b: values[:, block_at(b)], b)) for b in range(values.shape[1] // LANES)]


def row_blocks(table, rows):
    return [
        (b, functools.partial(lambda b: jnp.broadcast_to(table[b:b + 1, :], (rows, LANES)), b))
        for b in range(table.shape[0])
    ]


def row_blocks_of(row, rows):
    return [
        (b, functools.partial(lambda b: jnp.broadcast_to(row[:, block_at(b)], (rows, LANES)), b))
        for b in range(row.shape[1] // LANES)
    ]


def summed_powers(stacked, weights_ref, rows, total):
    for power in range(1, POWERS + 1):
        total = total + stacked[(power - 1) * rows:power * rows] * weights_ref[power - 1:power, :]
    return total


def sent_rows(send_ref, swaps):
    rows = []
    for axis, _, low, high, _ in swaps:
        odd, even = send_ref[high:high + 1, :], send_ref[low:low + 1, :]
        rows.append(jnp.where(is_odd(axis), odd, even))
    return rows


def first_kernel(swaps, *refs):
    (fields_hbm, *given), refs = refs[:ARGUMENTS], refs[ARGUMENTS:]
    (columns_ref, out_ref), refs = refs[:2], refs[2:]
    sends, refs = refs[:len(swaps)], refs[len(swaps):]
    *held, fields_ref, arrived = refs
    rows = out_ref.shape[0]
    elements = out_ref.shape[1]
    count = elements // LANES
    comp = fields_hbm.shape[0] // count
    trace_hbm, send_hbm, *others = given
    trace_ref, send_ref, *others_held = held
    pairs = [(fields_hbm, fields_ref.at[pl.ds(0, comp * count)]), (trace_hbm, trace_ref), (send_hbm, send_ref)]
    needed = len(pairs)
    pairs += [(source, target if source.shape == target.shape else target.at[pl.ds(0, source.shape[0])])
              for source, target in zip(others, others_held)]
    copies = [pltpu.make_async_copy(source, target, arrived.at[i]) for i, (source, target) in enumerate(pairs)]
    for copy in copies:
        copy.start()
    for copy in copies[:needed]:
        copy.wait()
    trace_high, trace_low = split(pad_rows(trace_ref[...], rows))
    fields = jnp.concatenate([fields_ref[pl.ds(b, comp, stride=count), :] for b in range(count)], axis=1)
    high, low = split(fields)
    upper = product(jnp.concatenate([trace_high, trace_low], axis=0), high)
    out_ref[...] = upper[:rows] + upper[rows:] + product(trace_high, low)
    for index, send in zip(sent_rows(send_ref, swaps), sends):
        send[...] = pick(ref_blocks(out_ref, count), index, index >> 7)[:send.shape[0]]
    columns_ref[...] = pad_rows(fields, columns_ref.shape[0])
    for copy in copies[needed:]:
        copy.wait()


def faces_in(joined_ref):
    return joined_ref.shape[0] // 2


def own_block(level, block, members_ref, joined_ref, columns_ref, heights_ref, own_ref, weights_ref):
    faces = faces_in(joined_ref)
    here, there = block_at(block), block_at(level * (BLOCK // LANES) + block)
    index = members_ref[0:1, there]
    own_ref[:, here] = pick(ref_blocks(columns_ref, columns_ref.shape[1] // LANES), index, index >> 7)
    pattern = jnp.broadcast_to(joined_ref[faces:faces + 1, there], (8, LANES))
    height = jnp.take_along_axis(
        jnp.broadcast_to(heights_ref[...], (8, LANES)), pattern, axis=1, mode="promise_in_bounds")
    weight = jnp.ones((8, LANES), f32)
    for power in range(1, POWERS + 1):
        weight = weight * height
        weights_ref[power - 1:power, here] = weight[0:1] * WEIGHTS[power]


def face_block(level, block, joined_ref, out_ref, faces_ref):
    trace_rows = out_ref.shape[0]
    here, there = block_at(block), block_at(level * (BLOCK // LANES) + block)
    for face in range(faces_in(joined_ref)):
        index = joined_ref[face:face + 1, there]
        faces_ref[face * trace_rows:(face + 1) * trace_rows, here] = pick(
            ref_blocks(out_ref, out_ref.shape[1] // LANES), index, index >> 7, jnp.zeros((trace_rows, LANES), f32))


def advanced_traces(loaded, matrix_ref, weights_ref, rows):
    stacked = product(matrix_ref[...], stacked_columns(loaded))
    return summed_powers(stacked[rows:], weights_ref, rows, stacked[:rows])


def local_messages(level, trace_ref, send_places_ref, sent, messages):
    for group, (before, message) in enumerate(zip(sent, messages)):
        index = send_places_ref[group:group + 1, :]
        which = (index >> 7) - level * (BLOCK // LANES)
        message[...] = pick(
            ref_blocks(trace_ref, BLOCK // LANES), index, which, pad_rows(before[...], message.shape[0]))


def row_chunks(rows):
    return [slice(low, low + ROW_CHUNK) for low in range(0, rows, ROW_CHUNK)]


def grown_rows(chunk, stacked, loaded, grow_ref, weights_ref):
    rows = loaded.shape[0]
    matrix = jnp.concatenate(
        [grow_ref[power * rows + chunk.start:power * rows + chunk.stop, :] for power in range(POWERS)], axis=0)
    return summed_powers(product(matrix, stacked), weights_ref, chunk.stop - chunk.start, loaded[chunk])


def matrix_powers(operator_ref, trace_ref, lift_ref, grow_ref, trace_grow_ref, mix_ref, lift_out_ref,
                  lift_first_ref):
    comp = operator_ref.shape[0]
    faces = lift_ref.shape[1]
    trace_comp = trace_ref.shape[0]
    rows = lift_out_ref.shape[0]
    trace_rows = trace_grow_ref.shape[0] // (POWERS + 1)
    operator = pad_rows(operator_ref[...], rows)
    operator = jnp.concatenate([operator, jnp.zeros((rows, rows - comp), f32)], axis=1)
    traces = pad_rows(trace_ref[...], trace_rows)
    traces = jnp.concatenate([traces, jnp.zeros((trace_rows, rows - comp), f32)], axis=1)
    filled = lax.broadcasted_iota(i32, (trace_rows, comp), 0) < trace_comp
    lift = jnp.concatenate([jnp.where(filled, lift_ref[:, face, :], 0.0) for face in range(faces)], axis=0)
    lift = pad_rows(jnp.transpose(lift), rows)
    lift_out_ref[...] = stacked_matrix(lift)
    lift_first_ref[...] = stacked_matrix(lift[:, :trace_rows])
    powers, have = operator, 1
    while have < POWERS:
        more = exact_product(jnp.concatenate([traces, powers], axis=0), powers[(have - 1) * rows:have * rows])
        traces = jnp.concatenate([traces, more[:have * trace_rows]], axis=0)
        powers = jnp.concatenate([powers, more[have * trace_rows:]], axis=0)
        have *= 2
        yield
    traces = jnp.concatenate([traces, exact_product(traces[:trace_rows], powers[-rows:])], axis=0)
    trace_grow_ref[...] = stacked_matrix(traces)
    yield
    mix_ref[...] = stacked_matrix(exact_product(traces, lift[:, :trace_rows]))
    grow_ref[...] = stacked_matrix(powers)
    yield


def plan_kernel(swaps, *refs):
    (trace_ref, send_ref, order_ref, pattern_ref, sizes_ref, neighbours_ref, operator_ref, lift_ref, heights_ref,
     columns_ref, out_ref), refs = refs[:11], refs[11:]
    messages = len(swaps)
    sent, refs = refs[:messages], refs[messages:]
    (members_ref, joined_ref, places_ref, send_places_ref, send_codes_ref, slot_weights_ref, flags_ref, loaded_ref,
     weights_ref, new_trace_ref, grow_ref, trace_grow_ref, mix_ref, lift_out_ref, lift_first_ref,
     wide_heights_ref), refs = refs[:16], refs[16:]
    prepared, (faces_ref,) = refs[:messages], refs[messages:]
    elements = columns_ref.shape[1]
    count = elements // LANES
    faces = neighbours_ref.shape[0]
    steps = matrix_powers(operator_ref, trace_ref, lift_ref, grow_ref, trace_grow_ref, mix_ref, lift_out_ref,
                          lift_first_ref)
    next(steps)
    sizes = sizes_ref[...].astype(f32)
    number = lax.broadcasted_iota(i32, sizes.shape, 1)
    starts = [jnp.sum(jnp.where(number < level, sizes, 0.0)).astype(i32) for level in range(LEVELS)]
    wide_order = jnp.broadcast_to(order_ref[...], (8, elements))
    neighbours = neighbours_ref[...]
    group = (neighbours >> 7) - count
    message = jnp.full(neighbours.shape, count + len(swaps), i32)
    for number, swap in enumerate(swaps):
        message = jnp.where(group == came_group(swap), count + number, message)
    neighbours = jnp.where(group >= 0, message * LANES + (neighbours & (LANES - 1)), neighbours)
    table = jnp.concatenate(
        [neighbours, pattern_ref[...], jnp.zeros((faces - 1, elements), i32)], axis=0)
    heights = heights_ref[...]
    wide_heights_ref[...] = jnp.concatenate(
        [heights, jnp.zeros((1, LANES - heights.shape[1]), f32)], axis=1)
    for level in range(LEVELS):
        shift = jnp.where(starts[level] == 0, 0, elements - starts[level])
        members_ref[:, level * BLOCK:(level + 1) * BLOCK] = pltpu.roll(wide_order, shift, 1)[:, :BLOCK]
    for block in range(LEVELS * BLOCK // LANES):
        index = members_ref[:, block_at(block)]
        joined_ref[:, block_at(block)] = pick(value_blocks(table), index, index >> 7)
    ranks = lax.broadcasted_iota(i32, (count, elements), 1)
    in_block = (wide_order[:count] >> 7) == lax.broadcasted_iota(i32, (count, elements), 0)
    left = jnp.concatenate([
        jnp.where(in_block, ranks >> 5, 0).astype(f32), jnp.where(in_block, ranks & 31, 0).astype(f32)], axis=0)
    at_lane = jnp.broadcast_to(order_ref[...] & (LANES - 1), (LANES, elements)) == lax.broadcasted_iota(
        i32, (LANES, elements), 0)
    rank = lax.dot_general(left.astype(bf16), jnp.where(at_lane, 1.0, 0.0).astype(bf16), (((1,), (1,)), ((), ())),
                           preferred_element_type=f32)
    place = rank[:count].astype(i32) * 32 + rank[count:].astype(i32)
    at = place
    for level in range(1, LEVELS):
        at = jnp.where(place >= starts[level], place - starts[level] + level * BLOCK, at)
    places_ref[...] = at
    index = pad_rows(jnp.concatenate(sent_rows(send_ref, swaps), axis=0), 8)
    send_places_ref[...] = pick(row_blocks(at, 8), index, index >> 7)
    send_codes_ref[...] = pick(row_blocks_of(neighbours[:1], 8), index, index >> 7)
    block = jnp.broadcast_to(neighbours[:1] >> 7, (8, elements)) - count
    named = jnp.where(block == lax.broadcasted_iota(i32, (8, elements), 0),
                      jnp.broadcast_to(pattern_ref[...], (8, elements)), 0).astype(f32).astype(bf16)
    slot_lane = jnp.broadcast_to(neighbours[:1] & (LANES - 1), (LANES, elements)) == lax.broadcasted_iota(
        i32, (LANES, elements), 0)
    slot_pattern = lax.dot_general(named, jnp.where(slot_lane, 1.0, 0.0).astype(bf16), (((1,), (1,)), ((), ())),
                                   preferred_element_type=f32).astype(i32)
    height = jnp.take_along_axis(jnp.broadcast_to(wide_heights_ref[...], (8, LANES)), slot_pattern & (LANES - 1),
                                 axis=1, mode="promise_in_bounds")
    weight = jnp.ones((8, LANES), f32)
    for power in range(1, POWERS + 1):
        weight = weight * height
        for number in range(messages):
            slot_weights_ref[power - 1:power, block_at(number)] = weight[number:number + 1] * WEIGHTS[power]
    for level in range(LEVELS):
        code = joined_ref[1:faces, level * BLOCK:(level + 1) * BLOCK]
        code = jnp.max(jnp.where(code >= elements, 1.0, 0.0), axis=0, keepdims=True)
        row = code[:, block_at(0)]
        for number in range(1, BLOCK // LANES):
            row = jnp.maximum(row, code[:, block_at(number)])
        flags_ref[level:level + 1, :] = row
    next(steps)
    for block in range(BLOCK // LANES):
        own_block(0, block, members_ref, joined_ref, columns_ref, wide_heights_ref, loaded_ref, weights_ref)
        face_block(0, block, joined_ref, out_ref, faces_ref)
        next(steps)
    loaded = loaded_ref[...] + product(lift_out_ref[...], stacked_columns(faces_ref[...]))
    loaded_ref[...] = loaded
    new_trace_ref[...] = advanced_traces(loaded, trace_grow_ref, weights_ref, out_ref.shape[0])
    local_messages(0, new_trace_ref, send_places_ref, sent, prepared)


def settle(level, blocks, places_ref, before, block):
    index = places_ref[block:block + 1, :]
    which = (index >> 7) - level * (BLOCK // LANES)
    return pick(blocks, index, which, before)


def received_blocks(received, count, rows):
    return [(count + i, functools.partial(lambda ref: pad_rows(ref[...], rows), ref)) for i, ref in enumerate(received)]


def received_traces(level, face, received, joined_ref, count):
    parts = []
    for block in range(BLOCK // LANES):
        index = joined_ref[face:face + 1, block_at(level * (BLOCK // LANES) + block)]
        rows = rounded_up(received[0].shape[0], 16)
        zeros = jnp.zeros((rows, LANES), f32)
        parts.append(pick(received_blocks(received, count, rows), index, index >> 7, zeros))
    return jnp.concatenate(parts, axis=1)


def gather_received(level, low, received, joined_ref, count, traces_ref):
    faces = faces_in(joined_ref)
    rows = traces_ref.shape[0] // faces
    if low:
        traces_ref[:low * rows, :] = jnp.zeros((low * rows, traces_ref.shape[1]), f32)

    def step(face, carry):
        for block in range(BLOCK // LANES):
            there = block_at(level * (BLOCK // LANES) + block)
            index = joined_ref[low:low + 1, there]
            for other in range(low + 1, faces):
                index = jnp.where(face == other, joined_ref[other:other + 1, there], index)
            traces_ref[pl.ds(pl.multiple_of(face * rows, rows), rows), block_at(block)] = pick(
                received_blocks(received, count, rows), index, index >> 7, jnp.zeros((rows, LANES), f32))
        return carry

    lax.fori_loop(low, faces, step, 0)


def for_blocks(body):
    def step(block, carry):
        body(pl.ds(pl.multiple_of(block * LANES, LANES), LANES))
        return carry

    lax.fori_loop(0, BLOCK // LANES, step, 0)


def any_other(level, flags_ref):
    return jnp.max(flags_ref[level:level + 1, :]) > 0.0


def between_kernel(level, messages, members_ref, joined_ref, places_ref, columns_ref, old_out_ref, old_trace_ref,
                   moved_ref, extra_ref, extra_trace_ref, heights_ref, local_ref, old_weights_ref, lift_ref,
                   lift_first_ref, grow_ref, trace_grow_ref, send_places_ref, *rest):
    received, rest = rest[:messages], rest[messages:]
    final = level == LEVELS - 1
    if not final:
        sent, rest = rest[:messages], rest[messages:]
    if level > 1:
        advanced_ref, rest = rest[0], rest[1:]
    if final:
        loaded_ref, weights_ref, new_advanced_ref, out_ref, faces_ref, trace_ref, whole_ref = rest
    else:
        out_ref, loaded_ref, weights_ref, new_trace_ref, new_advanced_ref = rest[:5]
        prepared, (faces_ref, trace_ref, whole_ref) = rest[5:5 + messages], rest[5 + messages:]
    count = places_ref.shape[0]
    done = level - 1
    first = received_traces(done, 0, received, joined_ref, count)
    inflow = product(lift_first_ref[...], stacked_columns(first))
    for block in range(BLOCK // LANES):
        here = block_at(block)
        index = joined_ref[0:1, block_at(done * (BLOCK // LANES) + block)]
        moved = [(count + i, read) for i, read in ref_blocks(moved_ref, messages)]
        trace_ref[:, here] = old_trace_ref[:, here] + extra_trace_ref[:, here] + pick(
            moved, index, index >> 7, jnp.zeros((old_trace_ref.shape[0], LANES), f32))
    whole = local_ref[...] + inflow + extra_ref[...]
    stacked = stacked_columns(whole)
    chunks = row_chunks(whole.shape[0])
    pieces = BLOCK // LANES

    def gather_own(part):
        for block in range(part * pieces // len(chunks), (part + 1) * pieces // len(chunks)):
            own_block(level, block, members_ref, joined_ref, columns_ref, heights_ref, loaded_ref, weights_ref)

    def gather_faces(part):
        for block in range(part * pieces // len(chunks), (part + 1) * pieces // len(chunks)):
            face_block(level, block, joined_ref, out_ref, faces_ref)

    def put_out(part):
        for block in range(part * count // len(chunks), (part + 1) * count // len(chunks)):
            here = block_at(block)
            out_ref[:, here] = settle(
                done, ref_blocks(trace_ref, pieces), places_ref, old_out_ref[:, here], block)

    def put_columns(chunk):
        for block in range(count):
            here = block_at(block)
            before = advanced_ref[chunk, here] if level > 1 else None
            new_advanced_ref[chunk, here] = settle(
                done, [(b, functools.partial(lambda b: whole_ref[chunk, block_at(b)], b)) for b in range(pieces)],
                places_ref, before, block)

    for part in range(len(chunks)):
        put_out(part)
    for part, chunk in enumerate(chunks):
        whole_ref[chunk, :] = grown_rows(chunk, stacked, whole, grow_ref, old_weights_ref)
        gather_own(part)
        gather_faces(part)
    loaded = loaded_ref[...] + product(lift_ref[...], stacked_columns(faces_ref[...]))
    put_columns(chunks[0])
    loaded_ref[...] = loaded
    if not final:
        traces = advanced_traces(loaded, trace_grow_ref, weights_ref, out_ref.shape[0])
    for chunk in chunks[1:]:
        put_columns(chunk)
    if not final:
        new_trace_ref[...] = traces
        local_messages(level, new_trace_ref, send_places_ref, sent, prepared)


def level_kernel(level, messages, count, flags_ref, joined_ref, weights_ref, slot_weights_ref, mix_ref, lift_ref,
                 trace_grow_ref, send_places_ref, send_codes_ref, *rest):
    received, rest = rest[:messages], rest[messages:]
    prepared, rest = rest[:messages], rest[messages:]
    moved_ref, extra_ref, extra_trace_ref, sends = rest[0], rest[1], rest[2], rest[3:3 + messages]
    traces_ref, = rest[3 + messages:]
    rows = moved_ref.shape[0]
    pieces = BLOCK // LANES
    other = any_other(level, flags_ref)
    arrived = jnp.concatenate([pad_rows(ref[...], rows) for ref in received], axis=1)
    stacked = product(mix_ref[...], stacked_columns(arrived))
    moved_ref[...] = summed_powers(stacked[rows:], slot_weights_ref, rows, stacked[:rows])
    extra_ref[...] = jnp.zeros(extra_ref.shape, f32)
    extra_trace_ref[...] = jnp.zeros(extra_trace_ref.shape, f32)
    moved = [(count + i, read) for i, read in ref_blocks(moved_ref, messages)]
    for group, (before, send) in enumerate(zip(prepared, sends)):
        place, code = send_places_ref[group:group + 1, :], send_codes_ref[group:group + 1, :]
        here = ((place >> 7) >= level * pieces) & ((place >> 7) < (level + 1) * pieces)
        total = before[...] + pick(moved, code, jnp.where(here, code >> 7, 0), jnp.zeros(before.shape, f32))
        send[...] = total[:send.shape[0]]

    @pl.when(other)
    def _():
        gather_received(level, 1, received, joined_ref, count, traces_ref)

        def add_block(here):
            extra = product(lift_ref[...], stacked_columns(traces_ref[:, here]))
            extra_ref[:, here] = extra
            extra_trace_ref[:, here] = advanced_traces(extra, trace_grow_ref, weights_ref[:, here], rows)

        for_blocks(add_block)
        for group, send in enumerate(sends):
            place = send_places_ref[group:group + 1, :]
            more = pick(
                ref_blocks(extra_trace_ref, pieces), place, (place >> 7) - level * pieces, jnp.zeros((rows, LANES), f32))
            send[...] = send[...] + more[:send.shape[0]]


def last_chunks(rows):
    units = rows // 16
    first = -(-units * 5 // 9)
    second = -(-(units - first) * 3 // 4)
    bounds = [0, first * 16, (first + second) * 16, rows]
    return [slice(low, high) for low, high in zip(bounds, bounds[1:]) if high > low]


def last_kernel(level, messages, flags_ref, joined_ref, local_ref, weights_ref, lift_ref, lift_first_ref, grow_ref,
                places_ref, advanced_ref, *rest):
    received, (final_hbm, final_ref, traces_ref, whole_ref, sent) = rest[:messages], rest[messages:]
    count = places_ref.shape[0]
    comp = final_hbm.shape[0] // count

    def finish(whole):
        stacked = stacked_columns(whole)
        copies = []

        def put(number, chunk, new):
            height = min(chunk.stop, comp) - chunk.start
            for block in range(count):
                done = settle(level, value_blocks(new), places_ref, advanced_ref[chunk, block_at(block)], block)
                final_ref[pl.ds(chunk.start * count + block, height, stride=count), :] = done[:height]
            part = pl.ds(chunk.start * count, height * count)
            copies.append(pltpu.make_async_copy(final_ref.at[part], final_hbm.at[part], sent.at[number]))
            copies[-1].start()

        ahead = None
        for number, chunk in enumerate(last_chunks(whole.shape[0])):
            new = grown_rows(chunk, stacked, whole, grow_ref, weights_ref)
            if ahead is not None:
                put(*ahead)
            ahead = (number, chunk, new)
        put(*ahead)
        for copy in copies:
            copy.wait()

    other = any_other(level, flags_ref)
    first = received_traces(level, 0, received, joined_ref, count)
    finish(local_ref[...] + product(lift_first_ref[...], stacked_columns(first)))

    @pl.when(other)
    def _():
        gather_received(level, 0, received, joined_ref, count, traces_ref)

        def load_block(here):
            whole_ref[:, here] = local_ref[:, here] + product(lift_ref[...], stacked_columns(traces_ref[:, here]))

        for_blocks(load_block)
        rows, height = whole_ref.shape[0], 16

        def step(number, carry):
            start = pl.multiple_of(number * height, height)
            matrix = jnp.concatenate(
                [grow_ref[pl.ds(power * rows + start, height), :] for power in range(POWERS)], axis=0)
            new = summed_powers(product(matrix, stacked_columns(whole_ref[...])), weights_ref, height,
                                whole_ref[pl.ds(start, height), :])
            for block in range(count):
                before = advanced_ref[pl.ds(start, height), block_at(block)]
                done = settle(level, value_blocks(new), places_ref, before, block)
                final_ref[pl.ds(start * count + block, height, stride=count), :] = done
            return carry

        lax.fori_loop(0, rows // height, step, 0)
        copy = pltpu.make_async_copy(final_ref.at[pl.ds(0, comp * count)], final_hbm, sent.at[0])
        copy.start()
        copy.wait()


def call(kernel, name, flops, operands, outs, scratch=(), hbm=False, out_hbm=False):
    vmem = pl.BlockSpec(memory_space=pltpu.VMEM)
    given = pl.BlockSpec(memory_space=pltpu.HBM) if hbm else vmem
    if hbm:
        operands = [pltpu.with_memory_space_constraint(one, pltpu.HBM) for one in operands]
    return pl.pallas_call(
        kernel,
        out_shape=tuple(jax.ShapeDtypeStruct(shape, dtype) for shape, dtype in outs),
        in_specs=[given] * len(operands),
        out_specs=tuple([pl.BlockSpec(memory_space=pltpu.HBM) if out_hbm else vmem] * len(outs)),
        scratch_shapes=[one if not isinstance(one, tuple) else pltpu.VMEM(*one) for one in scratch],
        compiler_params=pltpu.CompilerParams(vmem_limit_bytes=16 * 1024 * 1024),
        cost_estimate=pl.CostEstimate(flops=flops, bytes_accessed=1 << 20, transcendentals=0),
        name=name,
    )(*operands)


def is_odd(axis):
    return (lax.axis_index(axis) & 1) == 1


def swap_plan(axis, periodic, low, high):
    count = lax.axis_size(axis)
    plan = [(axis, [(i, i ^ 1) for i in range(count)], low, high, False)]
    if count > 2 or periodic:
        pairs = [(i, (i + 1) % count if i % 2 else (i - 1) % count) for i in range(count)]
        plan.append((axis, pairs, high, low, not periodic))
    return plan


def came_group(swap):
    axis, _, even, odd, is_open = swap
    came = jnp.where(is_odd(axis), even, odd)
    if is_open:
        index = lax.axis_index(axis)
        came = jnp.where((index == 0) | (index == lax.axis_size(axis) - 1), NO_GROUP, came)
    return came


def body(fields, pattern, tent_order, level_sizes, send_rows, neighbours, operator, trace_map, lift_map, tent_height):
    fields, order, sizes = fields[0, 0], tent_order[0], level_sizes[0]
    faces_of, send_list = neighbours[0, 0], send_rows[0, 0]
    comp, elements = fields.shape
    faces, trace = lift_map.shape[0], trace_map.shape[0]
    rows, trace_rows = rounded_up(comp, 16), rounded_up(trace, 16)
    padded, count = LEVELS * BLOCK, elements // LANES
    bnd = send_list.shape[-1]

    near, *far = swap_plan("sector", True, 0, 1)
    swaps = far + [near] + swap_plan("radial", False, 2, 3)
    messages = len(swaps)

    def exchange(sent):
        return [lax.ppermute(one, swap[0], swap[1]) for one, swap in zip(sent, swaps)]

    message = ((trace_rows, bnd), f32)
    own, face_stack = ((rows, BLOCK), f32), ((faces * trace_rows, BLOCK), f32)
    weight, table, traced = ((POWERS, BLOCK), f32), ((trace_rows, elements), f32), ((trace_rows, BLOCK), f32)
    whole = ((rows, elements), f32)
    flat = (comp * count, LANES)

    arguments = [trace_map, send_list, order, pattern[0], sizes, faces_of, operator,
                 jnp.transpose(lift_map, (2, 0, 1)), tent_height[None]]
    columns, out, *rest = call(
        functools.partial(first_kernel, swaps), "first", 10 ** 8, [fields.reshape(flat)] + arguments,
        [whole, table] + [message] * messages
        + [((trace_rows,) + one.shape[1:] if one.ndim == 3 else one.shape, one.dtype) for one in arguments],
        [((rows * count, LANES), f32), pltpu.SemaphoreType.DMA((ARGUMENTS,))], hbm=True)
    sent, held = rest[:messages], rest[messages:]
    received = exchange(sent)
    slots = ((trace_rows, messages * LANES), f32)
    (members, joined, places, send_places, send_codes, slot_weights, flags, loaded, weights, new_trace, grow,
     trace_grow, mix, lift, lift_first, heights, *prepared) = call(
        functools.partial(plan_kernel, swaps), "plan", 2 * 10 ** 9, held + [columns, out] + sent,
        [((8, padded), i32), ((2 * faces, padded), i32), ((count, LANES), i32), ((8, bnd), i32), ((8, bnd), i32),
         ((POWERS, messages * LANES), f32), ((LEVELS, LANES), f32), own, weight, traced,
         ((POWERS * rows, 3 * rows), bf16), (((POWERS + 1) * trace_rows, 3 * rows), bf16),
         (((POWERS + 1) * trace_rows, 3 * trace_rows), bf16), ((rows, 3 * faces * trace_rows), bf16), ((rows, 3 * trace_rows), bf16), ((1, LANES), f32)]
        + [message] * messages, [face_stack])
    advanced = []
    for level in range(LEVELS - 1):
        moved, extra, extra_trace, *sent = call(
            functools.partial(level_kernel, level, messages, count), "level", 10 ** 8,
            [flags, joined, weights, slot_weights, mix, lift, trace_grow, send_places, send_codes] + received + prepared,
            [slots, own, traced] + [message] * messages, [face_stack])
        arrived, received = received, exchange(sent)
        beside = functools.partial(between_kernel, level + 1, messages)
        operands = [members, joined, places, columns, out, new_trace, moved, extra, extra_trace, heights, loaded,
                    weights, lift, lift_first, grow, trace_grow, send_places] + arrived
        scratch = [face_stack, traced, own]
        if level + 1 < LEVELS - 1:
            out, loaded, weights, new_trace, *rest = call(
                beside, "between", 2 * 10 ** 9, operands + sent + advanced,
                [table, own, weight, traced, whole] + [message] * messages, scratch)
            advanced, prepared = rest[:1], rest[1:]
        else:
            loaded, weights, *advanced = call(
                beside, "between", 2 * 10 ** 9, operands + advanced, [own, weight, whole], [table] + scratch)
    final, = call(
        functools.partial(last_kernel, LEVELS - 1, messages), "last", 10 ** 9,
        [flags, joined, loaded, weights, lift, lift_first, grow, places] + advanced + received,
        [(flat, f32)],
        [((rows * count, LANES), f32), face_stack, own, pltpu.SemaphoreType.DMA((len(last_chunks(rows)),))], out_hbm=True)
    return final.reshape(1, 1, comp, elements)


def solution(mesh):
    in_specs = (
        P("sector", "radial", None, None),
        P("sector", "radial", None),
        P("sector", "radial", None),
        P("sector", "radial", None),
        P("sector", "radial", None, None),
        P("sector", "radial", None, None),
        P(),
        P(),
        P(),
        P(),
    )
    out_specs = P("sector", "radial", None, None)
    return jax.shard_map(body, mesh=mesh, in_specs=in_specs, out_specs=out_specs, check_vma=False)
```

```python
import functools
import math

import jax
import jax.numpy as jnp
from jax import lax
from jax.experimental import pallas as pl
from jax.experimental.pallas import tpu as pltpu
from jax.sharding import PartitionSpec as P

LEVELS = 4
SUBSTEPS = 2
TERMS = 4
BLOCK = 384
LANES = 128
NO_GROUP = 1 << 20
ARGUMENTS = 10
ROW_CHUNK = 48

f32, bf16, i32 = jnp.float32, jnp.bfloat16, jnp.int32
precise = lax.Precision.HIGHEST


def rounded_up(size, unit):
    return -(-size // unit) * unit


def taylor_weights():
    once = [1.0 / math.factorial(k) for k in range(TERMS + 1)]
    whole = [1.0]
    for _ in range(SUBSTEPS):
        longer = [0.0] * (len(whole) + TERMS)
        for i, a in enumerate(whole):
            for j, b in enumerate(once):
                longer[i + j] += a * b
        whole = longer
    return whole


WEIGHTS = taylor_weights()
POWERS = len(WEIGHTS) - 1


def split(values):
    high = values.astype(bf16)
    return high, (values - high.astype(f32)).astype(bf16)


def whole_lanes(size):
    return size // LANES * LANES


def stacked_columns(values):
    high, low = split(values)
    main = whole_lanes(values.shape[0])
    parts = [high[:main], low[:main], high[:main], high[main:], low[main:], high[main:]]
    return jnp.concatenate([part for part in parts if part.shape[0]], axis=0)


def stacked_matrix(values):
    high = values.astype(bf16).astype(f32)
    low = values - high
    main = whole_lanes(values.shape[1])
    parts = [high[:, :main], high[:, :main], low[:, :main], high[:, main:], high[:, main:], low[:, main:]]
    return jnp.concatenate([part for part in parts if part.shape[1]], axis=1).astype(bf16)


def product(matrix, columns):
    return jnp.dot(matrix, columns, preferred_element_type=f32)


def pad_rows(values, rows):
    short = rows - values.shape[0]
    if short == 0:
        return values
    return jnp.concatenate([values, jnp.zeros((short,) + values.shape[1:], values.dtype)], axis=0)


def exact_product(left, right):
    left_high, left_low = split(left)
    right_high, right_low = split(right)
    rows = left.shape[0]
    both = product(jnp.concatenate([left_high, left_low], axis=0), right_high)
    return both[:rows] + both[rows:] + product(left_high, right_low)


def pick(blocks, index, which, start=None):
    result = start
    for number, read in blocks:
        table = read()
        lane = jnp.broadcast_to(index & (LANES - 1), table.shape)
        got = jnp.take_along_axis(table, lane, axis=1, mode="promise_in_bounds")
        if result is None:
            result = got
        else:
            result = jnp.where(jnp.broadcast_to(which, table.shape) == number, got, result)
    return result


def block_at(block):
    return slice(block * LANES, (block + 1) * LANES)


def ref_blocks(ref, count):
    return [(b, functools.partial(lambda b: ref[:, block_at(b)], b)) for b in range(count)]


def value_blocks(values):
    return [(b, functools.partial(lambda b: values[:, block_at(b)], b)) for b in range(values.shape[1] // LANES)]


def row_blocks(table, rows):
    return [
        (b, functools.partial(lambda b: jnp.broadcast_to(table[b:b + 1, :], (rows, LANES)), b))
        for b in range(table.shape[0])
    ]


def row_blocks_of(row, rows):
    return [
        (b, functools.partial(lambda b: jnp.broadcast_to(row[:, block_at(b)], (rows, LANES)), b))
        for b in range(row.shape[1] // LANES)
    ]


def summed_powers(stacked, weights_ref, rows, total):
    for power in range(1, POWERS + 1):
        total = total + stacked[(power - 1) * rows:power * rows] * weights_ref[power - 1:power, :]
    return total


def sent_rows(send_ref, swaps):
    rows = []
    for axis, _, low, high, _ in swaps:
        odd, even = send_ref[high:high + 1, :], send_ref[low:low + 1, :]
        rows.append(jnp.where(is_odd(axis), odd, even))
    return rows


def first_kernel(swaps, *refs):
    (fields_hbm, *given), refs = refs[:ARGUMENTS], refs[ARGUMENTS:]
    (columns_ref, out_ref), refs = refs[:2], refs[2:]
    sends, refs = refs[:len(swaps)], refs[len(swaps):]
    *held, fields_ref, arrived = refs
    rows = out_ref.shape[0]
    elements = out_ref.shape[1]
    count = elements // LANES
    comp = fields_hbm.shape[0] // count
    trace_hbm, send_hbm, *others = given
    trace_ref, send_ref, *others_held = held
    pairs = [(fields_hbm, fields_ref.at[pl.ds(0, comp * count)]), (trace_hbm, trace_ref), (send_hbm, send_ref)]
    needed = len(pairs)
    pairs += [(source, target if source.shape == target.shape else target.at[pl.ds(0, source.shape[0])])
              for source, target in zip(others, others_held)]
    copies = [pltpu.make_async_copy(source, target, arrived.at[i]) for i, (source, target) in enumerate(pairs)]
    for copy in copies:
        copy.start()
    for copy in copies[:needed]:
        copy.wait()
    trace_high, trace_low = split(pad_rows(trace_ref[...], rows))
    fields = jnp.concatenate([fields_ref[pl.ds(b, comp, stride=count), :] for b in range(count)], axis=1)
    high, low = split(fields)
    upper = product(jnp.concatenate([trace_high, trace_low], axis=0), high)
    out_ref[...] = upper[:rows] + upper[rows:] + product(trace_high, low)
    for index, send in zip(sent_rows(send_ref, swaps), sends):
        send[...] = pick(ref_blocks(out_ref, count), index, index >> 7)[:send.shape[0]]
    columns_ref[...] = pad_rows(fields, columns_ref.shape[0])
    for copy in copies[needed:]:
        copy.wait()


def faces_in(joined_ref):
    return joined_ref.shape[0] // 2


def own_block(level, block, members_ref, joined_ref, columns_ref, heights_ref, own_ref, weights_ref):
    faces = faces_in(joined_ref)
    here, there = block_at(block), block_at(level * (BLOCK // LANES) + block)
    index = members_ref[0:1, there]
    own_ref[:, here] = pick(ref_blocks(columns_ref, columns_ref.shape[1] // LANES), index, index >> 7)
    pattern = jnp.broadcast_to(joined_ref[faces:faces + 1, there], (8, LANES))
    height = jnp.take_along_axis(
        jnp.broadcast_to(heights_ref[...], (8, LANES)), pattern, axis=1, mode="promise_in_bounds")
    weight = jnp.ones((8, LANES), f32)
    for power in range(1, POWERS + 1):
        weight = weight * height
        weights_ref[power - 1:power, here] = weight[0:1] * WEIGHTS[power]


def face_block(level, block, joined_ref, out_ref, faces_ref):
    trace_rows = out_ref.shape[0]
    here, there = block_at(block), block_at(level * (BLOCK // LANES) + block)
    for face in range(faces_in(joined_ref)):
        index = joined_ref[face:face + 1, there]
        faces_ref[face * trace_rows:(face + 1) * trace_rows, here] = pick(
            ref_blocks(out_ref, out_ref.shape[1] // LANES), index, index >> 7, jnp.zeros((trace_rows, LANES), f32))


def advanced_traces(loaded, matrix_ref, weights_ref, rows):
    stacked = product(matrix_ref[...], stacked_columns(loaded))
    return summed_powers(stacked[rows:], weights_ref, rows, stacked[:rows])


def local_messages(level, trace_ref, send_places_ref, sent, messages):
    for group, (before, message) in enumerate(zip(sent, messages)):
        index = send_places_ref[group:group + 1, :]
        which = (index >> 7) - level * (BLOCK // LANES)
        message[...] = pick(
            ref_blocks(trace_ref, BLOCK // LANES), index, which, pad_rows(before[...], message.shape[0]))


def row_chunks(rows):
    return [slice(low, low + ROW_CHUNK) for low in range(0, rows, ROW_CHUNK)]


def grown_rows(chunk, stacked, loaded, grow_ref, weights_ref):
    rows = loaded.shape[0]
    matrix = jnp.concatenate(
        [grow_ref[power * rows + chunk.start:power * rows + chunk.stop, :] for power in range(POWERS)], axis=0)
    return summed_powers(product(matrix, stacked), weights_ref, chunk.stop - chunk.start, loaded[chunk])


def matrix_powers(operator_ref, trace_ref, lift_ref, grow_ref, trace_grow_ref, mix_ref, lift_out_ref,
                  lift_first_ref):
    comp = operator_ref.shape[0]
    faces = lift_ref.shape[1]
    trace_comp = trace_ref.shape[0]
    rows = lift_out_ref.shape[0]
    trace_rows = trace_grow_ref.shape[0] // (POWERS + 1)
    operator = pad_rows(operator_ref[...], rows)
    operator = jnp.concatenate([operator, jnp.zeros((rows, rows - comp), f32)], axis=1)
    traces = pad_rows(trace_ref[...], trace_rows)
    traces = jnp.concatenate([traces, jnp.zeros((trace_rows, rows - comp), f32)], axis=1)
    filled = lax.broadcasted_iota(i32, (trace_rows, comp), 0) < trace_comp
    lift = jnp.concatenate([jnp.where(filled, lift_ref[:, face, :], 0.0) for face in range(faces)], axis=0)
    lift = pad_rows(jnp.transpose(lift), rows)
    lift_out_ref[...] = stacked_matrix(lift)
    lift_first_ref[...] = stacked_matrix(lift[:, :trace_rows])
    powers, have = operator, 1
    while have < POWERS:
        more = exact_product(jnp.concatenate([traces, powers], axis=0), powers[(have - 1) * rows:have * rows])
        traces = jnp.concatenate([traces, more[:have * trace_rows]], axis=0)
        powers = jnp.concatenate([powers, more[have * trace_rows:]], axis=0)
        have *= 2
        yield
    traces = jnp.concatenate([traces, exact_product(traces[:trace_rows], powers[-rows:])], axis=0)
    trace_grow_ref[...] = stacked_matrix(traces)
    yield
    mix_ref[...] = stacked_matrix(exact_product(traces, lift[:, :trace_rows]))
    grow_ref[...] = stacked_matrix(powers)
    yield


def plan_kernel(swaps, *refs):
    (trace_ref, send_ref, order_ref, pattern_ref, sizes_ref, neighbours_ref, operator_ref, lift_ref, heights_ref,
     columns_ref, out_ref), refs = refs[:11], refs[11:]
    messages = len(swaps)
    sent, refs = refs[:messages], refs[messages:]
    (members_ref, joined_ref, places_ref, send_places_ref, send_codes_ref, slot_weights_ref, flags_ref, loaded_ref,
     weights_ref, new_trace_ref, grow_ref, trace_grow_ref, mix_ref, lift_out_ref, lift_first_ref,
     wide_heights_ref), refs = refs[:16], refs[16:]
    prepared, (faces_ref,) = refs[:messages], refs[messages:]
    elements = columns_ref.shape[1]
    count = elements // LANES
    faces = neighbours_ref.shape[0]
    steps = matrix_powers(operator_ref, trace_ref, lift_ref, grow_ref, trace_grow_ref, mix_ref, lift_out_ref,
                          lift_first_ref)
    next(steps)
    sizes = sizes_ref[...].astype(f32)
    number = lax.broadcasted_iota(i32, sizes.shape, 1)
    starts = [jnp.sum(jnp.where(number < level, sizes, 0.0)).astype(i32) for level in range(LEVELS)]
    wide_order = jnp.broadcast_to(order_ref[...], (8, elements))
    neighbours = neighbours_ref[...]
    group = (neighbours >> 7) - count
    message = jnp.full(neighbours.shape, count + len(swaps), i32)
    for number, swap in enumerate(swaps):
        message = jnp.where(group == came_group(swap), count + number, message)
    neighbours = jnp.where(group >= 0, message * LANES + (neighbours & (LANES - 1)), neighbours)
    table = jnp.concatenate(
        [neighbours, pattern_ref[...], jnp.zeros((faces - 1, elements), i32)], axis=0)
    heights = heights_ref[...]
    wide_heights_ref[...] = jnp.concatenate(
        [heights, jnp.zeros((1, LANES - heights.shape[1]), f32)], axis=1)
    for level in range(LEVELS):
        shift = jnp.where(starts[level] == 0, 0, elements - starts[level])
        members_ref[:, level * BLOCK:(level + 1) * BLOCK] = pltpu.roll(wide_order, shift, 1)[:, :BLOCK]
    for block in range(LEVELS * BLOCK // LANES):
        index = members_ref[:, block_at(block)]
        joined_ref[:, block_at(block)] = pick(value_blocks(table), index, index >> 7)
    ranks = lax.broadcasted_iota(i32, (count, elements), 1)
    in_block = (wide_order[:count] >> 7) == lax.broadcasted_iota(i32, (count, elements), 0)
    left = jnp.concatenate([
        jnp.where(in_block, ranks >> 5, 0).astype(f32), jnp.where(in_block, ranks & 31, 0).astype(f32)], axis=0)
    at_lane = jnp.broadcast_to(order_ref[...] & (LANES - 1), (LANES, elements)) == lax.broadcasted_iota(
        i32, (LANES, elements), 0)
    rank = lax.dot_general(left.astype(bf16), jnp.where(at_lane, 1.0, 0.0).astype(bf16), (((1,), (1,)), ((), ())),
                           preferred_element_type=f32)
    place = rank[:count].astype(i32) * 32 + rank[count:].astype(i32)
    at = place
    for level in range(1, LEVELS):
        at = jnp.where(place >= starts[level], place - starts[level] + level * BLOCK, at)
    places_ref[...] = at
    index = pad_rows(jnp.concatenate(sent_rows(send_ref, swaps), axis=0), 8)
    send_places_ref[...] = pick(row_blocks(at, 8), index, index >> 7)
    send_codes_ref[...] = pick(row_blocks_of(neighbours[:1], 8), index, index >> 7)
    block = jnp.broadcast_to(neighbours[:1] >> 7, (8, elements)) - count
    named = jnp.where(block == lax.broadcasted_iota(i32, (8, elements), 0),
                      jnp.broadcast_to(pattern_ref[...], (8, elements)), 0).astype(f32).astype(bf16)
    slot_lane = jnp.broadcast_to(neighbours[:1] & (LANES - 1), (LANES, elements)) == lax.broadcasted_iota(
        i32, (LANES, elements), 0)
    slot_pattern = lax.dot_general(named, jnp.where(slot_lane, 1.0, 0.0).astype(bf16), (((1,), (1,)), ((), ())),
                                   preferred_element_type=f32).astype(i32)
    height = jnp.take_along_axis(jnp.broadcast_to(wide_heights_ref[...], (8, LANES)), slot_pattern & (LANES - 1),
                                 axis=1, mode="promise_in_bounds")
    weight = jnp.ones((8, LANES), f32)
    for power in range(1, POWERS + 1):
        weight = weight * height
        for number in range(messages):
            slot_weights_ref[power - 1:power, block_at(number)] = weight[number:number + 1] * WEIGHTS[power]
    for level in range(LEVELS):
        code = joined_ref[1:faces, level * BLOCK:(level + 1) * BLOCK]
        code = jnp.max(jnp.where(code >= elements, 1.0, 0.0), axis=0, keepdims=True)
        row = code[:, block_at(0)]
        for number in range(1, BLOCK // LANES):
            row = jnp.maximum(row, code[:, block_at(number)])
        flags_ref[level:level + 1, :] = row
    next(steps)
    for block in range(BLOCK // LANES):
        own_block(0, block, members_ref, joined_ref, columns_ref, wide_heights_ref, loaded_ref, weights_ref)
        face_block(0, block, joined_ref, out_ref, faces_ref)
        next(steps)
    loaded = loaded_ref[...] + product(lift_out_ref[...], stacked_columns(faces_ref[...]))
    loaded_ref[...] = loaded
    new_trace_ref[...] = advanced_traces(loaded, trace_grow_ref, weights_ref, out_ref.shape[0])
    local_messages(0, new_trace_ref, send_places_ref, sent, prepared)


def settle(level, blocks, places_ref, before, block):
    index = places_ref[block:block + 1, :]
    which = (index >> 7) - level * (BLOCK // LANES)
    return pick(blocks, index, which, before)


def received_blocks(received, count, rows):
    return [(count + i, functools.partial(lambda ref: pad_rows(ref[...], rows), ref)) for i, ref in enumerate(received)]


def received_traces(level, face, received, joined_ref, count):
    parts = []
    for block in range(BLOCK // LANES):
        index = joined_ref[face:face + 1, block_at(level * (BLOCK // LANES) + block)]
        rows = rounded_up(received[0].shape[0], 16)
        zeros = jnp.zeros((rows, LANES), f32)
        parts.append(pick(received_blocks(received, count, rows), index, index >> 7, zeros))
    return jnp.concatenate(parts, axis=1)


def gather_received(level, low, received, joined_ref, count, traces_ref):
    faces = faces_in(joined_ref)
    rows = traces_ref.shape[0] // faces
    if low:
        traces_ref[:low * rows, :] = jnp.zeros((low * rows, traces_ref.shape[1]), f32)

    def step(face, carry):
        for block in range(BLOCK // LANES):
            there = block_at(level * (BLOCK // LANES) + block)
            index = joined_ref[low:low + 1, there]
            for other in range(low + 1, faces):
                index = jnp.where(face == other, joined_ref[other:other + 1, there], index)
            traces_ref[pl.ds(pl.multiple_of(face * rows, rows), rows), block_at(block)] = pick(
                received_blocks(received, count, rows), index, index >> 7, jnp.zeros((rows, LANES), f32))
        return carry

    lax.fori_loop(low, faces, step, 0)


def for_blocks(body):
    def step(block, carry):
        body(pl.ds(pl.multiple_of(block * LANES, LANES), LANES))
        return carry

    lax.fori_loop(0, BLOCK // LANES, step, 0)


def any_other(level, flags_ref):
    return jnp.max(flags_ref[level:level + 1, :]) > 0.0


def between_kernel(level, messages, members_ref, joined_ref, places_ref, columns_ref, old_out_ref, old_trace_ref,
                   moved_ref, heights_ref, local_ref, old_weights_ref, lift_ref,
                   lift_first_ref, grow_ref, trace_grow_ref, send_places_ref, *rest):
    received, rest = rest[:messages], rest[messages:]
    final = level == LEVELS - 1
    if not final:
        sent, rest = rest[:messages], rest[messages:]
    if level > 1:
        advanced_ref, rest = rest[0], rest[1:]
    if final:
        loaded_ref, weights_ref, new_advanced_ref, out_ref, faces_ref, trace_ref, whole_ref = rest
    else:
        out_ref, loaded_ref, weights_ref, new_trace_ref, new_advanced_ref = rest[:5]
        prepared, (faces_ref, trace_ref, whole_ref) = rest[5:5 + messages], rest[5 + messages:]
    count = places_ref.shape[0]
    done = level - 1
    first = received_traces(done, 0, received, joined_ref, count)
    inflow = product(lift_first_ref[...], stacked_columns(first))
    for block in range(BLOCK // LANES):
        here = block_at(block)
        index = joined_ref[0:1, block_at(done * (BLOCK // LANES) + block)]
        moved = [(count + i, read) for i, read in ref_blocks(moved_ref, messages)]
        trace_ref[:, here] = old_trace_ref[:, here] + pick(
            moved, index, index >> 7, jnp.zeros((old_trace_ref.shape[0], LANES), f32))
    whole = local_ref[...] + inflow
    stacked = stacked_columns(whole)
    chunks = row_chunks(whole.shape[0])
    pieces = BLOCK // LANES

    def gather_own(part):
        for block in range(part * pieces // len(chunks), (part + 1) * pieces // len(chunks)):
            own_block(level, block, members_ref, joined_ref, columns_ref, heights_ref, loaded_ref, weights_ref)

    def gather_faces(part):
        for block in range(part * pieces // len(chunks), (part + 1) * pieces // len(chunks)):
            face_block(level, block, joined_ref, out_ref, faces_ref)

    def put_out(part):
        for block in range(part * count // len(chunks), (part + 1) * count // len(chunks)):
            here = block_at(block)
            out_ref[:, here] = settle(
                done, ref_blocks(trace_ref, pieces), places_ref, old_out_ref[:, here], block)

    def put_columns(chunk):
        for block in range(count):
            here = block_at(block)
            before = advanced_ref[chunk, here] if level > 1 else None
            new_advanced_ref[chunk, here] = settle(
                done, [(b, functools.partial(lambda b: whole_ref[chunk, block_at(b)], b)) for b in range(pieces)],
                places_ref, before, block)

    for part in range(len(chunks)):
        put_out(part)
    for part, chunk in enumerate(chunks):
        whole_ref[chunk, :] = grown_rows(chunk, stacked, whole, grow_ref, old_weights_ref)
        gather_own(part)
        gather_faces(part)
    loaded = loaded_ref[...] + product(lift_ref[...], stacked_columns(faces_ref[...]))
    put_columns(chunks[0])
    loaded_ref[...] = loaded
    if not final:
        traces = advanced_traces(loaded, trace_grow_ref, weights_ref, out_ref.shape[0])
    for chunk in chunks[1:]:
        put_columns(chunk)
    if not final:
        new_trace_ref[...] = traces
        local_messages(level, new_trace_ref, send_places_ref, sent, prepared)


def level_kernel(level, messages, count, flags_ref, joined_ref, weights_ref, slot_weights_ref, mix_ref, lift_ref,
                 trace_grow_ref, send_places_ref, send_codes_ref, *rest):
    received, rest = rest[:messages], rest[messages:]
    prepared, rest = rest[:messages], rest[messages:]
    (_, _), rest = rest[:2], rest[2:]
    moved_ref, loaded_any, trace_any, sends = rest[0], rest[1], rest[2], rest[3:3 + messages]
    traces_ref, extra_ref, extra_trace_ref, before_ref, before_trace_ref, moving = rest[3 + messages:]
    rows = moved_ref.shape[0]
    pieces = BLOCK // LANES
    other = any_other(level, flags_ref)
    arrived = jnp.concatenate([pad_rows(ref[...], rows) for ref in received], axis=1)
    stacked = product(mix_ref[...], stacked_columns(arrived))
    moved_ref[...] = summed_powers(stacked[rows:], slot_weights_ref, rows, stacked[:rows])
    moved = [(count + i, read) for i, read in ref_blocks(moved_ref, messages)]
    for group, (before, send) in enumerate(zip(prepared, sends)):
        place, code = send_places_ref[group:group + 1, :], send_codes_ref[group:group + 1, :]
        here = ((place >> 7) >= level * pieces) & ((place >> 7) < (level + 1) * pieces)
        total = before[...] + pick(moved, code, jnp.where(here, code >> 7, 0), jnp.zeros(before.shape, f32))
        send[...] = total[:send.shape[0]]

    @pl.when(other)
    def _():
        gather_received(level, 1, received, joined_ref, count, traces_ref)

        def add_block(here):
            extra = product(lift_ref[...], stacked_columns(traces_ref[:, here]))
            extra_ref[:, here] = extra
            extra_trace_ref[:, here] = advanced_traces(extra, trace_grow_ref, weights_ref[:, here], rows)

        for_blocks(add_block)
        for part, whole, before in ((extra_ref, loaded_any, before_ref), (extra_trace_ref, trace_any, before_trace_ref)):
            copy = pltpu.make_async_copy(whole, before, moving)
            copy.start()
            copy.wait()
            before[...] = before[...] + part[...]
            copy = pltpu.make_async_copy(before, whole, moving)
            copy.start()
            copy.wait()
        for group, send in enumerate(sends):
            place = send_places_ref[group:group + 1, :]
            more = pick(
                ref_blocks(extra_trace_ref, pieces), place, (place >> 7) - level * pieces, jnp.zeros((rows, LANES), f32))
            send[...] = send[...] + more[:send.shape[0]]


def last_chunks(rows):
    units = rows // 16
    first = -(-units * 5 // 9)
    second = -(-(units - first) * 3 // 4)
    bounds = [0, first * 16, (first + second) * 16, rows]
    return [slice(low, high) for low, high in zip(bounds, bounds[1:]) if high > low]


def last_kernel(level, messages, flags_ref, joined_ref, local_ref, weights_ref, lift_ref, lift_first_ref, grow_ref,
                places_ref, advanced_ref, *rest):
    received, (final_hbm, final_ref, traces_ref, whole_ref, sent) = rest[:messages], rest[messages:]
    count = places_ref.shape[0]
    comp = final_hbm.shape[0] // count

    def finish(whole):
        stacked = stacked_columns(whole)
        copies = []

        def put(number, chunk, new):
            height = min(chunk.stop, comp) - chunk.start
            for block in range(count):
                done = settle(level, value_blocks(new), places_ref, advanced_ref[chunk, block_at(block)], block)
                final_ref[pl.ds(chunk.start * count + block, height, stride=count), :] = done[:height]
            part = pl.ds(chunk.start * count, height * count)
            copies.append(pltpu.make_async_copy(final_ref.at[part], final_hbm.at[part], sent.at[number]))
            copies[-1].start()

        ahead = None
        for number, chunk in enumerate(last_chunks(whole.shape[0])):
            new = grown_rows(chunk, stacked, whole, grow_ref, weights_ref)
            if ahead is not None:
                put(*ahead)
            ahead = (number, chunk, new)
        put(*ahead)
        for copy in copies:
            copy.wait()

    other = any_other(level, flags_ref)
    first = received_traces(level, 0, received, joined_ref, count)
    finish(local_ref[...] + product(lift_first_ref[...], stacked_columns(first)))

    @pl.when(other)
    def _():
        gather_received(level, 0, received, joined_ref, count, traces_ref)

        def load_block(here):
            whole_ref[:, here] = local_ref[:, here] + product(lift_ref[...], stacked_columns(traces_ref[:, here]))

        for_blocks(load_block)
        rows, height = whole_ref.shape[0], 16

        def step(number, carry):
            start = pl.multiple_of(number * height, height)
            matrix = jnp.concatenate(
                [grow_ref[pl.ds(power * rows + start, height), :] for power in range(POWERS)], axis=0)
            new = summed_powers(product(matrix, stacked_columns(whole_ref[...])), weights_ref, height,
                                whole_ref[pl.ds(start, height), :])
            for block in range(count):
                before = advanced_ref[pl.ds(start, height), block_at(block)]
                done = settle(level, value_blocks(new), places_ref, before, block)
                final_ref[pl.ds(start * count + block, height, stride=count), :] = done
            return carry

        lax.fori_loop(0, rows // height, step, 0)
        copy = pltpu.make_async_copy(final_ref.at[pl.ds(0, comp * count)], final_hbm, sent.at[0])
        copy.start()
        copy.wait()


def call(kernel, name, flops, operands, outs, scratch=(), hbm=False, out_hbm=False, through=()):
    vmem = pl.BlockSpec(memory_space=pltpu.VMEM)
    given = pl.BlockSpec(memory_space=pltpu.HBM) if hbm else vmem
    if hbm:
        operands = [pltpu.with_memory_space_constraint(one, pltpu.HBM) for one in operands]
    return pl.pallas_call(
        kernel,
        out_shape=tuple(jax.ShapeDtypeStruct(shape, dtype) for shape, dtype in outs),
        in_specs=[pl.BlockSpec(memory_space=pl.ANY) if i in dict(through) else given for i in range(len(operands))],
        out_specs=tuple(
            pl.BlockSpec(memory_space=pltpu.HBM) if out_hbm else
            pl.BlockSpec(memory_space=pl.ANY) if i in dict(through).values() else vmem for i in range(len(outs))),
        input_output_aliases=dict(through),
        scratch_shapes=[one if not isinstance(one, tuple) else pltpu.VMEM(*one) for one in scratch],
        compiler_params=pltpu.CompilerParams(vmem_limit_bytes=16 * 1024 * 1024),
        cost_estimate=pl.CostEstimate(flops=flops, bytes_accessed=1 << 20, transcendentals=0),
        name=name,
    )(*operands)


def is_odd(axis):
    return (lax.axis_index(axis) & 1) == 1


def swap_plan(axis, periodic, low, high):
    count = lax.axis_size(axis)
    plan = [(axis, [(i, i ^ 1) for i in range(count)], low, high, False)]
    if count > 2 or periodic:
        pairs = [(i, (i + 1) % count if i % 2 else (i - 1) % count) for i in range(count)]
        plan.append((axis, pairs, high, low, not periodic))
    return plan


def came_group(swap):
    axis, _, even, odd, is_open = swap
    came = jnp.where(is_odd(axis), even, odd)
    if is_open:
        index = lax.axis_index(axis)
        came = jnp.where((index == 0) | (index == lax.axis_size(axis) - 1), NO_GROUP, came)
    return came


def body(fields, pattern, tent_order, level_sizes, send_rows, neighbours, operator, trace_map, lift_map, tent_height):
    fields, order, sizes = fields[0, 0], tent_order[0], level_sizes[0]
    faces_of, send_list = neighbours[0, 0], send_rows[0, 0]
    comp, elements = fields.shape
    faces, trace = lift_map.shape[0], trace_map.shape[0]
    rows, trace_rows = rounded_up(comp, 16), rounded_up(trace, 16)
    padded, count = LEVELS * BLOCK, elements // LANES
    bnd = send_list.shape[-1]

    near, *far = swap_plan("sector", True, 0, 1)
    swaps = far + [near] + swap_plan("radial", False, 2, 3)
    messages = len(swaps)

    def exchange(sent):
        return [lax.ppermute(one, swap[0], swap[1]) for one, swap in zip(sent, swaps)]

    message = ((trace_rows, bnd), f32)
    own, face_stack = ((rows, BLOCK), f32), ((faces * trace_rows, BLOCK), f32)
    weight, table, traced = ((POWERS, BLOCK), f32), ((trace_rows, elements), f32), ((trace_rows, BLOCK), f32)
    whole = ((rows, elements), f32)
    flat = (comp * count, LANES)

    arguments = [trace_map, send_list, order, pattern[0], sizes, faces_of, operator,
                 jnp.transpose(lift_map, (2, 0, 1)), tent_height[None]]
    columns, out, *rest = call(
        functools.partial(first_kernel, swaps), "first", 10 ** 8, [fields.reshape(flat)] + arguments,
        [whole, table] + [message] * messages
        + [((trace_rows,) + one.shape[1:] if one.ndim == 3 else one.shape, one.dtype) for one in arguments],
        [((rows * count, LANES), f32), pltpu.SemaphoreType.DMA((ARGUMENTS,))], hbm=True)
    sent, held = rest[:messages], rest[messages:]
    received = exchange(sent)
    slots = ((trace_rows, messages * LANES), f32)
    (members, joined, places, send_places, send_codes, slot_weights, flags, loaded, weights, new_trace, grow,
     trace_grow, mix, lift, lift_first, heights, *prepared) = call(
        functools.partial(plan_kernel, swaps), "plan", 2 * 10 ** 9, held + [columns, out] + sent,
        [((8, padded), i32), ((2 * faces, padded), i32), ((count, LANES), i32), ((8, bnd), i32), ((8, bnd), i32),
         ((POWERS, messages * LANES), f32), ((LEVELS, LANES), f32), own, weight, traced,
         ((POWERS * rows, 3 * rows), bf16), (((POWERS + 1) * trace_rows, 3 * rows), bf16),
         (((POWERS + 1) * trace_rows, 3 * trace_rows), bf16), ((rows, 3 * faces * trace_rows), bf16), ((rows, 3 * trace_rows), bf16), ((1, LANES), f32)]
        + [message] * messages, [face_stack])
    advanced = []
    for level in range(LEVELS - 1):
        operands = [flags, joined, weights, slot_weights, mix, lift, trace_grow, send_places, send_codes]
        operands += received + prepared + [loaded, new_trace]
        moved, loaded, new_trace, *sent = call(
            functools.partial(level_kernel, level, messages, count), "level", 10 ** 8,
            operands, [slots, own, traced] + [message] * messages,
            [face_stack, own, traced, own, traced, pltpu.SemaphoreType.DMA(())],
            through=[(len(operands) - 2, 1), (len(operands) - 1, 2)])
        arrived, received = received, exchange(sent)
        beside = functools.partial(between_kernel, level + 1, messages)
        operands = [members, joined, places, columns, out, new_trace, moved, heights, loaded,
                    weights, lift, lift_first, grow, trace_grow, send_places] + arrived
        scratch = [face_stack, traced, own]
        if level + 1 < LEVELS - 1:
            out, loaded, weights, new_trace, *rest = call(
                beside, "between", 2 * 10 ** 9, operands + sent + advanced,
                [table, own, weight, traced, whole] + [message] * messages, scratch)
            advanced, prepared = rest[:1], rest[1:]
        else:
            loaded, weights, *advanced = call(
                beside, "between", 2 * 10 ** 9, operands + advanced, [own, weight, whole], [table] + scratch)
    final, = call(
        functools.partial(last_kernel, LEVELS - 1, messages), "last", 10 ** 9,
        [flags, joined, loaded, weights, lift, lift_first, grow, places] + advanced + received,
        [(flat, f32)],
        [((rows * count, LANES), f32), face_stack, own, pltpu.SemaphoreType.DMA((len(last_chunks(rows)),))], out_hbm=True)
    return final.reshape(1, 1, comp, elements)


def solution(mesh):
    in_specs = (
        P("sector", "radial", None, None),
        P("sector", "radial", None),
        P("sector", "radial", None),
        P("sector", "radial", None),
        P("sector", "radial", None, None),
        P("sector", "radial", None, None),
        P(),
        P(),
        P(),
        P(),
    )
    out_specs = P("sector", "radial", None, None)
    return jax.shard_map(body, mesh=mesh, in_specs=in_specs, out_specs=out_specs, check_vma=False)
```

```python
import functools
import math

import jax
import jax.numpy as jnp
from jax import lax
from jax.experimental import pallas as pl
from jax.experimental.pallas import tpu as pltpu
from jax.sharding import PartitionSpec as P

LEVELS = 4
SUBSTEPS = 2
TERMS = 4
BLOCK = 384
LANES = 128
NO_GROUP = 1 << 20
ARGUMENTS = 10
ROW_CHUNK = 144

f32, bf16, i32 = jnp.float32, jnp.bfloat16, jnp.int32
precise = lax.Precision.HIGHEST


def rounded_up(size, unit):
    return -(-size // unit) * unit


def taylor_weights():
    once = [1.0 / math.factorial(k) for k in range(TERMS + 1)]
    whole = [1.0]
    for _ in range(SUBSTEPS):
        longer = [0.0] * (len(whole) + TERMS)
        for i, a in enumerate(whole):
            for j, b in enumerate(once):
                longer[i + j] += a * b
        whole = longer
    return whole


WEIGHTS = taylor_weights()
POWERS = len(WEIGHTS) - 1


def split(values):
    high = values.astype(bf16)
    return high, (values - high.astype(f32)).astype(bf16)


def whole_lanes(size):
    return size // LANES * LANES


def stacked_columns(values):
    high, low = split(values)
    main = whole_lanes(values.shape[0])
    parts = [high[:main], low[:main], high[:main], high[main:], low[main:], high[main:]]
    return jnp.concatenate([part for part in parts if part.shape[0]], axis=0)


def stacked_matrix(values):
    high = values.astype(bf16).astype(f32)
    low = values - high
    main = whole_lanes(values.shape[1])
    parts = [high[:, :main], high[:, :main], low[:, :main], high[:, main:], high[:, main:], low[:, main:]]
    return jnp.concatenate([part for part in parts if part.shape[1]], axis=1).astype(bf16)


def product(matrix, columns):
    return jnp.dot(matrix, columns, preferred_element_type=f32)


def pad_rows(values, rows):
    short = rows - values.shape[0]
    if short == 0:
        return values
    return jnp.concatenate([values, jnp.zeros((short,) + values.shape[1:], values.dtype)], axis=0)


def exact_product(left, right):
    left_high, left_low = split(left)
    right_high, right_low = split(right)
    rows = left.shape[0]
    both = product(jnp.concatenate([left_high, left_low], axis=0), right_high)
    return both[:rows] + both[rows:] + product(left_high, right_low)


def pick(blocks, index, which, start=None):
    result = start
    for number, read in blocks:
        table = read()
        lane = jnp.broadcast_to(index & (LANES - 1), table.shape)
        got = jnp.take_along_axis(table, lane, axis=1, mode="promise_in_bounds")
        if result is None:
            result = got
        else:
            result = jnp.where(jnp.broadcast_to(which, table.shape) == number, got, result)
    return result


def block_at(block):
    return slice(block * LANES, (block + 1) * LANES)


def ref_blocks(ref, count):
    return [(b, functools.partial(lambda b: ref[:, block_at(b)], b)) for b in range(count)]


def value_blocks(values):
    return [(b, functools.partial(lambda b: values[:, block_at(b)], b)) for b in range(values.shape[1] // LANES)]


def row_blocks(table, rows):
    return [
        (b, functools.partial(lambda b: jnp.broadcast_to(table[b:b + 1, :], (rows, LANES)), b))
        for b in range(table.shape[0])
    ]


def row_blocks_of(row, rows):
    return [
        (b, functools.partial(lambda b: jnp.broadcast_to(row[:, block_at(b)], (rows, LANES)), b))
        for b in range(row.shape[1] // LANES)
    ]


def summed_powers(stacked, weights_ref, rows, total):
    for power in range(1, POWERS + 1):
        total = total + stacked[(power - 1) * rows:power * rows] * weights_ref[power - 1:power, :]
    return total


def sent_rows(send_ref, swaps):
    rows = []
    for axis, _, low, high, _ in swaps:
        odd, even = send_ref[high:high + 1, :], send_ref[low:low + 1, :]
        rows.append(jnp.where(is_odd(axis), odd, even))
    return rows


def first_kernel(swaps, *refs):
    (fields_hbm, *given), refs = refs[:ARGUMENTS], refs[ARGUMENTS:]
    (columns_ref, out_ref), refs = refs[:2], refs[2:]
    sends, refs = refs[:len(swaps)], refs[len(swaps):]
    *held, fields_ref, arrived = refs
    rows = out_ref.shape[0]
    elements = out_ref.shape[1]
    count = elements // LANES
    comp = fields_hbm.shape[0] // count
    trace_hbm, send_hbm, *others = given
    trace_ref, send_ref, *others_held = held
    pairs = [(fields_hbm, fields_ref.at[pl.ds(0, comp * count)]), (trace_hbm, trace_ref), (send_hbm, send_ref)]
    needed = len(pairs)
    pairs += [(source, target if source.shape == target.shape else target.at[pl.ds(0, source.shape[0])])
              for source, target in zip(others, others_held)]
    copies = [pltpu.make_async_copy(source, target, arrived.at[i]) for i, (source, target) in enumerate(pairs)]
    for copy in copies:
        copy.start()
    for copy in copies[:needed]:
        copy.wait()
    trace_high, trace_low = split(pad_rows(trace_ref[...], rows))
    fields = jnp.concatenate([fields_ref[pl.ds(b, comp, stride=count), :] for b in range(count)], axis=1)
    high, low = split(fields)
    upper = product(jnp.concatenate([trace_high, trace_low], axis=0), high)
    out_ref[...] = upper[:rows] + upper[rows:] + product(trace_high, low)
    for index, send in zip(sent_rows(send_ref, swaps), sends):
        send[...] = pick(ref_blocks(out_ref, count), index, index >> 7)[:send.shape[0]]
    columns_ref[...] = pad_rows(fields, columns_ref.shape[0])
    for copy in copies[needed:]:
        copy.wait()


def faces_in(joined_ref):
    return joined_ref.shape[0] // 2


def own_block(level, block, members_ref, joined_ref, columns_ref, heights_ref, own_ref, weights_ref):
    faces = faces_in(joined_ref)
    here, there = block_at(block), block_at(level * (BLOCK // LANES) + block)
    index = members_ref[0:1, there]
    own_ref[:, here] = pick(ref_blocks(columns_ref, columns_ref.shape[1] // LANES), index, index >> 7)
    pattern = jnp.broadcast_to(joined_ref[faces:faces + 1, there], (8, LANES))
    height = jnp.take_along_axis(
        jnp.broadcast_to(heights_ref[...], (8, LANES)), pattern, axis=1, mode="promise_in_bounds")
    weight = jnp.ones((8, LANES), f32)
    for power in range(1, POWERS + 1):
        weight = weight * height
        weights_ref[power - 1:power, here] = weight[0:1] * WEIGHTS[power]


def face_block(level, block, joined_ref, out_ref, faces_ref):
    trace_rows = out_ref.shape[0]
    here, there = block_at(block), block_at(level * (BLOCK // LANES) + block)
    for face in range(faces_in(joined_ref)):
        index = joined_ref[face:face + 1, there]
        faces_ref[face * trace_rows:(face + 1) * trace_rows, here] = pick(
            ref_blocks(out_ref, out_ref.shape[1] // LANES), index, index >> 7, jnp.zeros((trace_rows, LANES), f32))


def advanced_traces(loaded, matrix_ref, weights_ref, rows):
    stacked = product(matrix_ref[...], stacked_columns(loaded))
    return summed_powers(stacked[rows:], weights_ref, rows, stacked[:rows])


def local_messages(level, trace_ref, send_places_ref, sent, messages):
    for group, (before, message) in enumerate(zip(sent, messages)):
        index = send_places_ref[group:group + 1, :]
        which = (index >> 7) - level * (BLOCK // LANES)
        message[...] = pick(
            ref_blocks(trace_ref, BLOCK // LANES), index, which, pad_rows(before[...], message.shape[0]))


def row_chunks(rows):
    return [slice(low, low + ROW_CHUNK) for low in range(0, rows, ROW_CHUNK)]


def grown_rows(chunk, stacked, loaded, grow_ref, weights_ref):
    rows = loaded.shape[0]
    matrix = jnp.concatenate(
        [grow_ref[power * rows + chunk.start:power * rows + chunk.stop, :] for power in range(POWERS)], axis=0)
    return summed_powers(product(matrix, stacked), weights_ref, chunk.stop - chunk.start, loaded[chunk])


def matrix_powers(operator_ref, trace_ref, lift_ref, grow_ref, trace_grow_ref, mix_ref, lift_out_ref,
                  lift_first_ref):
    comp = operator_ref.shape[0]
    faces = lift_ref.shape[1]
    trace_comp = trace_ref.shape[0]
    rows = lift_out_ref.shape[0]
    trace_rows = trace_grow_ref.shape[0] // (POWERS + 1)
    operator = pad_rows(operator_ref[...], rows)
    operator = jnp.concatenate([operator, jnp.zeros((rows, rows - comp), f32)], axis=1)
    traces = pad_rows(trace_ref[...], trace_rows)
    traces = jnp.concatenate([traces, jnp.zeros((trace_rows, rows - comp), f32)], axis=1)
    filled = lax.broadcasted_iota(i32, (trace_rows, comp), 0) < trace_comp
    lift = jnp.concatenate([jnp.where(filled, lift_ref[:, face, :], 0.0) for face in range(faces)], axis=0)
    lift = pad_rows(jnp.transpose(lift), rows)
    lift_out_ref[...] = stacked_matrix(lift)
    lift_first_ref[...] = stacked_matrix(lift[:, :trace_rows])
    powers, have = operator, 1
    while have < POWERS:
        more = exact_product(jnp.concatenate([traces, powers], axis=0), powers[(have - 1) * rows:have * rows])
        traces = jnp.concatenate([traces, more[:have * trace_rows]], axis=0)
        powers = jnp.concatenate([powers, more[have * trace_rows:]], axis=0)
        have *= 2
        yield
    traces = jnp.concatenate([traces, exact_product(traces[:trace_rows], powers[-rows:])], axis=0)
    trace_grow_ref[...] = stacked_matrix(traces)
    yield
    mix_ref[...] = stacked_matrix(exact_product(traces, lift[:, :trace_rows]))
    grow_ref[...] = stacked_matrix(powers)
    yield


def plan_kernel(swaps, *refs):
    (trace_ref, send_ref, order_ref, pattern_ref, sizes_ref, neighbours_ref, operator_ref, lift_ref, heights_ref,
     columns_ref, out_ref), refs = refs[:11], refs[11:]
    messages = len(swaps)
    sent, refs = refs[:messages], refs[messages:]
    (members_ref, joined_ref, places_ref, send_places_ref, send_codes_ref, slot_weights_ref, flags_ref, loaded_ref,
     weights_ref, new_trace_ref, grow_ref, trace_grow_ref, mix_ref, lift_out_ref, lift_first_ref,
     wide_heights_ref), refs = refs[:16], refs[16:]
    prepared, (faces_ref,) = refs[:messages], refs[messages:]
    elements = columns_ref.shape[1]
    count = elements // LANES
    faces = neighbours_ref.shape[0]
    steps = matrix_powers(operator_ref, trace_ref, lift_ref, grow_ref, trace_grow_ref, mix_ref, lift_out_ref,
                          lift_first_ref)
    next(steps)
    sizes = sizes_ref[...].astype(f32)
    number = lax.broadcasted_iota(i32, sizes.shape, 1)
    starts = [jnp.sum(jnp.where(number < level, sizes, 0.0)).astype(i32) for level in range(LEVELS)]
    wide_order = jnp.broadcast_to(order_ref[...], (8, elements))
    neighbours = neighbours_ref[...]
    group = (neighbours >> 7) - count
    message = jnp.full(neighbours.shape, count + len(swaps), i32)
    for number, swap in enumerate(swaps):
        message = jnp.where(group == came_group(swap), count + number, message)
    neighbours = jnp.where(group >= 0, message * LANES + (neighbours & (LANES - 1)), neighbours)
    table = jnp.concatenate(
        [neighbours, pattern_ref[...], jnp.zeros((faces - 1, elements), i32)], axis=0)
    heights = heights_ref[...]
    wide_heights_ref[...] = jnp.concatenate(
        [heights, jnp.zeros((1, LANES - heights.shape[1]), f32)], axis=1)
    for level in range(LEVELS):
        shift = jnp.where(starts[level] == 0, 0, elements - starts[level])
        members_ref[:, level * BLOCK:(level + 1) * BLOCK] = pltpu.roll(wide_order, shift, 1)[:, :BLOCK]
    for block in range(LEVELS * BLOCK // LANES):
        index = members_ref[:, block_at(block)]
        joined_ref[:, block_at(block)] = pick(value_blocks(table), index, index >> 7)
    ranks = lax.broadcasted_iota(i32, (count, elements), 1)
    in_block = (wide_order[:count] >> 7) == lax.broadcasted_iota(i32, (count, elements), 0)
    left = jnp.concatenate([
        jnp.where(in_block, ranks >> 5, 0).astype(f32), jnp.where(in_block, ranks & 31, 0).astype(f32)], axis=0)
    at_lane = jnp.broadcast_to(order_ref[...] & (LANES - 1), (LANES, elements)) == lax.broadcasted_iota(
        i32, (LANES, elements), 0)
    rank = lax.dot_general(left.astype(bf16), jnp.where(at_lane, 1.0, 0.0).astype(bf16), (((1,), (1,)), ((), ())),
                           preferred_element_type=f32)
    place = rank[:count].astype(i32) * 32 + rank[count:].astype(i32)
    at = place
    for level in range(1, LEVELS):
        at = jnp.where(place >= starts[level], place - starts[level] + level * BLOCK, at)
    places_ref[...] = at
    index = pad_rows(jnp.concatenate(sent_rows(send_ref, swaps), axis=0), 8)
    send_places_ref[...] = pick(row_blocks(at, 8), index, index >> 7)
    send_codes_ref[...] = pick(row_blocks_of(neighbours[:1], 8), index, index >> 7)
    block = jnp.broadcast_to(neighbours[:1] >> 7, (8, elements)) - count
    named = jnp.where(block == lax.broadcasted_iota(i32, (8, elements), 0),
                      jnp.broadcast_to(pattern_ref[...], (8, elements)), 0).astype(f32).astype(bf16)
    slot_lane = jnp.broadcast_to(neighbours[:1] & (LANES - 1), (LANES, elements)) == lax.broadcasted_iota(
        i32, (LANES, elements), 0)
    slot_pattern = lax.dot_general(named, jnp.where(slot_lane, 1.0, 0.0).astype(bf16), (((1,), (1,)), ((), ())),
                                   preferred_element_type=f32).astype(i32)
    height = jnp.take_along_axis(jnp.broadcast_to(wide_heights_ref[...], (8, LANES)), slot_pattern & (LANES - 1),
                                 axis=1, mode="promise_in_bounds")
    weight = jnp.ones((8, LANES), f32)
    for power in range(1, POWERS + 1):
        weight = weight * height
        for number in range(messages):
            slot_weights_ref[power - 1:power, block_at(number)] = weight[number:number + 1] * WEIGHTS[power]
    for level in range(LEVELS):
        code = joined_ref[1:faces, level * BLOCK:(level + 1) * BLOCK]
        code = jnp.max(jnp.where(code >= elements, 1.0, 0.0), axis=0, keepdims=True)
        row = code[:, block_at(0)]
        for number in range(1, BLOCK // LANES):
            row = jnp.maximum(row, code[:, block_at(number)])
        flags_ref[level:level + 1, :] = row
    next(steps)
    for block in range(BLOCK // LANES):
        own_block(0, block, members_ref, joined_ref, columns_ref, wide_heights_ref, loaded_ref, weights_ref)
        face_block(0, block, joined_ref, out_ref, faces_ref)
        next(steps)
    loaded = loaded_ref[...] + product(lift_out_ref[...], stacked_columns(faces_ref[...]))
    loaded_ref[...] = loaded
    new_trace_ref[...] = advanced_traces(loaded, trace_grow_ref, weights_ref, out_ref.shape[0])
    local_messages(0, new_trace_ref, send_places_ref, sent, prepared)


def settle(level, blocks, places_ref, before, block):
    index = places_ref[block:block + 1, :]
    which = (index >> 7) - level * (BLOCK // LANES)
    return pick(blocks, index, which, before)


def received_blocks(received, count, rows):
    return [(count + i, functools.partial(lambda ref: pad_rows(ref[...], rows), ref)) for i, ref in enumerate(received)]


def received_traces(level, face, received, joined_ref, count):
    parts = []
    for block in range(BLOCK // LANES):
        index = joined_ref[face:face + 1, block_at(level * (BLOCK // LANES) + block)]
        rows = rounded_up(received[0].shape[0], 16)
        zeros = jnp.zeros((rows, LANES), f32)
        parts.append(pick(received_blocks(received, count, rows), index, index >> 7, zeros))
    return jnp.concatenate(parts, axis=1)


def gather_received(level, low, received, joined_ref, count, traces_ref):
    faces = faces_in(joined_ref)
    rows = traces_ref.shape[0] // faces
    if low:
        traces_ref[:low * rows, :] = jnp.zeros((low * rows, traces_ref.shape[1]), f32)

    def step(face, carry):
        for block in range(BLOCK // LANES):
            there = block_at(level * (BLOCK // LANES) + block)
            index = joined_ref[low:low + 1, there]
            for other in range(low + 1, faces):
                index = jnp.where(face == other, joined_ref[other:other + 1, there], index)
            traces_ref[pl.ds(pl.multiple_of(face * rows, rows), rows), block_at(block)] = pick(
                received_blocks(received, count, rows), index, index >> 7, jnp.zeros((rows, LANES), f32))
        return carry

    lax.fori_loop(low, faces, step, 0)


def for_blocks(body):
    def step(block, carry):
        body(pl.ds(pl.multiple_of(block * LANES, LANES), LANES))
        return carry

    lax.fori_loop(0, BLOCK // LANES, step, 0)


def any_other(level, flags_ref):
    return jnp.max(flags_ref[level:level + 1, :]) > 0.0


def between_kernel(level, messages, members_ref, joined_ref, places_ref, columns_ref, old_out_ref, old_trace_ref,
                   moved_ref, extra_ref, extra_trace_ref, heights_ref, local_ref, old_weights_ref, lift_ref,
                   lift_first_ref, grow_ref, trace_grow_ref, send_places_ref, *rest):
    received, rest = rest[:messages], rest[messages:]
    final = level == LEVELS - 1
    if not final:
        sent, rest = rest[:messages], rest[messages:]
    if level > 1:
        advanced_ref, rest = rest[0], rest[1:]
    if final:
        loaded_ref, weights_ref, new_advanced_ref, out_ref, faces_ref, trace_ref, whole_ref = rest
    else:
        out_ref, loaded_ref, weights_ref, new_trace_ref, new_advanced_ref = rest[:5]
        prepared, (faces_ref, trace_ref, whole_ref) = rest[5:5 + messages], rest[5 + messages:]
    count = places_ref.shape[0]
    done = level - 1
    first = received_traces(done, 0, received, joined_ref, count)
    inflow = product(lift_first_ref[...], stacked_columns(first))
    for block in range(BLOCK // LANES):
        here = block_at(block)
        index = joined_ref[0:1, block_at(done * (BLOCK // LANES) + block)]
        moved = [(count + i, read) for i, read in ref_blocks(moved_ref, messages)]
        trace_ref[:, here] = old_trace_ref[:, here] + extra_trace_ref[:, here] + pick(
            moved, index, index >> 7, jnp.zeros((old_trace_ref.shape[0], LANES), f32))
    whole = local_ref[...] + inflow + extra_ref[...]
    stacked = stacked_columns(whole)
    chunks = row_chunks(whole.shape[0])
    pieces = BLOCK // LANES

    def gather_own(part):
        for block in range(part * pieces // len(chunks), (part + 1) * pieces // len(chunks)):
            own_block(level, block, members_ref, joined_ref, columns_ref, heights_ref, loaded_ref, weights_ref)

    def gather_faces(part):
        for block in range(part * pieces // len(chunks), (part + 1) * pieces // len(chunks)):
            face_block(level, block, joined_ref, out_ref, faces_ref)

    def put_out(part):
        for block in range(part * count // len(chunks), (part + 1) * count // len(chunks)):
            here = block_at(block)
            out_ref[:, here] = settle(
                done, ref_blocks(trace_ref, pieces), places_ref, old_out_ref[:, here], block)

    def put_columns(chunk):
        for block in range(count):
            here = block_at(block)
            before = advanced_ref[chunk, here] if level > 1 else None
            new_advanced_ref[chunk, here] = settle(
                done, [(b, functools.partial(lambda b: whole_ref[chunk, block_at(b)], b)) for b in range(pieces)],
                places_ref, before, block)

    for part in range(len(chunks)):
        put_out(part)
    for part, chunk in enumerate(chunks):
        whole_ref[chunk, :] = grown_rows(chunk, stacked, whole, grow_ref, old_weights_ref)
        gather_own(part)
        gather_faces(part)
    loaded = loaded_ref[...] + product(lift_ref[...], stacked_columns(faces_ref[...]))
    put_columns(chunks[0])
    loaded_ref[...] = loaded
    if not final:
        traces = advanced_traces(loaded, trace_grow_ref, weights_ref, out_ref.shape[0])
    for chunk in chunks[1:]:
        put_columns(chunk)
    if not final:
        new_trace_ref[...] = traces
        local_messages(level, new_trace_ref, send_places_ref, sent, prepared)


def level_kernel(level, messages, count, flags_ref, joined_ref, weights_ref, slot_weights_ref, mix_ref, lift_ref,
                 trace_grow_ref, send_places_ref, send_codes_ref, *rest):
    received, rest = rest[:messages], rest[messages:]
    prepared, rest = rest[:messages], rest[messages:]
    moved_ref, extra_ref, extra_trace_ref, sends = rest[0], rest[1], rest[2], rest[3:3 + messages]
    traces_ref, = rest[3 + messages:]
    rows = moved_ref.shape[0]
    pieces = BLOCK // LANES
    other = any_other(level, flags_ref)
    arrived = jnp.concatenate([pad_rows(ref[...], rows) for ref in received], axis=1)
    stacked = product(mix_ref[...], stacked_columns(arrived))
    moved_ref[...] = summed_powers(stacked[rows:], slot_weights_ref, rows, stacked[:rows])
    extra_ref[...] = jnp.zeros(extra_ref.shape, f32)
    extra_trace_ref[...] = jnp.zeros(extra_trace_ref.shape, f32)
    moved = [(count + i, read) for i, read in ref_blocks(moved_ref, messages)]
    for group, (before, send) in enumerate(zip(prepared, sends)):
        place, code = send_places_ref[group:group + 1, :], send_codes_ref[group:group + 1, :]
        here = ((place >> 7) >= level * pieces) & ((place >> 7) < (level + 1) * pieces)
        total = before[...] + pick(moved, code, jnp.where(here, code >> 7, 0), jnp.zeros(before.shape, f32))
        send[...] = total[:send.shape[0]]

    @pl.when(other)
    def _():
        gather_received(level, 1, received, joined_ref, count, traces_ref)

        def add_block(here):
            extra = product(lift_ref[...], stacked_columns(traces_ref[:, here]))
            extra_ref[:, here] = extra
            extra_trace_ref[:, here] = advanced_traces(extra, trace_grow_ref, weights_ref[:, here], rows)

        for_blocks(add_block)
        for group, send in enumerate(sends):
            place = send_places_ref[group:group + 1, :]
            more = pick(
                ref_blocks(extra_trace_ref, pieces), place, (place >> 7) - level * pieces, jnp.zeros((rows, LANES), f32))
            send[...] = send[...] + more[:send.shape[0]]


def last_chunks(rows):
    units = rows // 16
    first = -(-units * 5 // 9)
    second = -(-(units - first) * 3 // 4)
    bounds = [0, first * 16, (first + second) * 16, rows]
    return [slice(low, high) for low, high in zip(bounds, bounds[1:]) if high > low]


def last_kernel(level, messages, flags_ref, joined_ref, local_ref, weights_ref, lift_ref, lift_first_ref, grow_ref,
                places_ref, advanced_ref, *rest):
    received, (final_hbm, final_ref, traces_ref, whole_ref, sent) = rest[:messages], rest[messages:]
    count = places_ref.shape[0]
    comp = final_hbm.shape[0] // count

    def finish(whole):
        stacked = stacked_columns(whole)
        copies = []

        def put(number, chunk, new):
            height = min(chunk.stop, comp) - chunk.start
            for block in range(count):
                done = settle(level, value_blocks(new), places_ref, advanced_ref[chunk, block_at(block)], block)
                final_ref[pl.ds(chunk.start * count + block, height, stride=count), :] = done[:height]
            part = pl.ds(chunk.start * count, height * count)
            copies.append(pltpu.make_async_copy(final_ref.at[part], final_hbm.at[part], sent.at[number]))
            copies[-1].start()

        ahead = None
        for number, chunk in enumerate(last_chunks(whole.shape[0])):
            new = grown_rows(chunk, stacked, whole, grow_ref, weights_ref)
            if ahead is not None:
                put(*ahead)
            ahead = (number, chunk, new)
        put(*ahead)
        for copy in copies:
            copy.wait()

    other = any_other(level, flags_ref)
    first = received_traces(level, 0, received, joined_ref, count)
    finish(local_ref[...] + product(lift_first_ref[...], stacked_columns(first)))

    @pl.when(other)
    def _():
        gather_received(level, 0, received, joined_ref, count, traces_ref)

        def load_block(here):
            whole_ref[:, here] = local_ref[:, here] + product(lift_ref[...], stacked_columns(traces_ref[:, here]))

        for_blocks(load_block)
        rows, height = whole_ref.shape[0], 16

        def step(number, carry):
            start = pl.multiple_of(number * height, height)
            matrix = jnp.concatenate(
                [grow_ref[pl.ds(power * rows + start, height), :] for power in range(POWERS)], axis=0)
            new = summed_powers(product(matrix, stacked_columns(whole_ref[...])), weights_ref, height,
                                whole_ref[pl.ds(start, height), :])
            for block in range(count):
                before = advanced_ref[pl.ds(start, height), block_at(block)]
                done = settle(level, value_blocks(new), places_ref, before, block)
                final_ref[pl.ds(start * count + block, height, stride=count), :] = done
            return carry

        lax.fori_loop(0, rows // height, step, 0)
        copy = pltpu.make_async_copy(final_ref.at[pl.ds(0, comp * count)], final_hbm, sent.at[0])
        copy.start()
        copy.wait()


def call(kernel, name, flops, operands, outs, scratch=(), hbm=False, out_hbm=False):
    vmem = pl.BlockSpec(memory_space=pltpu.VMEM)
    given = pl.BlockSpec(memory_space=pltpu.HBM) if hbm else vmem
    if hbm:
        operands = [pltpu.with_memory_space_constraint(one, pltpu.HBM) for one in operands]
    return pl.pallas_call(
        kernel,
        out_shape=tuple(jax.ShapeDtypeStruct(shape, dtype) for shape, dtype in outs),
        in_specs=[given] * len(operands),
        out_specs=tuple([pl.BlockSpec(memory_space=pltpu.HBM) if out_hbm else vmem] * len(outs)),
        scratch_shapes=[one if not isinstance(one, tuple) else pltpu.VMEM(*one) for one in scratch],
        compiler_params=pltpu.CompilerParams(vmem_limit_bytes=16 * 1024 * 1024),
        cost_estimate=pl.CostEstimate(flops=flops, bytes_accessed=1 << 20, transcendentals=0),
        name=name,
    )(*operands)


def is_odd(axis):
    return (lax.axis_index(axis) & 1) == 1


def swap_plan(axis, periodic, low, high):
    count = lax.axis_size(axis)
    plan = [(axis, [(i, i ^ 1) for i in range(count)], low, high, False)]
    if count > 2 or periodic:
        pairs = [(i, (i + 1) % count if i % 2 else (i - 1) % count) for i in range(count)]
        plan.append((axis, pairs, high, low, not periodic))
    return plan


def came_group(swap):
    axis, _, even, odd, is_open = swap
    came = jnp.where(is_odd(axis), even, odd)
    if is_open:
        index = lax.axis_index(axis)
        came = jnp.where((index == 0) | (index == lax.axis_size(axis) - 1), NO_GROUP, came)
    return came


def body(fields, pattern, tent_order, level_sizes, send_rows, neighbours, operator, trace_map, lift_map, tent_height):
    fields, order, sizes = fields[0, 0], tent_order[0], level_sizes[0]
    faces_of, send_list = neighbours[0, 0], send_rows[0, 0]
    comp, elements = fields.shape
    faces, trace = lift_map.shape[0], trace_map.shape[0]
    rows, trace_rows = rounded_up(comp, 16), rounded_up(trace, 16)
    padded, count = LEVELS * BLOCK, elements // LANES
    bnd = send_list.shape[-1]

    near, *far = swap_plan("sector", True, 0, 1)
    swaps = far + [near] + swap_plan("radial", False, 2, 3)
    messages = len(swaps)

    def exchange(sent):
        return [lax.ppermute(one, swap[0], swap[1]) for one, swap in zip(sent, swaps)]

    message = ((trace_rows, bnd), f32)
    own, face_stack = ((rows, BLOCK), f32), ((faces * trace_rows, BLOCK), f32)
    weight, table, traced = ((POWERS, BLOCK), f32), ((trace_rows, elements), f32), ((trace_rows, BLOCK), f32)
    whole = ((rows, elements), f32)
    flat = (comp * count, LANES)

    arguments = [trace_map, send_list, order, pattern[0], sizes, faces_of, operator,
                 jnp.transpose(lift_map, (2, 0, 1)), tent_height[None]]
    columns, out, *rest = call(
        functools.partial(first_kernel, swaps), "first", 10 ** 8, [fields.reshape(flat)] + arguments,
        [whole, table] + [message] * messages
        + [((trace_rows,) + one.shape[1:] if one.ndim == 3 else one.shape, one.dtype) for one in arguments],
        [((rows * count, LANES), f32), pltpu.SemaphoreType.DMA((ARGUMENTS,))], hbm=True)
    sent, held = rest[:messages], rest[messages:]
    received = exchange(sent)
    slots = ((trace_rows, messages * LANES), f32)
    (members, joined, places, send_places, send_codes, slot_weights, flags, loaded, weights, new_trace, grow,
     trace_grow, mix, lift, lift_first, heights, *prepared) = call(
        functools.partial(plan_kernel, swaps), "plan", 2 * 10 ** 9, held + [columns, out] + sent,
        [((8, padded), i32), ((2 * faces, padded), i32), ((count, LANES), i32), ((8, bnd), i32), ((8, bnd), i32),
         ((POWERS, messages * LANES), f32), ((LEVELS, LANES), f32), own, weight, traced,
         ((POWERS * rows, 3 * rows), bf16), (((POWERS + 1) * trace_rows, 3 * rows), bf16),
         (((POWERS + 1) * trace_rows, 3 * trace_rows), bf16), ((rows, 3 * faces * trace_rows), bf16), ((rows, 3 * trace_rows), bf16), ((1, LANES), f32)]
        + [message] * messages, [face_stack])
    advanced = []
    for level in range(LEVELS - 1):
        moved, extra, extra_trace, *sent = call(
            functools.partial(level_kernel, level, messages, count), "level", 10 ** 8,
            [flags, joined, weights, slot_weights, mix, lift, trace_grow, send_places, send_codes] + received + prepared,
            [slots, own, traced] + [message] * messages, [face_stack])
        arrived, received = received, exchange(sent)
        beside = functools.partial(between_kernel, level + 1, messages)
        operands = [members, joined, places, columns, out, new_trace, moved, extra, extra_trace, heights, loaded,
                    weights, lift, lift_first, grow, trace_grow, send_places] + arrived
        scratch = [face_stack, traced, own]
        if level + 1 < LEVELS - 1:
            out, loaded, weights, new_trace, *rest = call(
                beside, "between", 2 * 10 ** 9, operands + sent + advanced,
                [table, own, weight, traced, whole] + [message] * messages, scratch)
            advanced, prepared = rest[:1], rest[1:]
        else:
            loaded, weights, *advanced = call(
                beside, "between", 2 * 10 ** 9, operands + advanced, [own, weight, whole], [table] + scratch)
    final, = call(
        functools.partial(last_kernel, LEVELS - 1, messages), "last", 10 ** 9,
        [flags, joined, loaded, weights, lift, lift_first, grow, places] + advanced + received,
        [(flat, f32)],
        [((rows * count, LANES), f32), face_stack, own, pltpu.SemaphoreType.DMA((len(last_chunks(rows)),))], out_hbm=True)
    return final.reshape(1, 1, comp, elements)


def solution(mesh):
    in_specs = (
        P("sector", "radial", None, None),
        P("sector", "radial", None),
        P("sector", "radial", None),
        P("sector", "radial", None),
        P("sector", "radial", None, None),
        P("sector", "radial", None, None),
        P(),
        P(),
        P(),
        P(),
    )
    out_specs = P("sector", "radial", None, None)
    return jax.shard_map(body, mesh=mesh, in_specs=in_specs, out_specs=out_specs, check_vma=False)
```
